32 devices in a mesh: lon: 16 (over z, x, core), lat: 2 (over y).
Axes of the slice: x: 2, y: 2, z: 4, core: 2. Of those that a mesh axis runs over, the one named last changes fastest.
Arguments:
- cotangent: bfloat16 [128, 32, 512], P('lon', 'lat'), may hold values from -6 to 6
- states: bfloat16 [3, 128, 32, 512], P(None, 'lon', 'lat'), may hold values from -6 to 6
- w_up: bfloat16 [512, 1024], replicated, may hold values from -0.25 to 0.25
- w_down: bfloat16 [512, 1024], replicated, may hold values from -0.1875 to 0.1875
- norm_gain: float32 [512], replicated, may hold values from 0.5 to 1.5
- kernel: float32 [3, 3, 512], replicated, may hold values from -0.6 to 0.6
- bilinear: float32 [3, 4, 128, 32], P(None, None, 'lon', 'lat'), may hold values from 0.05 to 0.5
- lon_move: int32 [3, 4], replicated, may hold values from 0 to 63, as said below
- lat_move: int32 [3, 4], replicated, may hold values from 0 to 31
Outputs:
- grad_state: bfloat16 [128, 32, 512], P('lon', 'lat')
- grad_up: float32 [512, 1024], P('lon', 'lat')
- grad_down: float32 [512, 1024], P('lon', 'lat')
- grad_kernel: float32 [3, 3, 512], replicated
- grad_gain: float32 [512], replicated
The draws below stay inside these ranges and needn't reach their ends.
Inputs may be any that keep to these rules, and one draw needn't show every extreme that they name: `lon_move`: a whole number of longitude tiles below 8, times 8, plus an offset below 8.
All inputs are finite; a program needn't handle non-finite values.
Results may differ from the reference program's by a relative error of at most 0.02.
Values may be sent and summed in bfloat16 or wider, within the bound.
No kernel may reach another device: no remote copies, remote signals or barrier semaphores. Data moves between devices by JAX's collectives and lax.ppermute only.
A program may use at most 64 MiB of HBM per device.

```python
import jax
import jax.numpy as jnp
from jax import lax

GROUP = 128
GROUPS = 4
HID = 1024
STEPS = 3
REACH = 8
CLON = 8
CLAT = 16
C = 512
NLON = 128
NLAT = 32


def draw_lon_move(key, part):
    tile_steps = jax.random.randint(jax.random.fold_in(key, 11), (STEPS, GROUPS), 0, REACH)
    levels = REACH.bit_length() - 1
    forced = jnp.array([1 << group_index % levels for group_index in range(GROUPS)], jnp.int32)
    tile_steps = jnp.bitwise_or(tile_steps, forced[None, :])
    offsets = jax.random.randint(jax.random.fold_in(key, 12), (STEPS, GROUPS), 0, CLON)
    return (tile_steps * CLON + offsets).astype(jnp.int32)


def draw_lat_move(key, part):
    upper_tile = jax.random.randint(jax.random.fold_in(key, 21), (STEPS, GROUPS), 0, 2)
    step_iota = lax.broadcasted_iota(jnp.int32, (STEPS, GROUPS), 0)
    group_iota = lax.broadcasted_iota(jnp.int32, (STEPS, GROUPS), 1)
    upper_tile = jnp.where(group_iota == step_iota % GROUPS, 1, upper_tile)
    offsets = jax.random.randint(jax.random.fold_in(key, 22), (STEPS, GROUPS), 0, CLAT)
    return (upper_tile * CLAT + offsets).astype(jnp.int32)


def block_levels(key, shape, cuts, least, top_value):
    loudness, own = 1.0, jax.random.fold_in(key, 6)
    for axis_at, shards_of in cuts:
        draws = jnp.exp(jax.random.uniform(jax.random.fold_in(own, axis_at), (shards_of,), jnp.float32, least / len(cuts), top_value / len(cuts)))
        loudness = loudness * jnp.repeat(draws, shape[axis_at] // shards_of).reshape([-1 if axis == axis_at else 1 for axis in range(len(shape))])
    return loudness


def gaussian(key, extent, deviation, limit, split=(), held_as=jnp.bfloat16):
    entries = jax.random.normal(key, extent, jnp.float32) * deviation
    if len(split) > 0:
        entries = block_levels(key, extent, split, -0.22, 0.18) * entries
    return jnp.clip(entries, min=-limit, max=limit).astype(held_as)


def setup_inputs(seed: int = 0) -> dict:
    key_list = jax.random.split(jax.random.key(seed), 10)
    return {
        "cotangent": gaussian(key_list[0], (NLON, NLAT, C), 1.0, 6.0, ((0, 16), (1, 2))),
        "states": gaussian(key_list[1], (STEPS, NLON, NLAT, C), 1.0, 6.0, ((1, 16), (2, 2))),
        "w_up": gaussian(key_list[2], (C, HID), C ** -0.5, 0.25),
        "w_down": gaussian(key_list[3], (C, HID), HID ** -0.5, 0.1875),
        "norm_gain": jnp.clip(1.0 + 0.1 * jax.random.normal(key_list[4], (C,), jnp.float32), 0.5, 1.5),
        "kernel": gaussian(key_list[5], (3, 3, C), 0.15, 0.6, (), jnp.float32),
        "bilinear": jnp.clip(0.05 + 0.45 * jax.random.uniform(key_list[6], (STEPS, 4, NLON, NLAT), jnp.float32) ** block_levels(key_list[6], (STEPS, 4, NLON, NLAT), ((2, 16), (3, 2)), -0.2, 0.2), 0.05, 0.5),
        "lon_move": draw_lon_move(jax.random.fold_in(key_list[9], 71), 0),
        "lat_move": draw_lat_move(jax.random.fold_in(key_list[9], 71), 0),
    }


EPSILON = 1e-06

def widen_field(field):
    beside_all = jnp.concatenate([field[-1:], field, field[:1]], axis=0)
    return jnp.pad(beside_all, ((0, 0), (1, 1), (0, 0)))

def tapped(padded, kernel, rows_out, cols_out, mirror):
    running = jnp.zeros((rows_out, cols_out, padded.shape[2]), jnp.float32)
    for row_tap in range(3):
        for col_tap in range(3):
            start_row = 2 - row_tap if mirror else row_tap
            start_col = 2 - col_tap if mirror else col_tap
            window = padded[start_row:start_row + rows_out, start_col:start_col + cols_out].astype(jnp.float32)
            running = running + kernel[row_tap, col_tap] * window
    return running

def next_lat(values):
    return jnp.concatenate([values[:, 1:], jnp.zeros_like(values[:, :1])], axis=1)

def step_back(state_now, upstream, w_up, w_down, norm_gain, kernel, weights_now, lon_now, lat_now):
    rows_out, cols_out, channels = state_now.shape
    padded_state = widen_field(state_now)
    mixed_field = state_now.astype(jnp.float32) + tapped(padded_state, kernel, rows_out, cols_out, False)
    inv_root = lax.rsqrt(lax.optimization_barrier(jnp.mean(mixed_field * mixed_field, axis=-1, keepdims=True)) + EPSILON)
    normed = mixed_field * inv_root
    normed_rows = (normed * norm_gain).astype(jnp.bfloat16).reshape(-1, channels)
    hidden_pre = jnp.dot(normed_rows, w_up, preferred_element_type=jnp.float32)
    hidden = jax.nn.silu(hidden_pre).astype(jnp.bfloat16)
    upstream_f = upstream.astype(jnp.float32)
    weighted = [weights_now[corner][:, :, None] * upstream_f for corner in range(4)]
    spread = weighted[0] + jnp.roll(weighted[1], -1, axis=0) + next_lat(weighted[2])
    spread = spread + next_lat(jnp.roll(weighted[3], -1, axis=0))
    spread = spread.astype(jnp.bfloat16)
    pieces = []
    for group_index in range(GROUPS):
        group_piece = spread[:, :, group_index * GROUP:(group_index + 1) * GROUP]
        group_piece = jnp.roll(group_piece, -lon_now[group_index], axis=0)
        padded = jnp.concatenate([group_piece, jnp.zeros_like(group_piece)], axis=1)
        pieces.append(lax.dynamic_slice_in_dim(padded, lat_now[group_index], cols_out, 1))
    moved_back = jnp.concatenate(pieces, axis=2)
    moved_rows = moved_back.reshape(-1, channels)
    grad_hidden = jnp.dot(moved_rows, w_down, preferred_element_type=jnp.float32)
    sigmoid_pre = jax.nn.sigmoid(hidden_pre)
    grad_pre = (grad_hidden * sigmoid_pre * (1.0 + hidden_pre * (1.0 - sigmoid_pre))).astype(jnp.bfloat16)
    grad_normed = lax.dot_general(grad_pre, w_up, (((1,), (1,)), ((), ())), preferred_element_type=jnp.float32)
    grad_normed = grad_normed.reshape(rows_out, cols_out, channels)
    lead_contract = (((0,), (0,)), ((), ()))
    term_up = lax.dot_general(normed_rows, grad_pre, lead_contract, preferred_element_type=jnp.float32)
    term_down = lax.dot_general(moved_rows, hidden, lead_contract, preferred_element_type=jnp.float32)
    term_gain = lax.optimization_barrier(jnp.sum(grad_normed * normed, axis=(0, 1)))
    scaled = grad_normed * norm_gain
    grad_mixed = inv_root * (scaled - normed * lax.optimization_barrier(jnp.mean(scaled * normed, axis=-1, keepdims=True)))
    grad_field = (moved_back.astype(jnp.float32) + grad_mixed).astype(jnp.bfloat16)
    padded_grad = widen_field(grad_field)
    result = grad_field.astype(jnp.float32) + tapped(padded_grad, kernel, rows_out, cols_out, True)
    grad_f = grad_field.astype(jnp.float32)
    term_kernel = jnp.stack([jnp.stack([lax.optimization_barrier(jnp.sum(padded_state[row_tap:row_tap + rows_out, col_tap:col_tap + cols_out].astype(jnp.float32) * grad_f, axis=(0, 1))) for col_tap in range(3)]) for row_tap in range(3)])
    return (result.astype(jnp.bfloat16), term_up, term_down, term_kernel, term_gain)

def reference(cotangent, states, w_up, w_down, norm_gain, kernel, bilinear, lon_move, lat_move):
    upstream = cotangent
    acc_up = jnp.zeros(w_up.shape, jnp.float32)
    acc_down = jnp.zeros(w_down.shape, jnp.float32)
    acc_kernel = jnp.zeros(kernel.shape, jnp.float32)
    acc_gain = jnp.zeros(norm_gain.shape, jnp.float32)
    for index_step in reversed(range(STEPS)):
        upstream, term_up, term_down, term_kernel, term_gain = step_back(states[index_step], upstream, w_up, w_down, norm_gain, kernel, bilinear[index_step], lon_move[index_step], lat_move[index_step])
        acc_up = acc_up + term_up
        acc_down = acc_down + term_down
        acc_kernel = acc_kernel + term_kernel
        acc_gain = acc_gain + term_gain
    return (upstream, acc_up, acc_down, acc_kernel, acc_gain)
```

```python
import functools

import jax
import jax.numpy as jnp
from jax import lax
from jax.experimental import pallas as pl
from jax.experimental.pallas import tpu as pltpu
from jax.sharding import PartitionSpec as P

EPSILON = 1e-06
AXES = ("lon", "lat")
ROWS = 16
LAT_REACH = 2
VMEM_LIMIT = 40 * 1024 * 1024


def with_halo(block, sides, width, periodic):
    for axis, dim in sides:
        count = lax.axis_size(axis)
        forward = [(i, i + 1) for i in range(count - 1)]
        if periodic:
            forward.append((count - 1, 0))
        backward = [(target, source) for source, target in forward]
        low = lax.ppermute(
            lax.slice_in_dim(block, block.shape[dim] - width, None, axis=dim), axis, forward
        )
        high = lax.ppermute(lax.slice_in_dim(block, 0, width, axis=dim), axis, backward)
        block = jnp.concatenate([low, block, high], axis=dim)
    return block


def pieces_of(value, count):
    parts = []
    for _ in range(count):
        part = lax.reduce_precision(value, 8, 7)
        parts.append(part.astype(jnp.bfloat16))
        value = value - part
    return parts


def exchanged(blocks):
    return lax.all_to_all(blocks, AXES, split_axis=0, concat_axis=0, tiled=True)


def call(kernel, out_shape, *operands, scratch=(), scalars=0, flops=0, moved=0):
    space = [pltpu.SMEM] * scalars + [pltpu.VMEM] * (len(operands) - scalars)
    return pl.pallas_call(
        kernel,
        out_shape=out_shape,
        in_specs=[pl.BlockSpec(memory_space=kind) for kind in space],
        out_specs=jax.tree.map(lambda _: pl.BlockSpec(memory_space=pltpu.VMEM), out_shape),
        scratch_shapes=scratch,
        compiler_params=pltpu.CompilerParams(vmem_limit_bytes=VMEM_LIMIT),
        cost_estimate=pl.CostEstimate(flops=flops, bytes_accessed=moved, transcendentals=0),
    )(*operands)


def forward_kernel(padded_ref, kernel_ref, gain_ref, up_ref, n_ref, normed_ref, inv_ref, hid_ref, slope_ref):
    rows_out, cols_out = padded_ref.shape[1] - 2, padded_ref.shape[2] - 2
    channels = padded_ref.shape[3]
    padded = padded_ref[0].astype(jnp.float32)
    mixed = padded[1 : 1 + rows_out, 1 : 1 + cols_out]
    running = jnp.zeros_like(mixed)
    for col_tap in range(3):
        shifted_cols = padded[:, col_tap : col_tap + cols_out]
        for row_tap in range(3):
            tap = kernel_ref[3 * row_tap + col_tap : 3 * row_tap + col_tap + 1]
            running = running + tap[None] * shifted_cols[row_tap : row_tap + rows_out]
    mixed = (mixed + running).reshape(rows_out * cols_out, channels).T
    inv_root = lax.rsqrt(jnp.mean(mixed * mixed, axis=0, keepdims=True) + EPSILON)
    normed = mixed * inv_root
    narrow = (normed * gain_ref[...]).astype(jnp.bfloat16)
    pre = jnp.dot(up_ref[...], narrow, preferred_element_type=jnp.float32)
    sigmoid = jax.nn.sigmoid(pre)
    n_ref[0] = narrow
    normed_ref[0] = normed
    inv_ref[0] = inv_root
    hid_ref[0] = (pre * sigmoid).astype(jnp.bfloat16)
    slope_ref[0] = sigmoid * (1.0 + pre * (1.0 - sigmoid))


def forward_parts(padded, kernel, gain, w_up_t):
    steps, rows_in, cols_in, channels = padded.shape
    hid = w_up_t.shape[0]
    count = (rows_in - 2) * (cols_in - 2)
    whole = lambda *shape: pl.BlockSpec(shape, lambda s: (0,) * len(shape))
    one = lambda *shape: pl.BlockSpec((1, *shape), lambda s: (steps - 1 - s, *([0] * len(shape))))
    sds = jax.ShapeDtypeStruct
    return pl.pallas_call(
        forward_kernel,
        grid=(steps,),
        in_specs=[one(rows_in, cols_in, channels), whole(9, channels), whole(channels, 1), whole(hid, channels)],
        out_specs=[one(channels, count), one(channels, count), one(1, count), one(hid, count), one(hid, count)],
        out_shape=[
            sds((steps, channels, count), jnp.bfloat16),
            sds((steps, channels, count), jnp.float32),
            sds((steps, 1, count), jnp.float32),
            sds((steps, hid, count), jnp.bfloat16),
            sds((steps, hid, count), jnp.float32),
        ],
        compiler_params=pltpu.CompilerParams(vmem_limit_bytes=VMEM_LIMIT),
        cost_estimate=pl.CostEstimate(
            flops=2 * steps * count * hid * channels, bytes_accessed=6 * 2**20, transcendentals=0
        ),
    )(padded, kernel.reshape(9, channels), gain, w_up_t)


def network_kernel(moved_ref, down_ref, up_ref, slope_ref, normed_ref, inv_ref, gain_ref, field_ref, grad_ref, term_ref):
    moved = moved_ref[...]
    grad_hidden = jnp.dot(down_ref[...], moved, preferred_element_type=jnp.float32)
    grad_pre = (grad_hidden * slope_ref[...]).astype(jnp.bfloat16)
    grad_ref[...] = grad_pre
    grad_n = jnp.dot(up_ref[...], grad_pre, preferred_element_type=jnp.float32)
    normed = normed_ref[...]
    term = grad_n * normed
    term_ref[...] = term
    gain = gain_ref[...]
    mean = jnp.mean(term * gain, axis=0, keepdims=True)
    field = moved.astype(jnp.float32) + inv_ref[...] * (grad_n * gain - normed * mean)
    field_ref[...] = field.astype(jnp.bfloat16)


def network_back(moved, w_down_t, w_up, slope, normed, inv_root, gain):
    channels, count = moved.shape
    hid = w_down_t.shape[0]
    sds = jax.ShapeDtypeStruct
    return call(
        network_kernel,
        [
            sds((channels, count), jnp.bfloat16),
            sds((hid, count), jnp.bfloat16),
            sds((channels, count), jnp.float32),
        ],
        moved,
        w_down_t,
        w_up,
        slope,
        normed,
        inv_root,
        gain,
        flops=4 * count * hid * channels,
        moved=4 * 2**20,
    )


def spatial_kernel(mode, near_lon, near_lat, *refs):
    refs = list(refs)
    take = lambda: refs.pop(0)
    with_move, with_stencil = mode != "last", mode != "first"
    move_ref = take() if with_move else None
    in_ref = take()
    state_ref, kern_ref = (take(), take()) if with_stencil else (None, None)
    weight_ref = take() if with_move else None
    out_ref = take()
    term_ref = take() if with_stencil else None
    high_ref, own_ref, low_ref, spread_ref = take(), take(), take(), take()
    tiles_lon, tiles_lat, rows, lanes = in_ref.shape
    lane = lax.broadcasted_iota(jnp.int32, (rows, lanes), 1)
    col = lax.rem(lane, near_lat)
    unroll = 16 if tiles_lon * tiles_lat <= 32 else 1
    zero = jnp.zeros((rows, lanes), jnp.float32)

    def turn(value, steps):
        return pltpu.roll(value, steps % lanes, 1) if isinstance(steps, int) else pltpu.roll(value, steps, 1)

    def lat_after(tiles):
        following = tiles[1:] + [None]
        return [
            jnp.where(col < near_lat - 1, turn(here, -1), 0.0 if after is None else turn(after, near_lat - 1))
            for here, after in zip(tiles, following)
        ]

    def lat_before(tiles):
        preceding = [None] + tiles[:-1]
        return [
            jnp.where(col > 0, turn(here, 1), 0.0 if before is None else turn(before, 1 - near_lat))
            for here, before in zip(tiles, preceding)
        ]

    def lon_after(here, after):
        return turn(jnp.where(lane < near_lat, after, here), -near_lat)

    def lon_before(here, before):
        return turn(jnp.where(lane >= lanes - near_lat, before, here), near_lat)

    def next_tile(a):
        return lax.rem(a + 1, tiles_lon)

    def last_tile(a):
        return lax.rem(a + tiles_lon - 1, tiles_lon)

    def read(ref, a):
        return [ref[a, b].astype(jnp.float32) for b in range(tiles_lat)]

    def loop(body, init=None):
        return lax.fori_loop(0, tiles_lon, body, init, unroll=unroll)

    if with_stencil:
        taps = [[kern_ref[3 * a + b] for b in range(3)] for a in range(3)]

        def mix(a, sums):
            here = read(in_ref, a)
            by_col = [lat_after(here), here, lat_before(here)]
            state, state_next, state_last = (read(state_ref, k) for k in (a, next_tile(a), last_tile(a)))
            sums = list(sums)
            for b in range(tiles_lat):
                by_row = [
                    lon_before(state[b], state_last[b]),
                    state[b],
                    lon_after(state[b], state_next[b]),
                ]
                mixes = []
                for row in range(3):
                    mixed = None
                    for c in range(3):
                        shifted = by_col[c][b]
                        sums[3 * row + c] = sums[3 * row + c] + by_row[row] * shifted
                        term = taps[row][c] * shifted
                        mixed = term if mixed is None else mixed + term
                    mixes.append(mixed)
                high_ref[a, b] = mixes[0]
                own_ref[a, b] = here[b] + mixes[1]
                low_ref[a, b] = mixes[2]
            return tuple(sums)

        sums = loop(mix, tuple(zero for _ in range(9)))
        for k in range(9):
            term_ref[k] = sums[k]

    def gather(a):
        if not with_stencil:
            return read(in_ref, a)
        result = []
        for b in range(tiles_lat):
            value = own_ref[a, b] + lon_after(high_ref[a, b], high_ref[next_tile(a), b])
            value = value + lon_before(low_ref[a, b], low_ref[last_tile(a), b])
            result.append(value)
        return result

    if not with_move:

        def finish(a, carry):
            for b, value in enumerate(gather(a)):
                out_ref[a, b] = value.astype(jnp.bfloat16)
            return carry

        loop(finish)
        return

    own2_ref, lon2_ref = refs

    def weigh(a, carry):
        here = [value.astype(jnp.bfloat16).astype(jnp.float32) for value in gather(a)]
        weights = [
            [weight_ref[a, b, k : k + 1].astype(jnp.float32) + weight_ref[a, b, 4 + k : 5 + k].astype(jnp.float32) for k in range(4)]
            for b in range(tiles_lat)
        ]
        own = lat_after([weights[b][2] * here[b] for b in range(tiles_lat)])
        lon = lat_after([weights[b][3] * here[b] for b in range(tiles_lat)])
        for b in range(tiles_lat):
            own2_ref[a, b] = weights[b][0] * here[b] + own[b]
            lon2_ref[a, b] = weights[b][1] * here[b] + lon[b]
        return carry

    loop(weigh)

    def spread(a, carry):
        for b in range(tiles_lat):
            value = own2_ref[a, b] + lon_after(lon2_ref[a, b], lon2_ref[next_tile(a), b])
            spread_ref[a, b] = value.astype(jnp.bfloat16).astype(jnp.float32)
        for b in range(LAT_REACH):
            spread_ref[a, tiles_lat + b] = zero
        return carry

    loop(spread)

    lon_move, lat_move = move_ref[0], move_ref[1]
    far_lon, off_lon = lon_move // near_lon, lax.rem(lon_move, near_lon)
    far_lat, off_lat = lat_move // near_lat, lax.rem(lat_move, near_lat)
    shift = off_lon * near_lat + off_lat
    turn_here = lax.rem(2 * lanes - shift, lanes)
    turn_next = lax.rem(2 * lanes - shift + near_lat, lanes)
    same_lon = lane >= off_lon * near_lat
    same_lat = col + off_lat < near_lat

    def move(a, carry):
        source = lax.rem(a + far_lon, tiles_lon)
        source_next = next_tile(source)
        for b in range(tiles_lat):
            here, after = (
                jnp.where(same_lon, spread_ref[source, far_lat + k], spread_ref[source_next, far_lat + k])
                for k in (b, b + 1)
            )
            value = jnp.where(same_lat, turn(here, turn_here), turn(after, turn_next))
            out_ref[a, b] = value.astype(jnp.bfloat16)
        return carry

    loop(move)


def spatial(mode, tile, field, state, kern, weights, moves):
    shape = field.shape
    tiles_lon, tiles_lat, rows, lanes = shape
    with_move, with_stencil = mode != "last", mode != "first"
    operands = ([moves] if with_move else []) + [field]
    operands += [state, kern] if with_stencil else []
    operands += [weights] if with_move else []
    sds = jax.ShapeDtypeStruct
    out = [sds(shape, jnp.bfloat16)]
    if with_stencil:
        out.append(sds((9, rows, lanes), jnp.float32))
    grid = pltpu.VMEM(shape, jnp.float32)
    scratch = [grid, grid, grid, pltpu.VMEM((tiles_lon, tiles_lat + LAT_REACH, rows, lanes), jnp.float32)]
    if with_move:
        scratch += [grid, grid]
    return call(
        functools.partial(spatial_kernel, mode, *tile),
        out,
        *operands,
        scratch=scratch,
        scalars=1 if with_move else 0,
        flops=2**22,
        moved=2**20,
    )


def halved(value, axis, bit, dim):
    count = lax.axis_size(axis)
    mine = lax.axis_index(axis) >> bit & 1
    kept = lax.dynamic_index_in_dim(value, mine, dim, keepdims=False)
    sent = lax.dynamic_index_in_dim(value, 1 - mine, dim, keepdims=False).astype(jnp.bfloat16)
    arrived = lax.ppermute(sent, axis, [(i, i ^ (1 << bit)) for i in range(count)])
    return kept + arrived.astype(jnp.float32)


def scattered(value, lat_first):
    channels, hid = value.shape
    lon_bits = lax.axis_size("lon").bit_length() - 1
    lat_bits = lax.axis_size("lat").bit_length() - 1
    rows = channels >> lon_bits
    value = value.reshape(*([2] * lon_bits), rows, *([2] * lat_bits), hid >> lat_bits)

    def over_lon(value, bit, left):
        return halved(value, "lon", bit, left.index(bit)), [k for k in left if k != bit]

    left_lon = list(range(lon_bits))[::-1]
    left_lat = list(range(lat_bits))[::-1]
    order = [("lon", 0), ("lon", 1)] + [("lat", k) for k in range(lat_bits)]
    if lat_first:
        order = [("lon", 0)] + [("lat", k) for k in range(lat_bits)] + [("lon", 1)]
    order += [("lon", k) for k in range(2, lon_bits)]
    for axis, bit in order:
        if axis == "lon":
            value, left_lon = over_lon(value, bit, left_lon)
        else:
            value = halved(value, "lat", bit, len(left_lon) + 1 + left_lat.index(bit))
            left_lat.remove(bit)
    return value


def local(cotangent, states, w_up, w_down, norm_gain, kernel, bilinear, lon_move, lat_move):
    steps, rows_out, cols_out, channels = states.shape
    tiles_lon, tiles_lat = lax.axis_size("lon"), lax.axis_size("lat")
    devices = tiles_lon * tiles_lat
    count = rows_out * cols_out
    tile = (rows_out, cols_out)
    share = channels // devices
    padded_share = -(-share // ROWS) * ROWS
    group_size = channels // lon_move.shape[1]
    me = lax.axis_index("lon") * tiles_lat + lax.axis_index("lat")

    def as_blocks(value):
        value = value.reshape(devices, share, count)
        if padded_share != share:
            value = jnp.pad(value, ((0, 0), (0, padded_share - share), (0, 0)))
        return value

    def as_rows(blocks):
        return blocks[:, :share].reshape(channels, count)

    def as_grid(blocks):
        return blocks.reshape(tiles_lon, tiles_lat, *blocks.shape[1:])

    weight_rows = pieces_of(bilinear.reshape(steps, 4, count), 2)
    weight_rows = jnp.concatenate(weight_rows, axis=1)

    def to_all(value):
        padding = -value.shape[0] % ROWS
        value = jnp.pad(value, ((0, padding), (0, 0)))
        return jnp.broadcast_to(value[None], (devices, *value.shape))

    blocks = as_blocks(cotangent.reshape(count, channels).T)
    arrived = exchanged(jnp.concatenate([blocks, to_all(weight_rows[steps - 1])], axis=1))
    grid_now = as_grid(arrived[:, :padded_share])
    weights = {steps - 1: as_grid(arrived[:, padded_share:])}

    state_blocks = [as_blocks(states[s].reshape(count, channels).T) for s in range(steps)]
    rest = [to_all(weight_rows[s]) for s in range(steps - 1)]
    arrived = exchanged(jnp.concatenate(state_blocks + rest, axis=1))
    grid_states = [as_grid(arrived[:, padded_share * s : padded_share * (s + 1)]) for s in range(steps)]
    for s in range(steps - 1):
        start = padded_share * steps + ROWS * s
        weights[s] = as_grid(arrived[:, start : start + ROWS])

    kern = lax.dynamic_slice_in_dim(kernel.reshape(9, channels), me * share, share, 1)
    kern = jnp.pad(kern, ((0, 0), (0, padded_share - share)))
    kern = jnp.broadcast_to(kern[:, :, None], (9, padded_share, count))
    group = me * share // group_size
    moves = jnp.stack([lon_move[:, group], lat_move[:, group]], axis=1)

    padded = with_halo(with_halo(states, (("lon", 1),), 1, True), (("lat", 2),), 1, False)
    gain = norm_gain[:, None]
    narrow, normed, inv_root, hidden, slope = forward_parts(padded, kernel, gain, w_up.T)
    w_down_t = w_down.T

    (grid_now,) = spatial("first", tile, grid_now, None, None, weights[steps - 1], moves[steps - 1])
    lanes_both = (((1,), (1,)), ((), ()))
    acc_up = acc_down = 0.0
    acc_gain = 0.0
    acc_kernel = 0.0
    for s in reversed(range(steps)):
        moved = as_rows(exchanged(grid_now.reshape(devices, padded_share, count)))
        field, grad_pre, term = network_back(moved, w_down_t, w_up, slope[s], normed[s], inv_root[s], gain)
        acc_up = acc_up + lax.dot_general(narrow[s], grad_pre, lanes_both, preferred_element_type=jnp.float32)
        acc_down = acc_down + lax.dot_general(moved, hidden[s], lanes_both, preferred_element_type=jnp.float32)
        acc_gain = acc_gain + term
        blocks = as_blocks(field)
        if s > 0:
            arrived = exchanged(blocks)
            grid_now, term = spatial(
                "mid", tile, as_grid(arrived), grid_states[s], kern, weights[s - 1], moves[s - 1]
            )
        else:
            sums = pieces_of(jnp.sum(acc_gain, axis=1, keepdims=True), 3)
            sums = jnp.pad(jnp.concatenate(sums, axis=1), ((0, 0), (0, count - 3)))
            arrived = exchanged(jnp.concatenate([blocks, as_blocks(sums)], axis=1))
            grid_now, term = spatial(
                "last", tile, as_grid(arrived[:, :padded_share]), grid_states[s], kern, None, None
            )
            total_gain = jnp.sum(arrived[:, padded_share:, :3].astype(jnp.float32), axis=(0, 2))
        acc_kernel = acc_kernel + term

    sums = jnp.concatenate([jnp.sum(acc_kernel, axis=2), total_gain[None]], axis=0)
    sums = jnp.concatenate(pieces_of(sums, 3), axis=0).T
    sums = jnp.pad(sums, ((0, 0), (0, count - sums.shape[1])))
    sums = jnp.broadcast_to(sums[None], (devices, padded_share, count))
    blocks = grid_now.reshape(devices, padded_share, count)
    arrived = exchanged(jnp.concatenate([blocks, sums], axis=1))
    grad_state = as_rows(arrived[:, :padded_share]).T.reshape(rows_out, cols_out, channels)
    sums = as_rows(arrived[:, padded_share:])[:, :30].astype(jnp.float32)
    sums = (sums[:, :10] + sums[:, 10:20] + sums[:, 20:30]).T
    grad_kernel = sums[:9].reshape(kernel.shape)
    return (grad_state, scattered(acc_up, False), scattered(acc_down, True), grad_kernel, sums[9])


def solution(mesh):
    placed = (
        P("lon", "lat", None),
        P(None, "lon", "lat", None),
        P(),
        P(),
        P(),
        P(),
        P(None, None, "lon", "lat"),
        P(),
        P(),
    )
    return jax.shard_map(
        local,
        mesh=mesh,
        in_specs=placed,
        out_specs=(P("lon", "lat", None), P("lon", "lat"), P("lon", "lat"), P(), P()),
        check_vma=False,
    )
```

```python
import functools

import jax
import jax.numpy as jnp
from jax import lax
from jax.experimental import pallas as pl
from jax.experimental.pallas import tpu as pltpu
from jax.sharding import PartitionSpec as P

EPSILON = 1e-06
AXES = ("lon", "lat")
ROWS = 16
LAT_REACH = 2
MIB = 1024 * 1024


def with_halo(block, sides, width, periodic):
    for axis, dim in sides:
        count = lax.axis_size(axis)
        forward = [(i, i + 1) for i in range(count - 1)]
        if periodic:
            forward.append((count - 1, 0))
        backward = [(target, source) for source, target in forward]
        low = lax.ppermute(
            lax.slice_in_dim(block, block.shape[dim] - width, None, axis=dim), axis, forward
        )
        high = lax.ppermute(lax.slice_in_dim(block, 0, width, axis=dim), axis, backward)
        block = jnp.concatenate([low, block, high], axis=dim)
    return block


def exchanged(blocks):
    return lax.all_to_all(blocks, AXES, split_axis=0, concat_axis=0, tiled=True)


def call(kernel, out_shape, *operands, scratch=(), scalars=0, flops=0, moved=0, limit=8):
    space = [pltpu.SMEM] * scalars + [pltpu.VMEM] * (len(operands) - scalars)
    return pl.pallas_call(
        kernel,
        out_shape=out_shape,
        in_specs=[pl.BlockSpec(memory_space=kind) for kind in space],
        out_specs=jax.tree.map(lambda _: pl.BlockSpec(memory_space=pltpu.VMEM), out_shape),
        scratch_shapes=scratch,
        compiler_params=pltpu.CompilerParams(vmem_limit_bytes=limit * MIB),
        cost_estimate=pl.CostEstimate(flops=flops, bytes_accessed=moved, transcendentals=0),
    )(*operands)


def split_three(value, lane, width):
    value = jnp.where(lane < width, value, 0.0)
    result = jnp.zeros_like(value)
    for k in range(3):
        piece = value.astype(jnp.bfloat16).astype(jnp.float32)
        result = result + (pltpu.roll(piece, k * width, 1) if k else piece)
        value = value - piece
    return result.astype(jnp.bfloat16)


def join_three(value, width):
    lanes = value.shape[1]
    return value + pltpu.roll(value, lanes - width, 1) + pltpu.roll(value, lanes - 2 * width, 1)


def pack_kernel(cotangent_ref, weight_ref, out_ref):
    channels = cotangent_ref.shape[1]
    devices, _, count = out_ref.shape
    share = channels // devices
    turned = cotangent_ref[...].astype(jnp.float32).T.astype(jnp.bfloat16)
    out_ref[:, :share] = turned.reshape(devices, share, count)
    rows = weight_ref.shape[0]
    weights = jnp.concatenate([weight_ref[:, i] for i in range(weight_ref.shape[1])], axis=1)
    weights = jnp.concatenate([weights, jnp.zeros((ROWS - rows, count), jnp.float32)], axis=0)
    weights = weights.astype(jnp.bfloat16)
    out_ref[:, share:] = jnp.broadcast_to(weights[None], (devices, ROWS, count))


def packed(cotangent, bilinear, devices):
    rows_out, cols_out, channels = cotangent.shape
    steps, corners = bilinear.shape[:2]
    count = rows_out * cols_out
    share = channels // devices
    if share % ROWS:
        blocks = cotangent.reshape(count, channels).T.reshape(devices, share, count)
        blocks = jnp.pad(blocks, ((0, 0), (0, -share % ROWS), (0, 0)))
        weights = bilinear.reshape(steps * corners, count).astype(jnp.bfloat16)
        weights = jnp.pad(weights, ((0, ROWS - steps * corners), (0, 0)))
        return jnp.concatenate([blocks, jnp.broadcast_to(weights[None], (devices, ROWS, count))], axis=1)
    return call(
        pack_kernel,
        jax.ShapeDtypeStruct((devices, share + ROWS, count), jnp.bfloat16),
        cotangent.reshape(count, channels),
        bilinear.reshape(steps * corners, rows_out, cols_out),
        moved=2**19,
    )


def forward_kernel(step, padded_ref, kernel_ref, gain_ref, up_ref, n_ref, normed_ref, inv_ref, hid_ref, slope_ref):
    rows_out, cols_out = padded_ref.shape[1] - 2, padded_ref.shape[2] - 2
    channels = padded_ref.shape[3]
    padded = padded_ref[step].astype(jnp.float32)
    mixed = padded[1 : 1 + rows_out, 1 : 1 + cols_out]
    running = jnp.zeros_like(mixed)
    for col_tap in range(3):
        shifted_cols = padded[:, col_tap : col_tap + cols_out]
        for row_tap in range(3):
            tap = kernel_ref[3 * row_tap + col_tap : 3 * row_tap + col_tap + 1]
            running = running + tap[None] * shifted_cols[row_tap : row_tap + rows_out]
    mixed = (mixed + running).reshape(rows_out * cols_out, channels).T
    inv_root = lax.rsqrt(jnp.mean(mixed * mixed, axis=0, keepdims=True) + EPSILON)
    normed = mixed * inv_root
    narrow = (normed * gain_ref[...]).astype(jnp.bfloat16)
    pre = jnp.dot(up_ref[...], narrow, preferred_element_type=jnp.float32)
    sigmoid = jax.nn.sigmoid(pre)
    n_ref[...] = narrow
    normed_ref[...] = normed
    inv_ref[...] = inv_root
    hid_ref[...] = (pre * sigmoid).astype(jnp.bfloat16)
    slope_ref[...] = sigmoid * (1.0 + pre * (1.0 - sigmoid))


def forward_parts(step, padded, taps, gain, w_up_t):
    _, rows_in, cols_in, channels = padded.shape
    hid = w_up_t.shape[0]
    count = (rows_in - 2) * (cols_in - 2)
    sds = jax.ShapeDtypeStruct
    return call(
        functools.partial(forward_kernel, step),
        [
            sds((channels, count), jnp.bfloat16),
            sds((channels, count), jnp.float32),
            sds((1, count), jnp.float32),
            sds((hid, count), jnp.bfloat16),
            sds((hid, count), jnp.float32),
        ],
        padded,
        taps,
        gain,
        w_up_t,
        flops=2 * count * hid * channels,
        moved=2**21,
        limit=12,
    )


def stencil_sums(step, padded_ref, field):
    rows_out, cols_out = padded_ref.shape[1] - 2, padded_ref.shape[2] - 2
    channels = padded_ref.shape[3]
    field = field.astype(jnp.float32).T.reshape(rows_out, cols_out, channels)
    padded = padded_ref[step].astype(jnp.float32)
    result = [None] * 9
    for col_tap in range(3):
        shifted_cols = padded[:, col_tap : col_tap + cols_out]
        for row_tap in range(3):
            products = jnp.sum(shifted_cols[row_tap : row_tap + rows_out] * field, axis=0)
            result[3 * row_tap + col_tap] = jnp.sum(products, axis=0, keepdims=True)
    return result


def stencil_kernel(steps, *refs):
    padded_ref, *field_refs, out_ref = refs
    total = None
    for step, ref in zip(steps, field_refs):
        rows = stencil_sums(step, padded_ref, ref[...])
        total = rows if total is None else [a + b for a, b in zip(total, rows)]
    out_ref[...] = jnp.zeros_like(out_ref)
    for k, row in enumerate(total):
        out_ref[k : k + 1] = row


def stencil_terms(steps, padded, fields):
    return call(
        functools.partial(stencil_kernel, steps),
        jax.ShapeDtypeStruct((ROWS, padded.shape[3]), jnp.float32),
        padded,
        *fields,
        moved=2**20,
        limit=12,
    )


def network_kernel(step, *refs):
    refs = list(refs)
    moved_ref, down_ref, up_ref, slope_ref, normed_ref, inv_ref, gain_ref = refs[:7]
    refs = refs[7:]
    before_ref = refs.pop(0) if step is not None or len(refs) > 3 else None
    moved = moved_ref[...]
    grad_hidden = jnp.dot(down_ref[...], moved, preferred_element_type=jnp.float32)
    grad_pre = (grad_hidden * slope_ref[...]).astype(jnp.bfloat16)
    grad_n = jnp.dot(up_ref[...], grad_pre, preferred_element_type=jnp.float32)
    normed = normed_ref[...]
    term = grad_n * normed
    gain = gain_ref[...]
    mean = jnp.mean(term * gain, axis=0, keepdims=True)
    field = moved.astype(jnp.float32) + inv_ref[...] * (grad_n * gain - normed * mean)
    field = field.astype(jnp.bfloat16)
    if before_ref is not None:
        term = before_ref[...] + term
    if step is None:
        field_ref, grad_ref, term_ref = refs
        field_ref[...] = field
        grad_ref[...] = grad_pre
        term_ref[...] = term
        return
    padded_ref, sums_ref, out_ref, grad_ref = refs
    grad_ref[...] = grad_pre
    devices, _, count = out_ref.shape
    channels = moved.shape[0]
    share = channels // devices
    rows = stencil_sums(step, padded_ref, field)
    rows = jnp.concatenate(rows + [jnp.zeros((count - 9, channels), jnp.float32)], axis=0)
    before = jnp.concatenate([sums_ref[...], jnp.zeros((count - ROWS, channels), jnp.float32)], axis=0)
    sums = (rows + before).T
    lane = lax.broadcasted_iota(jnp.int32, sums.shape, 1)
    sums = jnp.where(lane == 9, jnp.sum(term, axis=1, keepdims=True), sums)
    out_ref[:, :share] = field.reshape(devices, share, count)
    out_ref[:, share:] = split_three(sums, lane, ROWS).reshape(devices, share, count)


def network_back(step, devices, moved, w_down_t, w_up, slope, normed, inv_root, gain, before, padded=None, sums=None):
    channels, count = moved.shape
    hid = w_down_t.shape[0]
    sds = jax.ShapeDtypeStruct
    operands = [moved, w_down_t, w_up, slope, normed, inv_root, gain]
    operands += [] if before is None else [before]
    if padded is None:
        out = [
            sds((channels, count), jnp.bfloat16),
            sds((hid, count), jnp.bfloat16),
            sds((channels, count), jnp.float32),
        ]
    else:
        operands += [padded, sums]
        out = [
            sds((devices, 2 * channels // devices, count), jnp.bfloat16),
            sds((hid, count), jnp.bfloat16),
        ]
    return call(
        functools.partial(network_kernel, step if padded is not None else None),
        out,
        *operands,
        flops=4 * count * hid * channels,
        moved=4 * 2**20,
        limit=12,
    )


def final_kernel(arrived_ref, state_ref, sums_ref):
    devices, rows, count = arrived_ref.shape
    share = rows // 2
    channels = devices * share
    state = arrived_ref[:, :share].reshape(channels, count).astype(jnp.float32)
    state_ref[...] = state.T.astype(jnp.bfloat16)
    sums = arrived_ref[:, share:].reshape(channels, count).astype(jnp.float32)
    sums_ref[...] = join_three(sums, ROWS).T[:ROWS]


def final_parts(arrived, channels):
    devices, rows, count = arrived.shape
    sds = jax.ShapeDtypeStruct
    return call(
        final_kernel,
        [sds((count, channels), jnp.bfloat16), sds((ROWS, channels), jnp.float32)],
        arrived,
        moved=2**19,
    )


def spatial_kernel(mode, step, near_lon, near_lat, *refs):
    refs = list(refs)
    take = lambda: refs.pop(0)
    with_move, with_stencil = mode != "last", mode != "first"
    move_ref = take() if with_move else None
    in_ref = take()
    kern_ref = take() if with_stencil else None
    weight_ref = take() if with_move else None
    out_ref = take()
    high_ref, own_ref, low_ref, spread_ref = take(), take(), take(), take()
    tiles_lon, tiles_lat, _, lanes = in_ref.shape
    rows = high_ref.shape[2]
    lane = lax.broadcasted_iota(jnp.int32, (rows, lanes), 1)
    col = lax.rem(lane, near_lat)
    unroll = 16 if tiles_lon * tiles_lat <= 32 else 1
    zero = jnp.zeros((rows, lanes), jnp.float32)

    def turn(value, steps):
        return pltpu.roll(value, steps % lanes, 1) if isinstance(steps, int) else pltpu.roll(value, steps, 1)

    def lat_after(tiles):
        following = tiles[1:] + [None]
        return [
            jnp.where(col < near_lat - 1, turn(here, -1), 0.0 if after is None else turn(after, near_lat - 1))
            for here, after in zip(tiles, following)
        ]

    def lat_before(tiles):
        preceding = [None] + tiles[:-1]
        return [
            jnp.where(col > 0, turn(here, 1), 0.0 if before is None else turn(before, 1 - near_lat))
            for here, before in zip(tiles, preceding)
        ]

    def lon_after(here, after):
        return turn(jnp.where(lane < near_lat, after, here), -near_lat)

    def lon_before(here, before):
        return turn(jnp.where(lane >= lanes - near_lat, before, here), near_lat)

    def next_tile(a):
        return lax.rem(a + 1, tiles_lon)

    def last_tile(a):
        return lax.rem(a + tiles_lon - 1, tiles_lon)

    def read(ref, a):
        return [ref[a, b, :rows].astype(jnp.float32) for b in range(tiles_lat)]

    def loop(body, init=None):
        return lax.fori_loop(0, tiles_lon, body, init, unroll=unroll)

    if with_stencil:
        taps = [[kern_ref[3 * a + b] for b in range(3)] for a in range(3)]

        def mix(a, carry):
            here = read(in_ref, a)
            by_col = [lat_after(here), here, lat_before(here)]
            for b in range(tiles_lat):
                mixes = []
                for row in range(3):
                    mixed = None
                    for c in range(3):
                        shifted = by_col[c][b]
                        term = taps[row][c] * shifted
                        mixed = term if mixed is None else mixed + term
                    mixes.append(mixed)
                high_ref[a, b] = mixes[0]
                own_ref[a, b] = here[b] + mixes[1]
                low_ref[a, b] = mixes[2]
            return carry

        loop(mix)

    def gather(a):
        if not with_stencil:
            return read(in_ref, a)
        result = []
        for b in range(tiles_lat):
            value = own_ref[a, b] + lon_after(high_ref[a, b], high_ref[next_tile(a), b])
            value = value + lon_before(low_ref[a, b], low_ref[last_tile(a), b])
            result.append(value)
        return result

    if not with_move:

        def finish(a, carry):
            for b, value in enumerate(gather(a)):
                out_ref[a, b, :rows] = value.astype(jnp.bfloat16)
            return carry

        loop(finish)
        sums = jnp.sum(in_ref[:, :, rows:].astype(jnp.float32), axis=(0, 1))
        sums = split_three(join_three(sums, ROWS), lane, ROWS)
        out_ref[:, :, rows:] = jnp.broadcast_to(sums[None, None], (tiles_lon, tiles_lat, rows, lanes))
        return

    own2_ref, lon2_ref = refs
    weight_row = weight_ref.shape[2] - ROWS + 4 * step

    def weigh(a, carry):
        here = [value.astype(jnp.bfloat16).astype(jnp.float32) for value in gather(a)]
        weights = [
            [weight_ref[a, b, weight_row + k : weight_row + k + 1].astype(jnp.float32) for k in range(4)]
            for b in range(tiles_lat)
        ]
        own = lat_after([weights[b][2] * here[b] for b in range(tiles_lat)])
        lon = lat_after([weights[b][3] * here[b] for b in range(tiles_lat)])
        for b in range(tiles_lat):
            own2_ref[a, b] = weights[b][0] * here[b] + own[b]
            lon2_ref[a, b] = weights[b][1] * here[b] + lon[b]
        return carry

    loop(weigh)

    def spread(a, carry):
        for b in range(tiles_lat):
            value = own2_ref[a, b] + lon_after(lon2_ref[a, b], lon2_ref[next_tile(a), b])
            spread_ref[a, b] = value.astype(jnp.bfloat16).astype(jnp.float32)
        for b in range(LAT_REACH):
            spread_ref[a, tiles_lat + b] = zero
        return carry

    loop(spread)

    lon_move, lat_move = move_ref[0], move_ref[1]
    far_lon, off_lon = lon_move // near_lon, lax.rem(lon_move, near_lon)
    far_lat, off_lat = lat_move // near_lat, lax.rem(lat_move, near_lat)
    shift = off_lon * near_lat + off_lat
    turn_here = lax.rem(2 * lanes - shift, lanes)
    turn_next = lax.rem(2 * lanes - shift + near_lat, lanes)
    same_lon = lane >= off_lon * near_lat
    same_lat = col + off_lat < near_lat

    def move(a, carry):
        source = lax.rem(a + far_lon, tiles_lon)
        source_next = next_tile(source)
        for b in range(tiles_lat):
            here, after = (
                jnp.where(same_lon, spread_ref[source, far_lat + k], spread_ref[source_next, far_lat + k])
                for k in (b, b + 1)
            )
            value = jnp.where(same_lat, turn(here, turn_here), turn(after, turn_next))
            out_ref[a, b] = value.astype(jnp.bfloat16)
        return carry

    loop(move)


def spatial(mode, step, tile, rows, field, kern, weights, moves):
    tiles_lon, tiles_lat, _, lanes = field.shape
    with_move, with_stencil = mode != "last", mode != "first"
    operands = ([moves] if with_move else []) + [field]
    operands += [kern] if with_stencil else []
    operands += [weights] if with_move else []
    out_rows = rows if with_move else 2 * rows
    grid = pltpu.VMEM((tiles_lon, tiles_lat, rows, lanes), jnp.float32)
    scratch = [grid, grid, grid, pltpu.VMEM((tiles_lon, tiles_lat + LAT_REACH, rows, lanes), jnp.float32)]
    if with_move:
        scratch += [grid, grid]
    return call(
        functools.partial(spatial_kernel, mode, step, *tile),
        jax.ShapeDtypeStruct((tiles_lon, tiles_lat, out_rows, lanes), jnp.bfloat16),
        *operands,
        scratch=scratch,
        scalars=1 if with_move else 0,
        flops=2**22,
        moved=2**20,
        limit=max(8, 10 * tiles_lon * tiles_lat * rows * lanes * 4 // MIB),
    )


def halved(value, axis, bit, dim):
    count = lax.axis_size(axis)
    mine = lax.axis_index(axis) >> bit & 1
    kept = lax.dynamic_index_in_dim(value, mine, dim, keepdims=False)
    sent = lax.dynamic_index_in_dim(value, 1 - mine, dim, keepdims=False).astype(jnp.bfloat16)
    arrived = lax.ppermute(sent, axis, [(i, i ^ (1 << bit)) for i in range(count)])
    return kept + arrived.astype(jnp.float32)


def scattered(value, lat_first):
    channels, hid = value.shape
    lon_bits = lax.axis_size("lon").bit_length() - 1
    lat_bits = lax.axis_size("lat").bit_length() - 1
    rows = channels >> lon_bits
    value = value.reshape(*([2] * lon_bits), rows, *([2] * lat_bits), hid >> lat_bits)

    def over_lon(value, bit, left):
        return halved(value, "lon", bit, left.index(bit)), [k for k in left if k != bit]

    left_lon = list(range(lon_bits))[::-1]
    left_lat = list(range(lat_bits))[::-1]
    order = [("lon", 0), ("lon", 1)] + [("lat", k) for k in range(lat_bits)]
    if lat_first:
        order = [("lon", 0)] + [("lat", k) for k in range(lat_bits)] + [("lon", 1)]
    order += [("lon", k) for k in range(2, lon_bits)]
    for axis, bit in order:
        if axis == "lon":
            value, left_lon = over_lon(value, bit, left_lon)
        else:
            value = halved(value, "lat", bit, len(left_lon) + 1 + left_lat.index(bit))
            left_lat.remove(bit)
    return value


def gradient_kernel(row_groups, bit_ref, *refs):
    *inputs, send_ref, keep_ref = refs
    steps = len(inputs) // 4
    for k in range(2):
        left = inputs[2 * k * steps : (2 * k + 1) * steps]
        right = inputs[(2 * k + 1) * steps : (2 * k + 2) * steps]
        right = jnp.concatenate([ref[...] for ref in right], axis=1)
        channels = left[0].shape[0]
        chunk = channels // (2 * row_groups)
        for which, out_ref in ((1 - bit_ref[0], send_ref), (bit_ref[0], keep_ref)):
            rows = []
            for p in range(row_groups):
                start = pl.multiple_of((2 * p + which) * chunk, chunk)
                rows.append(jnp.concatenate([ref[pl.ds(start, chunk)] for ref in left], axis=1))
            rows = jnp.concatenate(rows, axis=0)
            value = lax.dot_general(rows, right, (((1,), (1,)), ((), ())), preferred_element_type=jnp.float32)
            out_ref[k] = value.astype(out_ref.dtype)


def halves_kernel(plan, together, bit_ref, *refs):
    refs = list(refs)
    count = len(plan)
    joint_in = len(refs) == 2 + (2 if together else 2 * count)
    if joint_in:
        kept, arrived = refs[0], refs[1]
        kept, arrived = [kept.at[k] for k in range(count)], [arrived.at[k] for k in range(count)]
        refs = refs[2:]
    else:
        kept, arrived = refs[:count], refs[count : 2 * count]
        refs = refs[2 * count :]
    if together:
        sends, keeps = [refs[0].at[k] for k in range(count)], [refs[1].at[k] for k in range(count)]
    else:
        sends, keeps = refs[:count], refs[count:]
    for k, (dim, groups, bit_at) in enumerate(plan):
        bit = bit_ref[bit_at]
        size = kept[k].shape[dim] // (2 * groups)
        for which, out_ref in ((1 - bit, sends[k]), (bit, keeps[k])):
            for p in range(groups):
                start = pl.multiple_of((2 * p + which) * size, size)
                place = (pl.ds(start, size),) if dim == 0 else (slice(None), pl.ds(start, size))
                goal = (pl.ds(p * size, size),) if dim == 0 else (slice(None), pl.ds(p * size, size))
                value = kept[k][place] + arrived[k][place].astype(jnp.float32)
                out_ref[goal] = value.astype(out_ref.dtype)


def halves(plan, together, bits, kept, arrived):
    shapes = []
    arrays = [kept[k] for k in range(len(plan))] if isinstance(kept, (list, tuple)) else kept
    for k, (dim, _, _) in enumerate(plan):
        shape = list(arrays[k].shape if isinstance(arrays, list) else arrays.shape[1:])
        shape[dim] //= 2
        shapes.append(tuple(shape))
    sds = jax.ShapeDtypeStruct
    if together:
        shape = (len(plan), *shapes[0])
        out = [sds(shape, jnp.bfloat16), sds(shape, jnp.float32)]
    else:
        out = [sds(shape, jnp.bfloat16) for shape in shapes] + [sds(shape, jnp.float32) for shape in shapes]
    operands = [*kept, *arrived] if isinstance(kept, (list, tuple)) else [kept, arrived]
    return call(
        functools.partial(halves_kernel, plan, together), out, bits, *operands, scalars=1, moved=2**20, limit=12
    )


def last_sum_kernel(kept_ref, arrived_ref, up_ref, down_ref):
    up_ref[...] = kept_ref[0] + arrived_ref[0].astype(jnp.float32)
    down_ref[...] = kept_ref[1] + arrived_ref[1].astype(jnp.float32)


def swapped(value, axis, bit):
    count = lax.axis_size(axis)
    return lax.ppermute(value, axis, [(i, i ^ (1 << bit)) for i in range(count)])


def projection_sums(narrow, grads, moved, hidden):
    channels, hid = narrow[0].shape[0], grads[0].shape[0]
    lon, lat = lax.axis_size("lon"), lax.axis_size("lat")
    if lat != 2 or lon != 16:
        lanes_both = (((1,), (1,)), ((), ()))
        dots = lambda left, right: sum(
            lax.dot_general(a, b, lanes_both, preferred_element_type=jnp.float32) for a, b in zip(left, right)
        )
        return scattered(dots(narrow, grads), False), scattered(dots(moved, hidden), True)
    here = lax.axis_index("lon")
    bits = jnp.stack([here >> k & 1 for k in range(4)] + [lax.axis_index("lat")]).astype(jnp.int32)
    sds = jax.ShapeDtypeStruct
    groups = lon // 2
    shape = (2, channels // 2, hid)
    send, keep = call(
        functools.partial(gradient_kernel, groups),
        [sds(shape, jnp.bfloat16), sds(shape, jnp.float32)],
        bits,
        *narrow,
        *grads,
        *moved,
        *hidden,
        scalars=1,
        flops=12 * 2**28,
        moved=6 * 2**20,
        limit=16,
    )
    arrived = swapped(send, "lon", 0)
    send_up, send_down, *keep = halves(((0, groups // 2, 1), (1, 1, 4)), False, bits, keep, arrived)
    arrived = [swapped(send_up, "lon", 1), swapped(send_down, "lat", 0)]
    send_up, send_down, *keep = halves(((1, 1, 4), (0, groups // 2, 1)), False, bits, keep, arrived)
    arrived = [swapped(send_up, "lat", 0), swapped(send_down, "lon", 1)]
    send, keep = halves(((0, groups // 4, 2), (0, groups // 4, 2)), True, bits, keep, arrived)
    arrived = swapped(send, "lon", 2)
    send, keep = halves(((0, groups // 8, 3), (0, groups // 8, 3)), True, bits, keep, arrived)
    arrived = swapped(send, "lon", 3)
    out = sds((channels // lon, hid // lat), jnp.float32)
    return call(last_sum_kernel, [out, out], keep, arrived, moved=2**18)


def local(cotangent, states, w_up, w_down, norm_gain, kernel, bilinear, lon_move, lat_move):
    steps, rows_out, cols_out, channels = states.shape
    tiles_lon, tiles_lat = lax.axis_size("lon"), lax.axis_size("lat")
    devices = tiles_lon * tiles_lat
    count = rows_out * cols_out
    tile = (rows_out, cols_out)
    share = channels // devices
    padded_share = -(-share // ROWS) * ROWS
    whole_share = share == padded_share
    group_size = channels // lon_move.shape[1]
    me = lax.axis_index("lon") * tiles_lat + lax.axis_index("lat")

    def as_blocks(value):
        value = value.reshape(devices, share, count)
        return value if whole_share else jnp.pad(value, ((0, 0), (0, padded_share - share), (0, 0)))

    def as_rows(blocks):
        return blocks[:, :share].reshape(channels, count)

    def as_grid(blocks):
        return blocks.reshape(tiles_lon, tiles_lat, *blocks.shape[1:])

    def as_pairs(blocks):
        if whole_share:
            return blocks
        parts = [blocks[:, :share], blocks[:, share:]]
        parts = [jnp.pad(part, ((0, 0), (0, padded_share - share), (0, 0))) for part in parts]
        return jnp.concatenate(parts, axis=1)

    def from_pairs(blocks):
        if whole_share:
            return blocks
        return jnp.concatenate([blocks[:, :share], blocks[:, padded_share : padded_share + share]], axis=1)

    arrived = as_grid(exchanged(packed(cotangent, bilinear, devices)))
    weights = arrived
    group = me * share // group_size
    moves = jnp.stack([lon_move[:, group], lat_move[:, group]], axis=1)
    grid_now = spatial("first", steps - 1, tile, padded_share, arrived, None, weights, moves[steps - 1])

    kern = lax.dynamic_slice_in_dim(kernel.reshape(9, channels), me * share, share, 1)
    kern = jnp.pad(kern, ((0, 0), (0, padded_share - share)))
    kern = jnp.broadcast_to(kern[:, :, None], (9, padded_share, count))

    padded = with_halo(with_halo(states, (("lon", 1),), 1, True), (("lat", 2),), 1, False)
    gain = norm_gain[:, None]
    taps = kernel.reshape(9, channels)
    w_up_t, w_down_t = w_up.T, w_down.T
    forward = {s: forward_parts(s, padded, taps, gain, w_up_t) for s in reversed(range(steps))}

    moved, grads, fields = {}, {}, {}
    term = None
    for s in reversed(range(steps)):
        moved[s] = as_rows(exchanged(grid_now.reshape(devices, padded_share, count)))
        narrow, normed, inv_root, hidden, slope = forward[s]
        common = (s, devices, moved[s], w_down_t, w_up, slope, normed, inv_root, gain, term)
        if s > 0:
            fields[s], grads[s], term = network_back(*common)
            arrived = as_grid(exchanged(as_blocks(fields[s])))
            grid_now = spatial("mid", s - 1, tile, padded_share, arrived, kern, weights, moves[s - 1])
        else:
            later = list(fields)
            sums = stencil_terms(later, padded, [fields[k] for k in later])
            blocks, grads[s] = network_back(*common, padded, sums)
            arrived = as_grid(exchanged(as_pairs(blocks)))
            grid_now = spatial("last", None, tile, padded_share, arrived, kern, None, None)

    arrived = exchanged(grid_now.reshape(devices, 2 * padded_share, count))
    grad_state, sums = final_parts(from_pairs(arrived), channels)
    order = list(reversed(range(steps)))
    grad_up, grad_down = projection_sums(
        [forward[s][0] for s in order],
        [grads[s] for s in order],
        [moved[s] for s in order],
        [forward[s][3] for s in order],
    )
    grad_kernel = sums[:9].reshape(kernel.shape)
    return (grad_state.reshape(cotangent.shape), grad_up, grad_down, grad_kernel, sums[9])


def solution(mesh):
    placed = (
        P("lon", "lat", None),
        P(None, "lon", "lat", None),
        P(),
        P(),
        P(),
        P(),
        P(None, None, "lon", "lat"),
        P(),
        P(),
    )
    return jax.shard_map(
        local,
        mesh=mesh,
        in_specs=placed,
        out_specs=(P("lon", "lat", None), P("lon", "lat"), P("lon", "lat"), P(), P()),
        check_vma=False,
    )
```

```python
import functools

import jax
import jax.numpy as jnp
from jax import lax
from jax.experimental import pallas as pl
from jax.experimental.pallas import tpu as pltpu
from jax.sharding import PartitionSpec as P

EPSILON = 1e-06
AXES = ("lon", "lat")
ROWS = 16
LAT_REACH = 2
MIB = 1024 * 1024


def exchanged(blocks):
    return lax.all_to_all(blocks, AXES, split_axis=0, concat_axis=0, tiled=True)


SPACES = {"s": pltpu.SMEM, "v": pltpu.VMEM, "h": pltpu.HBM}


def call(kernel, out_shape, operands, ins, outs, scratch=(), flops=0, moved=0, limit=8):
    return pl.pallas_call(
        kernel,
        out_shape=out_shape,
        in_specs=[pl.BlockSpec(memory_space=SPACES[kind]) for kind in ins],
        out_specs=[pl.BlockSpec(memory_space=SPACES[kind]) for kind in outs],
        scratch_shapes=scratch,
        compiler_params=pltpu.CompilerParams(vmem_limit_bytes=limit * MIB),
        cost_estimate=pl.CostEstimate(flops=flops, bytes_accessed=moved, transcendentals=0),
    )(*operands)


def copies(sems, first, pairs):
    started = [pltpu.make_async_copy(src, dst, sems.at[first + k]) for k, (src, dst) in enumerate(pairs)]
    for copy in started:
        copy.start()
    return started


def finish(started):
    for copy in started:
        copy.wait()


def split_three(value, lane, width):
    value = jnp.where(lane < width, value, 0.0)
    result = jnp.zeros_like(value)
    for k in range(3):
        piece = value.astype(jnp.bfloat16).astype(jnp.float32)
        result = result + (pltpu.roll(piece, k * width, 1) if k else piece)
        value = value - piece
    return result.astype(jnp.bfloat16)


def join_three(value, width):
    lanes = value.shape[1]
    return value + pltpu.roll(value, lanes - width, 1) + pltpu.roll(value, lanes - 2 * width, 1)


def pack_kernel(cotangent_hbm, weight_hbm, out_hbm, cotangent_ref, weight_ref, out_ref, sems):
    started = copies(sems, 0, [(cotangent_hbm, cotangent_ref), (weight_hbm, weight_ref)])
    channels = cotangent_ref.shape[1]
    devices, _, count = out_ref.shape
    share = channels // devices
    started[1].wait()
    rows = weight_ref.shape[0]
    weights = jnp.concatenate([weight_ref[:, i] for i in range(weight_ref.shape[1])], axis=1)
    weights = jnp.concatenate([weights, jnp.zeros((ROWS - rows, count), jnp.float32)], axis=0)
    weights = weights.astype(jnp.bfloat16)
    out_ref[:, share:] = jnp.broadcast_to(weights[None], (devices, ROWS, count))
    started[0].wait()
    turned = cotangent_ref[...].astype(jnp.float32).T.astype(jnp.bfloat16)
    out_ref[:, :share] = turned.reshape(devices, share, count)
    finish(copies(sems, 2, [(out_ref, out_hbm)]))


def packed(cotangent, bilinear, devices):
    rows_out, cols_out, channels = cotangent.shape
    steps, corners = bilinear.shape[:2]
    count = rows_out * cols_out
    share = channels // devices
    if share % ROWS:
        blocks = cotangent.reshape(count, channels).T.reshape(devices, share, count)
        blocks = jnp.pad(blocks, ((0, 0), (0, -share % ROWS), (0, 0)))
        weights = bilinear.reshape(steps * corners, count).astype(jnp.bfloat16)
        weights = jnp.pad(weights, ((0, ROWS - steps * corners), (0, 0)))
        return jnp.concatenate([blocks, jnp.broadcast_to(weights[None], (devices, ROWS, count))], axis=1)
    shape = (devices, share + ROWS, count)
    return call(
        pack_kernel,
        [jax.ShapeDtypeStruct(shape, jnp.bfloat16)],
        [cotangent.reshape(count, channels), bilinear.reshape(steps * corners, rows_out, cols_out)],
        "hh",
        "h",
        scratch=[
            pltpu.VMEM((count, channels), jnp.bfloat16),
            pltpu.VMEM((steps * corners, rows_out, cols_out), jnp.float32),
            pltpu.VMEM(shape, jnp.bfloat16),
            pltpu.SemaphoreType.DMA((3,)),
        ],
        moved=2**19,
    )[0]


def edges(states):
    lon, lat = lax.axis_size("lon"), lax.axis_size("lat")
    lat_at = lax.axis_index("lat")
    ahead = lambda value: lax.ppermute(value, "lon", [(i, (i + 1) % lon) for i in range(lon)])
    behind = lambda value: lax.ppermute(value, "lon", [(i, (i - 1) % lon) for i in range(lon)])
    low, high = ahead(states[:, -1:]), behind(states[:, :1])

    def sent(value, lon_by, pairs):
        both = [
            (i * lat + a, (i + lon_by) % lon * lat + b) for i in range(lon) for a, b in pairs
        ]
        return lax.ppermute(value, AXES, both)

    def column(edge, pairs):
        parts = [sent(edge[:, -1:], 1, pairs), sent(edge, 0, pairs), sent(edge[:, :1], -1, pairs)]
        return jnp.concatenate(parts, axis=1)

    first, last = states[:, :, :1], states[:, :, -1:]
    if lat == 2:
        arrived = column(jnp.where(lat_at == 0, last, first), [(0, 1), (1, 0)])
        before, after = jnp.where(lat_at == 0, 0, arrived), jnp.where(lat_at == 0, arrived, 0)
    else:
        before = column(last, [(i, i + 1) for i in range(lat - 1)])
        after = column(first, [(i + 1, i) for i in range(lat - 1)])
    return low, high, before, after


MARGIN = 8


def forward_kernel(
    states_hbm, low_ref, high_ref, before_ref, after_ref, kernel_ref, gain_ref, up_ref,
    n_hbm, aux_hbm, hid_hbm, slope_hbm, pad_hbm,
    states_ref, n_ref, aux_ref, hid_ref, slope_ref, pad_ref, sems,
):
    steps, rows_out, cols_out, channels = states_ref.shape
    count = rows_out * cols_out
    order = list(reversed(range(steps)))
    arriving = copies(sems, 0, [(states_hbm.at[s], states_ref.at[s]) for s in order])
    gain = jnp.broadcast_to(gain_ref[...], (count, channels)).T
    leaving = []
    for turn, s in enumerate(order):
        arriving[turn].wait()
        pad_ref[s, 1 : 1 + rows_out, MARGIN : MARGIN + cols_out] = states_ref[s].astype(jnp.float32)
        pad_ref[s, :1, MARGIN : MARGIN + cols_out] = low_ref[s].astype(jnp.float32)
        pad_ref[s, 1 + rows_out :, MARGIN : MARGIN + cols_out] = high_ref[s].astype(jnp.float32)
        pad_ref[s, :, MARGIN - 1 : MARGIN] = before_ref[s].astype(jnp.float32)
        pad_ref[s, :, MARGIN + cols_out : MARGIN + cols_out + 1] = after_ref[s].astype(jnp.float32)
        mixed = pad_ref[s, 1 : 1 + rows_out, MARGIN : MARGIN + cols_out]
        for col_tap in range(3):
            place = MARGIN - 1 + col_tap
            shifted_cols = pad_ref[s, :, place : place + cols_out]
            for row_tap in range(3):
                tap = kernel_ref[row_tap, col_tap : col_tap + 1]
                mixed = mixed + tap[None] * shifted_cols[row_tap : row_tap + rows_out]
        mixed = mixed.reshape(count, channels).T
        inv_root = lax.rsqrt(jnp.mean(mixed * mixed, axis=0, keepdims=True) + EPSILON)
        normed = mixed * inv_root
        narrow = (normed * gain).astype(jnp.bfloat16)
        pre = jnp.dot(up_ref[...], narrow, preferred_element_type=jnp.float32)
        sigmoid = jax.nn.sigmoid(pre)
        n_ref[s] = narrow
        aux_ref[s, :channels] = normed
        aux_ref[s, channels : 2 * channels] = gain
        aux_ref[s, 2 * channels :] = jnp.broadcast_to(inv_root, (8, count))
        hid_ref[s] = (pre * sigmoid).astype(jnp.bfloat16)
        slope_ref[s] = sigmoid * (1.0 + pre * (1.0 - sigmoid))
        pairs = [(slope_ref, slope_hbm), (aux_ref, aux_hbm), (n_ref, n_hbm), (hid_ref, hid_hbm), (pad_ref, pad_hbm)]
        leaving += copies(sems, steps + 5 * turn, [(src.at[s], dst.at[s]) for src, dst in pairs])
    finish(leaving)


def forward_parts(states, around, kernel, norm_gain, w_up_t):
    steps, rows_out, cols_out, channels = states.shape
    hid = w_up_t.shape[0]
    count = rows_out * cols_out
    shapes = [
        ((steps, channels, count), jnp.bfloat16),
        ((steps, 2 * channels + 8, count), jnp.float32),
        ((steps, hid, count), jnp.bfloat16),
        ((steps, hid, count), jnp.float32),
        ((steps, rows_out + 2, cols_out + 2 * MARGIN, channels), jnp.float32),
    ]
    return call(
        forward_kernel,
        [jax.ShapeDtypeStruct(*shape) for shape in shapes],
        [states, *around, kernel, norm_gain.reshape(1, channels), w_up_t],
        "hvvvvvvv",
        "hhhhh",
        scratch=[pltpu.VMEM(states.shape, jnp.bfloat16)]
        + [pltpu.VMEM(*shape) for shape in shapes]
        + [pltpu.SemaphoreType.DMA((6 * steps,))],
        flops=2 * steps * count * hid * channels,
        moved=2**23,
        limit=20,
    )


def stencil_sums(pad_ref, field, tile):
    rows_out, cols_out = tile
    channels = pad_ref.shape[-1]
    field = field.astype(jnp.float32).T.reshape(rows_out, cols_out, channels)
    result = [None] * 9
    for col_tap in range(3):
        place = MARGIN - 1 + col_tap
        shifted_cols = pad_ref[:, place : place + cols_out]
        for row_tap in range(3):
            products = jnp.sum(shifted_cols[row_tap : row_tap + rows_out] * field, axis=0)
            result[3 * row_tap + col_tap] = jnp.sum(products, axis=0, keepdims=True)
    return result


def stencil_kernel(steps, tile, *refs):
    pad_hbm, *field_hbm, out_ref, pad_ref, field_ref, sems = refs
    arriving = copies(sems, 0, [(pad_hbm.at[s], pad_ref.at[k]) for k, s in enumerate(steps)])
    arriving += copies(sems, len(steps), [(ref, field_ref.at[k]) for k, ref in enumerate(field_hbm)])
    total = None
    for k in range(len(steps)):
        arriving[k].wait()
        arriving[len(steps) + k].wait()
        rows = stencil_sums(pad_ref.at[k], field_ref[k], tile)
        total = rows if total is None else [a + b for a, b in zip(total, rows)]
    out_ref[...] = jnp.zeros_like(out_ref)
    for k, row in enumerate(total):
        out_ref[k : k + 1] = row


def stencil_terms(steps, tile, pad, fields):
    channels, count = fields[0].shape
    return call(
        functools.partial(stencil_kernel, steps, tile),
        [jax.ShapeDtypeStruct((ROWS, channels), jnp.float32)],
        [pad, *fields],
        "h" * (1 + len(fields)),
        "v",
        scratch=[
            pltpu.VMEM((len(steps), *pad.shape[1:]), jnp.float32),
            pltpu.VMEM((len(steps), channels, count), jnp.bfloat16),
            pltpu.SemaphoreType.DMA((2 * len(steps),)),
        ],
        moved=2**21,
        limit=12,
    )[0]


def network_kernel(step, tile, with_before, with_sums, *refs):
    refs = list(refs)
    take = lambda: refs.pop(0)
    moved_ref, down_ref, up_ref, slope_hbm, aux_hbm = (take() for _ in range(5))
    before_hbm = take() if with_before else None
    pad_hbm, sums_ref = (take(), take()) if with_sums else (None, None)
    out_hbm, grad_hbm, saved_hbm = take(), take(), take()
    term_hbm = None if with_sums else take()
    slope_ref, aux_ref, before_ref, out_ref, grad_ref, pad_ref, sems = refs
    pairs = [(slope_hbm.at[step], slope_ref), (aux_hbm.at[step], aux_ref)]
    if with_before:
        pairs.append((before_hbm, before_ref))
    if with_sums:
        pairs.append((pad_hbm.at[step], pad_ref))
    arriving = copies(sems, 0, pairs)
    leaving = copies(sems, 4, [(moved_ref, saved_hbm)])
    moved = moved_ref[...]
    channels, count = moved.shape
    grad_hidden = jnp.dot(down_ref[...], moved, preferred_element_type=jnp.float32)
    arriving[0].wait()
    grad_pre = (grad_hidden * slope_ref[...]).astype(jnp.bfloat16)
    grad_ref[...] = grad_pre
    leaving += copies(sems, 5, [(grad_ref, grad_hbm)])
    grad_n = jnp.dot(up_ref[...], grad_pre, preferred_element_type=jnp.float32)
    finish(arriving[1:])
    normed, gain = aux_ref[:channels], aux_ref[channels : 2 * channels]
    term = grad_n * normed
    mean = jnp.mean(term * gain, axis=0, keepdims=True)
    field = moved.astype(jnp.float32) + aux_ref[2 * channels : 2 * channels + 1] * (grad_n * gain - normed * mean)
    field = field.astype(jnp.bfloat16)
    if with_before:
        term = before_ref[...] + term
    if not with_sums:
        out_ref[...] = field
        leaving += copies(sems, 6, [(out_ref, out_hbm)])
        before_ref[...] = term
        leaving += copies(sems, 7, [(before_ref, term_hbm)])
        finish(leaving)
        return
    devices, _, count = out_ref.shape
    share = channels // devices
    rows = stencil_sums(pad_ref, field, tile)
    rows = jnp.concatenate(rows + [jnp.zeros((count - 9, channels), jnp.float32)], axis=0)
    before = jnp.concatenate([sums_ref[...], jnp.zeros((count - ROWS, channels), jnp.float32)], axis=0)
    sums = (rows + before).T
    lane = lax.broadcasted_iota(jnp.int32, sums.shape, 1)
    sums = jnp.where(lane == 9, jnp.sum(term, axis=1, keepdims=True), sums)
    out_ref[:, :share] = field.reshape(devices, share, count)
    out_ref[:, share:] = split_three(sums, lane, ROWS).reshape(devices, share, count)
    finish(leaving + copies(sems, 6, [(out_ref, out_hbm)]))


def network_back(step, tile, devices, moved, w_down_t, w_up, slope, aux, before, pad=None, sums=None):
    channels, count = moved.shape
    hid = w_down_t.shape[0]
    with_before, with_sums = before is not None, pad is not None
    out_shape = (devices, 2 * channels // devices, count) if with_sums else (channels, count)
    sds = jax.ShapeDtypeStruct
    out = [sds(out_shape, jnp.bfloat16), sds((hid, count), jnp.bfloat16), sds((channels, count), jnp.bfloat16)]
    out += [] if with_sums else [sds((channels, count), jnp.float32)]
    operands = [moved, w_down_t, w_up, slope, aux]
    operands += [before] if with_before else []
    operands += [pad, sums] if with_sums else []
    return call(
        functools.partial(network_kernel, step, tile, with_before, with_sums),
        out,
        operands,
        "vvvhh" + "h" * with_before + "hv" * with_sums,
        "h" * len(out),
        scratch=[
            pltpu.VMEM((hid, count), jnp.float32),
            pltpu.VMEM(aux.shape[1:], jnp.float32),
            pltpu.VMEM((channels, count), jnp.float32),
            pltpu.VMEM(out_shape, jnp.bfloat16),
            pltpu.VMEM((hid, count), jnp.bfloat16),
            pltpu.VMEM(pad.shape[1:] if with_sums else (8, count), jnp.float32),
            pltpu.SemaphoreType.DMA((8,)),
        ],
        flops=4 * count * hid * channels,
        moved=4 * 2**20,
        limit=12,
    )


def final_kernel(arrived_ref, state_hbm, taps_ref, gain_ref, state_ref, sems):
    devices, rows, count = arrived_ref.shape
    share = rows // 2
    channels = devices * share
    state = arrived_ref[:, :share].reshape(channels, count).astype(jnp.float32)
    state_ref[...] = state.T.astype(jnp.bfloat16)
    leaving = copies(sems, 0, [(state_ref, state_hbm)])
    sums = arrived_ref[:, share:].reshape(channels, count).astype(jnp.float32)
    sums = join_three(sums, ROWS).T
    for k in range(9):
        taps_ref[k // 3, k % 3 : k % 3 + 1] = sums[k : k + 1]
    gain_ref[...] = sums[9:10]
    finish(leaving)


def final_parts(arrived, channels):
    devices, rows, count = arrived.shape
    sds = jax.ShapeDtypeStruct
    return call(
        final_kernel,
        [sds((count, channels), jnp.bfloat16), sds((3, 3, channels), jnp.float32), sds((1, channels), jnp.float32)],
        [arrived],
        "v",
        "hvv",
        scratch=[pltpu.VMEM((count, channels), jnp.bfloat16), pltpu.SemaphoreType.DMA((1,))],
        moved=2**19,
    )


def spatial_kernel(mode, step, near_lon, near_lat, *refs):
    refs = list(refs)
    take = lambda: refs.pop(0)
    with_move, with_stencil = mode != "last", mode != "first"
    move_ref = take() if with_move else None
    in_ref = take()
    kern_ref = take() if with_stencil else None
    weight_hbm = take() if mode == "mid" else None
    out_hbm = take()
    saved_hbm = take() if mode == "first" else None
    high_ref, own_ref, low_ref, spread_ref, out_ref, sems = (take() for _ in range(6))
    tiles_lon, tiles_lat, _, lanes = in_ref.shape
    rows = high_ref.shape[2]
    lane = lax.broadcasted_iota(jnp.int32, (rows, lanes), 1)
    col = lax.rem(lane, near_lat)
    unroll = 16 if tiles_lon * tiles_lat <= 32 else 1
    zero = jnp.zeros((rows, lanes), jnp.float32)
    started = []
    if with_move:
        own2_ref, lon2_ref, weight_ref = refs
        if mode == "mid":
            arriving = copies(sems, 0, [(weight_hbm, weight_ref)])
        else:
            weight_ref[...] = in_ref[:, :, rows:]
            started += copies(sems, 0, [(weight_ref, saved_hbm)])

    def turn(value, steps):
        return pltpu.roll(value, steps % lanes, 1) if isinstance(steps, int) else pltpu.roll(value, steps, 1)

    def lat_after(tiles):
        following = tiles[1:] + [None]
        return [
            jnp.where(col < near_lat - 1, turn(here, -1), 0.0 if after is None else turn(after, near_lat - 1))
            for here, after in zip(tiles, following)
        ]

    def lat_before(tiles):
        preceding = [None] + tiles[:-1]
        return [
            jnp.where(col > 0, turn(here, 1), 0.0 if before is None else turn(before, 1 - near_lat))
            for here, before in zip(tiles, preceding)
        ]

    def lon_after(here, after):
        return turn(jnp.where(lane < near_lat, after, here), -near_lat)

    def lon_before(here, before):
        return turn(jnp.where(lane >= lanes - near_lat, before, here), near_lat)

    def next_tile(a):
        return lax.rem(a + 1, tiles_lon)

    def last_tile(a):
        return lax.rem(a + tiles_lon - 1, tiles_lon)

    def read(ref, a):
        return [ref[a, b, :rows].astype(jnp.float32) for b in range(tiles_lat)]

    def loop(body, init=None):
        return lax.fori_loop(0, tiles_lon, body, init, unroll=unroll)

    if with_stencil:
        taps = [
            [jnp.broadcast_to(kern_ref[:, 3 * a + b : 3 * a + b + 1], (rows, lanes)) for b in range(3)] for a in range(3)
        ]

        def mix(a, carry):
            here = read(in_ref, a)
            by_col = [lat_after(here), here, lat_before(here)]
            for b in range(tiles_lat):
                mixes = []
                for row in range(3):
                    mixed = None
                    for c in range(3):
                        shifted = by_col[c][b]
                        term = taps[row][c] * shifted
                        mixed = term if mixed is None else mixed + term
                    mixes.append(mixed)
                high_ref[a, b] = mixes[0]
                own_ref[a, b] = here[b] + mixes[1]
                low_ref[a, b] = mixes[2]
            return carry

        loop(mix)

    def gather(a):
        if not with_stencil:
            return read(in_ref, a)
        result = []
        for b in range(tiles_lat):
            value = own_ref[a, b] + lon_after(high_ref[a, b], high_ref[next_tile(a), b])
            value = value + lon_before(low_ref[a, b], low_ref[last_tile(a), b])
            result.append(value)
        return result

    if not with_move:

        def complete(a, carry):
            for b, value in enumerate(gather(a)):
                out_ref[a, b, :rows] = value.astype(jnp.bfloat16)
            return carry

        loop(complete)
        sums = jnp.sum(in_ref[:, :, rows:].astype(jnp.float32), axis=(0, 1))
        sums = split_three(join_three(sums, ROWS), lane, ROWS)
        out_ref[:, :, rows:] = jnp.broadcast_to(sums[None, None], (tiles_lon, tiles_lat, rows, lanes))
        finish(copies(sems, 1, [(out_ref, out_hbm)]))
        return

    weight_row = 4 * step
    if mode == "mid":
        finish(arriving)

    def weigh(a, carry):
        here = [value.astype(jnp.bfloat16).astype(jnp.float32) for value in gather(a)]
        weights = [
            [weight_ref[a, b, weight_row + k : weight_row + k + 1].astype(jnp.float32) for k in range(4)]
            for b in range(tiles_lat)
        ]
        own = lat_after([weights[b][2] * here[b] for b in range(tiles_lat)])
        lon = lat_after([weights[b][3] * here[b] for b in range(tiles_lat)])
        for b in range(tiles_lat):
            own2_ref[a, b] = weights[b][0] * here[b] + own[b]
            lon2_ref[a, b] = weights[b][1] * here[b] + lon[b]
        return carry

    loop(weigh)

    def spread(a, carry):
        for b in range(tiles_lat):
            value = own2_ref[a, b] + lon_after(lon2_ref[a, b], lon2_ref[next_tile(a), b])
            spread_ref[a, b] = value.astype(jnp.bfloat16).astype(jnp.float32)
        for b in range(LAT_REACH):
            spread_ref[a, tiles_lat + b] = zero
        return carry

    loop(spread)

    lon_move, lat_move = move_ref[0], move_ref[1]
    far_lon, off_lon = lon_move // near_lon, lax.rem(lon_move, near_lon)
    far_lat, off_lat = lat_move // near_lat, lax.rem(lat_move, near_lat)
    shift = off_lon * near_lat + off_lat
    turn_here = lax.rem(2 * lanes - shift, lanes)
    turn_next = lax.rem(2 * lanes - shift + near_lat, lanes)
    same_lon = lane >= off_lon * near_lat
    same_lat = col + off_lat < near_lat

    def move(a, carry):
        source = lax.rem(a + far_lon, tiles_lon)
        source_next = next_tile(source)
        for b in range(tiles_lat):
            here, after = (
                jnp.where(same_lon, spread_ref[source, far_lat + k], spread_ref[source_next, far_lat + k])
                for k in (b, b + 1)
            )
            value = jnp.where(same_lat, turn(here, turn_here), turn(after, turn_next))
            out_ref[a, b] = value.astype(jnp.bfloat16)
        return carry

    half = tiles_lon // 2
    for k in range(2):
        lax.fori_loop(k * half, (k + 1) * half, move, None, unroll=unroll if unroll == 1 else half)
        part = pl.ds(k * half, half)
        started += copies(sems, 1 + k, [(out_ref.at[part], out_hbm.at[part])])
    finish(started)


def spatial(mode, step, tile, rows, field, kern, weights, moves):
    tiles_lon, tiles_lat, _, lanes = field.shape
    with_move, with_stencil = mode != "last", mode != "first"
    operands = ([moves] if with_move else []) + [field]
    operands += [kern] if with_stencil else []
    operands += [weights] if mode == "mid" else []
    out_shape = (tiles_lon, tiles_lat, rows if with_move else 2 * rows, lanes)
    weight_shape = (tiles_lon, tiles_lat, ROWS, lanes)
    sds = jax.ShapeDtypeStruct
    out = [sds(out_shape, jnp.bfloat16)] + ([sds(weight_shape, jnp.bfloat16)] if mode == "first" else [])
    grid = pltpu.VMEM((tiles_lon, tiles_lat, rows, lanes), jnp.float32)
    scratch = [grid, grid, grid, pltpu.VMEM((tiles_lon, tiles_lat + LAT_REACH, rows, lanes), jnp.float32)]
    scratch += [pltpu.VMEM(out_shape, jnp.bfloat16), pltpu.SemaphoreType.DMA((3,))]
    if with_move:
        scratch += [grid, grid, pltpu.VMEM(weight_shape, jnp.bfloat16)]
    return call(
        functools.partial(spatial_kernel, mode, step, *tile),
        out,
        operands,
        "s" * with_move + "v" + "v" * with_stencil + "h" * (mode == "mid"),
        "h" * len(out),
        scratch=scratch,
        flops=2**22,
        moved=2**20,
        limit=max(8, 12 * tiles_lon * tiles_lat * rows * lanes * 4 // MIB),
    )


def halved(value, axis, bit, dim):
    count = lax.axis_size(axis)
    mine = lax.axis_index(axis) >> bit & 1
    kept = lax.dynamic_index_in_dim(value, mine, dim, keepdims=False)
    sent = lax.dynamic_index_in_dim(value, 1 - mine, dim, keepdims=False).astype(jnp.bfloat16)
    arrived = lax.ppermute(sent, axis, [(i, i ^ (1 << bit)) for i in range(count)])
    return kept + arrived.astype(jnp.float32)


def scattered(value, lat_first):
    channels, hid = value.shape
    lon_bits = lax.axis_size("lon").bit_length() - 1
    lat_bits = lax.axis_size("lat").bit_length() - 1
    rows = channels >> lon_bits
    value = value.reshape(*([2] * lon_bits), rows, *([2] * lat_bits), hid >> lat_bits)

    def over_lon(value, bit, left):
        return halved(value, "lon", bit, left.index(bit)), [k for k in left if k != bit]

    left_lon = list(range(lon_bits))[::-1]
    left_lat = list(range(lat_bits))[::-1]
    order = [("lon", 0), ("lon", 1)] + [("lat", k) for k in range(lat_bits)]
    if lat_first:
        order = [("lon", 0)] + [("lat", k) for k in range(lat_bits)] + [("lon", 1)]
    order += [("lon", k) for k in range(2, lon_bits)]
    for axis, bit in order:
        if axis == "lon":
            value, left_lon = over_lon(value, bit, left_lon)
        else:
            value = halved(value, "lat", bit, len(left_lon) + 1 + left_lat.index(bit))
            left_lat.remove(bit)
    return value


def gradient_kernel(row_groups, bit_ref, *refs):
    *inputs, send_ref, keep_ref, left_ref, right_ref, sems = refs
    steps = len(inputs) // 2 - 1
    narrow_hbm, hidden_hbm = inputs[:2]
    grads_hbm, moved_hbm = inputs[2 : 2 + steps], inputs[2 + steps :]
    channels, hid = left_ref.shape[1], right_ref.shape[1]
    count = narrow_hbm.shape[2]
    arriving = []
    for k in range(2):
        for s in range(steps):
            lanes = pl.ds(s * count, count)
            left = narrow_hbm.at[s] if k == 0 else moved_hbm[s]
            right = grads_hbm[s] if k == 0 else hidden_hbm.at[s]
            pairs = [(left, left_ref.at[k, :, lanes]), (right, right_ref.at[k, :, lanes])]
            arriving += copies(sems, 2 * (k * steps + s), pairs)
    chunk = channels // (2 * row_groups)
    for k in range(2):
        finish(arriving[2 * k * steps : 2 * (k + 1) * steps])
        right = right_ref[k]
        for which, out_ref in ((1 - bit_ref[0], send_ref), (bit_ref[0], keep_ref)):
            rows = []
            for p in range(row_groups):
                start = pl.multiple_of((2 * p + which) * chunk, chunk)
                rows.append(left_ref[k, pl.ds(start, chunk)])
            rows = jnp.concatenate(rows, axis=0)
            value = lax.dot_general(rows, right, (((1,), (1,)), ((), ())), preferred_element_type=jnp.float32)
            out_ref[k] = value.astype(out_ref.dtype)


def halves_kernel(plan, together, bit_ref, *refs):
    refs = list(refs)
    count = len(plan)
    joint_in = len(refs) == 2 + (2 if together else 2 * count)
    if joint_in:
        kept, arrived = refs[0], refs[1]
        kept, arrived = [kept.at[k] for k in range(count)], [arrived.at[k] for k in range(count)]
        refs = refs[2:]
    else:
        kept, arrived = refs[:count], refs[count : 2 * count]
        refs = refs[2 * count :]
    if together:
        sends, keeps = [refs[0].at[k] for k in range(count)], [refs[1].at[k] for k in range(count)]
    else:
        sends, keeps = refs[:count], refs[count:]
    for k, (dim, groups, bit_at) in enumerate(plan):
        bit = bit_ref[bit_at]
        size = kept[k].shape[dim] // (2 * groups)
        for which, out_ref in ((1 - bit, sends[k]), (bit, keeps[k])):
            for p in range(groups):
                start = pl.multiple_of((2 * p + which) * size, size)
                place = (pl.ds(start, size),) if dim == 0 else (slice(None), pl.ds(start, size))
                goal = (pl.ds(p * size, size),) if dim == 0 else (slice(None), pl.ds(p * size, size))
                value = kept[k][place].astype(jnp.float32) + arrived[k][place].astype(jnp.float32)
                out_ref[goal] = value.astype(out_ref.dtype)


def halves(plan, together, bits, kept, arrived):
    shapes = []
    arrays = [kept[k] for k in range(len(plan))] if isinstance(kept, (list, tuple)) else kept
    for k, (dim, _, _) in enumerate(plan):
        shape = list(arrays[k].shape if isinstance(arrays, list) else arrays.shape[1:])
        shape[dim] //= 2
        shapes.append(tuple(shape))
    sds = jax.ShapeDtypeStruct
    if together:
        shape = (len(plan), *shapes[0])
        out = [sds(shape, jnp.bfloat16), sds(shape, jnp.float32)]
    else:
        out = [sds(shape, jnp.bfloat16) for shape in shapes] + [sds(shape, jnp.float32) for shape in shapes]
    operands = [*kept, *arrived] if isinstance(kept, (list, tuple)) else [kept, arrived]
    return call(
        functools.partial(halves_kernel, plan, together),
        out,
        [bits, *operands],
        "s" + "v" * len(operands),
        "v" * len(out),
        moved=2**20,
        limit=12,
    )


def last_sum_kernel(kept_ref, arrived_ref, up_ref, down_ref):
    up_ref[...] = kept_ref[0] + arrived_ref[0].astype(jnp.float32)
    down_ref[...] = kept_ref[1] + arrived_ref[1].astype(jnp.float32)


def swapped(value, axis, bit):
    count = lax.axis_size(axis)
    return lax.ppermute(value, axis, [(i, i ^ (1 << bit)) for i in range(count)])


def projection_sums(narrow, hidden, grads, moved):
    steps, channels, count = narrow.shape
    hid = hidden.shape[1]
    lon, lat = lax.axis_size("lon"), lax.axis_size("lat")
    if lat != 2 or lon != 16:
        lanes_both = (((1,), (1,)), ((), ()))
        dots = lambda left, right: sum(
            lax.dot_general(left[s], right[s], lanes_both, preferred_element_type=jnp.float32) for s in range(steps)
        )
        return scattered(dots(narrow, grads), False), scattered(dots(moved, hidden), True)
    here = lax.axis_index("lon")
    bits = jnp.stack([here >> k & 1 for k in range(4)] + [lax.axis_index("lat")]).astype(jnp.int32)
    sds = jax.ShapeDtypeStruct
    groups = lon // 2
    shape = (2, channels // 2, hid)
    send, keep = call(
        functools.partial(gradient_kernel, groups),
        [sds(shape, jnp.bfloat16), sds(shape, jnp.bfloat16)],
        [bits, narrow, hidden, *grads, *moved],
        "shh" + "h" * 2 * steps,
        "vv",
        scratch=[
            pltpu.VMEM((2, channels, steps * count), jnp.bfloat16),
            pltpu.VMEM((2, hid, steps * count), jnp.bfloat16),
            pltpu.SemaphoreType.DMA((4 * steps,)),
        ],
        flops=12 * 2**28,
        moved=6 * 2**20,
        limit=16,
    )
    arrived = swapped(send, "lon", 0)
    send_up, send_down, *keep = halves(((0, groups // 2, 1), (1, 1, 4)), False, bits, keep, arrived)
    arrived = [swapped(send_up, "lon", 1), swapped(send_down, "lat", 0)]
    send_up, send_down, *keep = halves(((1, 1, 4), (0, groups // 2, 1)), False, bits, keep, arrived)
    arrived = [swapped(send_up, "lat", 0), swapped(send_down, "lon", 1)]
    send, keep = halves(((0, groups // 4, 2), (0, groups // 4, 2)), True, bits, keep, arrived)
    arrived = swapped(send, "lon", 2)
    send, keep = halves(((0, groups // 8, 3), (0, groups // 8, 3)), True, bits, keep, arrived)
    arrived = swapped(send, "lon", 3)
    out = sds((channels // lon, hid // lat), jnp.float32)
    return call(last_sum_kernel, [out, out], [keep, arrived], "vv", "vv", moved=2**18)


def local(cotangent, states, w_up, w_down, norm_gain, kernel, bilinear, lon_move, lat_move):
    steps, rows_out, cols_out, channels = states.shape
    tiles_lon, tiles_lat = lax.axis_size("lon"), lax.axis_size("lat")
    devices = tiles_lon * tiles_lat
    count = rows_out * cols_out
    tile = (rows_out, cols_out)
    share = channels // devices
    padded_share = -(-share // ROWS) * ROWS
    whole_share = share == padded_share
    group_size = channels // lon_move.shape[1]
    me = lax.axis_index("lon") * tiles_lat + lax.axis_index("lat")

    def as_blocks(value):
        value = value.reshape(devices, share, count)
        return value if whole_share else jnp.pad(value, ((0, 0), (0, padded_share - share), (0, 0)))

    def as_rows(blocks):
        return blocks[:, :share].reshape(channels, count)

    def as_grid(blocks):
        return blocks.reshape(tiles_lon, tiles_lat, *blocks.shape[1:])

    def as_pairs(blocks):
        if whole_share:
            return blocks
        parts = [blocks[:, :share], blocks[:, share:]]
        parts = [jnp.pad(part, ((0, 0), (0, padded_share - share), (0, 0))) for part in parts]
        return jnp.concatenate(parts, axis=1)

    def from_pairs(blocks):
        if whole_share:
            return blocks
        return jnp.concatenate([blocks[:, :share], blocks[:, padded_share : padded_share + share]], axis=1)

    arrived = as_grid(exchanged(packed(cotangent, bilinear, devices)))
    group = me * share // group_size
    moves = jnp.stack([lon_move[:, group], lat_move[:, group]], axis=1)
    grid_now, weights = spatial("first", steps - 1, tile, padded_share, arrived, None, None, moves[steps - 1])

    taps = lax.dynamic_slice_in_dim(kernel.reshape(9, channels), me * share, share, 1).T
    taps = jnp.pad(taps, ((0, padded_share - share), (0, count - 9)))

    around = edges(states)
    w_up_t, w_down_t = w_up.T, w_down.T
    grid_now, around = lax.optimization_barrier((grid_now, around))
    narrow, aux, hidden, slope, pad = forward_parts(states, around, kernel, norm_gain, w_up_t)

    moved, grads, fields = {}, {}, {}
    term = None
    for s in reversed(range(steps)):
        here = as_rows(exchanged(grid_now.reshape(devices, padded_share, count)))
        common = (s, tile, devices, here, w_down_t, w_up, slope, aux, term)
        if s > 0:
            fields[s], grads[s], moved[s], term = network_back(*common)
            arrived = as_grid(exchanged(as_blocks(fields[s])))
            (grid_now,) = spatial("mid", s - 1, tile, padded_share, arrived, taps, weights, moves[s - 1])
        else:
            later = list(fields)
            sums = stencil_terms(later, tile, pad, [fields[k] for k in later])
            blocks, grads[s], moved[s] = network_back(*common, pad, sums)
            arrived = as_grid(exchanged(as_pairs(blocks)))
            (grid_now,) = spatial("last", None, tile, padded_share, arrived, taps, None, None)

    arrived = exchanged(grid_now.reshape(devices, 2 * padded_share, count))
    grad_state, grad_kernel, grad_gain = final_parts(from_pairs(arrived), channels)
    by_step = lambda values: [values[s] for s in range(steps)]
    grad_up, grad_down = projection_sums(narrow, hidden, by_step(grads), by_step(moved))
    return (grad_state.reshape(cotangent.shape), grad_up, grad_down, grad_kernel, grad_gain.reshape(channels))


def solution(mesh):
    placed = (
        P("lon", "lat", None),
        P(None, "lon", "lat", None),
        P(),
        P(),
        P(),
        P(),
        P(None, None, "lon", "lat"),
        P(),
        P(),
    )
    return jax.shard_map(
        local,
        mesh=mesh,
        in_specs=placed,
        out_specs=(P("lon", "lat", None), P("lon", "lat"), P("lon", "lat"), P(), P()),
        check_vma=False,
    )
```

```python
import functools

import jax
import jax.numpy as jnp
from jax import lax
from jax.experimental import pallas as pl
from jax.experimental.pallas import tpu as pltpu
from jax.sharding import PartitionSpec as P

EPSILON = 1e-06
AXES = ("lon", "lat")
ROWS = 16
LAT_REACH = 2
MIB = 1024 * 1024


def exchanged(blocks):
    return lax.all_to_all(blocks, AXES, split_axis=0, concat_axis=0, tiled=True)


SPACES = {"s": pltpu.SMEM, "v": pltpu.VMEM, "h": pltpu.HBM}


def call(kernel, out_shape, operands, ins, outs, scratch=(), flops=0, moved=0, limit=8):
    operands = [
        pltpu.with_memory_space_constraint(value, pltpu.HBM) if kind == "h" else value
        for kind, value in zip(ins, operands, strict=True)
    ]
    out_shape = [
        pltpu.HBM(value.shape, value.dtype) if kind == "h" else value
        for kind, value in zip(outs, out_shape, strict=True)
    ]
    return pl.pallas_call(
        kernel,
        out_shape=out_shape,
        in_specs=[pl.BlockSpec(memory_space=SPACES[kind]) for kind in ins],
        out_specs=[pl.BlockSpec(memory_space=SPACES[kind]) for kind in outs],
        scratch_shapes=scratch,
        compiler_params=pltpu.CompilerParams(vmem_limit_bytes=limit * MIB),
        cost_estimate=pl.CostEstimate(flops=flops, bytes_accessed=moved, transcendentals=0),
    )(*operands)


def copies(sems, first, pairs):
    started = [pltpu.make_async_copy(src, dst, sems.at[first + k]) for k, (src, dst) in enumerate(pairs)]
    for copy in started:
        copy.start()
    return started


def finish(started):
    for copy in started:
        copy.wait()


def split_three(value, lane, width):
    value = jnp.where(lane < width, value, 0.0)
    result = jnp.zeros_like(value)
    for k in range(3):
        piece = value.astype(jnp.bfloat16).astype(jnp.float32)
        result = result + (pltpu.roll(piece, k * width, 1) if k else piece)
        value = value - piece
    return result.astype(jnp.bfloat16)


def join_three(value, width):
    lanes = value.shape[1]
    return value + pltpu.roll(value, lanes - width, 1) + pltpu.roll(value, lanes - 2 * width, 1)


def pack_kernel(cotangent_hbm, weight_hbm, out_hbm, cotangent_ref, weight_ref, out_ref, sems):
    started = copies(sems, 0, [(cotangent_hbm, cotangent_ref), (weight_hbm, weight_ref)])
    channels = cotangent_ref.shape[1]
    devices, _, count = out_ref.shape
    share = channels // devices
    started[1].wait()
    rows = weight_ref.shape[0]
    weights = jnp.concatenate([weight_ref[:, i] for i in range(weight_ref.shape[1])], axis=1)
    weights = jnp.concatenate([weights, jnp.zeros((ROWS - rows, count), jnp.float32)], axis=0)
    weights = weights.astype(jnp.bfloat16)
    out_ref[:, share:] = jnp.broadcast_to(weights[None], (devices, ROWS, count))
    started[0].wait()
    turned = cotangent_ref[...].astype(jnp.float32).T.astype(jnp.bfloat16)
    out_ref[:, :share] = turned.reshape(devices, share, count)
    finish(copies(sems, 2, [(out_ref, out_hbm)]))


def packed(cotangent, bilinear, devices):
    rows_out, cols_out, channels = cotangent.shape
    steps, corners = bilinear.shape[:2]
    count = rows_out * cols_out
    share = channels // devices
    if share % ROWS:
        blocks = cotangent.reshape(count, channels).T.reshape(devices, share, count)
        blocks = jnp.pad(blocks, ((0, 0), (0, -share % ROWS), (0, 0)))
        weights = bilinear.reshape(steps * corners, count).astype(jnp.bfloat16)
        weights = jnp.pad(weights, ((0, ROWS - steps * corners), (0, 0)))
        return jnp.concatenate([blocks, jnp.broadcast_to(weights[None], (devices, ROWS, count))], axis=1)
    shape = (devices, share + ROWS, count)
    return call(
        pack_kernel,
        [jax.ShapeDtypeStruct(shape, jnp.bfloat16)],
        [cotangent.reshape(count, channels), bilinear.reshape(steps * corners, rows_out, cols_out)],
        "hh",
        "h",
        scratch=[
            pltpu.VMEM((count, channels), jnp.bfloat16),
            pltpu.VMEM((steps * corners, rows_out, cols_out), jnp.float32),
            pltpu.VMEM(shape, jnp.bfloat16),
            pltpu.SemaphoreType.DMA((3,)),
        ],
        moved=2**19,
    )[0]


def edges(states):
    lon, lat = lax.axis_size("lon"), lax.axis_size("lat")
    lat_at = lax.axis_index("lat")
    ahead = lambda value: lax.ppermute(value, "lon", [(i, (i + 1) % lon) for i in range(lon)])
    behind = lambda value: lax.ppermute(value, "lon", [(i, (i - 1) % lon) for i in range(lon)])
    low, high = ahead(states[:, -1:]), behind(states[:, :1])

    def sent(value, lon_by, pairs):
        both = [
            (i * lat + a, (i + lon_by) % lon * lat + b) for i in range(lon) for a, b in pairs
        ]
        return lax.ppermute(value, AXES, both)

    def column(edge, pairs):
        parts = [sent(edge[:, -1:], 1, pairs), sent(edge, 0, pairs), sent(edge[:, :1], -1, pairs)]
        return jnp.concatenate(parts, axis=1)

    first, last = states[:, :, :1], states[:, :, -1:]
    if lat == 2:
        arrived = column(jnp.where(lat_at == 0, last, first), [(0, 1), (1, 0)])
        before, after = jnp.where(lat_at == 0, 0, arrived), jnp.where(lat_at == 0, arrived, 0)
    else:
        before = column(last, [(i, i + 1) for i in range(lat - 1)])
        after = column(first, [(i + 1, i) for i in range(lat - 1)])
    return low, high, before, after


MARGIN = 8


def forward_kernel(
    step, states_hbm, low_ref, high_ref, before_ref, after_ref, kernel_ref, gain_ref, up_ref,
    n_hbm, aux_hbm, hid_hbm, slope_hbm, pad_hbm,
    state_ref, n_ref, aux_ref, hid_ref, slope_ref, pad_ref, sems,
):
    rows_out, cols_out, channels = state_ref.shape
    count = rows_out * cols_out
    arriving = copies(sems, 0, [(states_hbm.at[step], state_ref)])
    gain = jnp.broadcast_to(gain_ref[...], (count, channels)).T
    aux_ref[channels : 2 * channels] = gain
    pad_ref[:1, MARGIN : MARGIN + cols_out] = low_ref[step].astype(jnp.float32)
    pad_ref[1 + rows_out :, MARGIN : MARGIN + cols_out] = high_ref[step].astype(jnp.float32)
    pad_ref[:, MARGIN - 1 : MARGIN] = before_ref[step].astype(jnp.float32)
    pad_ref[:, MARGIN + cols_out : MARGIN + cols_out + 1] = after_ref[step].astype(jnp.float32)
    finish(arriving)
    mixed = state_ref[...].astype(jnp.float32)
    pad_ref[1 : 1 + rows_out, MARGIN : MARGIN + cols_out] = mixed
    leaving = copies(sems, 1, [(pad_ref, pad_hbm)])
    for col_tap in range(3):
        place = MARGIN - 1 + col_tap
        shifted_cols = pad_ref[:, place : place + cols_out]
        for row_tap in range(3):
            tap = kernel_ref[row_tap, col_tap : col_tap + 1]
            mixed = mixed + tap[None] * shifted_cols[row_tap : row_tap + rows_out]
    mixed = mixed.reshape(count, channels).T
    inv_root = lax.rsqrt(jnp.mean(mixed * mixed, axis=0, keepdims=True) + EPSILON)
    normed = mixed * inv_root
    narrow = (normed * gain).astype(jnp.bfloat16)
    n_ref[...] = narrow
    aux_ref[:channels] = normed
    aux_ref[2 * channels :] = jnp.broadcast_to(inv_root, (8, count))
    leaving += copies(sems, 2, [(n_ref, n_hbm), (aux_ref, aux_hbm)])
    pre = jnp.dot(up_ref[...], narrow, preferred_element_type=jnp.float32)
    sigmoid = jax.nn.sigmoid(pre)
    hid_ref[...] = (pre * sigmoid).astype(jnp.bfloat16)
    slope_ref[...] = sigmoid * (1.0 + pre * (1.0 - sigmoid))
    finish(leaving + copies(sems, 4, [(hid_ref, hid_hbm), (slope_ref, slope_hbm)]))


def forward_parts(step, states, around, kernel, norm_gain, w_up_t):
    _, rows_out, cols_out, channels = states.shape
    hid = w_up_t.shape[0]
    count = rows_out * cols_out
    shapes = [
        ((channels, count), jnp.bfloat16),
        ((2 * channels + 8, count), jnp.float32),
        ((hid, count), jnp.bfloat16),
        ((hid, count), jnp.float32),
        ((rows_out + 2, cols_out + 2 * MARGIN, channels), jnp.float32),
    ]
    return call(
        functools.partial(forward_kernel, step),
        [jax.ShapeDtypeStruct(*shape) for shape in shapes],
        [states, *around, kernel, norm_gain.reshape(1, channels), w_up_t],
        "hvvvvvvv",
        "hhhhh",
        scratch=[pltpu.VMEM(states.shape[1:], jnp.bfloat16)]
        + [pltpu.VMEM(*shape) for shape in shapes]
        + [pltpu.SemaphoreType.DMA((6,))],
        flops=2 * count * hid * channels,
        moved=2**22,
        limit=12,
    )


def stencil_sums(pad_ref, field, tile):
    rows_out, cols_out = tile
    channels = pad_ref.shape[-1]
    field = field.astype(jnp.float32).T.reshape(rows_out, cols_out, channels)
    result = [None] * 9
    for col_tap in range(3):
        place = MARGIN - 1 + col_tap
        shifted_cols = pad_ref[:, place : place + cols_out]
        for row_tap in range(3):
            products = jnp.sum(shifted_cols[row_tap : row_tap + rows_out] * field, axis=0)
            result[3 * row_tap + col_tap] = jnp.sum(products, axis=0, keepdims=True)
    return result


def stencil_kernel(steps, tile, *refs):
    *inputs, out_ref, pad_ref, field_ref, sems = refs
    pad_hbm, field_hbm = inputs[:steps], inputs[steps:]
    arriving = copies(sems, 0, [(ref, pad_ref.at[k]) for k, ref in enumerate(pad_hbm)])
    arriving += copies(sems, steps, [(ref, field_ref.at[k]) for k, ref in enumerate(field_hbm)])
    total = None
    for k in range(steps):
        arriving[k].wait()
        arriving[steps + k].wait()
        rows = stencil_sums(pad_ref.at[k], field_ref[k], tile)
        total = rows if total is None else [a + b for a, b in zip(total, rows)]
    out_ref[...] = jnp.zeros_like(out_ref)
    for k, row in enumerate(total):
        out_ref[k : k + 1] = row


def stencil_terms(tile, pads, fields):
    steps = len(fields)
    channels, count = fields[0].shape
    return call(
        functools.partial(stencil_kernel, steps, tile),
        [jax.ShapeDtypeStruct((ROWS, channels), jnp.float32)],
        [*pads, *fields],
        "h" * 2 * steps,
        "v",
        scratch=[
            pltpu.VMEM((steps, *pads[0].shape), jnp.float32),
            pltpu.VMEM((steps, channels, count), jnp.bfloat16),
            pltpu.SemaphoreType.DMA((2 * steps,)),
        ],
        moved=2**21,
        limit=12,
    )[0]


def network_kernel(tile, with_before, with_sums, *refs):
    refs = list(refs)
    take = lambda: refs.pop(0)
    moved_ref, down_ref, up_ref, slope_hbm, aux_hbm = (take() for _ in range(5))
    before_hbm = take() if with_before else None
    pad_hbm, sums_ref = (take(), take()) if with_sums else (None, None)
    out_hbm, grad_hbm, saved_hbm = take(), take(), take()
    term_hbm = None if with_sums else take()
    slope_ref, aux_ref, before_ref, out_ref, grad_ref, pad_ref, sems = refs
    pairs = [(slope_hbm, slope_ref), (aux_hbm, aux_ref)]
    if with_before:
        pairs.append((before_hbm, before_ref))
    if with_sums:
        pairs.append((pad_hbm, pad_ref))
    arriving = copies(sems, 0, pairs)
    leaving = copies(sems, 4, [(moved_ref, saved_hbm)])
    moved = moved_ref[...]
    channels, count = moved.shape
    grad_hidden = jnp.dot(down_ref[...], moved, preferred_element_type=jnp.float32)
    arriving[0].wait()
    grad_pre = (grad_hidden * slope_ref[...]).astype(jnp.bfloat16)
    grad_ref[...] = grad_pre
    leaving += copies(sems, 5, [(grad_ref, grad_hbm)])
    grad_n = jnp.dot(up_ref[...], grad_pre, preferred_element_type=jnp.float32)
    finish(arriving[1:])
    normed, gain = aux_ref[:channels], aux_ref[channels : 2 * channels]
    term = grad_n * normed
    mean = jnp.mean(term * gain, axis=0, keepdims=True)
    field = moved.astype(jnp.float32) + aux_ref[2 * channels : 2 * channels + 1] * (grad_n * gain - normed * mean)
    field = field.astype(jnp.bfloat16)
    if with_before:
        term = before_ref[...] + term
    if not with_sums:
        out_ref[...] = field
        leaving += copies(sems, 6, [(out_ref, out_hbm)])
        before_ref[...] = term
        leaving += copies(sems, 7, [(before_ref, term_hbm)])
        finish(leaving)
        return
    devices, _, count = out_ref.shape
    share = channels // devices
    rows = stencil_sums(pad_ref, field, tile)
    rows = jnp.concatenate(rows + [jnp.zeros((count - 9, channels), jnp.float32)], axis=0)
    before = jnp.concatenate([sums_ref[...], jnp.zeros((count - ROWS, channels), jnp.float32)], axis=0)
    sums = (rows + before).T
    lane = lax.broadcasted_iota(jnp.int32, sums.shape, 1)
    sums = jnp.where(lane == 9, jnp.sum(term, axis=1, keepdims=True), sums)
    out_ref[:, :share] = field.reshape(devices, share, count)
    out_ref[:, share:] = split_three(sums, lane, ROWS).reshape(devices, share, count)
    finish(leaving + copies(sems, 6, [(out_ref, out_hbm)]))


def network_back(tile, devices, moved, w_down_t, w_up, slope, aux, before, pad=None, sums=None):
    channels, count = moved.shape
    hid = w_down_t.shape[0]
    with_before, with_sums = before is not None, pad is not None
    out_shape = (devices, 2 * channels // devices, count) if with_sums else (channels, count)
    sds = jax.ShapeDtypeStruct
    out = [sds(out_shape, jnp.bfloat16), sds((hid, count), jnp.bfloat16), sds((channels, count), jnp.bfloat16)]
    out += [] if with_sums else [sds((channels, count), jnp.float32)]
    operands = [moved, w_down_t, w_up, slope, aux]
    operands += [before] if with_before else []
    operands += [pad, sums] if with_sums else []
    return call(
        functools.partial(network_kernel, tile, with_before, with_sums),
        out,
        operands,
        "vvvhh" + "h" * with_before + "hv" * with_sums,
        "h" * len(out),
        scratch=[
            pltpu.VMEM((hid, count), jnp.float32),
            pltpu.VMEM(aux.shape, jnp.float32),
            pltpu.VMEM((channels, count), jnp.float32),
            pltpu.VMEM(out_shape, jnp.bfloat16),
            pltpu.VMEM((hid, count), jnp.bfloat16),
            pltpu.VMEM(pad.shape if with_sums else (8, count), jnp.float32),
            pltpu.SemaphoreType.DMA((8,)),
        ],
        flops=4 * count * hid * channels,
        moved=4 * 2**20,
        limit=12,
    )


def final_kernel(arrived_ref, state_hbm, taps_ref, gain_ref, state_ref, sems):
    devices, rows, count = arrived_ref.shape
    share = rows // 2
    channels = devices * share
    state = arrived_ref[:, :share].reshape(channels, count).astype(jnp.float32)
    state_ref[...] = state.T.astype(jnp.bfloat16)
    leaving = copies(sems, 0, [(state_ref, state_hbm)])
    sums = arrived_ref[:, share:].reshape(channels, count).astype(jnp.float32)
    sums = join_three(sums, ROWS).T
    for k in range(9):
        taps_ref[k // 3, k % 3 : k % 3 + 1] = sums[k : k + 1]
    gain_ref[...] = sums[9:10]
    finish(leaving)


def final_parts(arrived, channels):
    devices, rows, count = arrived.shape
    sds = jax.ShapeDtypeStruct
    return call(
        final_kernel,
        [sds((count, channels), jnp.bfloat16), sds((3, 3, channels), jnp.float32), sds((1, channels), jnp.float32)],
        [arrived],
        "v",
        "hvv",
        scratch=[pltpu.VMEM((count, channels), jnp.bfloat16), pltpu.SemaphoreType.DMA((1,))],
        moved=2**19,
    )


def spatial_kernel(mode, step, near_lon, near_lat, *refs):
    refs = list(refs)
    take = lambda: refs.pop(0)
    with_move, with_stencil = mode != "last", mode != "first"
    move_ref = take() if with_move else None
    in_ref = take()
    kern_ref = take() if with_stencil else None
    weight_hbm = take() if mode == "mid" else None
    out_hbm = take()
    saved_hbm = take() if mode == "first" else None
    high_ref, own_ref, low_ref, spread_ref, out_ref, sems = (take() for _ in range(6))
    tiles_lon, tiles_lat, _, lanes = in_ref.shape
    rows = high_ref.shape[2]
    lane = lax.broadcasted_iota(jnp.int32, (rows, lanes), 1)
    col = lax.rem(lane, near_lat)
    unroll = 16 if tiles_lon * tiles_lat <= 32 else 1
    zero = jnp.zeros((rows, lanes), jnp.float32)
    started = []
    if with_move:
        own2_ref, lon2_ref, weight_ref = refs
        if mode == "mid":
            arriving = copies(sems, 0, [(weight_hbm, weight_ref)])
        else:
            weight_ref[...] = in_ref[:, :, rows:]
            started += copies(sems, 0, [(weight_ref, saved_hbm)])

    def turn(value, steps):
        return pltpu.roll(value, steps % lanes, 1) if isinstance(steps, int) else pltpu.roll(value, steps, 1)

    def lat_after(tiles):
        following = tiles[1:] + [None]
        return [
            jnp.where(col < near_lat - 1, turn(here, -1), 0.0 if after is None else turn(after, near_lat - 1))
            for here, after in zip(tiles, following)
        ]

    def lat_before(tiles):
        preceding = [None] + tiles[:-1]
        return [
            jnp.where(col > 0, turn(here, 1), 0.0 if before is None else turn(before, 1 - near_lat))
            for here, before in zip(tiles, preceding)
        ]

    def lon_after(here, after):
        return turn(jnp.where(lane < near_lat, after, here), -near_lat)

    def lon_before(here, before):
        return turn(jnp.where(lane >= lanes - near_lat, before, here), near_lat)

    def next_tile(a):
        return lax.rem(a + 1, tiles_lon)

    def last_tile(a):
        return lax.rem(a + tiles_lon - 1, tiles_lon)

    def read(ref, a):
        return [ref[a, b, :rows].astype(jnp.float32) for b in range(tiles_lat)]

    def loop(body, init=None):
        return lax.fori_loop(0, tiles_lon, body, init, unroll=unroll)

    if with_stencil:
        taps = [
            [jnp.broadcast_to(kern_ref[:, 3 * a + b : 3 * a + b + 1], (rows, lanes)) for b in range(3)] for a in range(3)
        ]

        def mix(a, carry):
            here = read(in_ref, a)
            by_col = [lat_after(here), here, lat_before(here)]
            for b in range(tiles_lat):
                mixes = []
                for row in range(3):
                    mixed = None
                    for c in range(3):
                        shifted = by_col[c][b]
                        term = taps[row][c] * shifted
                        mixed = term if mixed is None else mixed + term
                    mixes.append(mixed)
                high_ref[a, b] = mixes[0]
                own_ref[a, b] = here[b] + mixes[1]
                low_ref[a, b] = mixes[2]
            return carry

        loop(mix)

    def gather(a):
        if not with_stencil:
            return read(in_ref, a)
        result = []
        for b in range(tiles_lat):
            value = own_ref[a, b] + lon_after(high_ref[a, b], high_ref[next_tile(a), b])
            value = value + lon_before(low_ref[a, b], low_ref[last_tile(a), b])
            result.append(value)
        return result

    if not with_move:

        def complete(a, carry):
            for b, value in enumerate(gather(a)):
                out_ref[a, b, :rows] = value.astype(jnp.bfloat16)
            return carry

        loop(complete)
        sums = jnp.sum(in_ref[:, :, rows:].astype(jnp.float32), axis=(0, 1))
        sums = split_three(join_three(sums, ROWS), lane, ROWS)
        out_ref[:, :, rows:] = jnp.broadcast_to(sums[None, None], (tiles_lon, tiles_lat, rows, lanes))
        finish(copies(sems, 1, [(out_ref, out_hbm)]))
        return

    weight_row = 4 * step
    if mode == "mid":
        finish(arriving)

    def weigh(a, carry):
        here = [value.astype(jnp.bfloat16).astype(jnp.float32) for value in gather(a)]
        weights = [
            [weight_ref[a, b, weight_row + k : weight_row + k + 1].astype(jnp.float32) for k in range(4)]
            for b in range(tiles_lat)
        ]
        own = lat_after([weights[b][2] * here[b] for b in range(tiles_lat)])
        lon = lat_after([weights[b][3] * here[b] for b in range(tiles_lat)])
        for b in range(tiles_lat):
            own2_ref[a, b] = weights[b][0] * here[b] + own[b]
            lon2_ref[a, b] = weights[b][1] * here[b] + lon[b]
        return carry

    loop(weigh)

    def spread(a, carry):
        for b in range(tiles_lat):
            value = own2_ref[a, b] + lon_after(lon2_ref[a, b], lon2_ref[next_tile(a), b])
            spread_ref[a, b] = value.astype(jnp.bfloat16).astype(jnp.float32)
        for b in range(LAT_REACH):
            spread_ref[a, tiles_lat + b] = zero
        return carry

    loop(spread)

    lon_move, lat_move = move_ref[0], move_ref[1]
    far_lon, off_lon = lon_move // near_lon, lax.rem(lon_move, near_lon)
    far_lat, off_lat = lat_move // near_lat, lax.rem(lat_move, near_lat)
    shift = off_lon * near_lat + off_lat
    turn_here = lax.rem(2 * lanes - shift, lanes)
    turn_next = lax.rem(2 * lanes - shift + near_lat, lanes)
    same_lon = lane >= off_lon * near_lat
    same_lat = col + off_lat < near_lat

    def move(a, carry):
        source = lax.rem(a + far_lon, tiles_lon)
        source_next = next_tile(source)
        for b in range(tiles_lat):
            here, after = (
                jnp.where(same_lon, spread_ref[source, far_lat + k], spread_ref[source_next, far_lat + k])
                for k in (b, b + 1)
            )
            value = jnp.where(same_lat, turn(here, turn_here), turn(after, turn_next))
            out_ref[a, b] = value.astype(jnp.bfloat16)
        return carry

    half = tiles_lon // 2
    for k in range(2):
        lax.fori_loop(k * half, (k + 1) * half, move, None, unroll=unroll if unroll == 1 else half)
        part = pl.ds(k * half, half)
        started += copies(sems, 1 + k, [(out_ref.at[part], out_hbm.at[part])])
    finish(started)


def spatial(mode, step, tile, rows, field, kern, weights, moves):
    tiles_lon, tiles_lat, _, lanes = field.shape
    with_move, with_stencil = mode != "last", mode != "first"
    operands = ([moves] if with_move else []) + [field]
    operands += [kern] if with_stencil else []
    operands += [weights] if mode == "mid" else []
    out_shape = (tiles_lon, tiles_lat, rows if with_move else 2 * rows, lanes)
    weight_shape = (tiles_lon, tiles_lat, ROWS, lanes)
    sds = jax.ShapeDtypeStruct
    out = [sds(out_shape, jnp.bfloat16)] + ([sds(weight_shape, jnp.bfloat16)] if mode == "first" else [])
    grid = pltpu.VMEM((tiles_lon, tiles_lat, rows, lanes), jnp.float32)
    scratch = [grid, grid, grid, pltpu.VMEM((tiles_lon, tiles_lat + LAT_REACH, rows, lanes), jnp.float32)]
    scratch += [pltpu.VMEM(out_shape, jnp.bfloat16), pltpu.SemaphoreType.DMA((3,))]
    if with_move:
        scratch += [grid, grid, pltpu.VMEM(weight_shape, jnp.bfloat16)]
    return call(
        functools.partial(spatial_kernel, mode, step, *tile),
        out,
        operands,
        "s" * with_move + "v" + "v" * with_stencil + "h" * (mode == "mid"),
        "h" * len(out),
        scratch=scratch,
        flops=2**22,
        moved=2**20,
        limit=max(8, 12 * tiles_lon * tiles_lat * rows * lanes * 4 // MIB),
    )


def halved(value, axis, bit, dim):
    count = lax.axis_size(axis)
    mine = lax.axis_index(axis) >> bit & 1
    kept = lax.dynamic_index_in_dim(value, mine, dim, keepdims=False)
    sent = lax.dynamic_index_in_dim(value, 1 - mine, dim, keepdims=False).astype(jnp.bfloat16)
    arrived = lax.ppermute(sent, axis, [(i, i ^ (1 << bit)) for i in range(count)])
    return kept + arrived.astype(jnp.float32)


def scattered(value, lat_first):
    channels, hid = value.shape
    lon_bits = lax.axis_size("lon").bit_length() - 1
    lat_bits = lax.axis_size("lat").bit_length() - 1
    rows = channels >> lon_bits
    value = value.reshape(*([2] * lon_bits), rows, *([2] * lat_bits), hid >> lat_bits)

    def over_lon(value, bit, left):
        return halved(value, "lon", bit, left.index(bit)), [k for k in left if k != bit]

    left_lon = list(range(lon_bits))[::-1]
    left_lat = list(range(lat_bits))[::-1]
    order = [("lon", 0), ("lon", 1)] + [("lat", k) for k in range(lat_bits)]
    if lat_first:
        order = [("lon", 0)] + [("lat", k) for k in range(lat_bits)] + [("lon", 1)]
    order += [("lon", k) for k in range(2, lon_bits)]
    for axis, bit in order:
        if axis == "lon":
            value, left_lon = over_lon(value, bit, left_lon)
        else:
            value = halved(value, "lat", bit, len(left_lon) + 1 + left_lat.index(bit))
            left_lat.remove(bit)
    return value


def gradient_kernel(row_groups, bit_ref, *refs):
    *inputs, send_ref, keep_ref, left_ref, right_ref, sems = refs
    steps = len(inputs) // 4
    narrow_hbm, hidden_hbm, grads_hbm, moved_hbm = (inputs[k * steps : (k + 1) * steps] for k in range(4))
    channels, hid = left_ref.shape[1], right_ref.shape[1]
    count = narrow_hbm[0].shape[1]
    arriving = []
    for k in range(2):
        for s in range(steps):
            lanes = pl.ds(s * count, count)
            left = narrow_hbm[s] if k == 0 else moved_hbm[s]
            right = grads_hbm[s] if k == 0 else hidden_hbm[s]
            pairs = [(left, left_ref.at[k, :, lanes]), (right, right_ref.at[k, :, lanes])]
            arriving += copies(sems, 2 * (k * steps + s), pairs)
    chunk = channels // (2 * row_groups)
    for k in range(2):
        finish(arriving[2 * k * steps : 2 * (k + 1) * steps])
        right = right_ref[k]
        for which, out_ref in ((1 - bit_ref[0], send_ref), (bit_ref[0], keep_ref)):
            rows = []
            for p in range(row_groups):
                start = pl.multiple_of((2 * p + which) * chunk, chunk)
                rows.append(left_ref[k, pl.ds(start, chunk)])
            rows = jnp.concatenate(rows, axis=0)
            value = lax.dot_general(rows, right, (((1,), (1,)), ((), ())), preferred_element_type=jnp.float32)
            out_ref[k] = value.astype(out_ref.dtype)


def halves_kernel(plan, together, bit_ref, *refs):
    refs = list(refs)
    count = len(plan)
    joint_in = len(refs) == 2 + (2 if together else 2 * count)
    if joint_in:
        kept, arrived = refs[0], refs[1]
        kept, arrived = [kept.at[k] for k in range(count)], [arrived.at[k] for k in range(count)]
        refs = refs[2:]
    else:
        kept, arrived = refs[:count], refs[count : 2 * count]
        refs = refs[2 * count :]
    if together:
        sends, keeps = [refs[0].at[k] for k in range(count)], [refs[1].at[k] for k in range(count)]
    else:
        sends, keeps = refs[:count], refs[count:]
    for k, (dim, groups, bit_at) in enumerate(plan):
        bit = bit_ref[bit_at]
        size = kept[k].shape[dim] // (2 * groups)
        for which, out_ref in ((1 - bit, sends[k]), (bit, keeps[k])):
            for p in range(groups):
                start = pl.multiple_of((2 * p + which) * size, size)
                place = (pl.ds(start, size),) if dim == 0 else (slice(None), pl.ds(start, size))
                goal = (pl.ds(p * size, size),) if dim == 0 else (slice(None), pl.ds(p * size, size))
                value = kept[k][place].astype(jnp.float32) + arrived[k][place].astype(jnp.float32)
                out_ref[goal] = value.astype(out_ref.dtype)


def halves(plan, together, bits, kept, arrived):
    shapes = []
    arrays = [kept[k] for k in range(len(plan))] if isinstance(kept, (list, tuple)) else kept
    for k, (dim, _, _) in enumerate(plan):
        shape = list(arrays[k].shape if isinstance(arrays, list) else arrays.shape[1:])
        shape[dim] //= 2
        shapes.append(tuple(shape))
    sds = jax.ShapeDtypeStruct
    if together:
        shape = (len(plan), *shapes[0])
        out = [sds(shape, jnp.bfloat16), sds(shape, jnp.float32)]
    else:
        out = [sds(shape, jnp.bfloat16) for shape in shapes] + [sds(shape, jnp.float32) for shape in shapes]
    operands = [*kept, *arrived] if isinstance(kept, (list, tuple)) else [kept, arrived]
    return call(
        functools.partial(halves_kernel, plan, together),
        out,
        [bits, *operands],
        "s" + "v" * len(operands),
        "v" * len(out),
        moved=2**20,
        limit=12,
    )


def last_sum_kernel(kept_ref, arrived_ref, up_ref, down_ref):
    up_ref[...] = kept_ref[0] + arrived_ref[0].astype(jnp.float32)
    down_ref[...] = kept_ref[1] + arrived_ref[1].astype(jnp.float32)


def swapped(value, axis, bit):
    count = lax.axis_size(axis)
    return lax.ppermute(value, axis, [(i, i ^ (1 << bit)) for i in range(count)])


def projection_sums(narrow, hidden, grads, moved):
    steps = len(narrow)
    channels, count = narrow[0].shape
    hid = hidden[0].shape[0]
    lon, lat = lax.axis_size("lon"), lax.axis_size("lat")
    if lat != 2 or lon != 16:
        lanes_both = (((1,), (1,)), ((), ()))
        dots = lambda left, right: sum(
            lax.dot_general(left[s], right[s], lanes_both, preferred_element_type=jnp.float32) for s in range(steps)
        )
        return scattered(dots(narrow, grads), False), scattered(dots(moved, hidden), True)
    here = lax.axis_index("lon")
    bits = jnp.stack([here >> k & 1 for k in range(4)] + [lax.axis_index("lat")]).astype(jnp.int32)
    sds = jax.ShapeDtypeStruct
    groups = lon // 2
    shape = (2, channels // 2, hid)
    send, keep = call(
        functools.partial(gradient_kernel, groups),
        [sds(shape, jnp.bfloat16), sds(shape, jnp.bfloat16)],
        [bits, *narrow, *hidden, *grads, *moved],
        "s" + "h" * 4 * steps,
        "vv",
        scratch=[
            pltpu.VMEM((2, channels, steps * count), jnp.bfloat16),
            pltpu.VMEM((2, hid, steps * count), jnp.bfloat16),
            pltpu.SemaphoreType.DMA((4 * steps,)),
        ],
        flops=12 * 2**28,
        moved=6 * 2**20,
        limit=16,
    )
    arrived = swapped(send, "lon", 0)
    send_up, send_down, *keep = halves(((0, groups // 2, 1), (1, 1, 4)), False, bits, keep, arrived)
    arrived = [swapped(send_up, "lon", 1), swapped(send_down, "lat", 0)]
    send_up, send_down, *keep = halves(((1, 1, 4), (0, groups // 2, 1)), False, bits, keep, arrived)
    arrived = [swapped(send_up, "lat", 0), swapped(send_down, "lon", 1)]
    send, keep = halves(((0, groups // 4, 2), (0, groups // 4, 2)), True, bits, keep, arrived)
    arrived = swapped(send, "lon", 2)
    send, keep = halves(((0, groups // 8, 3), (0, groups // 8, 3)), True, bits, keep, arrived)
    arrived = swapped(send, "lon", 3)
    out = sds((channels // lon, hid // lat), jnp.float32)
    return call(last_sum_kernel, [out, out], [keep, arrived], "vv", "vv", moved=2**18)


def local(cotangent, states, w_up, w_down, norm_gain, kernel, bilinear, lon_move, lat_move):
    steps, rows_out, cols_out, channels = states.shape
    tiles_lon, tiles_lat = lax.axis_size("lon"), lax.axis_size("lat")
    devices = tiles_lon * tiles_lat
    count = rows_out * cols_out
    tile = (rows_out, cols_out)
    share = channels // devices
    padded_share = -(-share // ROWS) * ROWS
    whole_share = share == padded_share
    group_size = channels // lon_move.shape[1]
    me = lax.axis_index("lon") * tiles_lat + lax.axis_index("lat")

    def as_blocks(value):
        value = value.reshape(devices, share, count)
        return value if whole_share else jnp.pad(value, ((0, 0), (0, padded_share - share), (0, 0)))

    def as_rows(blocks):
        return blocks[:, :share].reshape(channels, count)

    def as_grid(blocks):
        return blocks.reshape(tiles_lon, tiles_lat, *blocks.shape[1:])

    def as_pairs(blocks):
        if whole_share:
            return blocks
        parts = [blocks[:, :share], blocks[:, share:]]
        parts = [jnp.pad(part, ((0, 0), (0, padded_share - share), (0, 0))) for part in parts]
        return jnp.concatenate(parts, axis=1)

    def from_pairs(blocks):
        if whole_share:
            return blocks
        return jnp.concatenate([blocks[:, :share], blocks[:, padded_share : padded_share + share]], axis=1)

    blocks = packed(cotangent, bilinear, devices)
    blocks, states_later = lax.optimization_barrier((blocks, states))
    arrived = as_grid(exchanged(blocks))
    group = me * share // group_size
    moves = jnp.stack([lon_move[:, group], lat_move[:, group]], axis=1)
    grid_now, weights = spatial("first", steps - 1, tile, padded_share, arrived, None, None, moves[steps - 1])

    taps = lax.dynamic_slice_in_dim(kernel.reshape(9, channels), me * share, share, 1).T
    taps = jnp.pad(taps, ((0, padded_share - share), (0, count - 9)))

    around = edges(states_later)
    w_up_t, w_down_t = w_up.T, w_down.T
    grid_now, around = lax.optimization_barrier((grid_now, around))
    order = list(reversed(range(steps)))
    forward = {s: forward_parts(s, states, around, kernel, norm_gain, w_up_t) for s in order}
    narrow, aux, hidden, slope, pad = ({s: forward[s][k] for s in order} for k in range(5))

    moved, grads, fields = {}, {}, {}
    term = None
    for s in order:
        here = as_rows(exchanged(grid_now.reshape(devices, padded_share, count)))
        common = (tile, devices, here, w_down_t, w_up, slope[s], aux[s], term)
        if s > 0:
            fields[s], grads[s], moved[s], term = network_back(*common)
            arrived = as_grid(exchanged(as_blocks(fields[s])))
            (grid_now,) = spatial("mid", s - 1, tile, padded_share, arrived, taps, weights, moves[s - 1])
        else:
            later = list(fields)
            sums = stencil_terms(tile, [pad[k] for k in later], [fields[k] for k in later])
            blocks, grads[s], moved[s] = network_back(*common, pad[s], sums)
            arrived = as_grid(exchanged(as_pairs(blocks)))
            (grid_now,) = spatial("last", None, tile, padded_share, arrived, taps, None, None)

    arrived = exchanged(grid_now.reshape(devices, 2 * padded_share, count))
    grad_state, grad_kernel, grad_gain = final_parts(from_pairs(arrived), channels)
    by_step = lambda values: [values[s] for s in order]
    grad_up, grad_down = projection_sums(*map(by_step, (narrow, hidden, grads, moved)))
    return (grad_state.reshape(cotangent.shape), grad_up, grad_down, grad_kernel, grad_gain.reshape(channels))


def solution(mesh):
    placed = (
        P("lon", "lat", None),
        P(None, "lon", "lat", None),
        P(),
        P(),
        P(),
        P(),
        P(None, None, "lon", "lat"),
        P(),
        P(),
    )
    return jax.shard_map(
        local,
        mesh=mesh,
        in_specs=placed,
        out_specs=(P("lon", "lat", None), P("lon", "lat"), P("lon", "lat"), P(), P()),
        check_vma=False,
    )
```

```python
import functools

import jax
import jax.numpy as jnp
from jax import lax
from jax.experimental import pallas as pl
from jax.experimental.pallas import tpu as pltpu
from jax.sharding import PartitionSpec as P

EPSILON = 1e-06
AXES = ("lon", "lat")
ROWS = 16
LAT_REACH = 2
LON_REACH = 8
MIB = 1024 * 1024


def exchanged(blocks):
    return lax.all_to_all(blocks, AXES, split_axis=0, concat_axis=0, tiled=True)


SPACES = {"s": pltpu.SMEM, "v": pltpu.VMEM, "h": pltpu.HBM}


def call(kernel, out_shape, operands, ins, outs, scratch=(), flops=0, moved=0, limit=8):
    operands = [
        pltpu.with_memory_space_constraint(value, pltpu.HBM) if kind == "h" else value
        for kind, value in zip(ins, operands, strict=True)
    ]
    out_shape = [
        pltpu.HBM(value.shape, value.dtype) if kind == "h" else value
        for kind, value in zip(outs, out_shape, strict=True)
    ]
    return pl.pallas_call(
        kernel,
        out_shape=out_shape,
        in_specs=[pl.BlockSpec(memory_space=SPACES[kind]) for kind in ins],
        out_specs=[pl.BlockSpec(memory_space=SPACES[kind]) for kind in outs],
        scratch_shapes=scratch,
        compiler_params=pltpu.CompilerParams(vmem_limit_bytes=limit * MIB),
        cost_estimate=pl.CostEstimate(flops=flops, bytes_accessed=moved, transcendentals=0),
    )(*operands)


def copies(sems, first, pairs):
    started = [pltpu.make_async_copy(src, dst, sems.at[first + k]) for k, (src, dst) in enumerate(pairs)]
    for copy in started:
        copy.start()
    return started


def finish(started):
    for copy in started:
        copy.wait()


def split_three(value, lane, width):
    value = jnp.where(lane < width, value, 0.0)
    result = jnp.zeros_like(value)
    for k in range(3):
        piece = value.astype(jnp.bfloat16).astype(jnp.float32)
        result = result + (pltpu.roll(piece, k * width, 1) if k else piece)
        value = value - piece
    return result.astype(jnp.bfloat16)


def join_three(value, width):
    lanes = value.shape[1]
    return value + pltpu.roll(value, lanes - width, 1) + pltpu.roll(value, lanes - 2 * width, 1)


def pack_kernel(cotangent_hbm, weight_hbm, out_hbm, cotangent_ref, weight_ref, out_ref, sems):
    started = copies(sems, 0, [(cotangent_hbm, cotangent_ref), (weight_hbm, weight_ref)])
    channels = cotangent_ref.shape[1]
    devices, _, count = out_ref.shape
    share = channels // devices
    started[1].wait()
    rows = weight_ref.shape[0]
    weights = jnp.concatenate([weight_ref[:, i] for i in range(weight_ref.shape[1])], axis=1)
    weights = jnp.concatenate([weights, jnp.zeros((ROWS - rows, count), jnp.float32)], axis=0)
    weights = weights.astype(jnp.bfloat16)
    out_ref[:, share:] = jnp.broadcast_to(weights[None], (devices, ROWS, count))
    started[0].wait()
    turned = cotangent_ref[...].astype(jnp.float32).T.astype(jnp.bfloat16)
    out_ref[:, :share] = turned.reshape(devices, share, count)
    finish(copies(sems, 2, [(out_ref, out_hbm)]))


def packed(cotangent, bilinear, devices):
    rows_out, cols_out, channels = cotangent.shape
    steps, corners = bilinear.shape[:2]
    count = rows_out * cols_out
    share = channels // devices
    if share % ROWS:
        blocks = cotangent.reshape(count, channels).T.reshape(devices, share, count)
        blocks = jnp.pad(blocks, ((0, 0), (0, -share % ROWS), (0, 0)))
        weights = bilinear.reshape(steps * corners, count).astype(jnp.bfloat16)
        weights = jnp.pad(weights, ((0, ROWS - steps * corners), (0, 0)))
        return jnp.concatenate([blocks, jnp.broadcast_to(weights[None], (devices, ROWS, count))], axis=1)
    shape = (devices, share + ROWS, count)
    return call(
        pack_kernel,
        [jax.ShapeDtypeStruct(shape, jnp.bfloat16)],
        [cotangent.reshape(count, channels), bilinear.reshape(steps * corners, rows_out, cols_out)],
        "hh",
        "h",
        scratch=[
            pltpu.VMEM((count, channels), jnp.bfloat16),
            pltpu.VMEM((steps * corners, rows_out, cols_out), jnp.float32),
            pltpu.VMEM(shape, jnp.bfloat16),
            pltpu.SemaphoreType.DMA((3,)),
        ],
        moved=2**19,
    )[0]


def lon_edges(states):
    lon = lax.axis_size("lon")
    ahead = lambda value: lax.ppermute(value, "lon", [(i, (i + 1) % lon) for i in range(lon)])
    behind = lambda value: lax.ppermute(value, "lon", [(i, (i - 1) % lon) for i in range(lon)])
    return ahead(states[:, -1:]), behind(states[:, :1])


def lat_edges(states, low, high):
    lat, lat_at = lax.axis_size("lat"), lax.axis_index("lat")
    column = lambda place: jnp.concatenate([part[:, :, place] for part in (low, states, high)], axis=1)
    first, last = column(slice(0, 1)), column(slice(-1, None))
    if lat == 2:
        arrived = lax.ppermute(jnp.where(lat_at == 0, last, first), "lat", [(0, 1), (1, 0)])
        return jnp.where(lat_at == 0, 0, arrived), jnp.where(lat_at == 0, arrived, 0)
    return (
        lax.ppermute(last, "lat", [(i, i + 1) for i in range(lat - 1)]),
        lax.ppermute(first, "lat", [(i + 1, i) for i in range(lat - 1)]),
    )


MARGIN = 8


def forward_kernel(
    step, states_hbm, low_ref, high_ref, before_ref, after_ref, kernel_ref, gain_ref, up_ref,
    n_hbm, turned_hbm, inv_hbm, hid_hbm, slope_hbm, pad_hbm,
    n_ref, turned_ref, inv_ref, hid_ref, slope_ref, pad_ref, state_ref, wide_ref, sems,
):
    rows_out, cols_out, channels = state_ref.shape
    count = rows_out * cols_out
    arriving = copies(sems, 0, [(states_hbm.at[step], state_ref)])
    wide_ref[:1, MARGIN : MARGIN + cols_out] = low_ref[step].astype(jnp.float32)
    wide_ref[1 + rows_out :, MARGIN : MARGIN + cols_out] = high_ref[step].astype(jnp.float32)
    wide_ref[:, MARGIN - 1 : MARGIN] = before_ref[step].astype(jnp.float32)
    wide_ref[:, MARGIN + cols_out : MARGIN + cols_out + 1] = after_ref[step].astype(jnp.float32)
    finish(arriving)
    mixed = state_ref[...].astype(jnp.float32)
    wide_ref[1 : 1 + rows_out, MARGIN : MARGIN + cols_out] = mixed
    pad_ref[...] = wide_ref[...].astype(jnp.bfloat16)
    leaving = copies(sems, 1, [(pad_ref, pad_hbm)])
    for col_tap in range(3):
        place = MARGIN - 1 + col_tap
        shifted_cols = wide_ref[:, place : place + cols_out]
        for row_tap in range(3):
            tap = kernel_ref[row_tap, col_tap : col_tap + 1]
            mixed = mixed + tap[None] * shifted_cols[row_tap : row_tap + rows_out]
    mixed = mixed.reshape(count, channels)
    inv_root = lax.rsqrt(jnp.mean(mixed * mixed, axis=1, keepdims=True) + EPSILON)
    narrow = mixed * inv_root * gain_ref[...]
    n_ref[...] = narrow.astype(jnp.bfloat16)
    inv_ref[...] = jnp.broadcast_to(inv_root, inv_ref.shape)
    leaving += copies(sems, 2, [(n_ref, n_hbm), (inv_ref, inv_hbm)])
    pre = jnp.dot(n_ref[...], up_ref[...], preferred_element_type=jnp.float32)
    sigmoid = jax.nn.sigmoid(pre)
    slope_ref[...] = (sigmoid * (1.0 + pre * (1.0 - sigmoid))).astype(jnp.bfloat16)
    leaving += copies(sems, 4, [(slope_ref, slope_hbm)])
    hid_ref[...] = (pre * sigmoid).astype(jnp.bfloat16)
    turned_ref[...] = narrow.T.astype(jnp.bfloat16)
    finish(leaving + copies(sems, 5, [(hid_ref, hid_hbm), (turned_ref, turned_hbm)]))


def forward_parts(step, states, around, kernel, norm_gain, w_up):
    _, rows_out, cols_out, channels = states.shape
    hid = w_up.shape[1]
    count = rows_out * cols_out
    wide = (rows_out + 2, cols_out + 2 * MARGIN, channels)
    shapes = [
        ((count, channels), jnp.bfloat16),
        ((channels, count), jnp.bfloat16),
        ((count, 128), jnp.float32),
        ((count, hid), jnp.bfloat16),
        ((count, hid), jnp.bfloat16),
        (wide, jnp.bfloat16),
    ]
    return call(
        functools.partial(forward_kernel, step),
        [jax.ShapeDtypeStruct(*shape) for shape in shapes],
        [states, *around, kernel, norm_gain, w_up],
        "hvvvvvvv",
        "hhhhhh",
        scratch=[pltpu.VMEM(*shape) for shape in shapes]
        + [pltpu.VMEM(states.shape[1:], jnp.bfloat16), pltpu.VMEM(wide, jnp.float32), pltpu.SemaphoreType.DMA((7,))],
        flops=2 * count * hid * channels,
        moved=2**22,
        limit=12,
    )


def transposed(value):
    return value.astype(jnp.float32).T.astype(jnp.bfloat16)


LANES_BOTH = (((1,), (1,)), ((), ()))


def network_kernel(moved_ref, down_ref, up_ref, gain_ref, slope_hbm, n_hbm, inv_hbm, out_hbm, grad_hbm, saved_hbm, *refs):
    slope_ref, n_ref, inv_ref, out_ref, grad_ref, sems = refs
    arriving = copies(sems, 0, [(slope_hbm, slope_ref), (n_hbm, n_ref), (inv_hbm, inv_ref)])
    leaving = copies(sems, 3, [(moved_ref, saved_hbm)])
    moved = moved_ref[...].astype(jnp.float32).T
    grad_hidden = jnp.dot(moved.astype(jnp.bfloat16), down_ref[...], preferred_element_type=jnp.float32)
    arriving[0].wait()
    grad_pre = (grad_hidden * slope_ref[...].astype(jnp.float32)).astype(jnp.bfloat16)
    grad_ref[...] = grad_pre
    leaving += copies(sems, 4, [(grad_ref, grad_hbm)])
    grad_n = lax.dot_general(grad_pre, up_ref[...], LANES_BOTH, preferred_element_type=jnp.float32)
    finish(arriving[1:])
    narrow, gain = n_ref[...].astype(jnp.float32), gain_ref[...]
    mean = jnp.mean(grad_n * narrow, axis=1, keepdims=True)
    field = moved + inv_ref[:, :1] * (grad_n * gain - narrow * (mean / gain))
    out_ref[...] = field.T.astype(jnp.bfloat16)
    finish(leaving + copies(sems, 5, [(out_ref, out_hbm)]))


def network_back(moved, w_down, w_up, norm_gain, slope, narrow, inv_root):
    channels, count = moved.shape
    hid = w_down.shape[1]
    shapes = [((channels, count), jnp.bfloat16), ((count, hid), jnp.bfloat16), ((channels, count), jnp.bfloat16)]
    return call(
        network_kernel,
        [jax.ShapeDtypeStruct(*shape) for shape in shapes],
        [moved, w_down, w_up, norm_gain, slope, narrow, inv_root],
        "vvvvhhh",
        "hhh",
        scratch=[pltpu.VMEM(value.shape, value.dtype) for value in (slope, narrow, inv_root)]
        + [pltpu.VMEM(*shape) for shape in shapes[:2]]
        + [pltpu.SemaphoreType.DMA((6,))],
        flops=4 * count * hid * channels,
        moved=4 * 2**20,
        limit=12,
    )


def stencil_sums(pad_ref, field, tile):
    rows_out, cols_out = tile
    field = field.reshape(rows_out, cols_out, -1)
    padded = pad_ref[...].astype(jnp.float32)
    result = [None] * 9
    for col_tap in range(3):
        place = MARGIN - 1 + col_tap
        shifted_cols = padded[:, place : place + cols_out]
        for row_tap in range(3):
            products = jnp.sum(shifted_cols[row_tap : row_tap + rows_out] * field, axis=0)
            result[3 * row_tap + col_tap] = jnp.sum(products, axis=0, keepdims=True)
    return result


def sums_kernel(steps, tile, last, *refs):
    up_ref, gain_ref, *refs = refs
    inputs, refs = refs[: 4 * steps], refs[4 * steps :]
    if last:
        before_ref, out_hbm, *refs, out_ref = refs
    else:
        out_ref, *refs = refs
    pads, fields, grads, narrows, sems = refs
    places = [(ref, place.at[k]) for k in range(steps) for ref, place in zip(inputs[4 * k : 4 * k + 4], refs[:4])]
    arriving = copies(sems, 0, places)
    channels, count = fields.shape[1:]
    rows, term = None, None
    for k in range(steps):
        finish(arriving[4 * k : 4 * k + 4])
        grad_n = lax.dot_general(grads[k], up_ref[...], LANES_BOTH, preferred_element_type=jnp.float32)
        product = grad_n * narrows[k].astype(jnp.float32)
        term = product if term is None else term + product
        more = stencil_sums(pads.at[k], fields[k].astype(jnp.float32).T, tile)
        rows = more if rows is None else [a + b for a, b in zip(rows, more)]
    rows = rows + [jnp.sum(term, axis=0, keepdims=True) / gain_ref[...], jnp.zeros((6, channels), jnp.float32)]
    sums = jnp.concatenate(rows, axis=0)
    if not last:
        out_ref[...] = sums
        return
    sums = jnp.concatenate([sums + before_ref[...], jnp.zeros((count - ROWS, channels), jnp.float32)], axis=0).T
    lane = lax.broadcasted_iota(jnp.int32, (channels, count), 1)
    devices = out_ref.shape[0]
    share = channels // devices
    out_ref[:, :share] = fields[0].reshape(devices, share, count)
    out_ref[:, share:] = split_three(sums, lane, ROWS).reshape(devices, share, count)
    finish(copies(sems, 4 * steps, [(out_ref, out_hbm)]))


def channel_sums(tile, devices, w_up, norm_gain, pads, fields, grads, narrows, before):
    steps = len(fields)
    last = before is not None
    channels, count = fields[0].shape
    shape = (devices, 2 * channels // devices, count) if last else (ROWS, channels)
    dtype = jnp.bfloat16 if last else jnp.float32
    inputs = [value for group in zip(pads, fields, grads, narrows) for value in group]
    return call(
        functools.partial(sums_kernel, steps, tile, last),
        [jax.ShapeDtypeStruct(shape, dtype)],
        [w_up, norm_gain, *inputs] + [before] * last,
        "vv" + "h" * 4 * steps + "v" * last,
        "h" if last else "v",
        scratch=[pltpu.VMEM((steps, *value.shape), value.dtype) for value in inputs[:4]]
        + [pltpu.SemaphoreType.DMA((4 * steps + 1,))]
        + [pltpu.VMEM(shape, dtype)] * last,
        moved=2**21,
        limit=12,
    )[0]


def final_kernel(arrived_ref, state_hbm, taps_ref, gain_ref, state_ref, sems):
    devices, rows, count = arrived_ref.shape
    share = rows // 2
    channels = devices * share
    state = arrived_ref[:, :share].reshape(channels, count).astype(jnp.float32)
    state_ref[...] = state.T.astype(jnp.bfloat16)
    leaving = copies(sems, 0, [(state_ref, state_hbm)])
    sums = arrived_ref[:, share:].reshape(channels, count).astype(jnp.float32)
    sums = join_three(sums, ROWS).T
    for k in range(9):
        taps_ref[k // 3, k % 3 : k % 3 + 1] = sums[k : k + 1]
    gain_ref[...] = sums[9:10]
    finish(leaving)


def final_parts(arrived, channels):
    devices, rows, count = arrived.shape
    sds = jax.ShapeDtypeStruct
    return call(
        final_kernel,
        [sds((count, channels), jnp.bfloat16), sds((3, 3, channels), jnp.float32), sds((1, channels), jnp.float32)],
        [arrived],
        "v",
        "hvv",
        scratch=[pltpu.VMEM((count, channels), jnp.bfloat16), pltpu.SemaphoreType.DMA((1,))],
        moved=2**19,
    )


def spatial_kernel(mode, step, near_lon, near_lat, *refs):
    refs = list(refs)
    take = lambda: refs.pop(0)
    with_move, with_stencil = mode != "last", mode != "first"
    move_ref = take() if with_move else None
    in_ref = take()
    kern_ref = take() if with_stencil else None
    weight_hbm = take() if mode == "mid" else None
    out_hbm = take()
    saved_hbm = take() if mode == "first" else None
    out_ref, sems = take(), take()
    spread_ref, weight_ref = (take(), take()) if with_move else (None, None)
    tiles_lon, tiles_lat, _, lanes = in_ref.shape
    rows = out_ref.shape[2] if with_move else out_ref.shape[2] // 2
    started = []
    if mode == "mid":
        arriving = copies(sems, 0, [(weight_hbm, weight_ref)])
    if mode == "first":
        weight_ref[...] = in_ref[:, :, rows:]
        started += copies(sems, 0, [(weight_ref, saved_hbm)])
    lane = lax.broadcasted_iota(jnp.int32, (rows, lanes), 1)
    col = lax.rem(lane, near_lat)
    lat_last, lat_first = col == near_lat - 1, col == 0
    lon_last, lon_first = lane >= lanes - near_lat, lane < near_lat
    tiles = [(a, b) for a in range(tiles_lon) for b in range(tiles_lat)]

    def turn(value, steps):
        return pltpu.roll(value, steps % lanes if isinstance(steps, int) else steps, 1)

    def lat_after(grid):
        turned = {key: turn(value, -1) for key, value in grid.items()}
        wrapped = {key: turn(grid[key], near_lat - 1) for key in tiles if key[1] > 0}
        return {(a, b): jnp.where(lat_last, wrapped.get((a, b + 1), 0.0), turned[a, b]) for a, b in tiles}

    def lat_before(grid):
        turned = {key: turn(value, 1) for key, value in grid.items()}
        wrapped = {key: turn(grid[key], 1 - near_lat) for key in tiles if key[1] < tiles_lat - 1}
        return {(a, b): jnp.where(lat_first, wrapped.get((a, b - 1), 0.0), turned[a, b]) for a, b in tiles}

    def lon_after(grid):
        return {
            (a, b): turn(jnp.where(lon_first, grid[(a + 1) % tiles_lon, b], grid[a, b]), -near_lat) for a, b in tiles
        }

    def lon_before(grid):
        return {(a, b): turn(jnp.where(lon_last, grid[(a - 1) % tiles_lon, b], grid[a, b]), near_lat) for a, b in tiles}

    grid = {(a, b): in_ref[a, b, :rows].astype(jnp.float32) for a, b in tiles}
    if with_stencil:
        taps = [
            [jnp.broadcast_to(kern_ref[:, 3 * a + b : 3 * a + b + 1], (rows, lanes)) for b in range(3)] for a in range(3)
        ]
        by_col = [lat_after(grid), grid, lat_before(grid)]
        mix = [
            {key: sum(taps[row][c] * by_col[c][key] for c in range(1, 3)) + taps[row][0] * by_col[0][key] for key in tiles}
            for row in range(3)
        ]
        high, low = lon_after(mix[0]), lon_before(mix[2])
        grid = {key: grid[key] + mix[1][key] + (high[key] + low[key]) for key in tiles}
    if not with_move:
        for a, b in tiles:
            out_ref[a, b, :rows] = grid[a, b].astype(jnp.bfloat16)
        sums = jnp.sum(in_ref[:, :, rows:].astype(jnp.float32), axis=(0, 1))
        sums = split_three(join_three(sums, ROWS), lane, ROWS)
        out_ref[:, :, rows:] = jnp.broadcast_to(sums[None, None], (tiles_lon, tiles_lat, rows, lanes))
        finish(copies(sems, 1, [(out_ref, out_hbm)]))
        return

    if mode == "mid":
        grid = {key: value.astype(jnp.bfloat16).astype(jnp.float32) for key, value in grid.items()}
        finish(arriving)
    weights = {}
    for a, b in tiles:
        four = weight_ref[a, b].astype(jnp.float32)[4 * step : 4 * step + 4]
        weights[a, b] = [jnp.broadcast_to(four[k : k + 1], (rows, lanes)) for k in range(4)]
    weighted = [{key: weights[key][k] * grid[key] for key in tiles} for k in range(4)]
    own, lon = lat_after(weighted[2]), lat_after(weighted[3])
    lon = lon_after({key: weighted[1][key] + lon[key] for key in tiles})
    for a, b in tiles:
        value = (weighted[0][a, b] + own[a, b] + lon[a, b]).astype(jnp.bfloat16).astype(jnp.float32)
        for place in range(a, tiles_lon + LON_REACH, tiles_lon):
            spread_ref[place, b] = value
    spread_ref[:, tiles_lat:] = jnp.zeros((tiles_lon + LON_REACH, LAT_REACH, rows, lanes), jnp.float32)

    lon_move, lat_move = move_ref[0], move_ref[1]
    far_lon, off_lon = lon_move // near_lon, lax.rem(lon_move, near_lon)
    far_lat, off_lat = lat_move // near_lat, lax.rem(lat_move, near_lat)
    shift = off_lon * near_lat + off_lat
    turn_here = lax.rem(2 * lanes - shift, lanes)
    turn_next = lax.rem(2 * lanes - shift + near_lat, lanes)
    same_lon = lane >= off_lon * near_lat
    same_lat = col + off_lat < near_lat
    half = tiles_lon // 2
    for a in range(tiles_lon):
        met = [
            jnp.where(same_lon, spread_ref[far_lon + a, far_lat + b], spread_ref[far_lon + a + 1, far_lat + b])
            for b in range(tiles_lat + 1)
        ]
        for b in range(tiles_lat):
            value = jnp.where(same_lat, turn(met[b], turn_here), turn(met[b + 1], turn_next))
            out_ref[a, b] = value.astype(jnp.bfloat16)
        if (a + 1) % half == 0:
            part = pl.ds(a + 1 - half, half)
            started += copies(sems, 1 + a // half, [(out_ref.at[part], out_hbm.at[part])])
    finish(started)


def spatial(mode, step, tile, rows, field, kern, weights, moves):
    tiles_lon, tiles_lat, _, lanes = field.shape
    with_move, with_stencil = mode != "last", mode != "first"
    operands = ([moves] if with_move else []) + [field]
    operands += [kern] if with_stencil else []
    operands += [weights] if mode == "mid" else []
    out_shape = (tiles_lon, tiles_lat, rows if with_move else 2 * rows, lanes)
    weight_shape = (tiles_lon, tiles_lat, ROWS, lanes)
    sds = jax.ShapeDtypeStruct
    out = [sds(out_shape, jnp.bfloat16)] + ([sds(weight_shape, jnp.bfloat16)] if mode == "first" else [])
    scratch = [pltpu.VMEM(out_shape, jnp.bfloat16), pltpu.SemaphoreType.DMA((3,))]
    if with_move:
        spread_shape = (tiles_lon + LON_REACH, tiles_lat + LAT_REACH, rows, lanes)
        scratch += [pltpu.VMEM(spread_shape, jnp.float32), pltpu.VMEM(weight_shape, jnp.bfloat16)]
    return call(
        functools.partial(spatial_kernel, mode, step, *tile),
        out,
        operands,
        "s" * with_move + "v" + "v" * with_stencil + "h" * (mode == "mid"),
        "h" * len(out),
        scratch=scratch,
        flops=2**22,
        moved=2**20,
        limit=max(8, 14 * tiles_lon * tiles_lat * rows * lanes * 4 // MIB),
    )


def halved(value, axis, bit, dim):
    count = lax.axis_size(axis)
    mine = lax.axis_index(axis) >> bit & 1
    kept = lax.dynamic_index_in_dim(value, mine, dim, keepdims=False)
    sent = lax.dynamic_index_in_dim(value, 1 - mine, dim, keepdims=False).astype(jnp.bfloat16)
    arrived = lax.ppermute(sent, axis, [(i, i ^ (1 << bit)) for i in range(count)])
    return kept + arrived.astype(jnp.float32)


def scattered(value, lat_first):
    channels, hid = value.shape
    lon_bits = lax.axis_size("lon").bit_length() - 1
    lat_bits = lax.axis_size("lat").bit_length() - 1
    rows = channels >> lon_bits
    value = value.reshape(*([2] * lon_bits), rows, *([2] * lat_bits), hid >> lat_bits)

    def over_lon(value, bit, left):
        return halved(value, "lon", bit, left.index(bit)), [k for k in left if k != bit]

    left_lon = list(range(lon_bits))[::-1]
    left_lat = list(range(lat_bits))[::-1]
    order = [("lon", 0), ("lon", 1)] + [("lat", k) for k in range(lat_bits)]
    if lat_first:
        order = [("lon", 0)] + [("lat", k) for k in range(lat_bits)] + [("lon", 1)]
    order += [("lon", k) for k in range(2, lon_bits)]
    for axis, bit in order:
        if axis == "lon":
            value, left_lon = over_lon(value, bit, left_lon)
        else:
            value = halved(value, "lat", bit, len(left_lon) + 1 + left_lat.index(bit))
            left_lat.remove(bit)
    return value


def gradient_kernel(row_groups, bit_ref, *refs):
    *inputs, send_ref, keep_ref, left_ref, right_ref, sems = refs
    steps = len(inputs) // 4
    count = inputs[0].shape[1]
    arriving = []
    for k in range(2):
        for s in range(steps):
            part = pl.ds(s * count, count)
            pairs = [(inputs[2 * k * steps + s], left_ref.at[k, :, part])]
            pairs += [(inputs[(2 * k + 1) * steps + s], right_ref.at[k, part])]
            arriving += copies(sems, 2 * (k * steps + s), pairs)
    chunk = left_ref.shape[1] // (2 * row_groups)
    for k in range(2):
        finish(arriving[2 * k * steps : 2 * (k + 1) * steps])
        for which, out_ref in ((1 - bit_ref[0], send_ref), (bit_ref[0], keep_ref)):
            rows = []
            for p in range(row_groups):
                start = pl.multiple_of((2 * p + which) * chunk, chunk)
                rows.append(left_ref[k, pl.ds(start, chunk)])
            rows = jnp.concatenate(rows, axis=0)
            out_ref[k] = jnp.dot(rows, right_ref[k], preferred_element_type=jnp.float32).astype(jnp.bfloat16)


def halves_kernel(plan, together, bit_ref, *refs):
    refs = list(refs)
    count = len(plan)
    joint_in = len(refs) == 2 + (2 if together else 2 * count)
    if joint_in:
        kept, arrived = refs[0], refs[1]
        kept, arrived = [kept.at[k] for k in range(count)], [arrived.at[k] for k in range(count)]
        refs = refs[2:]
    else:
        kept, arrived = refs[:count], refs[count : 2 * count]
        refs = refs[2 * count :]
    if together:
        sends, keeps = [refs[0].at[k] for k in range(count)], [refs[1].at[k] for k in range(count)]
    else:
        sends, keeps = refs[:count], refs[count:]
    for k, (dim, groups, bit_at) in enumerate(plan):
        bit = bit_ref[bit_at]
        size = kept[k].shape[dim] // (2 * groups)
        for which, out_ref in ((1 - bit, sends[k]), (bit, keeps[k])):
            for p in range(groups):
                start = pl.multiple_of((2 * p + which) * size, size)
                place = (pl.ds(start, size),) if dim == 0 else (slice(None), pl.ds(start, size))
                goal = (pl.ds(p * size, size),) if dim == 0 else (slice(None), pl.ds(p * size, size))
                value = kept[k][place].astype(jnp.float32) + arrived[k][place].astype(jnp.float32)
                out_ref[goal] = value.astype(out_ref.dtype)


def halves(plan, together, bits, kept, arrived):
    shapes = []
    arrays = [kept[k] for k in range(len(plan))] if isinstance(kept, (list, tuple)) else kept
    for k, (dim, _, _) in enumerate(plan):
        shape = list(arrays[k].shape if isinstance(arrays, list) else arrays.shape[1:])
        shape[dim] //= 2
        shapes.append(tuple(shape))
    sds = jax.ShapeDtypeStruct
    if together:
        shape = (len(plan), *shapes[0])
        out = [sds(shape, jnp.bfloat16), sds(shape, jnp.float32)]
    else:
        out = [sds(shape, jnp.bfloat16) for shape in shapes] + [sds(shape, jnp.float32) for shape in shapes]
    operands = [*kept, *arrived] if isinstance(kept, (list, tuple)) else [kept, arrived]
    return call(
        functools.partial(halves_kernel, plan, together),
        out,
        [bits, *operands],
        "s" + "v" * len(operands),
        "v" * len(out),
        moved=2**20,
        limit=12,
    )


def last_sum_kernel(kept_ref, arrived_ref, up_ref, down_ref):
    up_ref[...] = kept_ref[0] + arrived_ref[0].astype(jnp.float32)
    down_ref[...] = kept_ref[1] + arrived_ref[1].astype(jnp.float32)


def swapped(value, axis, bit):
    count = lax.axis_size(axis)
    return lax.ppermute(value, axis, [(i, i ^ (1 << bit)) for i in range(count)])


def projection_sums(narrow, hidden, grads, moved):
    steps = len(narrow)
    channels, count = narrow[0].shape
    hid = hidden[0].shape[1]
    lon, lat = lax.axis_size("lon"), lax.axis_size("lat")
    if lat != 2 or lon != 16:
        dots = lambda left, right: sum(
            jnp.dot(left[s], right[s], preferred_element_type=jnp.float32) for s in range(steps)
        )
        return scattered(dots(narrow, grads), False), scattered(dots(moved, hidden), True)
    here = lax.axis_index("lon")
    bits = jnp.stack([here >> k & 1 for k in range(4)] + [lax.axis_index("lat")]).astype(jnp.int32)
    sds = jax.ShapeDtypeStruct
    groups = lon // 2
    shape = (2, channels // 2, hid)
    send, keep = call(
        functools.partial(gradient_kernel, groups),
        [sds(shape, jnp.bfloat16), sds(shape, jnp.bfloat16)],
        [bits, *narrow, *grads, *moved, *hidden],
        "s" + "h" * 4 * steps,
        "vv",
        scratch=[
            pltpu.VMEM((2, channels, steps * count), jnp.bfloat16),
            pltpu.VMEM((2, steps * count, hid), jnp.bfloat16),
            pltpu.SemaphoreType.DMA((4 * steps,)),
        ],
        flops=12 * 2**28,
        moved=6 * 2**20,
        limit=16,
    )
    arrived = swapped(send, "lon", 0)
    send_up, send_down, *keep = halves(((0, groups // 2, 1), (1, 1, 4)), False, bits, keep, arrived)
    arrived = [swapped(send_up, "lon", 1), swapped(send_down, "lat", 0)]
    send_up, send_down, *keep = halves(((1, 1, 4), (0, groups // 2, 1)), False, bits, keep, arrived)
    arrived = [swapped(send_up, "lat", 0), swapped(send_down, "lon", 1)]
    send, keep = halves(((0, groups // 4, 2), (0, groups // 4, 2)), True, bits, keep, arrived)
    arrived = swapped(send, "lon", 2)
    send, keep = halves(((0, groups // 8, 3), (0, groups // 8, 3)), True, bits, keep, arrived)
    arrived = swapped(send, "lon", 3)
    out = sds((channels // lon, hid // lat), jnp.float32)
    return call(last_sum_kernel, [out, out], [keep, arrived], "vv", "vv", moved=2**18)


def local(cotangent, states, w_up, w_down, norm_gain, kernel, bilinear, lon_move, lat_move):
    steps, rows_out, cols_out, channels = states.shape
    tiles_lon, tiles_lat = lax.axis_size("lon"), lax.axis_size("lat")
    devices = tiles_lon * tiles_lat
    count = rows_out * cols_out
    tile = (rows_out, cols_out)
    share = channels // devices
    padded_share = -(-share // ROWS) * ROWS
    whole_share = share == padded_share
    group_size = channels // lon_move.shape[1]
    me = lax.axis_index("lon") * tiles_lat + lax.axis_index("lat")

    def as_blocks(value):
        value = value.reshape(devices, share, count)
        return value if whole_share else jnp.pad(value, ((0, 0), (0, padded_share - share), (0, 0)))

    def as_rows(blocks):
        return blocks[:, :share].reshape(channels, count)

    def as_grid(blocks):
        return blocks.reshape(tiles_lon, tiles_lat, *blocks.shape[1:])

    def as_pairs(blocks):
        if whole_share:
            return blocks
        parts = [blocks[:, :share], blocks[:, share:]]
        parts = [jnp.pad(part, ((0, 0), (0, padded_share - share), (0, 0))) for part in parts]
        return jnp.concatenate(parts, axis=1)

    def from_pairs(blocks):
        if whole_share:
            return blocks
        return jnp.concatenate([blocks[:, :share], blocks[:, padded_share : padded_share + share]], axis=1)

    blocks = packed(cotangent, bilinear, devices)
    blocks, states_later = lax.optimization_barrier((blocks, states))
    arrived = as_grid(exchanged(blocks))
    group = me * share // group_size
    moves = jnp.stack([lon_move[:, group], lat_move[:, group]], axis=1)
    grid_now, weights = spatial("first", steps - 1, tile, padded_share, arrived, None, None, moves[steps - 1])

    taps = lax.dynamic_slice_in_dim(kernel.reshape(9, channels), me * share, share, 1).T
    taps = jnp.pad(taps, ((0, padded_share - share), (0, count - 9)))

    low, high = lon_edges(states_later)
    grid_now, low, high = lax.optimization_barrier((grid_now, low, high))
    around = (low, high, *lat_edges(states, low, high))
    order = list(reversed(range(steps)))
    gain = norm_gain.reshape(1, channels)
    forward = {s: forward_parts(s, states, around, kernel, gain, w_up) for s in order}

    moved, grads, fields = {}, {}, {}
    sums = None
    by_step = lambda values, steps_now: [values[s] for s in steps_now]

    def sums_of(steps_now, before):
        parts = [[forward[s][5] for s in steps_now], by_step(fields, steps_now), by_step(grads, steps_now)]
        return channel_sums(tile, devices, w_up, gain, *parts, [forward[s][0] for s in steps_now], before)

    for s in order:
        here = as_rows(exchanged(grid_now.reshape(devices, padded_share, count)))
        if s == order[-1]:
            sums = sums_of(order[:-1], None)
            here, sums = lax.optimization_barrier((here, sums))
        elif s != order[0]:
            here, forward = lax.optimization_barrier((here, forward))
        narrow, _, inv_root, _, slope, _ = forward[s]
        fields[s], grads[s], moved[s] = network_back(here, w_down, w_up, gain, slope, narrow, inv_root)
        if s > 0:
            arrived = as_grid(exchanged(as_blocks(fields[s])))
            (grid_now,) = spatial("mid", s - 1, tile, padded_share, arrived, taps, weights, moves[s - 1])
    arrived = as_grid(exchanged(as_pairs(sums_of(order[-1:], sums))))
    (grid_now,) = spatial("last", None, tile, padded_share, arrived, taps, None, None)

    arrived = exchanged(grid_now.reshape(devices, 2 * padded_share, count))
    grad_state, grad_kernel, grad_gain = final_parts(from_pairs(arrived), channels)
    narrow, hidden = ([forward[s][k] for s in order] for k in (1, 3))
    grad_up, grad_down = projection_sums(narrow, hidden, by_step(grads, order), by_step(moved, order))
    return (grad_state.reshape(cotangent.shape), grad_up, grad_down, grad_kernel, grad_gain.reshape(channels))


def solution(mesh):
    placed = (
        P("lon", "lat", None),
        P(None, "lon", "lat", None),
        P(),
        P(),
        P(),
        P(),
        P(None, None, "lon", "lat"),
        P(),
        P(),
    )
    return jax.shard_map(
        local,
        mesh=mesh,
        in_specs=placed,
        out_specs=(P("lon", "lat", None), P("lon", "lat"), P("lon", "lat"), P(), P()),
        check_vma=False,
    )
```

```python
import functools

import jax
import jax.numpy as jnp
from jax import lax
from jax.experimental import pallas as pl
from jax.experimental.pallas import tpu as pltpu
from jax.sharding import PartitionSpec as P

EPSILON = 1e-06
AXES = ("lon", "lat")
ROWS = 16
LAT_REACH = 2
LON_REACH = 8
MIB = 1024 * 1024


def exchanged(blocks):
    return lax.all_to_all(blocks, AXES, split_axis=0, concat_axis=0, tiled=True)


SPACES = {"s": pltpu.SMEM, "v": pltpu.VMEM, "p": pltpu.VMEM, "h": pltpu.HBM}
PINNED = {"p": pltpu.VMEM, "h": pltpu.HBM}


def call(kernel, out_shape, operands, ins, outs, scratch=(), flops=0, moved=0, limit=8):
    operands = [
        pltpu.with_memory_space_constraint(value, PINNED[kind]) if kind in PINNED else value
        for kind, value in zip(ins, operands, strict=True)
    ]
    out_shape = [
        PINNED[kind](value.shape, value.dtype) if kind in PINNED else value
        for kind, value in zip(outs, out_shape, strict=True)
    ]
    return pl.pallas_call(
        kernel,
        out_shape=out_shape,
        in_specs=[pl.BlockSpec(memory_space=SPACES[kind]) for kind in ins],
        out_specs=[pl.BlockSpec(memory_space=SPACES[kind]) for kind in outs],
        scratch_shapes=scratch,
        compiler_params=pltpu.CompilerParams(vmem_limit_bytes=limit * MIB),
        cost_estimate=pl.CostEstimate(flops=flops, bytes_accessed=moved, transcendentals=0),
    )(*operands)


def copies(sems, first, pairs):
    started = [pltpu.make_async_copy(src, dst, sems.at[first + k]) for k, (src, dst) in enumerate(pairs)]
    for copy in started:
        copy.start()
    return started


def finish(started):
    for copy in started:
        copy.wait()


PIECES = 3


def pieces_of(value):
    parts = []
    for _ in range(PIECES):
        parts.append(value.astype(jnp.bfloat16))
        value = value - parts[-1].astype(jnp.float32)
    return jnp.concatenate(parts, axis=0)


def whole_of(parts):
    rows = parts.shape[0] // PIECES
    parts = parts.astype(jnp.float32)
    return (parts[:rows] + parts[rows : 2 * rows]) + parts[2 * rows :]


def pack_kernel(cotangent_hbm, weight_hbm, out_hbm, cotangent_ref, weight_ref, out_ref, sems):
    started = copies(sems, 0, [(cotangent_hbm, cotangent_ref), (weight_hbm, weight_ref)])
    channels = cotangent_ref.shape[1]
    devices, _, count = out_ref.shape
    share = channels // devices
    started[1].wait()
    rows = weight_ref.shape[0]
    weights = jnp.concatenate([weight_ref[:, i] for i in range(weight_ref.shape[1])], axis=1)
    weights = jnp.concatenate([weights, jnp.zeros((ROWS - rows, count), jnp.float32)], axis=0)
    weights = weights.astype(jnp.bfloat16)
    out_ref[:, share:] = jnp.broadcast_to(weights[None], (devices, ROWS, count))
    started[0].wait()
    turned = cotangent_ref[...].astype(jnp.float32).T.astype(jnp.bfloat16)
    out_ref[:, :share] = turned.reshape(devices, share, count)
    finish(copies(sems, 2, [(out_ref, out_hbm)]))


def packed(cotangent, bilinear, devices):
    rows_out, cols_out, channels = cotangent.shape
    steps, corners = bilinear.shape[:2]
    count = rows_out * cols_out
    share = channels // devices
    if share % ROWS:
        blocks = cotangent.reshape(count, channels).T.reshape(devices, share, count)
        blocks = jnp.pad(blocks, ((0, 0), (0, -share % ROWS), (0, 0)))
        weights = bilinear.reshape(steps * corners, count).astype(jnp.bfloat16)
        weights = jnp.pad(weights, ((0, ROWS - steps * corners), (0, 0)))
        return jnp.concatenate([blocks, jnp.broadcast_to(weights[None], (devices, ROWS, count))], axis=1)
    shape = (devices, share + ROWS, count)
    return call(
        pack_kernel,
        [jax.ShapeDtypeStruct(shape, jnp.bfloat16)],
        [cotangent.reshape(count, channels), bilinear.reshape(steps * corners, rows_out, cols_out)],
        "hh",
        "h",
        scratch=[
            pltpu.VMEM((count, channels), jnp.bfloat16),
            pltpu.VMEM((steps * corners, rows_out, cols_out), jnp.float32),
            pltpu.VMEM(shape, jnp.bfloat16),
            pltpu.SemaphoreType.DMA((3,)),
        ],
        moved=2**19,
    )[0]


def lat_edges(states):
    lat, lat_at = lax.axis_size("lat"), lax.axis_index("lat")
    first, last = states[:, :, :1], states[:, :, -1:]
    if lat == 2:
        arrived = lax.ppermute(jnp.where(lat_at == 0, last, first), "lat", [(0, 1), (1, 0)])
        return jnp.where(lat_at == 0, 0, arrived), jnp.where(lat_at == 0, arrived, 0)
    return (
        lax.ppermute(last, "lat", [(i, i + 1) for i in range(lat - 1)]),
        lax.ppermute(first, "lat", [(i + 1, i) for i in range(lat - 1)]),
    )


def lon_edges(states, before, after):
    lon = lax.axis_size("lon")
    ahead = lambda value: lax.ppermute(value, "lon", [(i, (i + 1) % lon) for i in range(lon)])
    behind = lambda value: lax.ppermute(value, "lon", [(i, (i - 1) % lon) for i in range(lon)])
    row = lambda place: jnp.concatenate([part[:, place] for part in (before, states, after)], axis=2)
    return ahead(row(slice(-1, None))), behind(row(slice(0, 1)))


MARGIN = 8


def forward_kernel(
    step, states_ref, before_ref, after_ref, low_ref, high_ref, kernel_ref, gain_ref, up_ref,
    n_hbm, turned_hbm, inv_hbm, hid_hbm, slope_hbm, pad_hbm,
    n_ref, turned_ref, inv_ref, hid_ref, slope_ref, pad_ref, wide_ref, sems,
):
    rows_out, cols_out, channels = states_ref.shape[1:]
    count = rows_out * cols_out
    mixed = states_ref[step].astype(jnp.float32)
    fill_margins(wide_ref, before_ref[step], after_ref[step], low_ref[step], high_ref[step], mixed)
    pad_ref[...] = wide_ref[...].astype(jnp.bfloat16)
    leaving = copies(sems, 1, [(pad_ref, pad_hbm)])
    for col_tap in range(3):
        place = MARGIN - 1 + col_tap
        shifted_cols = wide_ref[:, place : place + cols_out]
        for row_tap in range(3):
            tap = kernel_ref[row_tap, col_tap : col_tap + 1]
            mixed = mixed + tap[None] * shifted_cols[row_tap : row_tap + rows_out]
    mixed = mixed.reshape(count, channels)
    inv_root = lax.rsqrt(jnp.mean(mixed * mixed, axis=1, keepdims=True) + EPSILON)
    narrow = mixed * inv_root * gain_ref[...]
    n_ref[...] = narrow.astype(jnp.bfloat16)
    inv_ref[...] = jnp.broadcast_to(inv_root, inv_ref.shape)
    leaving += copies(sems, 2, [(n_ref, n_hbm), (inv_ref, inv_hbm)])
    pre = jnp.dot(n_ref[...], up_ref[...], preferred_element_type=jnp.float32)
    sigmoid = jax.nn.sigmoid(pre)
    slope_ref[...] = (sigmoid * (1.0 + pre * (1.0 - sigmoid))).astype(jnp.bfloat16)
    leaving += copies(sems, 4, [(slope_ref, slope_hbm)])
    hid_ref[...] = (pre * sigmoid).astype(jnp.bfloat16)
    turned_ref[...] = narrow.T.astype(jnp.bfloat16)
    finish(leaving + copies(sems, 5, [(hid_ref, hid_hbm), (turned_ref, turned_hbm)]))


def forward_parts(step, states, around, kernel, norm_gain, w_up):
    _, rows_out, cols_out, channels = states.shape
    hid = w_up.shape[1]
    count = rows_out * cols_out
    wide = (rows_out + 2, cols_out + 2 * MARGIN, channels)
    shapes = [
        ((count, channels), jnp.bfloat16),
        ((channels, count), jnp.bfloat16),
        ((count, 128), jnp.float32),
        ((count, hid), jnp.bfloat16),
        ((count, hid), jnp.bfloat16),
        (wide, jnp.bfloat16),
    ]
    return call(
        functools.partial(forward_kernel, step),
        [jax.ShapeDtypeStruct(*shape) for shape in shapes],
        [states, *around, kernel, norm_gain, w_up],
        "vvvvvvvv",
        "hhhhhh",
        scratch=[pltpu.VMEM(*shape) for shape in shapes]
        + [pltpu.VMEM(wide, jnp.float32), pltpu.SemaphoreType.DMA((7,))],
        flops=2 * count * hid * channels,
        moved=2**22,
        limit=12,
    )


def transposed(value):
    return value.astype(jnp.float32).T.astype(jnp.bfloat16)


LANES_BOTH = (((1,), (1,)), ((), ()))


def network_kernel(moved_ref, down_ref, up_ref, gain_ref, slope_hbm, n_hbm, inv_hbm, out_hbm, grad_hbm, saved_hbm, *refs):
    slope_ref, n_ref, inv_ref, out_ref, grad_ref, sems = refs
    arriving = copies(sems, 0, [(slope_hbm, slope_ref), (n_hbm, n_ref), (inv_hbm, inv_ref)])
    leaving = copies(sems, 3, [(moved_ref, saved_hbm)])
    moved = moved_ref[...].astype(jnp.float32).T
    grad_hidden = jnp.dot(moved.astype(jnp.bfloat16), down_ref[...], preferred_element_type=jnp.float32)
    arriving[0].wait()
    grad_pre = (grad_hidden * slope_ref[...].astype(jnp.float32)).astype(jnp.bfloat16)
    grad_ref[...] = grad_pre
    leaving += copies(sems, 4, [(grad_ref, grad_hbm)])
    grad_n = lax.dot_general(grad_pre, up_ref[...], LANES_BOTH, preferred_element_type=jnp.float32)
    finish(arriving[1:])
    narrow, gain = n_ref[...].astype(jnp.float32), gain_ref[...]
    mean = jnp.mean(grad_n * narrow, axis=1, keepdims=True)
    field = moved + inv_ref[:, :1] * (grad_n * gain - narrow * (mean / gain))
    out_ref[...] = field.T.astype(jnp.bfloat16)
    finish(leaving + copies(sems, 5, [(out_ref, out_hbm)]))


def network_back(moved, w_down, w_up, norm_gain, slope, narrow, inv_root):
    channels, count = moved.shape
    hid = w_down.shape[1]
    shapes = [((channels, count), jnp.bfloat16), ((count, hid), jnp.bfloat16), ((channels, count), jnp.bfloat16)]
    return call(
        network_kernel,
        [jax.ShapeDtypeStruct(*shape) for shape in shapes],
        [moved, w_down, w_up, norm_gain, slope, narrow, inv_root],
        "vvvvhhh",
        "hhh",
        scratch=[pltpu.VMEM(value.shape, value.dtype) for value in (slope, narrow, inv_root)]
        + [pltpu.VMEM(*shape) for shape in shapes[:2]]
        + [pltpu.SemaphoreType.DMA((6,))],
        flops=4 * count * hid * channels,
        moved=4 * 2**20,
        limit=12,
    )


def stencil_sums(pad_ref, field, tile):
    rows_out, cols_out = tile
    field = field.reshape(rows_out, cols_out, -1)
    padded = pad_ref[...].astype(jnp.float32)
    result = [None] * 9
    for col_tap in range(3):
        place = MARGIN - 1 + col_tap
        shifted_cols = padded[:, place : place + cols_out]
        for row_tap in range(3):
            products = jnp.sum(shifted_cols[row_tap : row_tap + rows_out] * field, axis=0)
            result[3 * row_tap + col_tap] = jnp.sum(products, axis=0, keepdims=True)
    return result


def sums_rows(rows, term, gain):
    rows = rows + [jnp.sum(term, axis=0, keepdims=True) / gain, jnp.zeros((ROWS - 10, term.shape[1]), jnp.float32)]
    return jnp.concatenate(rows, axis=0)


def sums_kernel(steps, tile, up_ref, gain_ref, *refs):
    inputs, (out_ref, *refs) = refs[: 4 * steps], refs[4 * steps :]
    pads, fields, grads, narrows, sems = refs
    places = [(ref, place.at[k]) for k in range(steps) for ref, place in zip(inputs[4 * k : 4 * k + 4], refs[:4])]
    arriving = copies(sems, 0, places)
    rows, term = None, None
    for k in range(steps):
        finish(arriving[4 * k : 4 * k + 4])
        grad_n = lax.dot_general(grads[k], up_ref[...], LANES_BOTH, preferred_element_type=jnp.float32)
        product = grad_n * narrows[k].astype(jnp.float32)
        term = product if term is None else term + product
        more = stencil_sums(pads.at[k], fields[k].astype(jnp.float32).T, tile)
        rows = more if rows is None else [a + b for a, b in zip(rows, more)]
    out_ref[...] = sums_rows(rows, term, gain_ref[...])


def channel_sums(tile, w_up, norm_gain, pads, fields, grads, narrows):
    steps = len(fields)
    inputs = [value for group in zip(pads, fields, grads, narrows) for value in group]
    return call(
        functools.partial(sums_kernel, steps, tile),
        [jax.ShapeDtypeStruct((ROWS, fields[0].shape[0]), jnp.float32)],
        [w_up, norm_gain, *inputs],
        "vv" + "h" * 4 * steps,
        "v",
        scratch=[pltpu.VMEM((steps, *value.shape), value.dtype) for value in inputs[:4]]
        + [pltpu.SemaphoreType.DMA((4 * steps,))],
        moved=2**21,
        limit=12,
    )[0]


QUADRANTS = 4


def lon_bit(at):
    return lax.axis_index("lon") >> at & 1


def last_kernel(steps, tile, lon_groups, moved_ref, down_ref, up_ref, gain_ref, sums_ref, *refs):
    slope_hbm, n_hbm, inv_hbm, pad_hbm, *refs = refs
    inputs, refs = refs[: 4 * steps - 2], refs[4 * steps - 2 :]
    field_ref, total_ref, send_ref, keep_ref, slope_ref, n_ref, inv_ref, pad_ref, left_ref, right_ref, sems = refs
    arriving = copies(
        sems, 0, [(slope_hbm, slope_ref), (n_hbm, n_ref), (inv_hbm, inv_ref), (pad_hbm, pad_ref)]
    )
    count = slope_ref.shape[0]
    part = lambda s: pl.ds(s * count, count)
    narrows, grads = inputs[:steps], inputs[steps : 2 * steps - 1]
    moveds, hiddens = inputs[2 * steps - 1 : 3 * steps - 2], inputs[3 * steps - 2 :]
    pairs = [(ref, left_ref.at[0, :, part(s)]) for s, ref in enumerate(narrows)]
    pairs += [(ref, right_ref.at[0, part(s)]) for s, ref in enumerate(grads)]
    pairs += [(ref, left_ref.at[1, :, part(s)]) for s, ref in enumerate(moveds)]
    pairs += [(ref, right_ref.at[1, part(s)]) for s, ref in enumerate(hiddens)]
    later = copies(sems, 4, pairs)
    left_ref[1, :, (steps - 1) * count :] = moved_ref[...]
    moved = moved_ref[...].astype(jnp.float32).T
    channels = moved.shape[1]
    grad_hidden = jnp.dot(moved.astype(jnp.bfloat16), down_ref[...], preferred_element_type=jnp.float32)
    arriving[0].wait()
    grad_pre = (grad_hidden * slope_ref[...].astype(jnp.float32)).astype(jnp.bfloat16)
    right_ref[0, (steps - 1) * count :] = grad_pre
    grad_n = lax.dot_general(grad_pre, up_ref[...], LANES_BOTH, preferred_element_type=jnp.float32)
    finish(arriving[1:])
    narrow, gain = n_ref[...].astype(jnp.float32), gain_ref[...]
    term = grad_n * narrow
    mean = jnp.mean(term, axis=1, keepdims=True)
    field = moved + inv_ref[:, :1] * (grad_n * gain - narrow * (mean / gain))
    narrow_field = field.astype(jnp.bfloat16)
    field_ref[...] = narrow_field
    total = sums_ref[...] + sums_rows(stencil_sums(pad_ref, narrow_field.astype(jnp.float32), tile), term, gain)
    total_ref[...] = total
    finish(later)
    if send_ref.ndim == 3:
        for k in range(2):
            send_ref[k] = jnp.dot(left_ref[k], right_ref[k], preferred_element_type=jnp.float32).astype(jnp.bfloat16)
        keep_ref[...] = jnp.zeros_like(keep_ref)
        return
    quadrant_rows = channels // 4
    send_ref[2 * QUADRANTS * quadrant_rows :] = pieces_of(total)
    chunk = channels // (4 * lon_groups)
    width = right_ref.shape[2] // 2
    for k in range(2):
        rows = []
        for core in (1 - lon_bit(0), lon_bit(0)):
            for x in range(2):
                for z in range(lon_groups):
                    start = pl.multiple_of((4 * z + 2 * x + core) * chunk, chunk)
                    rows.append(left_ref[k, pl.ds(start, chunk)])
        rows = jnp.concatenate(rows, axis=0)
        value = jnp.dot(rows, right_ref[k], preferred_element_type=jnp.float32).astype(jnp.bfloat16)
        size = lon_groups * chunk
        for q in range(QUADRANTS):
            x, lat = q // 2, q % 2
            columns = slice(lat * width, (lat + 1) * width)
            start = (k * QUADRANTS + q) * quadrant_rows
            send_ref[start : start + quadrant_rows] = value[x * size : (x + 1) * size, columns]
            keep_ref[k, q] = value[(2 + x) * size : (3 + x) * size, columns]


def last_step(tile, moved, w_down, w_up, norm_gain, sums, forward, grads, moveds):
    steps = len(forward)
    channels, count = moved.shape
    hid = w_down.shape[1]
    narrow, _, inv_root, _, slope, pad = forward[-1]
    lon_groups = lax.axis_size("lon") // 4
    by_quadrant = lax.axis_size("lat") == 2 and lon_groups == 4
    send = (2, channels, hid)
    keep = (8, 128)
    if by_quadrant:
        send = (2 * channels + PIECES * ROWS, hid // 2)
        keep = (2, QUADRANTS, channels // 4, hid // 2)
    sds = jax.ShapeDtypeStruct
    inputs = [parts[1] for parts in forward] + grads + moveds + [parts[3] for parts in forward]
    return call(
        functools.partial(last_kernel, steps, tile, lon_groups),
        [
            sds((count, channels), jnp.bfloat16),
            sds((ROWS, channels), jnp.float32),
            sds(send, jnp.bfloat16),
            sds(keep, jnp.bfloat16),
        ],
        [moved, w_down, w_up, norm_gain, sums, slope, narrow, inv_root, pad, *inputs],
        "vvvvv" + "h" * (4 + len(inputs)),
        "vppp",
        scratch=[pltpu.VMEM(value.shape, value.dtype) for value in (slope, narrow, inv_root, pad)]
        + [pltpu.VMEM((2, channels, steps * count), jnp.bfloat16), pltpu.VMEM((2, steps * count, hid), jnp.bfloat16)]
        + [pltpu.SemaphoreType.DMA((len(inputs) + 4,))],
        flops=2**31,
        moved=6 * 2**20,
        limit=20,
    )


def fill_margins(wide_ref, before, after, low, high, middle):
    rows_out, cols_out, _ = middle.shape
    around = slice(MARGIN - 1, MARGIN + cols_out + 1)
    wide_ref[:1, around] = low.astype(jnp.float32)
    wide_ref[1 + rows_out :, around] = high.astype(jnp.float32)
    wide_ref[1 : 1 + rows_out, MARGIN - 1 : MARGIN] = before.astype(jnp.float32)
    wide_ref[1 : 1 + rows_out, MARGIN + cols_out : MARGIN + cols_out + 1] = after.astype(jnp.float32)
    wide_ref[1 : 1 + rows_out, MARGIN : MARGIN + cols_out] = middle


def final_kernel(field_ref, before_ref, after_ref, low_ref, high_ref, kernel_ref, out_ref, wide_ref):
    rows_out, cols_out, _ = field_ref.shape
    result = field_ref[...].astype(jnp.float32)
    fill_margins(wide_ref, before_ref[0], after_ref[0], low_ref[0], high_ref[0], result)
    for col_tap in range(3):
        place = MARGIN + 1 - col_tap
        shifted_cols = wide_ref[:, place : place + cols_out]
        for row_tap in range(3):
            tap = kernel_ref[row_tap, col_tap : col_tap + 1]
            result = result + tap[None] * shifted_cols[2 - row_tap : 2 - row_tap + rows_out]
    out_ref[...] = result.astype(jnp.bfloat16)


def final_parts(field, around, kernel):
    rows_out, cols_out, channels = field.shape
    return call(
        final_kernel,
        [jax.ShapeDtypeStruct(field.shape, jnp.bfloat16)],
        [field, *around, kernel],
        "v" * 6,
        "v",
        scratch=[pltpu.VMEM((rows_out + 2, cols_out + 2 * MARGIN, channels), jnp.float32)],
        moved=2**19,
    )[0]


def spatial_kernel(mode, step, near_lon, near_lat, *refs):
    refs = list(refs)
    take = lambda: refs.pop(0)
    with_stencil = mode != "first"
    move_hbm = take()
    in_ref = take()
    kern_ref = take() if with_stencil else None
    weight_hbm = take() if mode == "mid" else None
    out_hbm = take()
    saved_hbm = take() if mode == "first" else None
    out_ref, sems = take(), take()
    spread_ref, weight_ref, move_ref = take(), take(), take()
    moving = copies(sems, 3, [(move_hbm, move_ref)])
    tiles_lon, tiles_lat, _, lanes = in_ref.shape
    rows = out_ref.shape[2]
    started = []
    if mode == "mid":
        arriving = copies(sems, 0, [(weight_hbm, weight_ref)])
    if mode == "first":
        weight_ref[...] = in_ref[:, :, rows:]
        started += copies(sems, 0, [(weight_ref, saved_hbm)])
    lane = lax.broadcasted_iota(jnp.int32, (rows, lanes), 1)
    col = lax.rem(lane, near_lat)
    lat_last, lat_first = col == near_lat - 1, col == 0
    lon_last, lon_first = lane >= lanes - near_lat, lane < near_lat
    tiles = [(a, b) for a in range(tiles_lon) for b in range(tiles_lat)]

    def turn(value, steps):
        return pltpu.roll(value, steps % lanes if isinstance(steps, int) else steps, 1)

    def lat_after(grid):
        turned = {key: turn(value, -1) for key, value in grid.items()}
        wrapped = {key: turn(grid[key], near_lat - 1) for key in tiles if key[1] > 0}
        return {(a, b): jnp.where(lat_last, wrapped.get((a, b + 1), 0.0), turned[a, b]) for a, b in tiles}

    def lat_before(grid):
        turned = {key: turn(value, 1) for key, value in grid.items()}
        wrapped = {key: turn(grid[key], 1 - near_lat) for key in tiles if key[1] < tiles_lat - 1}
        return {(a, b): jnp.where(lat_first, wrapped.get((a, b - 1), 0.0), turned[a, b]) for a, b in tiles}

    def lon_after(grid):
        return {
            (a, b): turn(jnp.where(lon_first, grid[(a + 1) % tiles_lon, b], grid[a, b]), -near_lat) for a, b in tiles
        }

    def lon_before(grid):
        return {(a, b): turn(jnp.where(lon_last, grid[(a - 1) % tiles_lon, b], grid[a, b]), near_lat) for a, b in tiles}

    grid = {(a, b): in_ref[a, b, :rows].astype(jnp.float32) for a, b in tiles}
    if with_stencil:
        taps = [
            [jnp.broadcast_to(kern_ref[:, 3 * a + b : 3 * a + b + 1], (rows, lanes)) for b in range(3)] for a in range(3)
        ]
        by_col = [lat_after(grid), grid, lat_before(grid)]
        mix = [
            {key: sum(taps[row][c] * by_col[c][key] for c in range(1, 3)) + taps[row][0] * by_col[0][key] for key in tiles}
            for row in range(3)
        ]
        high, low = lon_after(mix[0]), lon_before(mix[2])
        grid = {key: grid[key] + mix[1][key] + (high[key] + low[key]) for key in tiles}
    if mode == "mid":
        grid = {key: value.astype(jnp.bfloat16).astype(jnp.float32) for key, value in grid.items()}
        finish(arriving)
    weights = {}
    for a, b in tiles:
        four = weight_ref[a, b].astype(jnp.float32)[4 * step : 4 * step + 4]
        weights[a, b] = [jnp.broadcast_to(four[k : k + 1], (rows, lanes)) for k in range(4)]
    weighted = [{key: weights[key][k] * grid[key] for key in tiles} for k in range(4)]
    own, lon = lat_after(weighted[2]), lat_after(weighted[3])
    lon = lon_after({key: weighted[1][key] + lon[key] for key in tiles})
    for a, b in tiles:
        value = (weighted[0][a, b] + own[a, b] + lon[a, b]).astype(jnp.bfloat16).astype(jnp.float32)
        for place in range(a, tiles_lon + LON_REACH, tiles_lon):
            spread_ref[place, b] = value
    spread_ref[:, tiles_lat:] = jnp.zeros((tiles_lon + LON_REACH, LAT_REACH, rows, lanes), jnp.float32)

    finish(moving)
    lon_move, lat_move = move_ref[step, 0], move_ref[step, 1]
    far_lon, off_lon = lon_move // near_lon, lax.rem(lon_move, near_lon)
    far_lat, off_lat = lat_move // near_lat, lax.rem(lat_move, near_lat)
    shift = off_lon * near_lat + off_lat
    turn_here = lax.rem(2 * lanes - shift, lanes)
    turn_next = lax.rem(2 * lanes - shift + near_lat, lanes)
    same_lon = lane >= off_lon * near_lat
    same_lat = col + off_lat < near_lat
    half = tiles_lon // 2
    for a in range(tiles_lon):
        met = [
            jnp.where(same_lon, spread_ref[far_lon + a, far_lat + b], spread_ref[far_lon + a + 1, far_lat + b])
            for b in range(tiles_lat + 1)
        ]
        for b in range(tiles_lat):
            value = jnp.where(same_lat, turn(met[b], turn_here), turn(met[b + 1], turn_next))
            out_ref[a, b] = value.astype(jnp.bfloat16)
        if (a + 1) % half == 0:
            part = pl.ds(a + 1 - half, half)
            started += copies(sems, 1 + a // half, [(out_ref.at[part], out_hbm.at[part])])
    finish(started)


def spatial(mode, step, tile, rows, field, kern, weights, moves):
    tiles_lon, tiles_lat, _, lanes = field.shape
    with_stencil = mode != "first"
    operands = [moves, field]
    operands += [kern] if with_stencil else []
    operands += [weights] if mode == "mid" else []
    out_shape = (tiles_lon, tiles_lat, rows, lanes)
    weight_shape = (tiles_lon, tiles_lat, ROWS, lanes)
    sds = jax.ShapeDtypeStruct
    out = [sds(out_shape, jnp.bfloat16)] + ([sds(weight_shape, jnp.bfloat16)] if mode == "first" else [])
    scratch = [pltpu.VMEM(out_shape, jnp.bfloat16), pltpu.SemaphoreType.DMA((4,))]
    spread_shape = (tiles_lon + LON_REACH, tiles_lat + LAT_REACH, rows, lanes)
    scratch += [pltpu.VMEM(spread_shape, jnp.float32), pltpu.VMEM(weight_shape, jnp.bfloat16)]
    scratch += [pltpu.SMEM(moves.shape, jnp.int32)]
    return call(
        functools.partial(spatial_kernel, mode, step, *tile),
        out,
        operands,
        "hv" + "v" * with_stencil + "h" * (mode == "mid"),
        "h" * len(out),
        scratch=scratch,
        flops=2**22,
        moved=2**20,
        limit=max(8, 14 * tiles_lon * tiles_lat * rows * lanes * 4 // MIB),
    )


def halved(value, axis, bit, dim):
    count = lax.axis_size(axis)
    mine = lax.axis_index(axis) >> bit & 1
    kept = lax.dynamic_index_in_dim(value, mine, dim, keepdims=False)
    sent = lax.dynamic_index_in_dim(value, 1 - mine, dim, keepdims=False).astype(jnp.bfloat16)
    arrived = lax.ppermute(sent, axis, [(i, i ^ (1 << bit)) for i in range(count)])
    return kept + arrived.astype(jnp.float32)


def scattered(value, lat_first):
    channels, hid = value.shape
    lon_bits = lax.axis_size("lon").bit_length() - 1
    lat_bits = lax.axis_size("lat").bit_length() - 1
    rows = channels >> lon_bits
    value = value.reshape(*([2] * lon_bits), rows, *([2] * lat_bits), hid >> lat_bits)

    def over_lon(value, bit, left):
        return halved(value, "lon", bit, left.index(bit)), [k for k in left if k != bit]

    left_lon = list(range(lon_bits))[::-1]
    left_lat = list(range(lat_bits))[::-1]
    order = [("lon", 0), ("lon", 1)] + [("lat", k) for k in range(lat_bits)]
    if lat_first:
        order = [("lon", 0)] + [("lat", k) for k in range(lat_bits)] + [("lon", 1)]
    order += [("lon", k) for k in range(2, lon_bits)]
    for axis, bit in order:
        if axis == "lon":
            value, left_lon = over_lon(value, bit, left_lon)
        else:
            value = halved(value, "lat", bit, len(left_lon) + 1 + left_lat.index(bit))
            left_lat.remove(bit)
    return value


def add_parts(pairs, kept, arrived):
    for q, out_ref, place in pairs:
        value = kept(q).astype(jnp.float32) + arrived(q).astype(jnp.float32)
        out_ref[place] = value.astype(out_ref.dtype)


def quadrant_kernel(kept_ref, total_ref, arrived_ref, send_ref, keep_ref, chip_ref):
    core, x, lat = lon_bit(0), lon_bit(1), lax.axis_index("lat")
    rows = kept_ref.shape[2]
    for k in range(2):
        for j in range(2):
            kept = (1 - core) * (2 * x + j) + core * (2 * j + lat)
            sent = (1 - core) * (2 * (1 - x) + j) + core * (2 * j + 1 - lat)
            pairs = [(sent, send_ref, pl.ds((2 * k + j) * rows, rows)), (kept, keep_ref, (k, j))]
            arrived = lambda q: arrived_ref[pl.ds(pl.multiple_of((k * QUADRANTS + q) * rows, rows), rows)]
            add_parts(pairs, lambda q: kept_ref[k, q], arrived)
    chip = total_ref[...] + whole_of(arrived_ref[2 * QUADRANTS * rows :])
    chip_ref[...] = chip
    send_ref[4 * rows :] = pieces_of(chip)


def half_kernel(kept_ref, chip_ref, arrived_ref, send_ref, keep_ref, beside_ref):
    core, x, lat = lon_bit(0), lon_bit(1), lax.axis_index("lat")
    mine = (1 - core) * lat + core * x
    rows = kept_ref.shape[2]
    for k in range(2):
        pairs = [(1 - mine, send_ref, pl.ds(k * rows, rows)), (mine, keep_ref, k)]
        arrived = lambda q: arrived_ref[pl.ds(pl.multiple_of((2 * k + q) * rows, rows), rows)]
        add_parts(pairs, lambda q: kept_ref[k, q], arrived)
    sums = PIECES * ROWS
    beside = arrived_ref[4 * rows :]
    beside_ref[...] = whole_of(beside)
    send_ref[2 * rows : 2 * rows + sums] = pieces_of(chip_ref[...])
    send_ref[2 * rows + sums :] = beside


def rows_kernel(groups, bit_at, *refs):
    kept_ref, *total_refs, arrived_ref, send_ref, keep_ref, total_ref = refs
    bit = lon_bit(bit_at)
    rows = kept_ref.shape[1]
    chunk = rows // (2 * groups)
    for k in range(2):
        for p in range(groups):
            goal = pl.ds(p * chunk, chunk)
            places = [pl.multiple_of((2 * p + which) * chunk, chunk) for which in (1 - bit, bit)]
            pairs = [
                (places[0], send_ref, pl.ds(k * groups * chunk + p * chunk, chunk)),
                (places[1], keep_ref, (k, goal)),
            ]
            arrived = lambda q: arrived_ref[pl.ds(pl.multiple_of(k * rows + q, chunk), chunk)]
            add_parts(pairs, lambda q: kept_ref[k, pl.ds(q, chunk)], arrived)
    total = add_sums(total_refs, arrived_ref, 2 * rows)
    total_ref[...] = total
    send_ref[2 * groups * chunk :] = pieces_of(total)


def add_sums(total_refs, arrived_ref, start):
    size = PIECES * ROWS
    arrived = whole_of(arrived_ref[start : start + size])
    if len(total_refs) == 1:
        return total_refs[0][...] + arrived
    chip, beside = (ref[...] for ref in total_refs)
    return (chip + whole_of(arrived_ref[start + size :])) + (beside + arrived)


def last_sum_kernel(kept_ref, total_ref, arrived_ref, up_ref, down_ref, taps_ref, gain_ref):
    rows = kept_ref.shape[1]
    up_ref[...] = kept_ref[0] + arrived_ref[:rows].astype(jnp.float32)
    down_ref[...] = kept_ref[1] + arrived_ref[rows : 2 * rows].astype(jnp.float32)
    total = add_sums([total_ref], arrived_ref, 2 * rows)
    for k in range(9):
        taps_ref[k // 3, k % 3 : k % 3 + 1] = total[k : k + 1]
    gain_ref[...] = total[9:10]


def all_sums(send, keep, total):
    lon, lat = lax.axis_size("lon"), lax.axis_size("lat")
    channels = total.shape[1]
    if send.ndim == 3:
        parts = [scattered(send[k].astype(jnp.float32), k == 1) for k in range(2)]
        total = lax.psum(total, AXES)
        return (*parts, total[:9].reshape(3, 3, channels), total[9])
    places = [(i, j) for i in range(lon) for j in range(lat)]
    flat = lambda i, j: i * lat + j

    def traded(value, partner):
        return lax.ppermute(value, AXES, [(flat(i, j), flat(*partner(i, j))) for i, j in places])

    sds = jax.ShapeDtypeStruct

    def stage(kernel, shape, kept, totals, arrived, sums):
        sent = 2 * shape[-2] * (shape[1] if len(shape) == 4 else 1) + PIECES * ROWS * sums
        out = [sds((sent, shape[-1]), jnp.bfloat16), sds(shape, jnp.float32), sds(total.shape, jnp.float32)]
        operands = [kept, *totals, arrived]
        return call(kernel, out, operands, "v" * len(operands), "ppp", moved=2**20, limit=12)

    rows, width = keep.shape[2:]
    arrived = traded(send, lambda i, j: (i ^ 1, j))
    send, keep, chip = stage(quadrant_kernel, (2, 2, rows, width), keep, [total], arrived, 1)
    arrived = traded(send, lambda i, j: (i, j ^ 1) if i & 1 else (i ^ 2, j))
    send, keep, beside = stage(half_kernel, (2, rows, width), keep, [chip], arrived, 2)
    arrived = traded(send, lambda i, j: (i ^ 2, j) if i & 1 else (i, j ^ 1))
    kernel = functools.partial(rows_kernel, 2, 2)
    send, keep, total = stage(kernel, (2, rows // 2, width), keep, [chip, beside], arrived, 1)
    arrived = traded(send, lambda i, j: (i ^ 4, j))
    kernel = functools.partial(rows_kernel, 1, 3)
    send, keep, total = stage(kernel, (2, rows // 4, width), keep, [total], arrived, 1)
    arrived = traded(send, lambda i, j: (i ^ 8, j))
    part = sds((rows // 4, width), jnp.float32)
    out = [part, part, sds((3, 3, channels), jnp.float32), sds((1, channels), jnp.float32)]
    up, down, taps, gain = call(last_sum_kernel, out, [keep, total, arrived], "vvv", "vvvv", moved=2**18)
    return up, down, taps, gain.reshape(channels)


def local(cotangent, states, w_up, w_down, norm_gain, kernel, bilinear, lon_move, lat_move):
    steps, rows_out, cols_out, channels = states.shape
    tiles_lon, tiles_lat = lax.axis_size("lon"), lax.axis_size("lat")
    devices = tiles_lon * tiles_lat
    count = rows_out * cols_out
    tile = (rows_out, cols_out)
    share = channels // devices
    padded_share = -(-share // ROWS) * ROWS
    whole_share = share == padded_share
    group_size = channels // lon_move.shape[1]
    me = lax.axis_index("lon") * tiles_lat + lax.axis_index("lat")

    def as_blocks(value):
        value = value.reshape(devices, share, count)
        return value if whole_share else jnp.pad(value, ((0, 0), (0, padded_share - share), (0, 0)))

    def as_rows(blocks):
        return blocks[:, :share].reshape(channels, count)

    def as_grid(blocks):
        return blocks.reshape(tiles_lon, tiles_lat, *blocks.shape[1:])

    blocks = packed(cotangent, bilinear, devices)
    blocks, states_later = lax.optimization_barrier((blocks, states))
    arrived = as_grid(exchanged(blocks))
    group = me * share // group_size
    moves = jnp.stack([lon_move[:, group], lat_move[:, group]], axis=1)
    grid_now, weights = spatial("first", steps - 1, tile, padded_share, arrived, None, None, moves)

    taps = lax.dynamic_slice_in_dim(kernel.reshape(9, channels), me * share, share, 1).T
    taps = jnp.pad(taps, ((0, padded_share - share), (0, count - 9)))

    before, after = lat_edges(states_later)
    grid_now, before, after = lax.optimization_barrier((grid_now, before, after))
    around = (before, after, *lon_edges(states, before, after))
    order = list(reversed(range(steps)))
    gain = norm_gain.reshape(1, channels)
    forward = {s: forward_parts(s, states, around, kernel, gain, w_up) for s in order}

    moved, grads, fields = {}, {}, {}
    for s in order[:-1]:
        here = as_rows(exchanged(grid_now.reshape(devices, padded_share, count)))
        if s != order[0]:
            here, forward = lax.optimization_barrier((here, forward))
        narrow, _, inv_root, _, slope, _ = forward[s]
        fields[s], grads[s], moved[s] = network_back(here, w_down, w_up, gain, slope, narrow, inv_root)
        arrived = as_grid(exchanged(as_blocks(fields[s])))
        (grid_now,) = spatial("mid", s - 1, tile, padded_share, arrived, taps, weights, moves)

    here = as_rows(exchanged(grid_now.reshape(devices, padded_share, count)))
    earlier = lambda values: [values[s] for s in order[:-1]]
    pads, narrows = ([forward[s][k] for s in order[:-1]] for k in (5, 0))
    sums = channel_sums(tile, w_up, gain, pads, earlier(fields), earlier(grads), narrows)
    here, sums = lax.optimization_barrier((here, sums))
    parts = ([forward[s] for s in order], earlier(grads), earlier(moved))
    field, total, send, keep = last_step(tile, here, w_down, w_up, gain, sums, *parts)
    field = field.reshape(cotangent.shape)
    before, after = lat_edges(field[None])
    grad_state = final_parts(field, (before, after, *lon_edges(field[None], before, after)), kernel)
    return (grad_state, *all_sums(send, keep, total))


def solution(mesh):
    placed = (
        P("lon", "lat", None),
        P(None, "lon", "lat", None),
        P(),
        P(),
        P(),
        P(),
        P(None, None, "lon", "lat"),
        P(),
        P(),
    )
    return jax.shard_map(
        local,
        mesh=mesh,
        in_specs=placed,
        out_specs=(P("lon", "lat", None), P("lon", "lat"), P("lon", "lat"), P(), P()),
        check_vma=False,
    )
```

```python
import functools

import jax
import jax.numpy as jnp
from jax import lax
from jax.experimental import pallas as pl
from jax.experimental.pallas import tpu as pltpu
from jax.sharding import PartitionSpec as P

EPSILON = 1e-06
AXES = ("lon", "lat")
ROWS = 16
LAT_REACH = 2
LON_REACH = 8
MIB = 1024 * 1024


def exchanged(blocks):
    return lax.all_to_all(blocks, AXES, split_axis=0, concat_axis=0, tiled=True)


SPACES = {"s": pltpu.SMEM, "v": pltpu.VMEM, "p": pltpu.VMEM, "h": pltpu.HBM}
PINNED = {"p": pltpu.VMEM, "h": pltpu.HBM}


def call(kernel, out_shape, operands, ins, outs, scratch=(), flops=0, moved=0, limit=8):
    operands = [
        pltpu.with_memory_space_constraint(value, PINNED[kind]) if kind in PINNED else value
        for kind, value in zip(ins, operands, strict=True)
    ]
    out_shape = [
        PINNED[kind](value.shape, value.dtype) if kind in PINNED else value
        for kind, value in zip(outs, out_shape, strict=True)
    ]
    return pl.pallas_call(
        kernel,
        out_shape=out_shape,
        in_specs=[pl.BlockSpec(memory_space=SPACES[kind]) for kind in ins],
        out_specs=[pl.BlockSpec(memory_space=SPACES[kind]) for kind in outs],
        scratch_shapes=scratch,
        compiler_params=pltpu.CompilerParams(vmem_limit_bytes=limit * MIB),
        cost_estimate=pl.CostEstimate(flops=flops, bytes_accessed=moved, transcendentals=0),
    )(*operands)


def copies(sems, first, pairs):
    started = [pltpu.make_async_copy(src, dst, sems.at[first + k]) for k, (src, dst) in enumerate(pairs)]
    for copy in started:
        copy.start()
    return started


def finish(started):
    for copy in started:
        copy.wait()


PIECES = 3
SUMS = 10
SUM_ROWS = 32


def pieces_of(value):
    value = value[:SUMS]
    parts = []
    for _ in range(PIECES):
        parts.append(value.astype(jnp.bfloat16).astype(jnp.float32))
        value = value - parts[-1]
    parts.append(jnp.zeros((SUM_ROWS - PIECES * SUMS, value.shape[1]), jnp.float32))
    return jnp.concatenate(parts, axis=0).astype(jnp.bfloat16)


def whole_of(parts):
    parts = parts.astype(jnp.float32)
    total = (parts[:SUMS] + parts[SUMS : 2 * SUMS]) + parts[2 * SUMS : 3 * SUMS]
    return jnp.concatenate([total, jnp.zeros((ROWS - SUMS, parts.shape[1]), jnp.float32)], axis=0)


def pack_kernel(cotangent_hbm, weight_hbm, out_hbm, cotangent_ref, weight_ref, out_ref, sems):
    started = copies(sems, 0, [(cotangent_hbm, cotangent_ref), (weight_hbm, weight_ref)])
    channels = cotangent_ref.shape[1]
    devices, _, count = out_ref.shape
    share = channels // devices
    started[1].wait()
    rows = weight_ref.shape[0]
    weights = jnp.concatenate([weight_ref[:, i] for i in range(weight_ref.shape[1])], axis=1)
    weights = jnp.concatenate([weights, jnp.zeros((ROWS - rows, count), jnp.float32)], axis=0)
    weights = weights.astype(jnp.bfloat16)
    out_ref[:, share:] = jnp.broadcast_to(weights[None], (devices, ROWS, count))
    started[0].wait()
    turned = cotangent_ref[...].astype(jnp.float32).T.astype(jnp.bfloat16)
    out_ref[:, :share] = turned.reshape(devices, share, count)
    finish(copies(sems, 2, [(out_ref, out_hbm)]))


def packed(cotangent, bilinear, devices):
    rows_out, cols_out, channels = cotangent.shape
    steps, corners = bilinear.shape[:2]
    count = rows_out * cols_out
    share = channels // devices
    if share % ROWS:
        blocks = cotangent.reshape(count, channels).T.reshape(devices, share, count)
        blocks = jnp.pad(blocks, ((0, 0), (0, -share % ROWS), (0, 0)))
        weights = bilinear.reshape(steps * corners, count).astype(jnp.bfloat16)
        weights = jnp.pad(weights, ((0, ROWS - steps * corners), (0, 0)))
        return jnp.concatenate([blocks, jnp.broadcast_to(weights[None], (devices, ROWS, count))], axis=1)
    shape = (devices, share + ROWS, count)
    return call(
        pack_kernel,
        [jax.ShapeDtypeStruct(shape, jnp.bfloat16)],
        [cotangent.reshape(count, channels), bilinear.reshape(steps * corners, rows_out, cols_out)],
        "hh",
        "h",
        scratch=[
            pltpu.VMEM((count, channels), jnp.bfloat16),
            pltpu.VMEM((steps * corners, rows_out, cols_out), jnp.float32),
            pltpu.VMEM(shape, jnp.bfloat16),
            pltpu.SemaphoreType.DMA((3,)),
        ],
        moved=2**19,
    )[0]


def lat_edges(states, held=lambda value: value):
    lat, lat_at = lax.axis_size("lat"), lax.axis_index("lat")
    first, last = states[:, :, :1], states[:, :, -1:]
    if lat == 2:
        arrived = lax.ppermute(jnp.where(lat_at == 0, last, first), "lat", [(0, 1), (1, 0)])
        arrived = held(arrived)
        return jnp.where(lat_at == 0, 0, arrived), jnp.where(lat_at == 0, arrived, 0)
    return (
        lax.ppermute(last, "lat", [(i, i + 1) for i in range(lat - 1)]),
        lax.ppermute(first, "lat", [(i + 1, i) for i in range(lat - 1)]),
    )


def lon_edges(states, before, after):
    lon = lax.axis_size("lon")
    ahead = lambda value: lax.ppermute(value, "lon", [(i, (i + 1) % lon) for i in range(lon)])
    behind = lambda value: lax.ppermute(value, "lon", [(i, (i - 1) % lon) for i in range(lon)])
    row = lambda place: jnp.concatenate([part[:, place] for part in (before, states, after)], axis=2)
    return ahead(row(slice(-1, None))), behind(row(slice(0, 1)))


MARGIN = 8


def forward_kernel(
    step, states_ref, before_ref, after_ref, low_ref, high_ref, kernel_ref, gain_ref, up_ref,
    n_hbm, turned_hbm, inv_hbm, hid_hbm, slope_hbm, pad_hbm,
    n_ref, turned_ref, inv_ref, hid_ref, slope_ref, pad_ref, wide_ref, sems,
):
    rows_out, cols_out, channels = states_ref.shape[1:]
    count = rows_out * cols_out
    mixed = states_ref[step].astype(jnp.float32)
    fill_margins(wide_ref, before_ref[step], after_ref[step], low_ref[step], high_ref[step], mixed)
    pad_ref[...] = wide_ref[...].astype(jnp.bfloat16)
    leaving = copies(sems, 1, [(pad_ref, pad_hbm)])
    for col_tap in range(3):
        place = MARGIN - 1 + col_tap
        shifted_cols = wide_ref[:, place : place + cols_out]
        for row_tap in range(3):
            tap = kernel_ref[row_tap, col_tap : col_tap + 1]
            mixed = mixed + tap[None] * shifted_cols[row_tap : row_tap + rows_out]
    mixed = mixed.reshape(count, channels)
    inv_root = lax.rsqrt(jnp.mean(mixed * mixed, axis=1, keepdims=True) + EPSILON)
    narrow = mixed * inv_root * gain_ref[...]
    n_ref[...] = narrow.astype(jnp.bfloat16)
    inv_ref[...] = jnp.broadcast_to(inv_root, inv_ref.shape)
    leaving += copies(sems, 2, [(n_ref, n_hbm), (inv_ref, inv_hbm)])
    pre = jnp.dot(n_ref[...], up_ref[...], preferred_element_type=jnp.float32)
    sigmoid = jax.nn.sigmoid(pre)
    slope_ref[...] = (sigmoid * (1.0 + pre * (1.0 - sigmoid))).astype(jnp.bfloat16)
    leaving += copies(sems, 4, [(slope_ref, slope_hbm)])
    hid_ref[...] = (pre * sigmoid).astype(jnp.bfloat16)
    turned_ref[...] = narrow.T.astype(jnp.bfloat16)
    finish(leaving + copies(sems, 5, [(hid_ref, hid_hbm), (turned_ref, turned_hbm)]))


def forward_parts(step, states, around, kernel, norm_gain, w_up):
    _, rows_out, cols_out, channels = states.shape
    hid = w_up.shape[1]
    count = rows_out * cols_out
    wide = (rows_out + 2, cols_out + 2 * MARGIN, channels)
    shapes = [
        ((count, channels), jnp.bfloat16),
        ((channels, count), jnp.bfloat16),
        ((count, 128), jnp.float32),
        ((count, hid), jnp.bfloat16),
        ((count, hid), jnp.bfloat16),
        (wide, jnp.bfloat16),
    ]
    return call(
        functools.partial(forward_kernel, step),
        [jax.ShapeDtypeStruct(*shape) for shape in shapes],
        [states, *around, kernel, norm_gain, w_up],
        "vvvvvvvv",
        "hhhhhh",
        scratch=[pltpu.VMEM(*shape) for shape in shapes]
        + [pltpu.VMEM(wide, jnp.float32), pltpu.SemaphoreType.DMA((7,))],
        flops=2 * count * hid * channels,
        moved=2**22,
        limit=12,
    )


def transposed(value):
    return value.astype(jnp.float32).T.astype(jnp.bfloat16)


LANES_BOTH = (((1,), (1,)), ((), ()))


def network_kernel(moved_ref, down_ref, up_ref, gain_ref, slope_hbm, n_hbm, inv_hbm, out_hbm, grad_hbm, saved_hbm, *refs):
    slope_ref, n_ref, inv_ref, out_ref, grad_ref, sems = refs
    arriving = copies(sems, 0, [(slope_hbm, slope_ref), (n_hbm, n_ref), (inv_hbm, inv_ref)])
    leaving = copies(sems, 3, [(moved_ref, saved_hbm)])
    moved = moved_ref[...].astype(jnp.float32).T
    grad_hidden = jnp.dot(moved.astype(jnp.bfloat16), down_ref[...], preferred_element_type=jnp.float32)
    arriving[0].wait()
    grad_pre = (grad_hidden * slope_ref[...].astype(jnp.float32)).astype(jnp.bfloat16)
    grad_ref[...] = grad_pre
    leaving += copies(sems, 4, [(grad_ref, grad_hbm)])
    grad_n = lax.dot_general(grad_pre, up_ref[...], LANES_BOTH, preferred_element_type=jnp.float32)
    finish(arriving[1:])
    narrow, gain = n_ref[...].astype(jnp.float32), gain_ref[...]
    mean = jnp.mean(grad_n * narrow, axis=1, keepdims=True)
    field = moved + inv_ref[:, :1] * (grad_n * gain - narrow * (mean / gain))
    out_ref[...] = field.T.astype(jnp.bfloat16)
    finish(leaving + copies(sems, 5, [(out_ref, out_hbm)]))


def network_back(moved, w_down, w_up, norm_gain, slope, narrow, inv_root):
    channels, count = moved.shape
    hid = w_down.shape[1]
    shapes = [((channels, count), jnp.bfloat16), ((count, hid), jnp.bfloat16), ((channels, count), jnp.bfloat16)]
    return call(
        network_kernel,
        [jax.ShapeDtypeStruct(*shape) for shape in shapes],
        [moved, w_down, w_up, norm_gain, slope, narrow, inv_root],
        "vvvvhhh",
        "hhh",
        scratch=[pltpu.VMEM(value.shape, value.dtype) for value in (slope, narrow, inv_root)]
        + [pltpu.VMEM(*shape) for shape in shapes[:2]]
        + [pltpu.SemaphoreType.DMA((6,))],
        flops=4 * count * hid * channels,
        moved=4 * 2**20,
        limit=12,
    )


def stencil_sums(pad_ref, field, tile):
    rows_out, cols_out = tile
    field = field.reshape(rows_out, cols_out, -1)
    padded = pad_ref[...].astype(jnp.float32)
    result = [None] * 9
    for col_tap in range(3):
        place = MARGIN - 1 + col_tap
        shifted_cols = padded[:, place : place + cols_out]
        for row_tap in range(3):
            products = jnp.sum(shifted_cols[row_tap : row_tap + rows_out] * field, axis=0)
            result[3 * row_tap + col_tap] = jnp.sum(products, axis=0, keepdims=True)
    return result


def sums_rows(rows, term, gain):
    rows = rows + [jnp.sum(term, axis=0, keepdims=True) / gain, jnp.zeros((ROWS - 10, term.shape[1]), jnp.float32)]
    return jnp.concatenate(rows, axis=0)


def sums_kernel(steps, tile, up_ref, gain_ref, *refs):
    inputs, (out_ref, *refs) = refs[: 4 * steps], refs[4 * steps :]
    pads, fields, grads, narrows, sems = refs
    places = [(ref, place.at[k]) for k in range(steps) for ref, place in zip(inputs[4 * k : 4 * k + 4], refs[:4])]
    arriving = copies(sems, 0, places)
    rows, term = None, None
    for k in range(steps):
        finish(arriving[4 * k : 4 * k + 4])
        grad_n = lax.dot_general(grads[k], up_ref[...], LANES_BOTH, preferred_element_type=jnp.float32)
        product = grad_n * narrows[k].astype(jnp.float32)
        term = product if term is None else term + product
        more = stencil_sums(pads.at[k], fields[k].astype(jnp.float32).T, tile)
        rows = more if rows is None else [a + b for a, b in zip(rows, more)]
    out_ref[...] = sums_rows(rows, term, gain_ref[...])


def channel_sums(tile, w_up, norm_gain, pads, fields, grads, narrows):
    steps = len(fields)
    inputs = [value for group in zip(pads, fields, grads, narrows) for value in group]
    return call(
        functools.partial(sums_kernel, steps, tile),
        [jax.ShapeDtypeStruct((ROWS, fields[0].shape[0]), jnp.float32)],
        [w_up, norm_gain, *inputs],
        "vv" + "h" * 4 * steps,
        "v",
        scratch=[pltpu.VMEM((steps, *value.shape), value.dtype) for value in inputs[:4]]
        + [pltpu.SemaphoreType.DMA((4 * steps,))],
        moved=2**21,
        limit=12,
    )[0]


QUADRANTS = 4


def lon_bit(at):
    return lax.axis_index("lon") >> at & 1


def gradient_quadrants(left_ref, right_ref, send_ref, keep_ref):
    channels, width = left_ref.shape[0], right_ref.shape[1] // 2
    if keep_ref.ndim == 2:
        send_ref[:channels] = jnp.dot(left_ref[...], right_ref[...], preferred_element_type=jnp.float32).astype(jnp.bfloat16)
        keep_ref[...] = jnp.zeros_like(keep_ref)
        return
    size = channels // QUADRANTS
    groups = lax.axis_size("lon") // 4
    chunk = size // groups
    rows = []
    for core in (1 - lon_bit(0), lon_bit(0)):
        for x in range(2):
            for z in range(groups):
                start = pl.multiple_of((4 * z + 2 * x + core) * chunk, chunk)
                rows.append(left_ref[pl.ds(start, chunk)])
    rows = jnp.concatenate(rows, axis=0)
    value = jnp.dot(rows, right_ref[...], preferred_element_type=jnp.float32).astype(jnp.bfloat16)
    for q in range(QUADRANTS):
        x, lat = q // 2, q % 2
        columns = slice(lat * width, (lat + 1) * width)
        send_ref[q * size : (q + 1) * size] = value[x * size : (x + 1) * size, columns]
        keep_ref[q] = value[(2 + x) * size : (3 + x) * size, columns]


def quadrant_shapes(channels, hid, sums):
    if lax.axis_size("lat") != 2 or lax.axis_size("lon") != 16:
        return (channels, hid), (8, 128)
    return (channels + SUM_ROWS * sums, hid // 2), (QUADRANTS, channels // QUADRANTS, hid // 2)


def side_by_side(refs, goal_ref, axis):
    size = refs[0].shape[axis]
    places = [pl.ds(s * size, size) for s in range(len(refs))]
    return [(ref, goal_ref.at[:, place] if axis else goal_ref.at[place]) for ref, place in zip(refs, places)]


def last_kernel(steps, tile, moved_ref, down_ref, up_ref, gain_ref, sums_ref, *refs):
    slope_hbm, n_hbm, inv_hbm, pad_hbm, *refs = refs
    inputs, refs = refs[: 2 * steps - 1], refs[2 * steps - 1 :]
    field_ref, total_ref, send_ref, keep_ref, slope_ref, n_ref, inv_ref, pad_ref, left_ref, right_ref, sems = refs
    arriving = copies(
        sems, 0, [(slope_hbm, slope_ref), (n_hbm, n_ref), (inv_hbm, inv_ref), (pad_hbm, pad_ref)]
    )
    count = slope_ref.shape[0]
    pairs = side_by_side(inputs[:steps], left_ref, 1) + side_by_side(inputs[steps:], right_ref, 0)
    later = copies(sems, 4, pairs)
    moved = moved_ref[...].astype(jnp.float32).T
    grad_hidden = jnp.dot(moved.astype(jnp.bfloat16), down_ref[...], preferred_element_type=jnp.float32)
    arriving[0].wait()
    grad_pre = (grad_hidden * slope_ref[...].astype(jnp.float32)).astype(jnp.bfloat16)
    right_ref[(steps - 1) * count :] = grad_pre
    grad_n = lax.dot_general(grad_pre, up_ref[...], LANES_BOTH, preferred_element_type=jnp.float32)
    finish(arriving[1:])
    narrow, gain = n_ref[...].astype(jnp.float32), gain_ref[...]
    term = grad_n * narrow
    mean = jnp.mean(term, axis=1, keepdims=True)
    field = moved + inv_ref[:, :1] * (grad_n * gain - narrow * (mean / gain))
    field = field.astype(jnp.bfloat16)
    field_ref[...] = field
    total = sums_ref[...] + sums_rows(stencil_sums(pad_ref, field.astype(jnp.float32), tile), term, gain)
    total_ref[...] = total
    finish(later)
    gradient_quadrants(left_ref, right_ref, send_ref, keep_ref)
    if keep_ref.ndim > 2:
        send_ref[left_ref.shape[0] :] = pieces_of(total)


def last_step(tile, moved, w_down, w_up, norm_gain, sums, forward, grads):
    steps = len(forward)
    channels, count = moved.shape
    hid = w_down.shape[1]
    narrow, _, inv_root, _, slope, pad = forward[-1]
    send, keep = quadrant_shapes(channels, hid, 1)
    sds = jax.ShapeDtypeStruct
    inputs = [parts[1] for parts in forward] + grads
    return call(
        functools.partial(last_kernel, steps, tile),
        [
            sds((count, channels), jnp.bfloat16),
            sds((ROWS, channels), jnp.float32),
            sds(send, jnp.bfloat16),
            sds(keep, jnp.bfloat16),
        ],
        [moved, w_down, w_up, norm_gain, sums, slope, narrow, inv_root, pad, *inputs],
        "vvvvv" + "h" * (4 + len(inputs)),
        "vppp",
        scratch=[pltpu.VMEM(value.shape, value.dtype) for value in (slope, narrow, inv_root, pad)]
        + [pltpu.VMEM((channels, steps * count), jnp.bfloat16), pltpu.VMEM((steps * count, hid), jnp.bfloat16)]
        + [pltpu.SemaphoreType.DMA((len(inputs) + 4,))],
        flops=2**30,
        moved=6 * 2**20,
        limit=20,
    )


def down_kernel(steps, moved_ref, *refs):
    inputs, (send_ref, keep_ref, left_ref, right_ref, sems) = refs[: 2 * steps - 1], refs[2 * steps - 1 :]
    count = moved_ref.shape[1]
    pairs = side_by_side(inputs[: steps - 1], left_ref, 1) + side_by_side(inputs[steps - 1 :], right_ref, 0)
    arriving = copies(sems, 0, pairs)
    left_ref[:, (steps - 1) * count :] = moved_ref[...]
    finish(arriving)
    gradient_quadrants(left_ref, right_ref, send_ref, keep_ref)


def down_gradients(moved, forward, moveds):
    steps = len(forward)
    channels, count = moved.shape
    hid = forward[0][3].shape[1]
    inputs = moveds + [parts[3] for parts in forward]
    return call(
        functools.partial(down_kernel, steps),
        [jax.ShapeDtypeStruct(shape, jnp.bfloat16) for shape in quadrant_shapes(channels, hid, 0)],
        [moved, *inputs],
        "v" + "h" * len(inputs),
        "pp",
        scratch=[pltpu.VMEM((channels, steps * count), jnp.bfloat16), pltpu.VMEM((steps * count, hid), jnp.bfloat16)]
        + [pltpu.SemaphoreType.DMA((len(inputs),))],
        flops=2**29,
        moved=2**21,
        limit=16,
    )


def fill_margins(wide_ref, before, after, low, high, middle):
    rows_out, cols_out, _ = middle.shape
    around = slice(MARGIN - 1, MARGIN + cols_out + 1)
    wide_ref[:1, around] = low.astype(jnp.float32)
    wide_ref[1 + rows_out :, around] = high.astype(jnp.float32)
    wide_ref[1 : 1 + rows_out, MARGIN - 1 : MARGIN] = before.astype(jnp.float32)
    wide_ref[1 : 1 + rows_out, MARGIN + cols_out : MARGIN + cols_out + 1] = after.astype(jnp.float32)
    wide_ref[1 : 1 + rows_out, MARGIN : MARGIN + cols_out] = middle


def final_kernel(field_ref, before_ref, after_ref, low_ref, high_ref, kernel_ref, out_ref, wide_ref):
    rows_out, cols_out, _ = field_ref.shape
    result = field_ref[...].astype(jnp.float32)
    fill_margins(wide_ref, before_ref[0], after_ref[0], low_ref[0], high_ref[0], result)
    for col_tap in range(3):
        place = MARGIN + 1 - col_tap
        shifted_cols = wide_ref[:, place : place + cols_out]
        for row_tap in range(3):
            tap = kernel_ref[row_tap, col_tap : col_tap + 1]
            result = result + tap[None] * shifted_cols[2 - row_tap : 2 - row_tap + rows_out]
    out_ref[...] = result.astype(jnp.bfloat16)


def final_parts(field, around, kernel):
    rows_out, cols_out, channels = field.shape
    return call(
        final_kernel,
        [jax.ShapeDtypeStruct(field.shape, jnp.bfloat16)],
        [field, *around, kernel],
        "v" * 6,
        "v",
        scratch=[pltpu.VMEM((rows_out + 2, cols_out + 2 * MARGIN, channels), jnp.float32)],
        moved=2**19,
    )[0]


def spatial_kernel(mode, step, near_lon, near_lat, *refs):
    refs = list(refs)
    take = lambda: refs.pop(0)
    with_stencil = mode != "first"
    move_hbm = take()
    in_ref = take()
    kern_ref = take() if with_stencil else None
    weight_hbm = take() if mode == "mid" else None
    out_hbm = take()
    saved_hbm = take() if mode == "first" else None
    out_ref, sems = take(), take()
    spread_ref, weight_ref, move_ref = take(), take(), take()
    moving = copies(sems, 3, [(move_hbm, move_ref)])
    tiles_lon, tiles_lat, _, lanes = in_ref.shape
    rows = out_ref.shape[2]
    started = []
    if mode == "mid":
        arriving = copies(sems, 0, [(weight_hbm, weight_ref)])
    if mode == "first":
        weight_ref[...] = in_ref[:, :, rows:]
        started += copies(sems, 0, [(weight_ref, saved_hbm)])
    lane = lax.broadcasted_iota(jnp.int32, (rows, lanes), 1)
    col = lax.rem(lane, near_lat)
    lat_last, lat_first = col == near_lat - 1, col == 0
    lon_last, lon_first = lane >= lanes - near_lat, lane < near_lat
    tiles = [(a, b) for a in range(tiles_lon) for b in range(tiles_lat)]

    def turn(value, steps):
        return pltpu.roll(value, steps % lanes if isinstance(steps, int) else steps, 1)

    def lat_after(grid):
        turned = {key: turn(value, -1) for key, value in grid.items()}
        wrapped = {key: turn(grid[key], near_lat - 1) for key in tiles if key[1] > 0}
        return {(a, b): jnp.where(lat_last, wrapped.get((a, b + 1), 0.0), turned[a, b]) for a, b in tiles}

    def lat_before(grid):
        turned = {key: turn(value, 1) for key, value in grid.items()}
        wrapped = {key: turn(grid[key], 1 - near_lat) for key in tiles if key[1] < tiles_lat - 1}
        return {(a, b): jnp.where(lat_first, wrapped.get((a, b - 1), 0.0), turned[a, b]) for a, b in tiles}

    def lon_after(grid):
        return {
            (a, b): turn(jnp.where(lon_first, grid[(a + 1) % tiles_lon, b], grid[a, b]), -near_lat) for a, b in tiles
        }

    def lon_before(grid):
        return {(a, b): turn(jnp.where(lon_last, grid[(a - 1) % tiles_lon, b], grid[a, b]), near_lat) for a, b in tiles}

    grid = {(a, b): in_ref[a, b, :rows].astype(jnp.float32) for a, b in tiles}
    if with_stencil:
        taps = [
            [jnp.broadcast_to(kern_ref[:, 3 * a + b : 3 * a + b + 1], (rows, lanes)) for b in range(3)] for a in range(3)
        ]
        by_col = [lat_after(grid), grid, lat_before(grid)]
        mix = [
            {key: sum(taps[row][c] * by_col[c][key] for c in range(1, 3)) + taps[row][0] * by_col[0][key] for key in tiles}
            for row in range(3)
        ]
        high, low = lon_after(mix[0]), lon_before(mix[2])
        grid = {key: grid[key] + mix[1][key] + (high[key] + low[key]) for key in tiles}
    if mode == "mid":
        grid = {key: value.astype(jnp.bfloat16).astype(jnp.float32) for key, value in grid.items()}
        finish(arriving)
    weights = {}
    for a, b in tiles:
        four = weight_ref[a, b].astype(jnp.float32)[4 * step : 4 * step + 4]
        weights[a, b] = [jnp.broadcast_to(four[k : k + 1], (rows, lanes)) for k in range(4)]
    weighted = [{key: weights[key][k] * grid[key] for key in tiles} for k in range(4)]
    own, lon = lat_after(weighted[2]), lat_after(weighted[3])
    lon = lon_after({key: weighted[1][key] + lon[key] for key in tiles})
    for a, b in tiles:
        value = (weighted[0][a, b] + own[a, b] + lon[a, b]).astype(jnp.bfloat16).astype(jnp.float32)
        for place in range(a, tiles_lon + LON_REACH, tiles_lon):
            spread_ref[place, b] = value
    spread_ref[:, tiles_lat:] = jnp.zeros((tiles_lon + LON_REACH, LAT_REACH, rows, lanes), jnp.float32)

    finish(moving)
    lon_move, lat_move = move_ref[step, 0], move_ref[step, 1]
    far_lon, off_lon = lon_move // near_lon, lax.rem(lon_move, near_lon)
    far_lat, off_lat = lat_move // near_lat, lax.rem(lat_move, near_lat)
    shift = off_lon * near_lat + off_lat
    turn_here = lax.rem(2 * lanes - shift, lanes)
    turn_next = lax.rem(2 * lanes - shift + near_lat, lanes)
    same_lon = lane >= off_lon * near_lat
    same_lat = col + off_lat < near_lat
    half = tiles_lon // 2
    for a in range(tiles_lon):
        met = [
            jnp.where(same_lon, spread_ref[far_lon + a, far_lat + b], spread_ref[far_lon + a + 1, far_lat + b])
            for b in range(tiles_lat + 1)
        ]
        for b in range(tiles_lat):
            value = jnp.where(same_lat, turn(met[b], turn_here), turn(met[b + 1], turn_next))
            out_ref[a, b] = value.astype(jnp.bfloat16)
        if (a + 1) % half == 0:
            part = pl.ds(a + 1 - half, half)
            started += copies(sems, 1 + a // half, [(out_ref.at[part], out_hbm.at[part])])
    finish(started)


def spatial(mode, step, tile, rows, field, kern, weights, moves):
    tiles_lon, tiles_lat, _, lanes = field.shape
    with_stencil = mode != "first"
    operands = [moves, field]
    operands += [kern] if with_stencil else []
    operands += [weights] if mode == "mid" else []
    out_shape = (tiles_lon, tiles_lat, rows, lanes)
    weight_shape = (tiles_lon, tiles_lat, ROWS, lanes)
    sds = jax.ShapeDtypeStruct
    out = [sds(out_shape, jnp.bfloat16)] + ([sds(weight_shape, jnp.bfloat16)] if mode == "first" else [])
    scratch = [pltpu.VMEM(out_shape, jnp.bfloat16), pltpu.SemaphoreType.DMA((4,))]
    spread_shape = (tiles_lon + LON_REACH, tiles_lat + LAT_REACH, rows, lanes)
    scratch += [pltpu.VMEM(spread_shape, jnp.float32), pltpu.VMEM(weight_shape, jnp.bfloat16)]
    scratch += [pltpu.SMEM(moves.shape, jnp.int32)]
    return call(
        functools.partial(spatial_kernel, mode, step, *tile),
        out,
        operands,
        "hv" + "v" * with_stencil + "h" * (mode == "mid"),
        "h" * len(out),
        scratch=scratch,
        flops=2**22,
        moved=2**20,
        limit=max(8, 14 * tiles_lon * tiles_lat * rows * lanes * 4 // MIB),
    )


def halved(value, axis, bit, dim):
    count = lax.axis_size(axis)
    mine = lax.axis_index(axis) >> bit & 1
    kept = lax.dynamic_index_in_dim(value, mine, dim, keepdims=False)
    sent = lax.dynamic_index_in_dim(value, 1 - mine, dim, keepdims=False).astype(jnp.bfloat16)
    arrived = lax.ppermute(sent, axis, [(i, i ^ (1 << bit)) for i in range(count)])
    return kept + arrived.astype(jnp.float32)


def scattered(value, lat_first):
    channels, hid = value.shape
    lon_bits = lax.axis_size("lon").bit_length() - 1
    lat_bits = lax.axis_size("lat").bit_length() - 1
    rows = channels >> lon_bits
    value = value.reshape(*([2] * lon_bits), rows, *([2] * lat_bits), hid >> lat_bits)

    def over_lon(value, bit, left):
        return halved(value, "lon", bit, left.index(bit)), [k for k in left if k != bit]

    left_lon = list(range(lon_bits))[::-1]
    left_lat = list(range(lat_bits))[::-1]
    order = [("lon", 0), ("lon", 1)] + [("lat", k) for k in range(lat_bits)]
    if lat_first:
        order = [("lon", 0)] + [("lat", k) for k in range(lat_bits)] + [("lon", 1)]
    order += [("lon", k) for k in range(2, lon_bits)]
    for axis, bit in order:
        if axis == "lon":
            value, left_lon = over_lon(value, bit, left_lon)
        else:
            value = halved(value, "lat", bit, len(left_lon) + 1 + left_lat.index(bit))
            left_lat.remove(bit)
    return value


def add_parts(pairs, kept, arrived):
    for q, out_ref, place in pairs:
        value = kept(q).astype(jnp.float32) + arrived(q).astype(jnp.float32)
        out_ref[place] = value.astype(out_ref.dtype)


def first_axis(flip):
    core = lon_bit(0)
    return 1 - core if flip else core


def quadrant_kernel(flip, *refs):
    kept_ref, *total_refs, arrived_ref, send_ref, keep_ref = refs[: 4 + len(refs) // 6]
    axis, x, lat = first_axis(flip), lon_bit(1), lax.axis_index("lat")
    rows = kept_ref.shape[1]
    for j in range(2):
        kept = (1 - axis) * (2 * x + j) + axis * (2 * j + lat)
        sent = (1 - axis) * (2 * (1 - x) + j) + axis * (2 * j + 1 - lat)
        pairs = [(sent, send_ref, pl.ds(j * rows, rows)), (kept, keep_ref, j)]
        arrived = lambda q: arrived_ref[pl.ds(pl.multiple_of(q * rows, rows), rows)]
        add_parts(pairs, lambda q: kept_ref[q], arrived)
    if total_refs:
        chip = total_refs[0][...] + whole_of(arrived_ref[QUADRANTS * rows :])
        refs[-1][...] = chip
        send_ref[2 * rows :] = pieces_of(chip)


def half_kernel(flip, *refs):
    kept_ref, *total_refs, arrived_ref, send_ref, keep_ref = refs[: 4 + len(refs) // 6]
    axis, x, lat = first_axis(flip), lon_bit(1), lax.axis_index("lat")
    mine = (1 - axis) * lat + axis * x
    rows = kept_ref.shape[1]
    pairs = [(1 - mine, send_ref, pl.ds(0, rows)), (mine, keep_ref, slice(None))]
    arrived = lambda q: arrived_ref[pl.ds(pl.multiple_of(q * rows, rows), rows)]
    add_parts(pairs, lambda q: kept_ref[q], arrived)
    if total_refs:
        beside = arrived_ref[2 * rows :]
        refs[-1][...] = whole_of(beside)
        send_ref[rows : rows + SUM_ROWS] = pieces_of(total_refs[0][...])
        send_ref[rows + SUM_ROWS :] = beside


def rows_kernel(groups, bit_at, totals, *refs):
    kept_ref, *refs = refs
    total_refs, (arrived_ref, send_ref, keep_ref, *total_ref) = refs[:totals], refs[totals:]
    bit = lon_bit(bit_at)
    rows = kept_ref.shape[0]
    chunk = rows // (2 * groups)
    for p in range(groups):
        goal = pl.ds(p * chunk, chunk)
        places = [pl.multiple_of((2 * p + which) * chunk, chunk) for which in (1 - bit, bit)]
        pairs = [(places[0], send_ref, goal), (places[1], keep_ref, goal)]
        add_parts(pairs, lambda q: kept_ref[pl.ds(q, chunk)], lambda q: arrived_ref[pl.ds(q, chunk)])
    if totals:
        total = add_sums(total_refs, arrived_ref, rows)
        total_ref[0][...] = total
        send_ref[rows // 2 :] = pieces_of(total)


def add_sums(total_refs, arrived_ref, start):
    arrived = whole_of(arrived_ref[start : start + SUM_ROWS])
    if len(total_refs) == 1:
        return total_refs[0][...] + arrived
    chip, beside = (ref[...] for ref in total_refs)
    return (chip + whole_of(arrived_ref[start + SUM_ROWS :])) + (beside + arrived)


def finish_kernel(kept_ref, total_ref, arrived_ref, kept_down_ref, arrived_down_ref, up_hbm, down_hbm, taps_ref, gain_ref, *refs):
    up_ref, down_ref, sems = refs
    rows = kept_ref.shape[0]
    down_ref[...] = kept_down_ref[...] + arrived_down_ref[...].astype(jnp.float32)
    leaving = copies(sems, 0, [(down_ref, down_hbm)])
    up_ref[...] = kept_ref[...] + arrived_ref[:rows].astype(jnp.float32)
    leaving += copies(sems, 1, [(up_ref, up_hbm)])
    total = add_sums([total_ref], arrived_ref, rows)
    for k in range(9):
        taps_ref[k // 3, k % 3 : k % 3 + 1] = total[k : k + 1]
    gain_ref[...] = total[9:10]
    finish(leaving)


def after(value, first):
    return lax.optimization_barrier((value, first))[0]


def halving(flip, send, keep, total):
    lon, lat = lax.axis_size("lon"), lax.axis_size("lat")
    places = [(i, j) for i in range(lon) for j in range(lat)]
    flat = lambda i, j: i * lat + j
    along_lat = lambda i: (i & 1) != flip
    sds = jax.ShapeDtypeStruct
    rows, width = keep.shape[1:]
    sums = [] if total is None else [total]
    with_sums = len(sums)
    plan = [
        (lambda i, j: (i ^ 1, j), functools.partial(quadrant_kernel, flip), (2, rows, width), 1),
        (
            lambda i, j: (i, j ^ 1) if along_lat(i) else (i ^ 2, j),
            functools.partial(half_kernel, flip),
            (rows, width),
            2,
        ),
        (
            lambda i, j: (i ^ 2, j) if along_lat(i) else (i, j ^ 1),
            functools.partial(rows_kernel, 2, 2, 2 * with_sums),
            (rows // 2, width),
            1,
        ),
        (lambda i, j: (i ^ 4, j), functools.partial(rows_kernel, 1, 3, with_sums), (rows // 4, width), 1),
    ]
    for at, (partner, kernel, shape, parts) in enumerate(plan):
        send = yield send
        arrived = lax.ppermute(send, AXES, [(flat(i, j), flat(*partner(i, j))) for i, j in places])
        arrived = yield arrived
        sent = shape[-2] * (shape[0] if len(shape) == 3 else 1) + SUM_ROWS * parts * with_sums
        out = [sds((sent, shape[-1]), jnp.bfloat16), sds(shape, jnp.float32)]
        out += [sds(value.shape, jnp.float32) for value in sums[:1]]
        operands = [keep, *sums, arrived]
        send, keep, *more = call(kernel, out, operands, "v" * len(operands), "p" * len(out), moved=2**19, limit=12)
        sums = sums + more if at == 1 else more
    send = yield send
    arrived = lax.ppermute(send, AXES, [(flat(i, j), flat(i ^ 8, j)) for i, j in places])
    yield (keep, *sums, arrived)


def all_sums(up, down, total, field, kernel):
    channels = total.shape[1]
    field = field[None]
    if up[1].ndim == 2:
        parts = [scattered(send.astype(jnp.float32), flip) for flip, (send, _) in enumerate((up, down))]
        total = lax.psum(total, AXES)
        around = lat_edges(field)
        state = final_parts(field[0], (*around, *lon_edges(field, *around)), kernel)
        return (state, *parts, total[:9].reshape(3, 3, channels), total[9])
    ahead, behind = halving(False, *up, total), halving(True, *down, None)
    send, later = next(ahead), next(behind)
    arrived = ahead.send(send)
    send = ahead.send(after(arrived, later))
    field = after(field, send)
    arrived_later = behind.send(after(later, send))
    later = behind.send(arrived_later)
    around = lat_edges(field, lambda value: after(value, later))
    state = final_parts(field[0], (*around, *lon_edges(field, *around)), kernel)
    for at in range(1, 4):
        arrived = ahead.send(send)
        arrived_later = behind.send(later)
        send = ahead.send(after(arrived, later))
        later = behind.send(after(arrived_later, send))
    final_ahead = ahead.send(send)
    final_behind = behind.send(later)
    sds = jax.ShapeDtypeStruct
    part = sds(final_ahead[0].shape, jnp.float32)
    out = [part, part, sds((3, 3, channels), jnp.float32), sds((1, channels), jnp.float32)]
    up, down, taps, gain = call(
        finish_kernel,
        out,
        [*final_ahead, *final_behind],
        "vvvvv",
        "hhvv",
        scratch=[pltpu.VMEM(part.shape, part.dtype)] * 2 + [pltpu.SemaphoreType.DMA((2,))],
        moved=2**18,
    )
    return state, up, down, taps, gain.reshape(channels)


def local(cotangent, states, w_up, w_down, norm_gain, kernel, bilinear, lon_move, lat_move):
    steps, rows_out, cols_out, channels = states.shape
    tiles_lon, tiles_lat = lax.axis_size("lon"), lax.axis_size("lat")
    devices = tiles_lon * tiles_lat
    count = rows_out * cols_out
    tile = (rows_out, cols_out)
    share = channels // devices
    padded_share = -(-share // ROWS) * ROWS
    whole_share = share == padded_share
    group_size = channels // lon_move.shape[1]
    me = lax.axis_index("lon") * tiles_lat + lax.axis_index("lat")

    def as_blocks(value):
        value = value.reshape(devices, share, count)
        return value if whole_share else jnp.pad(value, ((0, 0), (0, padded_share - share), (0, 0)))

    def as_rows(blocks):
        return blocks[:, :share].reshape(channels, count)

    def as_grid(blocks):
        return blocks.reshape(tiles_lon, tiles_lat, *blocks.shape[1:])

    blocks = packed(cotangent, bilinear, devices)
    blocks, states_later = lax.optimization_barrier((blocks, states))
    arrived = as_grid(exchanged(blocks))
    group = me * share // group_size
    moves = jnp.stack([lon_move[:, group], lat_move[:, group]], axis=1)
    grid_now, weights = spatial("first", steps - 1, tile, padded_share, arrived, None, None, moves)

    taps = lax.dynamic_slice_in_dim(kernel.reshape(9, channels), me * share, share, 1).T
    taps = jnp.pad(taps, ((0, padded_share - share), (0, count - 9)))

    around = lat_edges(states_later)
    grid_now, *around = lax.optimization_barrier((grid_now, *around))
    around = (*around, *lon_edges(states, *around))
    order = list(reversed(range(steps)))
    gain = norm_gain.reshape(1, channels)
    forward = {s: forward_parts(s, states, around, kernel, gain, w_up) for s in order}

    moved, grads, fields = {}, {}, {}
    for s in order[:-1]:
        here = as_rows(exchanged(grid_now.reshape(devices, padded_share, count)))
        if s != order[0]:
            here, forward = lax.optimization_barrier((here, forward))
        narrow, _, inv_root, _, slope, _ = forward[s]
        fields[s], grads[s], moved[s] = network_back(here, w_down, w_up, gain, slope, narrow, inv_root)
        arrived = as_grid(exchanged(as_blocks(fields[s])))
        (grid_now,) = spatial("mid", s - 1, tile, padded_share, arrived, taps, weights, moves)

    here = as_rows(exchanged(grid_now.reshape(devices, padded_share, count)))
    earlier = lambda values: [values[s] for s in order[:-1]]
    pads, narrows = ([forward[s][k] for s in order[:-1]] for k in (5, 0))
    sums = channel_sums(tile, w_up, gain, pads, earlier(fields), earlier(grads), narrows)
    here, sums = lax.optimization_barrier((here, sums))
    parts = [forward[s] for s in order]
    field, total, send, keep = last_step(tile, here, w_down, w_up, gain, sums, parts, earlier(grads))
    down = down_gradients(here, parts, earlier(moved))
    field = field.reshape(cotangent.shape)
    return all_sums((send, keep), down, total, field, kernel)


def solution(mesh):
    placed = (
        P("lon", "lat", None),
        P(None, "lon", "lat", None),
        P(),
        P(),
        P(),
        P(),
        P(None, None, "lon", "lat"),
        P(),
        P(),
    )
    return jax.shard_map(
        local,
        mesh=mesh,
        in_specs=placed,
        out_specs=(P("lon", "lat", None), P("lon", "lat"), P("lon", "lat"), P(), P()),
        check_vma=False,
    )
```

```python
import functools

import jax
import jax.numpy as jnp
from jax import lax
from jax.experimental import pallas as pl
from jax.experimental.pallas import tpu as pltpu
from jax.sharding import PartitionSpec as P

EPSILON = 1e-06
AXES = ("lon", "lat")
ROWS = 16
LAT_REACH = 2
LON_REACH = 8
MIB = 1024 * 1024


def exchanged(blocks):
    return lax.all_to_all(blocks, AXES, split_axis=0, concat_axis=0, tiled=True)


SPACES = {"s": pltpu.SMEM, "v": pltpu.VMEM, "p": pltpu.VMEM, "h": pltpu.HBM}
PINNED = {"p": pltpu.VMEM, "h": pltpu.HBM}


def call(kernel, out_shape, operands, ins, outs, scratch=(), flops=0, moved=0, limit=8):
    operands = [
        pltpu.with_memory_space_constraint(value, PINNED[kind]) if kind in PINNED else value
        for kind, value in zip(ins, operands, strict=True)
    ]
    out_shape = [
        PINNED[kind](value.shape, value.dtype) if kind in PINNED else value
        for kind, value in zip(outs, out_shape, strict=True)
    ]
    return pl.pallas_call(
        kernel,
        out_shape=out_shape,
        in_specs=[pl.BlockSpec(memory_space=SPACES[kind]) for kind in ins],
        out_specs=[pl.BlockSpec(memory_space=SPACES[kind]) for kind in outs],
        scratch_shapes=scratch,
        compiler_params=pltpu.CompilerParams(vmem_limit_bytes=limit * MIB),
        cost_estimate=pl.CostEstimate(flops=flops, bytes_accessed=moved, transcendentals=0),
    )(*operands)


def copies(sems, first, pairs):
    started = [pltpu.make_async_copy(src, dst, sems.at[first + k]) for k, (src, dst) in enumerate(pairs)]
    for copy in started:
        copy.start()
    return started


def finish(started):
    for copy in started:
        copy.wait()


PIECES = 3
SUMS = 10
SUM_ROWS = 32


def pieces_of(value):
    value = value[:SUMS]
    parts = []
    for _ in range(PIECES):
        parts.append(value.astype(jnp.bfloat16).astype(jnp.float32))
        value = value - parts[-1]
    parts.append(jnp.zeros((SUM_ROWS - PIECES * SUMS, value.shape[1]), jnp.float32))
    return jnp.concatenate(parts, axis=0).astype(jnp.bfloat16)


def whole_of(parts):
    parts = parts.astype(jnp.float32)
    total = (parts[:SUMS] + parts[SUMS : 2 * SUMS]) + parts[2 * SUMS : 3 * SUMS]
    return jnp.concatenate([total, jnp.zeros((ROWS - SUMS, parts.shape[1]), jnp.float32)], axis=0)


def after(value, first):
    return lax.optimization_barrier((value, first))[0]


def pack_kernel(cotangent_hbm, weight_hbm, out_hbm, cotangent_ref, weight_ref, out_ref, sems):
    started = copies(sems, 0, [(cotangent_hbm, cotangent_ref), (weight_hbm, weight_ref)])
    channels = cotangent_ref.shape[1]
    devices, _, count = out_ref.shape
    share = channels // devices
    started[1].wait()
    rows = weight_ref.shape[0]
    weights = jnp.concatenate([weight_ref[:, i] for i in range(weight_ref.shape[1])], axis=1)
    weights = jnp.concatenate([weights, jnp.zeros((ROWS - rows, count), jnp.float32)], axis=0)
    weights = weights.astype(jnp.bfloat16)
    out_ref[:, share:] = jnp.broadcast_to(weights[None], (devices, ROWS, count))
    started[0].wait()
    turned = cotangent_ref[...].astype(jnp.float32).T.astype(jnp.bfloat16)
    out_ref[:, :share] = turned.reshape(devices, share, count)
    finish(copies(sems, 2, [(out_ref, out_hbm)]))


def packed(cotangent, bilinear, devices):
    rows_out, cols_out, channels = cotangent.shape
    steps, corners = bilinear.shape[:2]
    count = rows_out * cols_out
    share = channels // devices
    if share % ROWS:
        blocks = cotangent.reshape(count, channels).T.reshape(devices, share, count)
        blocks = jnp.pad(blocks, ((0, 0), (0, -share % ROWS), (0, 0)))
        weights = bilinear.reshape(steps * corners, count).astype(jnp.bfloat16)
        weights = jnp.pad(weights, ((0, ROWS - steps * corners), (0, 0)))
        return jnp.concatenate([blocks, jnp.broadcast_to(weights[None], (devices, ROWS, count))], axis=1)
    shape = (devices, share + ROWS, count)
    return call(
        pack_kernel,
        [jax.ShapeDtypeStruct(shape, jnp.bfloat16)],
        [cotangent.reshape(count, channels), bilinear.reshape(steps * corners, rows_out, cols_out)],
        "hh",
        "h",
        scratch=[
            pltpu.VMEM((count, channels), jnp.bfloat16),
            pltpu.VMEM((steps * corners, rows_out, cols_out), jnp.float32),
            pltpu.VMEM(shape, jnp.bfloat16),
            pltpu.SemaphoreType.DMA((3,)),
        ],
        moved=2**19,
    )[0]


def lat_edges(states, held=lambda value: value):
    lat, lat_at = lax.axis_size("lat"), lax.axis_index("lat")
    first, last = states[:, :, :1], states[:, :, -1:]
    if lat == 2:
        arrived = lax.ppermute(jnp.where(lat_at == 0, last, first), "lat", [(0, 1), (1, 0)])
        arrived = held(arrived)
        return jnp.where(lat_at == 0, 0, arrived), jnp.where(lat_at == 0, arrived, 0)
    return (
        lax.ppermute(last, "lat", [(i, i + 1) for i in range(lat - 1)]),
        lax.ppermute(first, "lat", [(i + 1, i) for i in range(lat - 1)]),
    )


def lon_edges(states, before, after):
    lon = lax.axis_size("lon")
    ahead = lambda value: lax.ppermute(value, "lon", [(i, (i + 1) % lon) for i in range(lon)])
    behind = lambda value: lax.ppermute(value, "lon", [(i, (i - 1) % lon) for i in range(lon)])
    row = lambda place: jnp.concatenate([part[:, place] for part in (before, states, after)], axis=2)
    return ahead(row(slice(-1, None))), behind(row(slice(0, 1)))


MARGIN = 8


def forward_math(step, places, sems, leaving, outs):
    states_ref, before_ref, after_ref, low_ref, high_ref, kernel_ref, gain_ref, up_ref = places
    n_ref, turned_ref, inv_ref, hid_ref, slope_ref, pad_ref, wide_ref = outs
    rows_out, cols_out, channels = states_ref.shape[1:]
    count = rows_out * cols_out
    mixed = states_ref[step].astype(jnp.float32)
    fill_margins(wide_ref, before_ref[step], after_ref[step], low_ref[step], high_ref[step], mixed)
    pad_ref[...] = wide_ref[...].astype(jnp.bfloat16)
    leaving("pad")
    for col_tap in range(3):
        place = MARGIN - 1 + col_tap
        shifted_cols = wide_ref[:, place : place + cols_out]
        for row_tap in range(3):
            tap = kernel_ref[row_tap, col_tap : col_tap + 1]
            mixed = mixed + tap[None] * shifted_cols[row_tap : row_tap + rows_out]
    mixed = mixed.reshape(count, channels)
    inv_root = lax.rsqrt(jnp.mean(mixed * mixed, axis=1, keepdims=True) + EPSILON)
    narrow = mixed * inv_root * gain_ref[...]
    n_ref[...] = narrow.astype(jnp.bfloat16)
    inv_ref[...] = jnp.broadcast_to(inv_root, inv_ref.shape)
    leaving("n", "inv")
    pre = jnp.dot(n_ref[...], up_ref[...], preferred_element_type=jnp.float32)
    sigmoid = jax.nn.sigmoid(pre)
    slope_ref[...] = (sigmoid * (1.0 + pre * (1.0 - sigmoid))).astype(jnp.bfloat16)
    leaving("slope")
    hid_ref[...] = (pre * sigmoid).astype(jnp.bfloat16)
    turned_ref[...] = narrow.T.astype(jnp.bfloat16)
    leaving("hid", "turned")


FORWARD = ("n", "turned", "inv", "hid", "slope", "pad")


def sender(sems, refs, goals, started):
    names = list(goals)

    def leave(*which):
        for name in which:
            if name in goals:
                started.extend(copies(sems, names.index(name), [(refs[name], goals[name])]))

    return leave


def forward_kernel(step, *refs):
    places, goals, outs, sems = refs[:8], refs[8:14], refs[14:21], refs[21]
    started = []
    leave = sender(sems, dict(zip(FORWARD, outs)), dict(zip(FORWARD, goals)), started)
    forward_math(step, places, sems, leave, outs)
    finish(started)


def forward_shapes(states, w_up):
    _, rows_out, cols_out, channels = states.shape
    hid = w_up.shape[1]
    count = rows_out * cols_out
    wide = (rows_out + 2, cols_out + 2 * MARGIN, channels)
    return [
        ((count, channels), jnp.bfloat16),
        ((channels, count), jnp.bfloat16),
        ((count, 128), jnp.float32),
        ((count, hid), jnp.bfloat16),
        ((count, hid), jnp.bfloat16),
        (wide, jnp.bfloat16),
    ]


def forward_scratch(shapes):
    scratch = [pltpu.VMEM(*shape) for shape in shapes]
    return scratch + [pltpu.VMEM(shapes[-1][0], jnp.float32)]


def forward_parts(step, states, around, kernel, norm_gain, w_up):
    shapes = forward_shapes(states, w_up)
    return call(
        functools.partial(forward_kernel, step),
        [jax.ShapeDtypeStruct(*shape) for shape in shapes],
        [states, *around, kernel, norm_gain, w_up],
        "vvvvvvvv",
        "hhhhhh",
        scratch=forward_scratch(shapes) + [pltpu.SemaphoreType.DMA((6,))],
        flops=2**27,
        moved=2**22,
        limit=12,
    )


LANES_BOTH = (((1,), (1,)), ((), ()))


def fetch_kernel(*refs):
    count = len(refs) // 2
    *pairs, sems = refs
    finish(copies(sems, 0, list(zip(pairs[:count], pairs[count:]))))


def fetched(values, first):
    values = after(values, first)
    return call(
        fetch_kernel,
        [jax.ShapeDtypeStruct(value.shape, value.dtype) for value in values],
        values,
        "h" * len(values),
        "v" * len(values),
        scratch=[pltpu.SemaphoreType.DMA((len(values),))],
        moved=2**19,
    )


def network_math(moved_ref, down_ref, up_ref, gain_ref, slope_ref, n_ref, inv_ref, out_ref, grad_ref, leave):
    leave("moved")
    moved = moved_ref[...].astype(jnp.float32).T
    grad_hidden = jnp.dot(moved.astype(jnp.bfloat16), down_ref[...], preferred_element_type=jnp.float32)
    grad_pre = (grad_hidden * slope_ref[...].astype(jnp.float32)).astype(jnp.bfloat16)
    grad_ref[...] = grad_pre
    leave("grad")
    grad_n = lax.dot_general(grad_pre, up_ref[...], LANES_BOTH, preferred_element_type=jnp.float32)
    narrow, gain = n_ref[...].astype(jnp.float32), gain_ref[...]
    mean = jnp.mean(grad_n * narrow, axis=1, keepdims=True)
    field = moved + inv_ref[:, :1] * (grad_n * gain - narrow * (mean / gain))
    out_ref[...] = field.T.astype(jnp.bfloat16)
    leave("field")


def network_kernel(moved_ref, down_ref, up_ref, gain_ref, slope_ref, n_ref, inv_ref, *refs):
    *goals, out_ref, grad_ref, sems = refs
    started = []
    names = ("field", "grad", "moved")
    leave = sender(sems, dict(zip(names, (out_ref, grad_ref, moved_ref))), dict(zip(names, goals)), started)
    network_math(moved_ref, down_ref, up_ref, gain_ref, slope_ref, n_ref, inv_ref, out_ref, grad_ref, leave)
    finish(started)


def first_kernel(step, *refs):
    (moved_ref, down_ref), places, refs = refs[:2], refs[2:10], refs[10:]
    goals, outs, (out_ref, grad_ref, sems) = refs[:7], refs[7:14], refs[14:]
    started = []
    names = ("n", "turned", "hid", "pad", "field", "grad", "moved")
    values = dict(zip(FORWARD, outs)) | {"field": out_ref, "grad": grad_ref, "moved": moved_ref}
    leave = sender(sems, values, dict(zip(names, goals)), started)
    forward_math(step, places, sems, leave, outs)
    n_ref, _, inv_ref, _, slope_ref = outs[:5]
    gain_ref, up_ref = places[6:]
    network_math(moved_ref, down_ref, up_ref, gain_ref, slope_ref, n_ref, inv_ref, out_ref, grad_ref, leave)
    finish(started)


def first_step(step, moved, w_down, states, around, kernel, norm_gain, w_up):
    shapes = forward_shapes(states, w_up)
    channels, count = moved.shape
    hid = w_down.shape[1]
    backs = [((channels, count), jnp.bfloat16), ((count, hid), jnp.bfloat16), ((channels, count), jnp.bfloat16)]
    results = [shapes[k] for k in (0, 1, 3, 5)] + backs
    return call(
        functools.partial(first_kernel, step),
        [jax.ShapeDtypeStruct(*shape) for shape in results],
        [moved, w_down, states, *around, kernel, norm_gain, w_up],
        "v" * 10,
        "h" * 7,
        scratch=forward_scratch(shapes) + [pltpu.VMEM(*shape) for shape in backs[:2]] + [pltpu.SemaphoreType.DMA((7,))],
        flops=2**28,
        moved=2**22,
        limit=16,
    )


def network_back(moved, w_down, w_up, norm_gain, slope, narrow, inv_root):
    channels, count = moved.shape
    hid = w_down.shape[1]
    shapes = [((channels, count), jnp.bfloat16), ((count, hid), jnp.bfloat16), ((channels, count), jnp.bfloat16)]
    return call(
        network_kernel,
        [jax.ShapeDtypeStruct(*shape) for shape in shapes],
        [moved, w_down, w_up, norm_gain, slope, narrow, inv_root],
        "vvvvvvv",
        "hhh",
        scratch=[pltpu.VMEM(*shape) for shape in shapes[:2]] + [pltpu.SemaphoreType.DMA((3,))],
        flops=4 * count * hid * channels,
        moved=4 * 2**20,
        limit=8,
    )


def stencil_sums(pad_ref, field, tile):
    rows_out, cols_out = tile
    field = field.reshape(rows_out, cols_out, -1)
    padded = pad_ref[...].astype(jnp.float32)
    result = [None] * 9
    for col_tap in range(3):
        place = MARGIN - 1 + col_tap
        shifted_cols = padded[:, place : place + cols_out]
        for row_tap in range(3):
            products = jnp.sum(shifted_cols[row_tap : row_tap + rows_out] * field, axis=0)
            result[3 * row_tap + col_tap] = jnp.sum(products, axis=0, keepdims=True)
    return result


def sums_rows(rows, term, gain):
    rows = rows + [jnp.sum(term, axis=0, keepdims=True) / gain, jnp.zeros((ROWS - 10, term.shape[1]), jnp.float32)]
    return jnp.concatenate(rows, axis=0)


def sums_kernel(steps, tile, up_ref, gain_ref, *refs):
    inputs, (out_ref, *refs) = refs[: 4 * steps], refs[4 * steps :]
    pads, fields, grads, narrows, sems = refs
    places = [(ref, place.at[k]) for k in range(steps) for ref, place in zip(inputs[4 * k : 4 * k + 4], refs[:4])]
    arriving = copies(sems, 0, places)
    rows, term = None, None
    for k in range(steps):
        finish(arriving[4 * k : 4 * k + 4])
        grad_n = lax.dot_general(grads[k], up_ref[...], LANES_BOTH, preferred_element_type=jnp.float32)
        product = grad_n * narrows[k].astype(jnp.float32)
        term = product if term is None else term + product
        more = stencil_sums(pads.at[k], fields[k].astype(jnp.float32).T, tile)
        rows = more if rows is None else [a + b for a, b in zip(rows, more)]
    out_ref[...] = sums_rows(rows, term, gain_ref[...])


def channel_sums(tile, w_up, norm_gain, pads, fields, grads, narrows):
    steps = len(fields)
    inputs = [value for group in zip(pads, fields, grads, narrows) for value in group]
    return call(
        functools.partial(sums_kernel, steps, tile),
        [jax.ShapeDtypeStruct((ROWS, fields[0].shape[0]), jnp.float32)],
        [w_up, norm_gain, *inputs],
        "vv" + "h" * 4 * steps,
        "v",
        scratch=[pltpu.VMEM((steps, *value.shape), value.dtype) for value in inputs[:4]]
        + [pltpu.SemaphoreType.DMA((4 * steps,))],
        moved=2**21,
        limit=12,
    )[0]


QUADRANTS = 4


def lon_bit(at):
    return lax.axis_index("lon") >> at & 1


def gradient_quadrants(left_ref, right_ref, send_ref, keep_ref):
    channels, width = left_ref.shape[0], right_ref.shape[1] // 2
    if keep_ref.ndim == 2:
        send_ref[:channels] = jnp.dot(left_ref[...], right_ref[...], preferred_element_type=jnp.float32).astype(jnp.bfloat16)
        keep_ref[...] = jnp.zeros_like(keep_ref)
        return
    size = channels // QUADRANTS
    groups = lax.axis_size("lon") // 4
    chunk = size // groups
    rows = []
    for core in (1 - lon_bit(0), lon_bit(0)):
        for x in range(2):
            for z in range(groups):
                start = pl.multiple_of((4 * z + 2 * x + core) * chunk, chunk)
                rows.append(left_ref[pl.ds(start, chunk)])
    rows = jnp.concatenate(rows, axis=0)
    value = jnp.dot(rows, right_ref[...], preferred_element_type=jnp.float32).astype(jnp.bfloat16)
    for q in range(QUADRANTS):
        x, lat = q // 2, q % 2
        columns = slice(lat * width, (lat + 1) * width)
        send_ref[q * size : (q + 1) * size] = value[x * size : (x + 1) * size, columns]
        keep_ref[q] = value[(2 + x) * size : (3 + x) * size, columns]


def quadrant_shapes(channels, hid, sums):
    if lax.axis_size("lat") != 2 or lax.axis_size("lon") != 16:
        return (channels, hid), (8, 128)
    return (channels + SUM_ROWS * sums, hid // 2), (QUADRANTS, channels // QUADRANTS, hid // 2)


def side_by_side(refs, goal_ref, axis):
    size = refs[0].shape[axis]
    places = [pl.ds(s * size, size) for s in range(len(refs))]
    return [(ref, goal_ref.at[:, place] if axis else goal_ref.at[place]) for ref, place in zip(refs, places)]


def last_kernel(steps, tile, moved_ref, down_ref, up_ref, gain_ref, sums_ref, *refs):
    slope_ref, n_ref, inv_ref, pad_ref, *refs = refs
    inputs, refs = refs[: 2 * steps - 1], refs[2 * steps - 1 :]
    field_ref, total_ref, send_ref, keep_ref, left_ref, right_ref, sems = refs
    count = slope_ref.shape[0]
    pairs = side_by_side(inputs[:steps], left_ref, 1) + side_by_side(inputs[steps:], right_ref, 0)
    later = copies(sems, 0, pairs)
    moved = moved_ref[...].astype(jnp.float32).T
    grad_hidden = jnp.dot(moved.astype(jnp.bfloat16), down_ref[...], preferred_element_type=jnp.float32)
    grad_pre = (grad_hidden * slope_ref[...].astype(jnp.float32)).astype(jnp.bfloat16)
    right_ref[(steps - 1) * count :] = grad_pre
    grad_n = lax.dot_general(grad_pre, up_ref[...], LANES_BOTH, preferred_element_type=jnp.float32)
    narrow, gain = n_ref[...].astype(jnp.float32), gain_ref[...]
    term = grad_n * narrow
    mean = jnp.mean(term, axis=1, keepdims=True)
    field = moved + inv_ref[:, :1] * (grad_n * gain - narrow * (mean / gain))
    field = field.astype(jnp.bfloat16)
    field_ref[...] = field
    total = sums_ref[...] + sums_rows(stencil_sums(pad_ref, field.astype(jnp.float32), tile), term, gain)
    total_ref[...] = total
    finish(later)
    gradient_quadrants(left_ref, right_ref, send_ref, keep_ref)
    if keep_ref.ndim > 2:
        send_ref[left_ref.shape[0] :] = pieces_of(total)


def last_step(tile, moved, w_down, w_up, norm_gain, sums, near, turned, grads):
    steps = len(turned)
    channels, count = moved.shape
    hid = w_down.shape[1]
    send, keep = quadrant_shapes(channels, hid, 1)
    sds = jax.ShapeDtypeStruct
    inputs = turned + grads
    return call(
        functools.partial(last_kernel, steps, tile),
        [
            sds((count, channels), jnp.bfloat16),
            sds((ROWS, channels), jnp.float32),
            sds(send, jnp.bfloat16),
            sds(keep, jnp.bfloat16),
        ],
        [moved, w_down, w_up, norm_gain, sums, *near, *inputs],
        "v" * 9 + "h" * len(inputs),
        "vppp",
        scratch=[pltpu.VMEM((channels, steps * count), jnp.bfloat16), pltpu.VMEM((steps * count, hid), jnp.bfloat16)]
        + [pltpu.SemaphoreType.DMA((len(inputs),))],
        flops=2**30,
        moved=6 * 2**20,
        limit=20,
    )


def down_kernel(steps, moved_ref, *refs):
    inputs, (send_ref, keep_ref, left_ref, right_ref, sems) = refs[: 2 * steps - 1], refs[2 * steps - 1 :]
    count = moved_ref.shape[1]
    pairs = side_by_side(inputs[: steps - 1], left_ref, 1) + side_by_side(inputs[steps - 1 :], right_ref, 0)
    arriving = copies(sems, 0, pairs)
    left_ref[:, (steps - 1) * count :] = moved_ref[...]
    finish(arriving)
    gradient_quadrants(left_ref, right_ref, send_ref, keep_ref)


def down_gradients(moved, moveds, hidden):
    steps = len(hidden)
    channels, count = moved.shape
    hid = hidden[0].shape[1]
    inputs = moveds + hidden
    return call(
        functools.partial(down_kernel, steps),
        [jax.ShapeDtypeStruct(shape, jnp.bfloat16) for shape in quadrant_shapes(channels, hid, 0)],
        [moved, *inputs],
        "v" + "h" * len(inputs),
        "pp",
        scratch=[pltpu.VMEM((channels, steps * count), jnp.bfloat16), pltpu.VMEM((steps * count, hid), jnp.bfloat16)]
        + [pltpu.SemaphoreType.DMA((len(inputs),))],
        flops=2**29,
        moved=2**21,
        limit=16,
    )


def fill_margins(wide_ref, before, after, low, high, middle):
    rows_out, cols_out, _ = middle.shape
    around = slice(MARGIN - 1, MARGIN + cols_out + 1)
    wide_ref[:1, around] = low.astype(jnp.float32)
    wide_ref[1 + rows_out :, around] = high.astype(jnp.float32)
    wide_ref[1 : 1 + rows_out, MARGIN - 1 : MARGIN] = before.astype(jnp.float32)
    wide_ref[1 : 1 + rows_out, MARGIN + cols_out : MARGIN + cols_out + 1] = after.astype(jnp.float32)
    wide_ref[1 : 1 + rows_out, MARGIN : MARGIN + cols_out] = middle


def final_kernel(field_ref, before_ref, after_ref, low_ref, high_ref, kernel_ref, out_ref, wide_ref):
    rows_out, cols_out, _ = field_ref.shape
    result = field_ref[...].astype(jnp.float32)
    fill_margins(wide_ref, before_ref[0], after_ref[0], low_ref[0], high_ref[0], result)
    for col_tap in range(3):
        place = MARGIN + 1 - col_tap
        shifted_cols = wide_ref[:, place : place + cols_out]
        for row_tap in range(3):
            tap = kernel_ref[row_tap, col_tap : col_tap + 1]
            result = result + tap[None] * shifted_cols[2 - row_tap : 2 - row_tap + rows_out]
    out_ref[...] = result.astype(jnp.bfloat16)


def final_parts(field, around, kernel):
    rows_out, cols_out, channels = field.shape
    return call(
        final_kernel,
        [jax.ShapeDtypeStruct(field.shape, jnp.bfloat16)],
        [field, *around, kernel],
        "v" * 6,
        "v",
        scratch=[pltpu.VMEM((rows_out + 2, cols_out + 2 * MARGIN, channels), jnp.float32)],
        moved=2**19,
    )[0]


def spatial_kernel(mode, step, near_lon, near_lat, *refs):
    refs = list(refs)
    take = lambda: refs.pop(0)
    with_stencil = mode != "first"
    move_hbm = take()
    in_ref = take()
    kern_ref = take() if with_stencil else None
    weight_hbm = take() if mode == "mid" else None
    out_hbm = take()
    saved_hbm = take() if mode == "first" else None
    out_ref, sems = take(), take()
    spread_ref, weight_ref, move_ref = take(), take(), take()
    moving = copies(sems, 3, [(move_hbm, move_ref)])
    tiles_lon, tiles_lat, _, lanes = in_ref.shape
    rows = out_ref.shape[2]
    started = []
    if mode == "mid":
        arriving = copies(sems, 0, [(weight_hbm, weight_ref)])
    if mode == "first":
        weight_ref[...] = in_ref[:, :, rows:]
        started += copies(sems, 0, [(weight_ref, saved_hbm)])
    lane = lax.broadcasted_iota(jnp.int32, (rows, lanes), 1)
    col = lax.rem(lane, near_lat)
    lat_last, lat_first = col == near_lat - 1, col == 0
    lon_last, lon_first = lane >= lanes - near_lat, lane < near_lat
    tiles = [(a, b) for a in range(tiles_lon) for b in range(tiles_lat)]

    def turn(value, steps):
        return pltpu.roll(value, steps % lanes if isinstance(steps, int) else steps, 1)

    def lat_after(grid):
        turned = {key: turn(value, -1) for key, value in grid.items()}
        wrapped = {key: turn(grid[key], near_lat - 1) for key in tiles if key[1] > 0}
        return {(a, b): jnp.where(lat_last, wrapped.get((a, b + 1), 0.0), turned[a, b]) for a, b in tiles}

    def lat_before(grid):
        turned = {key: turn(value, 1) for key, value in grid.items()}
        wrapped = {key: turn(grid[key], 1 - near_lat) for key in tiles if key[1] < tiles_lat - 1}
        return {(a, b): jnp.where(lat_first, wrapped.get((a, b - 1), 0.0), turned[a, b]) for a, b in tiles}

    def lon_after(grid):
        return {
            (a, b): turn(jnp.where(lon_first, grid[(a + 1) % tiles_lon, b], grid[a, b]), -near_lat) for a, b in tiles
        }

    def lon_before(grid):
        return {(a, b): turn(jnp.where(lon_last, grid[(a - 1) % tiles_lon, b], grid[a, b]), near_lat) for a, b in tiles}

    grid = {(a, b): in_ref[a, b, :rows].astype(jnp.float32) for a, b in tiles}
    if with_stencil:
        taps = [
            [jnp.broadcast_to(kern_ref[:, 3 * a + b : 3 * a + b + 1], (rows, lanes)) for b in range(3)] for a in range(3)
        ]
        by_col = [lat_after(grid), grid, lat_before(grid)]
        mix = [
            {key: sum(taps[row][c] * by_col[c][key] for c in range(1, 3)) + taps[row][0] * by_col[0][key] for key in tiles}
            for row in range(3)
        ]
        high, low = lon_after(mix[0]), lon_before(mix[2])
        grid = {key: grid[key] + mix[1][key] + (high[key] + low[key]) for key in tiles}
    if mode == "mid":
        grid = {key: value.astype(jnp.bfloat16).astype(jnp.float32) for key, value in grid.items()}
        finish(arriving)
    weights = {}
    for a, b in tiles:
        four = weight_ref[a, b].astype(jnp.float32)[4 * step : 4 * step + 4]
        weights[a, b] = [jnp.broadcast_to(four[k : k + 1], (rows, lanes)) for k in range(4)]
    weighted = [{key: weights[key][k] * grid[key] for key in tiles} for k in range(4)]
    own, lon = lat_after(weighted[2]), lat_after(weighted[3])
    lon = lon_after({key: weighted[1][key] + lon[key] for key in tiles})
    for a, b in tiles:
        value = (weighted[0][a, b] + own[a, b] + lon[a, b]).astype(jnp.bfloat16).astype(jnp.float32)
        for place in range(a, tiles_lon + LON_REACH, tiles_lon):
            spread_ref[place, b] = value
    spread_ref[:, tiles_lat:] = jnp.zeros((tiles_lon + LON_REACH, LAT_REACH, rows, lanes), jnp.float32)

    finish(moving)
    lon_move, lat_move = move_ref[step, 0], move_ref[step, 1]
    far_lon, off_lon = lon_move // near_lon, lax.rem(lon_move, near_lon)
    far_lat, off_lat = lat_move // near_lat, lax.rem(lat_move, near_lat)
    shift = off_lon * near_lat + off_lat
    turn_here = lax.rem(2 * lanes - shift, lanes)
    turn_next = lax.rem(2 * lanes - shift + near_lat, lanes)
    same_lon = lane >= off_lon * near_lat
    same_lat = col + off_lat < near_lat
    half = tiles_lon // 2
    for a in range(tiles_lon):
        met = [
            jnp.where(same_lon, spread_ref[far_lon + a, far_lat + b], spread_ref[far_lon + a + 1, far_lat + b])
            for b in range(tiles_lat + 1)
        ]
        for b in range(tiles_lat):
            value = jnp.where(same_lat, turn(met[b], turn_here), turn(met[b + 1], turn_next))
            out_ref[a, b] = value.astype(jnp.bfloat16)
        if (a + 1) % half == 0:
            part = pl.ds(a + 1 - half, half)
            started += copies(sems, 1 + a // half, [(out_ref.at[part], out_hbm.at[part])])
    finish(started)


def spatial(mode, step, tile, rows, field, kern, weights, moves):
    tiles_lon, tiles_lat, _, lanes = field.shape
    with_stencil = mode != "first"
    operands = [moves, field]
    operands += [kern] if with_stencil else []
    operands += [weights] if mode == "mid" else []
    out_shape = (tiles_lon, tiles_lat, rows, lanes)
    weight_shape = (tiles_lon, tiles_lat, ROWS, lanes)
    sds = jax.ShapeDtypeStruct
    out = [sds(out_shape, jnp.bfloat16)] + ([sds(weight_shape, jnp.bfloat16)] if mode == "first" else [])
    scratch = [pltpu.VMEM(out_shape, jnp.bfloat16), pltpu.SemaphoreType.DMA((4,))]
    spread_shape = (tiles_lon + LON_REACH, tiles_lat + LAT_REACH, rows, lanes)
    scratch += [pltpu.VMEM(spread_shape, jnp.float32), pltpu.VMEM(weight_shape, jnp.bfloat16)]
    scratch += [pltpu.SMEM(moves.shape, jnp.int32)]
    return call(
        functools.partial(spatial_kernel, mode, step, *tile),
        out,
        operands,
        "hv" + "v" * with_stencil + "h" * (mode == "mid"),
        "h" * len(out),
        scratch=scratch,
        flops=2**22,
        moved=2**20,
        limit=max(8, 14 * tiles_lon * tiles_lat * rows * lanes * 4 // MIB),
    )


def halved(value, axis, bit, dim):
    count = lax.axis_size(axis)
    mine = lax.axis_index(axis) >> bit & 1
    kept = lax.dynamic_index_in_dim(value, mine, dim, keepdims=False)
    sent = lax.dynamic_index_in_dim(value, 1 - mine, dim, keepdims=False).astype(jnp.bfloat16)
    arrived = lax.ppermute(sent, axis, [(i, i ^ (1 << bit)) for i in range(count)])
    return kept + arrived.astype(jnp.float32)


def scattered(value, lat_first):
    channels, hid = value.shape
    lon_bits = lax.axis_size("lon").bit_length() - 1
    lat_bits = lax.axis_size("lat").bit_length() - 1
    rows = channels >> lon_bits
    value = value.reshape(*([2] * lon_bits), rows, *([2] * lat_bits), hid >> lat_bits)

    def over_lon(value, bit, left):
        return halved(value, "lon", bit, left.index(bit)), [k for k in left if k != bit]

    left_lon = list(range(lon_bits))[::-1]
    left_lat = list(range(lat_bits))[::-1]
    order = [("lon", 0), ("lon", 1)] + [("lat", k) for k in range(lat_bits)]
    if lat_first:
        order = [("lon", 0)] + [("lat", k) for k in range(lat_bits)] + [("lon", 1)]
    order += [("lon", k) for k in range(2, lon_bits)]
    for axis, bit in order:
        if axis == "lon":
            value, left_lon = over_lon(value, bit, left_lon)
        else:
            value = halved(value, "lat", bit, len(left_lon) + 1 + left_lat.index(bit))
            left_lat.remove(bit)
    return value


def add_parts(pairs, kept, arrived):
    for q, out_ref, place in pairs:
        value = kept(q).astype(jnp.float32) + arrived(q).astype(jnp.float32)
        out_ref[place] = value.astype(out_ref.dtype)


def first_axis(flip):
    core = lon_bit(0)
    return 1 - core if flip else core


def quadrant_kernel(flip, *refs):
    kept_ref, *total_refs, arrived_ref, send_ref, keep_ref = refs[: 4 + len(refs) // 6]
    axis, x, lat = first_axis(flip), lon_bit(1), lax.axis_index("lat")
    rows = kept_ref.shape[1]
    for j in range(2):
        kept = (1 - axis) * (2 * x + j) + axis * (2 * j + lat)
        sent = (1 - axis) * (2 * (1 - x) + j) + axis * (2 * j + 1 - lat)
        pairs = [(sent, send_ref, pl.ds(j * rows, rows)), (kept, keep_ref, j)]
        arrived = lambda q: arrived_ref[pl.ds(pl.multiple_of(q * rows, rows), rows)]
        add_parts(pairs, lambda q: kept_ref[q], arrived)
    if total_refs:
        chip = total_refs[0][...] + whole_of(arrived_ref[QUADRANTS * rows :])
        refs[-1][...] = chip
        send_ref[2 * rows :] = pieces_of(chip)


def half_kernel(flip, *refs):
    kept_ref, *total_refs, arrived_ref, send_ref, keep_ref = refs[: 4 + len(refs) // 6]
    axis, x, lat = first_axis(flip), lon_bit(1), lax.axis_index("lat")
    mine = (1 - axis) * lat + axis * x
    rows = kept_ref.shape[1]
    pairs = [(1 - mine, send_ref, pl.ds(0, rows)), (mine, keep_ref, slice(None))]
    arrived = lambda q: arrived_ref[pl.ds(pl.multiple_of(q * rows, rows), rows)]
    add_parts(pairs, lambda q: kept_ref[q], arrived)
    if total_refs:
        beside = arrived_ref[2 * rows :]
        refs[-1][...] = whole_of(beside)
        send_ref[rows : rows + SUM_ROWS] = pieces_of(total_refs[0][...])
        send_ref[rows + SUM_ROWS :] = beside


def rows_kernel(groups, bit_at, totals, *refs):
    kept_ref, *refs = refs
    total_refs, (arrived_ref, send_ref, keep_ref, *total_ref) = refs[:totals], refs[totals:]
    bit = lon_bit(bit_at)
    rows = kept_ref.shape[0]
    chunk = rows // (2 * groups)
    for p in range(groups):
        goal = pl.ds(p * chunk, chunk)
        places = [pl.multiple_of((2 * p + which) * chunk, chunk) for which in (1 - bit, bit)]
        pairs = [(places[0], send_ref, goal), (places[1], keep_ref, goal)]
        add_parts(pairs, lambda q: kept_ref[pl.ds(q, chunk)], lambda q: arrived_ref[pl.ds(q, chunk)])
    if totals:
        total = add_sums(total_refs, arrived_ref, rows)
        total_ref[0][...] = total
        send_ref[rows // 2 :] = pieces_of(total)


def add_sums(total_refs, arrived_ref, start):
    arrived = whole_of(arrived_ref[start : start + SUM_ROWS])
    if len(total_refs) == 1:
        return total_refs[0][...] + arrived
    chip, beside = (ref[...] for ref in total_refs)
    return (chip + whole_of(arrived_ref[start + SUM_ROWS :])) + (beside + arrived)


def finish_kernel(kept_ref, total_ref, arrived_ref, kept_down_ref, arrived_down_ref, up_hbm, down_hbm, taps_ref, gain_ref, *refs):
    up_ref, down_ref, sems = refs
    rows = kept_ref.shape[0]
    down_ref[...] = kept_down_ref[...] + arrived_down_ref[...].astype(jnp.float32)
    leaving = copies(sems, 0, [(down_ref, down_hbm)])
    up_ref[...] = kept_ref[...] + arrived_ref[:rows].astype(jnp.float32)
    leaving += copies(sems, 1, [(up_ref, up_hbm)])
    total = add_sums([total_ref], arrived_ref, rows)
    for k in range(9):
        taps_ref[k // 3, k % 3 : k % 3 + 1] = total[k : k + 1]
    gain_ref[...] = total[9:10]
    finish(leaving)


def halving(flip, send, keep, total):
    lon, lat = lax.axis_size("lon"), lax.axis_size("lat")
    places = [(i, j) for i in range(lon) for j in range(lat)]
    flat = lambda i, j: i * lat + j
    along_lat = lambda i: (i & 1) != flip
    sds = jax.ShapeDtypeStruct
    rows, width = keep.shape[1:]
    sums = [] if total is None else [total]
    with_sums = len(sums)
    plan = [
        (lambda i, j: (i ^ 1, j), functools.partial(quadrant_kernel, flip), (2, rows, width), 1),
        (
            lambda i, j: (i, j ^ 1) if along_lat(i) else (i ^ 2, j),
            functools.partial(half_kernel, flip),
            (rows, width),
            2,
        ),
        (
            lambda i, j: (i ^ 2, j) if along_lat(i) else (i, j ^ 1),
            functools.partial(rows_kernel, 2, 2, 2 * with_sums),
            (rows // 2, width),
            1,
        ),
        (lambda i, j: (i ^ 4, j), functools.partial(rows_kernel, 1, 3, with_sums), (rows // 4, width), 1),
    ]
    for at, (partner, kernel, shape, parts) in enumerate(plan):
        send = yield send
        arrived = lax.ppermute(send, AXES, [(flat(i, j), flat(*partner(i, j))) for i, j in places])
        arrived = yield arrived
        sent = shape[-2] * (shape[0] if len(shape) == 3 else 1) + SUM_ROWS * parts * with_sums
        out = [sds((sent, shape[-1]), jnp.bfloat16), sds(shape, jnp.float32)]
        out += [sds(value.shape, jnp.float32) for value in sums[:1]]
        operands = [keep, *sums, arrived]
        send, keep, *more = call(kernel, out, operands, "v" * len(operands), "p" * len(out), moved=2**19, limit=12)
        sums = sums + more if at == 1 else more
    send = yield send
    arrived = lax.ppermute(send, AXES, [(flat(i, j), flat(i ^ 8, j)) for i, j in places])
    yield (keep, *sums, arrived)


def all_sums(up, down, total, field, kernel):
    channels = total.shape[1]
    field = field[None]
    if up[1].ndim == 2:
        parts = [scattered(send.astype(jnp.float32), flip) for flip, (send, _) in enumerate((up, down))]
        total = lax.psum(total, AXES)
        around = lat_edges(field)
        state = final_parts(field[0], (*around, *lon_edges(field, *around)), kernel)
        return (state, *parts, total[:9].reshape(3, 3, channels), total[9])
    ahead, behind = halving(False, *up, total), halving(True, *down, None)
    send, later = next(ahead), next(behind)
    arrived = ahead.send(send)
    send = ahead.send(after(arrived, later))
    field = after(field, send)
    arrived_later = behind.send(after(later, send))
    later = behind.send(arrived_later)
    around = lat_edges(field, lambda value: after(value, later))
    state = final_parts(field[0], (*around, *lon_edges(field, *around)), kernel)
    for at in range(1, 4):
        arrived = ahead.send(send)
        arrived_later = behind.send(later)
        send = ahead.send(after(arrived, later))
        later = behind.send(after(arrived_later, send))
    final_ahead = ahead.send(send)
    final_behind = behind.send(later)
    sds = jax.ShapeDtypeStruct
    part = sds(final_ahead[0].shape, jnp.float32)
    out = [part, part, sds((3, 3, channels), jnp.float32), sds((1, channels), jnp.float32)]
    up, down, taps, gain = call(
        finish_kernel,
        out,
        [*final_ahead, *final_behind],
        "vvvvv",
        "hhvv",
        scratch=[pltpu.VMEM(part.shape, part.dtype)] * 2 + [pltpu.SemaphoreType.DMA((2,))],
        moved=2**18,
    )
    return state, up, down, taps, gain.reshape(channels)


def local(cotangent, states, w_up, w_down, norm_gain, kernel, bilinear, lon_move, lat_move):
    steps, rows_out, cols_out, channels = states.shape
    tiles_lon, tiles_lat = lax.axis_size("lon"), lax.axis_size("lat")
    devices = tiles_lon * tiles_lat
    count = rows_out * cols_out
    tile = (rows_out, cols_out)
    share = channels // devices
    padded_share = -(-share // ROWS) * ROWS
    whole_share = share == padded_share
    group_size = channels // lon_move.shape[1]
    me = lax.axis_index("lon") * tiles_lat + lax.axis_index("lat")

    def as_blocks(value):
        value = value.reshape(devices, share, count)
        return value if whole_share else jnp.pad(value, ((0, 0), (0, padded_share - share), (0, 0)))

    def as_rows(blocks):
        return blocks[:, :share].reshape(channels, count)

    def as_grid(blocks):
        return blocks.reshape(tiles_lon, tiles_lat, *blocks.shape[1:])

    blocks = packed(cotangent, bilinear, devices)
    blocks, states_later = lax.optimization_barrier((blocks, states))
    arrived = as_grid(exchanged(blocks))
    group = me * share // group_size
    moves = jnp.stack([lon_move[:, group], lat_move[:, group]], axis=1)
    grid_now, weights = spatial("first", steps - 1, tile, padded_share, arrived, None, None, moves)

    taps = lax.dynamic_slice_in_dim(kernel.reshape(9, channels), me * share, share, 1).T
    taps = jnp.pad(taps, ((0, padded_share - share), (0, count - 9)))

    around = lat_edges(states_later)
    grid_now, *around = lax.optimization_barrier((grid_now, *around))
    around = (*around, *lon_edges(states, *around))
    order = list(reversed(range(steps)))
    gain = norm_gain.reshape(1, channels)
    now, *others = order
    forward = {s: forward_parts(s, states, around, kernel, gain, w_up) for s in others}
    names = {k: {s: forward[s][at] for s in others} for at, k in enumerate(FORWARD)}

    def taken_back(grid):
        return as_rows(exchanged(grid.reshape(devices, padded_share, count)))

    def spread_on(s, field, grid_kernel=taps):
        arrived = as_grid(exchanged(as_blocks(field)))
        return spatial("mid", s, tile, padded_share, arrived, grid_kernel, weights, moves)[0]

    fields, grads, moved = {}, {}, {}
    (near,) = fetched([w_down], grid_now)
    here = after(taken_back(grid_now), near)
    parts = first_step(now, here, near, states, around, kernel, gain, w_up)
    for k, value in zip(("n", "turned", "hid", "pad"), parts):
        names[k][now] = value
    fields[now], grads[now], moved[now] = parts[4:]
    for s in others:
        grid_now = spread_on(s, fields[s + 1])
        here = taken_back(grid_now)
        wanted = ("slope", "n", "inv") + ("pad",) * (s == others[-1])
        near = fetched([names[k][s] for k in wanted], grid_now)
        if s == others[-1]:
            break
        here = after(here, (near, forward))
        fields[s], grads[s], moved[s] = network_back(here, w_down, w_up, gain, *near)

    earlier = lambda values: [values[s] for s in order[:-1]]
    all_of = lambda values: [values[s] for s in order]
    sums = channel_sums(tile, w_up, gain, *map(earlier, (names["pad"], fields, grads, names["n"])))
    here = after(here, (near, sums))
    field, total, send, keep = last_step(tile, here, w_down, w_up, gain, sums, near, all_of(names["turned"]), earlier(grads))
    down = down_gradients(here, earlier(moved), all_of(names["hid"]))
    field = field.reshape(cotangent.shape)
    return all_sums((send, keep), down, total, field, kernel)


def solution(mesh):
    placed = (
        P("lon", "lat", None),
        P(None, "lon", "lat", None),
        P(),
        P(),
        P(),
        P(),
        P(None, None, "lon", "lat"),
        P(),
        P(),
    )
    return jax.shard_map(
        local,
        mesh=mesh,
        in_specs=placed,
        out_specs=(P("lon", "lat", None), P("lon", "lat"), P("lon", "lat"), P(), P()),
        check_vma=False,
    )
```

```python
import functools

import jax
import jax.numpy as jnp
from jax import lax
from jax.experimental import pallas as pl
from jax.experimental.pallas import tpu as pltpu
from jax.sharding import PartitionSpec as P

EPSILON = 1e-06
AXES = ("lon", "lat")
ROWS = 16
LAT_REACH = 2
LON_REACH = 8
MIB = 1024 * 1024


def exchanged(blocks):
    return lax.all_to_all(blocks, AXES, split_axis=0, concat_axis=0, tiled=True)


SPACES = {"s": pltpu.SMEM, "v": pltpu.VMEM, "p": pltpu.VMEM, "h": pltpu.HBM}
PINNED = {"p": pltpu.VMEM, "h": pltpu.HBM}


def call(kernel, out_shape, operands, ins, outs, scratch=(), flops=0, moved=0, limit=8):
    operands = [
        pltpu.with_memory_space_constraint(value, PINNED[kind]) if kind in PINNED else value
        for kind, value in zip(ins, operands, strict=True)
    ]
    out_shape = [
        PINNED[kind](value.shape, value.dtype) if kind in PINNED else value
        for kind, value in zip(outs, out_shape, strict=True)
    ]
    return pl.pallas_call(
        kernel,
        out_shape=out_shape,
        in_specs=[pl.BlockSpec(memory_space=SPACES[kind]) for kind in ins],
        out_specs=[pl.BlockSpec(memory_space=SPACES[kind]) for kind in outs],
        scratch_shapes=scratch,
        compiler_params=pltpu.CompilerParams(vmem_limit_bytes=limit * MIB),
        cost_estimate=pl.CostEstimate(flops=flops, bytes_accessed=moved, transcendentals=0),
    )(*operands)


def copies(sems, first, pairs):
    started = [pltpu.make_async_copy(src, dst, sems.at[first + k]) for k, (src, dst) in enumerate(pairs)]
    for copy in started:
        copy.start()
    return started


def finish(started):
    for copy in started:
        copy.wait()


PIECES = 3
SUMS = 10
SUM_ROWS = 32


def pieces_of(value):
    value = value[:SUMS]
    parts = []
    for _ in range(PIECES):
        parts.append(value.astype(jnp.bfloat16).astype(jnp.float32))
        value = value - parts[-1]
    parts.append(jnp.zeros((SUM_ROWS - PIECES * SUMS, value.shape[1]), jnp.float32))
    return jnp.concatenate(parts, axis=0).astype(jnp.bfloat16)


def whole_of(parts):
    parts = parts.astype(jnp.float32)
    total = (parts[:SUMS] + parts[SUMS : 2 * SUMS]) + parts[2 * SUMS : 3 * SUMS]
    return jnp.concatenate([total, jnp.zeros((ROWS - SUMS, parts.shape[1]), jnp.float32)], axis=0)


def after(value, first):
    return lax.optimization_barrier((value, first))[0]


def pack_kernel(cotangent_hbm, weight_hbm, out_hbm, cotangent_ref, weight_ref, out_ref, sems):
    started = copies(sems, 0, [(cotangent_hbm, cotangent_ref), (weight_hbm, weight_ref)])
    channels = cotangent_ref.shape[1]
    devices, _, count = out_ref.shape
    share = channels // devices
    started[1].wait()
    rows = weight_ref.shape[0]
    weights = jnp.concatenate([weight_ref[:, i] for i in range(weight_ref.shape[1])], axis=1)
    weights = jnp.concatenate([weights, jnp.zeros((ROWS - rows, count), jnp.float32)], axis=0)
    weights = weights.astype(jnp.bfloat16)
    out_ref[:, share:] = jnp.broadcast_to(weights[None], (devices, ROWS, count))
    started[0].wait()
    turned = cotangent_ref[...].astype(jnp.float32).T.astype(jnp.bfloat16)
    out_ref[:, :share] = turned.reshape(devices, share, count)
    finish(copies(sems, 2, [(out_ref, out_hbm)]))


def packed(cotangent, bilinear, devices):
    rows_out, cols_out, channels = cotangent.shape
    steps, corners = bilinear.shape[:2]
    count = rows_out * cols_out
    share = channels // devices
    if share % ROWS:
        blocks = cotangent.reshape(count, channels).T.reshape(devices, share, count)
        blocks = jnp.pad(blocks, ((0, 0), (0, -share % ROWS), (0, 0)))
        weights = bilinear.reshape(steps * corners, count).astype(jnp.bfloat16)
        weights = jnp.pad(weights, ((0, ROWS - steps * corners), (0, 0)))
        return jnp.concatenate([blocks, jnp.broadcast_to(weights[None], (devices, ROWS, count))], axis=1)
    shape = (devices, share + ROWS, count)
    return call(
        pack_kernel,
        [jax.ShapeDtypeStruct(shape, jnp.bfloat16)],
        [cotangent.reshape(count, channels), bilinear.reshape(steps * corners, rows_out, cols_out)],
        "hh",
        "h",
        scratch=[
            pltpu.VMEM((count, channels), jnp.bfloat16),
            pltpu.VMEM((steps * corners, rows_out, cols_out), jnp.float32),
            pltpu.VMEM(shape, jnp.bfloat16),
            pltpu.SemaphoreType.DMA((3,)),
        ],
        moved=2**19,
    )[0]


def lat_edges(states, held=lambda value: value):
    lat, lat_at = lax.axis_size("lat"), lax.axis_index("lat")
    first, last = states[:, :, :1], states[:, :, -1:]
    if lat == 2:
        arrived = lax.ppermute(jnp.where(lat_at == 0, last, first), "lat", [(0, 1), (1, 0)])
        arrived = held(arrived)
        return jnp.where(lat_at == 0, 0, arrived), jnp.where(lat_at == 0, arrived, 0)
    return (
        lax.ppermute(last, "lat", [(i, i + 1) for i in range(lat - 1)]),
        lax.ppermute(first, "lat", [(i + 1, i) for i in range(lat - 1)]),
    )


def lon_edges(states, before, after):
    lon = lax.axis_size("lon")
    even = lax.axis_index("lon") % 2 == 0
    row = lambda place: jnp.concatenate([part[:, place] for part in (before, states, after)], axis=2)
    first, last = row(slice(0, 1)), row(slice(-1, None))
    with_next = lax.ppermute(jnp.where(even, last, first), "lon", [(i, i ^ 1) for i in range(lon)])
    pairs = [(i, (i - 1) % lon if i % 2 == 0 else (i + 1) % lon) for i in range(lon)]
    with_last = lax.ppermute(jnp.where(even, first, last), "lon", pairs)
    return jnp.where(even, with_last, with_next), jnp.where(even, with_next, with_last)


def lon_edges_ring(states, before, after):
    lon = lax.axis_size("lon")
    ahead = lambda value: lax.ppermute(value, "lon", [(i, (i + 1) % lon) for i in range(lon)])
    behind = lambda value: lax.ppermute(value, "lon", [(i, (i - 1) % lon) for i in range(lon)])
    row = lambda place: jnp.concatenate([part[:, place] for part in (before, states, after)], axis=2)
    return ahead(row(slice(-1, None))), behind(row(slice(0, 1)))


MARGIN = 8


def forward_math(step, places, sems, leaving, outs):
    states_ref, before_ref, after_ref, low_ref, high_ref, kernel_ref, gain_ref, up_ref = places
    n_ref, turned_ref, inv_ref, hid_ref, slope_ref, pad_ref, wide_ref = outs
    rows_out, cols_out, channels = states_ref.shape[1:]
    count = rows_out * cols_out
    mixed = states_ref[step].astype(jnp.float32)
    fill_margins(wide_ref, before_ref[step], after_ref[step], low_ref[step], high_ref[step], mixed)
    pad_ref[...] = wide_ref[...].astype(jnp.bfloat16)
    leaving("pad")
    for col_tap in range(3):
        place = MARGIN - 1 + col_tap
        shifted_cols = wide_ref[:, place : place + cols_out]
        for row_tap in range(3):
            tap = kernel_ref[row_tap, col_tap : col_tap + 1]
            mixed = mixed + tap[None] * shifted_cols[row_tap : row_tap + rows_out]
    mixed = mixed.reshape(count, channels)
    inv_root = lax.rsqrt(jnp.mean(mixed * mixed, axis=1, keepdims=True) + EPSILON)
    narrow = mixed * inv_root * gain_ref[...]
    n_ref[...] = narrow.astype(jnp.bfloat16)
    inv_ref[...] = jnp.broadcast_to(inv_root, inv_ref.shape)
    leaving("n", "inv")
    pre = jnp.dot(n_ref[...], up_ref[...], preferred_element_type=jnp.float32)
    sigmoid = jax.nn.sigmoid(pre)
    slope_ref[...] = (sigmoid * (1.0 + pre * (1.0 - sigmoid))).astype(jnp.bfloat16)
    leaving("slope")
    hid_ref[...] = (pre * sigmoid).astype(jnp.bfloat16)
    turned_ref[...] = narrow.T.astype(jnp.bfloat16)
    leaving("hid", "turned")


FORWARD = ("n", "turned", "inv", "hid", "slope", "pad")


def sender(sems, refs, goals, started):
    names = list(goals)

    def leave(*which):
        for name in which:
            if name in goals:
                started.extend(copies(sems, names.index(name), [(refs[name], goals[name])]))

    return leave


def forward_kernel(step, *refs):
    places, goals, outs, sems = refs[:8], refs[8:14], refs[14:21], refs[21]
    started = []
    leave = sender(sems, dict(zip(FORWARD, outs)), dict(zip(FORWARD, goals)), started)
    forward_math(step, places, sems, leave, outs)
    finish(started)


def forward_shapes(states, w_up):
    _, rows_out, cols_out, channels = states.shape
    hid = w_up.shape[1]
    count = rows_out * cols_out
    wide = (rows_out + 2, cols_out + 2 * MARGIN, channels)
    return [
        ((count, channels), jnp.bfloat16),
        ((channels, count), jnp.bfloat16),
        ((count, 128), jnp.float32),
        ((count, hid), jnp.bfloat16),
        ((count, hid), jnp.bfloat16),
        (wide, jnp.bfloat16),
    ]


def forward_scratch(shapes):
    scratch = [pltpu.VMEM(*shape) for shape in shapes]
    return scratch + [pltpu.VMEM(shapes[-1][0], jnp.float32)]


def forward_parts(step, states, around, kernel, norm_gain, w_up):
    shapes = forward_shapes(states, w_up)
    return call(
        functools.partial(forward_kernel, step),
        [jax.ShapeDtypeStruct(*shape) for shape in shapes],
        [states, *around, kernel, norm_gain, w_up],
        "vvvvvvvv",
        "hhhhhh",
        scratch=forward_scratch(shapes) + [pltpu.SemaphoreType.DMA((6,))],
        flops=2**27,
        moved=2**22,
        limit=12,
    )


LANES_BOTH = (((1,), (1,)), ((), ()))


def fetch_kernel(*refs):
    count = len(refs) // 2
    *pairs, sems = refs
    finish(copies(sems, 0, list(zip(pairs[:count], pairs[count:]))))


def fetched(values, first):
    values = after(values, first)
    return call(
        fetch_kernel,
        [jax.ShapeDtypeStruct(value.shape, value.dtype) for value in values],
        values,
        "h" * len(values),
        "v" * len(values),
        scratch=[pltpu.SemaphoreType.DMA((len(values),))],
        moved=2**19,
    )


def network_math(moved_ref, down_ref, up_ref, gain_ref, slope_ref, n_ref, inv_ref, out_ref, grad_ref, leave):
    leave("moved")
    moved = moved_ref[...].astype(jnp.float32).T
    grad_hidden = jnp.dot(moved.astype(jnp.bfloat16), down_ref[...], preferred_element_type=jnp.float32)
    grad_pre = (grad_hidden * slope_ref[...].astype(jnp.float32)).astype(jnp.bfloat16)
    grad_ref[...] = grad_pre
    leave("grad")
    grad_n = lax.dot_general(grad_pre, up_ref[...], LANES_BOTH, preferred_element_type=jnp.float32)
    narrow, gain = n_ref[...].astype(jnp.float32), gain_ref[...]
    mean = jnp.mean(grad_n * narrow, axis=1, keepdims=True)
    field = moved + inv_ref[:, :1] * (grad_n * gain - narrow * (mean / gain))
    out_ref[...] = field.T.astype(jnp.bfloat16)
    leave("field")


def network_kernel(moved_ref, down_ref, up_ref, gain_ref, slope_ref, n_ref, inv_ref, *refs):
    *goals, out_ref, grad_ref, sems = refs
    started = []
    names = ("field", "grad", "moved")
    leave = sender(sems, dict(zip(names, (out_ref, grad_ref, moved_ref))), dict(zip(names, goals)), started)
    network_math(moved_ref, down_ref, up_ref, gain_ref, slope_ref, n_ref, inv_ref, out_ref, grad_ref, leave)
    finish(started)


def first_kernel(step, *refs):
    (moved_ref, down_ref), places, refs = refs[:2], refs[2:10], refs[10:]
    goals, outs, (out_ref, grad_ref, sems) = refs[:7], refs[7:14], refs[14:]
    started = []
    names = ("n", "turned", "hid", "pad", "field", "grad", "moved")
    values = dict(zip(FORWARD, outs)) | {"field": out_ref, "grad": grad_ref, "moved": moved_ref}
    leave = sender(sems, values, dict(zip(names, goals)), started)
    forward_math(step, places, sems, leave, outs)
    n_ref, _, inv_ref, _, slope_ref = outs[:5]
    gain_ref, up_ref = places[6:]
    network_math(moved_ref, down_ref, up_ref, gain_ref, slope_ref, n_ref, inv_ref, out_ref, grad_ref, leave)
    finish(started)


def first_step(step, moved, w_down, states, around, kernel, norm_gain, w_up):
    shapes = forward_shapes(states, w_up)
    channels, count = moved.shape
    hid = w_down.shape[1]
    backs = [((channels, count), jnp.bfloat16), ((count, hid), jnp.bfloat16), ((channels, count), jnp.bfloat16)]
    results = [shapes[k] for k in (0, 1, 3, 5)] + backs
    return call(
        functools.partial(first_kernel, step),
        [jax.ShapeDtypeStruct(*shape) for shape in results],
        [moved, w_down, states, *around, kernel, norm_gain, w_up],
        "v" * 10,
        "h" * 7,
        scratch=forward_scratch(shapes) + [pltpu.VMEM(*shape) for shape in backs[:2]] + [pltpu.SemaphoreType.DMA((7,))],
        flops=2**28,
        moved=2**22,
        limit=16,
    )


def network_back(moved, w_down, w_up, norm_gain, slope, narrow, inv_root):
    channels, count = moved.shape
    hid = w_down.shape[1]
    shapes = [((channels, count), jnp.bfloat16), ((count, hid), jnp.bfloat16), ((channels, count), jnp.bfloat16)]
    return call(
        network_kernel,
        [jax.ShapeDtypeStruct(*shape) for shape in shapes],
        [moved, w_down, w_up, norm_gain, slope, narrow, inv_root],
        "vvvvvvv",
        "hhh",
        scratch=[pltpu.VMEM(*shape) for shape in shapes[:2]] + [pltpu.SemaphoreType.DMA((3,))],
        flops=4 * count * hid * channels,
        moved=4 * 2**20,
        limit=8,
    )


def stencil_sums(pad_ref, field, tile):
    rows_out, cols_out = tile
    field = field.reshape(rows_out, cols_out, -1)
    padded = pad_ref[...].astype(jnp.float32)
    result = [None] * 9
    for col_tap in range(3):
        place = MARGIN - 1 + col_tap
        shifted_cols = padded[:, place : place + cols_out]
        for row_tap in range(3):
            products = jnp.sum(shifted_cols[row_tap : row_tap + rows_out] * field, axis=0)
            result[3 * row_tap + col_tap] = jnp.sum(products, axis=0, keepdims=True)
    return result


def sums_rows(rows, term, gain):
    rows = rows + [jnp.sum(term, axis=0, keepdims=True) / gain, jnp.zeros((ROWS - 10, term.shape[1]), jnp.float32)]
    return jnp.concatenate(rows, axis=0)


def sums_kernel(steps, tile, up_ref, gain_ref, *refs):
    inputs, (out_ref, *refs) = refs[: 4 * steps], refs[4 * steps :]
    pads, fields, grads, narrows, sems = refs
    places = [(ref, place.at[k]) for k in range(steps) for ref, place in zip(inputs[4 * k : 4 * k + 4], refs[:4])]
    arriving = copies(sems, 0, places)
    rows, term = None, None
    for k in range(steps):
        finish(arriving[4 * k : 4 * k + 4])
        grad_n = lax.dot_general(grads[k], up_ref[...], LANES_BOTH, preferred_element_type=jnp.float32)
        product = grad_n * narrows[k].astype(jnp.float32)
        term = product if term is None else term + product
        more = stencil_sums(pads.at[k], fields[k].astype(jnp.float32).T, tile)
        rows = more if rows is None else [a + b for a, b in zip(rows, more)]
    out_ref[...] = sums_rows(rows, term, gain_ref[...])


def channel_sums(tile, w_up, norm_gain, pads, fields, grads, narrows):
    steps = len(fields)
    inputs = [value for group in zip(pads, fields, grads, narrows) for value in group]
    return call(
        functools.partial(sums_kernel, steps, tile),
        [jax.ShapeDtypeStruct((ROWS, fields[0].shape[0]), jnp.float32)],
        [w_up, norm_gain, *inputs],
        "vv" + "h" * 4 * steps,
        "v",
        scratch=[pltpu.VMEM((steps, *value.shape), value.dtype) for value in inputs[:4]]
        + [pltpu.SemaphoreType.DMA((4 * steps,))],
        moved=2**21,
        limit=12,
    )[0]


QUADRANTS = 4


def lon_bit(at):
    return lax.axis_index("lon") >> at & 1


def gradient_quadrants(left_ref, right_ref, send_ref, keep_ref):
    channels, width = left_ref.shape[0], right_ref.shape[1] // 2
    if keep_ref.ndim == 2:
        send_ref[:channels] = jnp.dot(left_ref[...], right_ref[...], preferred_element_type=jnp.float32).astype(jnp.bfloat16)
        keep_ref[...] = jnp.zeros_like(keep_ref)
        return
    size = channels // QUADRANTS
    groups = lax.axis_size("lon") // 4
    chunk = size // groups
    rows = []
    for core in (1 - lon_bit(0), lon_bit(0)):
        for x in range(2):
            for z in range(groups):
                start = pl.multiple_of((4 * z + 2 * x + core) * chunk, chunk)
                rows.append(left_ref[pl.ds(start, chunk)])
    rows = jnp.concatenate(rows, axis=0)
    value = jnp.dot(rows, right_ref[...], preferred_element_type=jnp.float32).astype(jnp.bfloat16)
    for q in range(QUADRANTS):
        x, lat = q // 2, q % 2
        columns = slice(lat * width, (lat + 1) * width)
        send_ref[q * size : (q + 1) * size] = value[x * size : (x + 1) * size, columns]
        keep_ref[q] = value[(2 + x) * size : (3 + x) * size, columns]


def quadrant_shapes(channels, hid, sums):
    if lax.axis_size("lat") != 2 or lax.axis_size("lon") != 16:
        return (channels, hid), (8, 128)
    return (channels + SUM_ROWS * sums, hid // 2), (QUADRANTS, channels // QUADRANTS, hid // 2)


def side_by_side(refs, goal_ref, axis):
    size = refs[0].shape[axis]
    places = [pl.ds(s * size, size) for s in range(len(refs))]
    return [(ref, goal_ref.at[:, place] if axis else goal_ref.at[place]) for ref, place in zip(refs, places)]


def last_kernel(steps, tile, moved_ref, down_ref, up_ref, gain_ref, sums_ref, *refs):
    slope_ref, n_ref, inv_ref, pad_ref, *refs = refs
    inputs, refs = refs[: 2 * steps - 1], refs[2 * steps - 1 :]
    field_ref, total_ref, send_ref, keep_ref, left_ref, right_ref, sems = refs
    count = slope_ref.shape[0]
    pairs = side_by_side(inputs[:steps], left_ref, 1) + side_by_side(inputs[steps:], right_ref, 0)
    later = copies(sems, 0, pairs)
    moved = moved_ref[...].astype(jnp.float32).T
    grad_hidden = jnp.dot(moved.astype(jnp.bfloat16), down_ref[...], preferred_element_type=jnp.float32)
    grad_pre = (grad_hidden * slope_ref[...].astype(jnp.float32)).astype(jnp.bfloat16)
    right_ref[(steps - 1) * count :] = grad_pre
    grad_n = lax.dot_general(grad_pre, up_ref[...], LANES_BOTH, preferred_element_type=jnp.float32)
    narrow, gain = n_ref[...].astype(jnp.float32), gain_ref[...]
    term = grad_n * narrow
    mean = jnp.mean(term, axis=1, keepdims=True)
    field = moved + inv_ref[:, :1] * (grad_n * gain - narrow * (mean / gain))
    field = field.astype(jnp.bfloat16)
    field_ref[...] = field
    total = sums_ref[...] + sums_rows(stencil_sums(pad_ref, field.astype(jnp.float32), tile), term, gain)
    total_ref[...] = total
    finish(later)
    gradient_quadrants(left_ref, right_ref, send_ref, keep_ref)
    if keep_ref.ndim > 2:
        send_ref[left_ref.shape[0] :] = pieces_of(total)


def last_step(tile, moved, w_down, w_up, norm_gain, sums, near, turned, grads):
    steps = len(turned)
    channels, count = moved.shape
    hid = w_down.shape[1]
    send, keep = quadrant_shapes(channels, hid, 1)
    sds = jax.ShapeDtypeStruct
    inputs = turned + grads
    return call(
        functools.partial(last_kernel, steps, tile),
        [
            sds((count, channels), jnp.bfloat16),
            sds((ROWS, channels), jnp.float32),
            sds(send, jnp.bfloat16),
            sds(keep, jnp.bfloat16),
        ],
        [moved, w_down, w_up, norm_gain, sums, *near, *inputs],
        "v" * 9 + "h" * len(inputs),
        "vppp",
        scratch=[pltpu.VMEM((channels, steps * count), jnp.bfloat16), pltpu.VMEM((steps * count, hid), jnp.bfloat16)]
        + [pltpu.SemaphoreType.DMA((len(inputs),))],
        flops=2**30,
        moved=6 * 2**20,
        limit=20,
    )


def down_kernel(steps, moved_ref, *refs):
    inputs, (send_ref, keep_ref, left_ref, right_ref, sems) = refs[: 2 * steps - 1], refs[2 * steps - 1 :]
    count = moved_ref.shape[1]
    pairs = side_by_side(inputs[: steps - 1], left_ref, 1) + side_by_side(inputs[steps - 1 :], right_ref, 0)
    arriving = copies(sems, 0, pairs)
    left_ref[:, (steps - 1) * count :] = moved_ref[...]
    finish(arriving)
    gradient_quadrants(left_ref, right_ref, send_ref, keep_ref)


def down_gradients(moved, moveds, hidden):
    steps = len(hidden)
    channels, count = moved.shape
    hid = hidden[0].shape[1]
    inputs = moveds + hidden
    return call(
        functools.partial(down_kernel, steps),
        [jax.ShapeDtypeStruct(shape, jnp.bfloat16) for shape in quadrant_shapes(channels, hid, 0)],
        [moved, *inputs],
        "v" + "h" * len(inputs),
        "pp",
        scratch=[pltpu.VMEM((channels, steps * count), jnp.bfloat16), pltpu.VMEM((steps * count, hid), jnp.bfloat16)]
        + [pltpu.SemaphoreType.DMA((len(inputs),))],
        flops=2**29,
        moved=2**21,
        limit=16,
    )


def fill_margins(wide_ref, before, after, low, high, middle):
    rows_out, cols_out, _ = middle.shape
    around = slice(MARGIN - 1, MARGIN + cols_out + 1)
    wide_ref[:1, around] = low.astype(jnp.float32)
    wide_ref[1 + rows_out :, around] = high.astype(jnp.float32)
    wide_ref[1 : 1 + rows_out, MARGIN - 1 : MARGIN] = before.astype(jnp.float32)
    wide_ref[1 : 1 + rows_out, MARGIN + cols_out : MARGIN + cols_out + 1] = after.astype(jnp.float32)
    wide_ref[1 : 1 + rows_out, MARGIN : MARGIN + cols_out] = middle


def final_kernel(field_ref, before_ref, after_ref, low_ref, high_ref, kernel_ref, out_ref, wide_ref):
    rows_out, cols_out, _ = field_ref.shape
    result = field_ref[...].astype(jnp.float32)
    fill_margins(wide_ref, before_ref[0], after_ref[0], low_ref[0], high_ref[0], result)
    for col_tap in range(3):
        place = MARGIN + 1 - col_tap
        shifted_cols = wide_ref[:, place : place + cols_out]
        for row_tap in range(3):
            tap = kernel_ref[row_tap, col_tap : col_tap + 1]
            result = result + tap[None] * shifted_cols[2 - row_tap : 2 - row_tap + rows_out]
    out_ref[...] = result.astype(jnp.bfloat16)


def final_parts(field, around, kernel):
    rows_out, cols_out, channels = field.shape
    return call(
        final_kernel,
        [jax.ShapeDtypeStruct(field.shape, jnp.bfloat16)],
        [field, *around, kernel],
        "v" * 6,
        "v",
        scratch=[pltpu.VMEM((rows_out + 2, cols_out + 2 * MARGIN, channels), jnp.float32)],
        moved=2**19,
    )[0]


def spatial_kernel(mode, step, near_lon, near_lat, *refs):
    refs = list(refs)
    take = lambda: refs.pop(0)
    with_stencil = mode != "first"
    move_hbm = take()
    in_ref = take()
    kern_ref = take() if with_stencil else None
    weight_hbm = take() if mode == "mid" else None
    out_hbm = take()
    saved_hbm = take() if mode == "first" else None
    out_ref, sems = take(), take()
    spread_ref, weight_ref, move_ref = take(), take(), take()
    moving = copies(sems, 3, [(move_hbm, move_ref)])
    tiles_lon, tiles_lat, _, lanes = in_ref.shape
    rows = out_ref.shape[2]
    started = []
    if mode == "mid":
        arriving = copies(sems, 0, [(weight_hbm, weight_ref)])
    if mode == "first":
        weight_ref[...] = in_ref[:, :, rows:]
        started += copies(sems, 0, [(weight_ref, saved_hbm)])
    lane = lax.broadcasted_iota(jnp.int32, (rows, lanes), 1)
    col = lax.rem(lane, near_lat)
    lat_last, lat_first = col == near_lat - 1, col == 0
    lon_last, lon_first = lane >= lanes - near_lat, lane < near_lat
    tiles = [(a, b) for a in range(tiles_lon) for b in range(tiles_lat)]

    def turn(value, steps):
        return pltpu.roll(value, steps % lanes if isinstance(steps, int) else steps, 1)

    def lat_after(grid):
        turned = {key: turn(value, -1) for key, value in grid.items()}
        wrapped = {key: turn(grid[key], near_lat - 1) for key in tiles if key[1] > 0}
        return {(a, b): jnp.where(lat_last, wrapped.get((a, b + 1), 0.0), turned[a, b]) for a, b in tiles}

    def lat_before(grid):
        turned = {key: turn(value, 1) for key, value in grid.items()}
        wrapped = {key: turn(grid[key], 1 - near_lat) for key in tiles if key[1] < tiles_lat - 1}
        return {(a, b): jnp.where(lat_first, wrapped.get((a, b - 1), 0.0), turned[a, b]) for a, b in tiles}

    def lon_after(grid):
        return {
            (a, b): turn(jnp.where(lon_first, grid[(a + 1) % tiles_lon, b], grid[a, b]), -near_lat) for a, b in tiles
        }

    def lon_before(grid):
        return {(a, b): turn(jnp.where(lon_last, grid[(a - 1) % tiles_lon, b], grid[a, b]), near_lat) for a, b in tiles}

    grid = {(a, b): in_ref[a, b, :rows].astype(jnp.float32) for a, b in tiles}
    if with_stencil:
        taps = [
            [jnp.broadcast_to(kern_ref[:, 3 * a + b : 3 * a + b + 1], (rows, lanes)) for b in range(3)] for a in range(3)
        ]
        by_col = [lat_after(grid), grid, lat_before(grid)]
        mix = [
            {key: sum(taps[row][c] * by_col[c][key] for c in range(1, 3)) + taps[row][0] * by_col[0][key] for key in tiles}
            for row in range(3)
        ]
        high, low = lon_after(mix[0]), lon_before(mix[2])
        grid = {key: grid[key] + mix[1][key] + (high[key] + low[key]) for key in tiles}
    if mode == "mid":
        grid = {key: value.astype(jnp.bfloat16).astype(jnp.float32) for key, value in grid.items()}
        finish(arriving)
    weights = {}
    for a, b in tiles:
        four = weight_ref[a, b].astype(jnp.float32)[4 * step : 4 * step + 4]
        weights[a, b] = [jnp.broadcast_to(four[k : k + 1], (rows, lanes)) for k in range(4)]
    weighted = [{key: weights[key][k] * grid[key] for key in tiles} for k in range(4)]
    own, lon = lat_after(weighted[2]), lat_after(weighted[3])
    lon = lon_after({key: weighted[1][key] + lon[key] for key in tiles})
    for a, b in tiles:
        value = (weighted[0][a, b] + own[a, b] + lon[a, b]).astype(jnp.bfloat16).astype(jnp.float32)
        for place in range(a, tiles_lon + LON_REACH, tiles_lon):
            spread_ref[place, b] = value
    spread_ref[:, tiles_lat:] = jnp.zeros((tiles_lon + LON_REACH, LAT_REACH, rows, lanes), jnp.float32)

    finish(moving)
    lon_move, lat_move = move_ref[step, 0], move_ref[step, 1]
    far_lon, off_lon = lon_move // near_lon, lax.rem(lon_move, near_lon)
    far_lat, off_lat = lat_move // near_lat, lax.rem(lat_move, near_lat)
    shift = off_lon * near_lat + off_lat
    turn_here = lax.rem(2 * lanes - shift, lanes)
    turn_next = lax.rem(2 * lanes - shift + near_lat, lanes)
    same_lon = lane >= off_lon * near_lat
    same_lat = col + off_lat < near_lat
    half = tiles_lon // 2
    for a in range(tiles_lon):
        met = [
            jnp.where(same_lon, spread_ref[far_lon + a, far_lat + b], spread_ref[far_lon + a + 1, far_lat + b])
            for b in range(tiles_lat + 1)
        ]
        for b in range(tiles_lat):
            value = jnp.where(same_lat, turn(met[b], turn_here), turn(met[b + 1], turn_next))
            out_ref[a, b] = value.astype(jnp.bfloat16)
        if (a + 1) % half == 0:
            part = pl.ds(a + 1 - half, half)
            started += copies(sems, 1 + a // half, [(out_ref.at[part], out_hbm.at[part])])
    finish(started)


def spatial(mode, step, tile, rows, field, kern, weights, moves):
    tiles_lon, tiles_lat, _, lanes = field.shape
    with_stencil = mode != "first"
    operands = [moves, field]
    operands += [kern] if with_stencil else []
    operands += [weights] if mode == "mid" else []
    out_shape = (tiles_lon, tiles_lat, rows, lanes)
    weight_shape = (tiles_lon, tiles_lat, ROWS, lanes)
    sds = jax.ShapeDtypeStruct
    out = [sds(out_shape, jnp.bfloat16)] + ([sds(weight_shape, jnp.bfloat16)] if mode == "first" else [])
    scratch = [pltpu.VMEM(out_shape, jnp.bfloat16), pltpu.SemaphoreType.DMA((4,))]
    spread_shape = (tiles_lon + LON_REACH, tiles_lat + LAT_REACH, rows, lanes)
    scratch += [pltpu.VMEM(spread_shape, jnp.float32), pltpu.VMEM(weight_shape, jnp.bfloat16)]
    scratch += [pltpu.SMEM(moves.shape, jnp.int32)]
    return call(
        functools.partial(spatial_kernel, mode, step, *tile),
        out,
        operands,
        "hv" + "v" * with_stencil + "h" * (mode == "mid"),
        "h" * len(out),
        scratch=scratch,
        flops=2**22,
        moved=2**20,
        limit=max(8, 14 * tiles_lon * tiles_lat * rows * lanes * 4 // MIB),
    )


def halved(value, axis, bit, dim):
    count = lax.axis_size(axis)
    mine = lax.axis_index(axis) >> bit & 1
    kept = lax.dynamic_index_in_dim(value, mine, dim, keepdims=False)
    sent = lax.dynamic_index_in_dim(value, 1 - mine, dim, keepdims=False).astype(jnp.bfloat16)
    arrived = lax.ppermute(sent, axis, [(i, i ^ (1 << bit)) for i in range(count)])
    return kept + arrived.astype(jnp.float32)


def scattered(value, lat_first):
    channels, hid = value.shape
    lon_bits = lax.axis_size("lon").bit_length() - 1
    lat_bits = lax.axis_size("lat").bit_length() - 1
    rows = channels >> lon_bits
    value = value.reshape(*([2] * lon_bits), rows, *([2] * lat_bits), hid >> lat_bits)

    def over_lon(value, bit, left):
        return halved(value, "lon", bit, left.index(bit)), [k for k in left if k != bit]

    left_lon = list(range(lon_bits))[::-1]
    left_lat = list(range(lat_bits))[::-1]
    order = [("lon", 0), ("lon", 1)] + [("lat", k) for k in range(lat_bits)]
    if lat_first:
        order = [("lon", 0)] + [("lat", k) for k in range(lat_bits)] + [("lon", 1)]
    order += [("lon", k) for k in range(2, lon_bits)]
    for axis, bit in order:
        if axis == "lon":
            value, left_lon = over_lon(value, bit, left_lon)
        else:
            value = halved(value, "lat", bit, len(left_lon) + 1 + left_lat.index(bit))
            left_lat.remove(bit)
    return value


def add_parts(pairs, kept, arrived):
    for q, out_ref, place in pairs:
        value = kept(q).astype(jnp.float32) + arrived(q).astype(jnp.float32)
        out_ref[place] = value.astype(out_ref.dtype)


def first_axis(flip):
    core = lon_bit(0)
    return 1 - core if flip else core


def quadrant_kernel(flip, *refs):
    kept_ref, *total_refs, arrived_ref, send_ref, keep_ref = refs[: 4 + len(refs) // 6]
    axis, x, lat = first_axis(flip), lon_bit(1), lax.axis_index("lat")
    rows = kept_ref.shape[1]
    for j in range(2):
        kept = (1 - axis) * (2 * x + j) + axis * (2 * j + lat)
        sent = (1 - axis) * (2 * (1 - x) + j) + axis * (2 * j + 1 - lat)
        pairs = [(sent, send_ref, pl.ds(j * rows, rows)), (kept, keep_ref, j)]
        arrived = lambda q: arrived_ref[pl.ds(pl.multiple_of(q * rows, rows), rows)]
        add_parts(pairs, lambda q: kept_ref[q], arrived)
    if total_refs:
        chip = total_refs[0][...] + whole_of(arrived_ref[QUADRANTS * rows :])
        refs[-1][...] = chip
        send_ref[2 * rows :] = pieces_of(chip)


def half_kernel(flip, *refs):
    kept_ref, *total_refs, arrived_ref, send_ref, keep_ref = refs[: 4 + len(refs) // 6]
    axis, x, lat = first_axis(flip), lon_bit(1), lax.axis_index("lat")
    mine = (1 - axis) * lat + axis * x
    rows = kept_ref.shape[1]
    pairs = [(1 - mine, send_ref, pl.ds(0, rows)), (mine, keep_ref, slice(None))]
    arrived = lambda q: arrived_ref[pl.ds(pl.multiple_of(q * rows, rows), rows)]
    add_parts(pairs, lambda q: kept_ref[q], arrived)
    if total_refs:
        beside = arrived_ref[2 * rows :]
        refs[-1][...] = whole_of(beside)
        send_ref[rows : rows + SUM_ROWS] = pieces_of(total_refs[0][...])
        send_ref[rows + SUM_ROWS :] = beside


def rows_kernel(groups, bit_at, totals, *refs):
    kept_ref, *refs = refs
    total_refs, (arrived_ref, send_ref, keep_ref, *total_ref) = refs[:totals], refs[totals:]
    bit = lon_bit(bit_at)
    rows = kept_ref.shape[0]
    chunk = rows // (2 * groups)
    for p in range(groups):
        goal = pl.ds(p * chunk, chunk)
        places = [pl.multiple_of((2 * p + which) * chunk, chunk) for which in (1 - bit, bit)]
        pairs = [(places[0], send_ref, goal), (places[1], keep_ref, goal)]
        add_parts(pairs, lambda q: kept_ref[pl.ds(q, chunk)], lambda q: arrived_ref[pl.ds(q, chunk)])
    if totals:
        total = add_sums(total_refs, arrived_ref, rows)
        total_ref[0][...] = total
        send_ref[rows // 2 :] = pieces_of(total)


def add_sums(total_refs, arrived_ref, start):
    arrived = whole_of(arrived_ref[start : start + SUM_ROWS])
    if len(total_refs) == 1:
        return total_refs[0][...] + arrived
    chip, beside = (ref[...] for ref in total_refs)
    return (chip + whole_of(arrived_ref[start + SUM_ROWS :])) + (beside + arrived)


def finish_kernel(kept_ref, total_ref, arrived_ref, kept_down_ref, arrived_down_ref, up_hbm, down_hbm, taps_ref, gain_ref, *refs):
    up_ref, down_ref, sems = refs
    rows = kept_ref.shape[0]
    down_ref[...] = kept_down_ref[...] + arrived_down_ref[...].astype(jnp.float32)
    leaving = copies(sems, 0, [(down_ref, down_hbm)])
    up_ref[...] = kept_ref[...] + arrived_ref[:rows].astype(jnp.float32)
    leaving += copies(sems, 1, [(up_ref, up_hbm)])
    total = add_sums([total_ref], arrived_ref, rows)
    for k in range(9):
        taps_ref[k // 3, k % 3 : k % 3 + 1] = total[k : k + 1]
    gain_ref[...] = total[9:10]
    finish(leaving)


def halving(flip, send, keep, total):
    lon, lat = lax.axis_size("lon"), lax.axis_size("lat")
    places = [(i, j) for i in range(lon) for j in range(lat)]
    flat = lambda i, j: i * lat + j
    along_lat = lambda i: (i & 1) != flip
    sds = jax.ShapeDtypeStruct
    rows, width = keep.shape[1:]
    sums = [] if total is None else [total]
    with_sums = len(sums)
    plan = [
        (lambda i, j: (i ^ 1, j), functools.partial(quadrant_kernel, flip), (2, rows, width), 1),
        (
            lambda i, j: (i, j ^ 1) if along_lat(i) else (i ^ 2, j),
            functools.partial(half_kernel, flip),
            (rows, width),
            2,
        ),
        (
            lambda i, j: (i ^ 2, j) if along_lat(i) else (i, j ^ 1),
            functools.partial(rows_kernel, 2, 2, 2 * with_sums),
            (rows // 2, width),
            1,
        ),
        (lambda i, j: (i ^ 4, j), functools.partial(rows_kernel, 1, 3, with_sums), (rows // 4, width), 1),
    ]
    for at, (partner, kernel, shape, parts) in enumerate(plan):
        send = yield send
        arrived = lax.ppermute(send, AXES, [(flat(i, j), flat(*partner(i, j))) for i, j in places])
        arrived = yield arrived
        sent = shape[-2] * (shape[0] if len(shape) == 3 else 1) + SUM_ROWS * parts * with_sums
        out = [sds((sent, shape[-1]), jnp.bfloat16), sds(shape, jnp.float32)]
        out += [sds(value.shape, jnp.float32) for value in sums[:1]]
        operands = [keep, *sums, arrived]
        send, keep, *more = call(kernel, out, operands, "v" * len(operands), "p" * len(out), moved=2**19, limit=12)
        sums = sums + more if at == 1 else more
    send = yield send
    arrived = lax.ppermute(send, AXES, [(flat(i, j), flat(i ^ 8, j)) for i, j in places])
    yield (keep, *sums, arrived)


def all_sums(up, down, total, field, kernel):
    channels = total.shape[1]
    field = field[None]
    if up[1].ndim == 2:
        parts = [scattered(send.astype(jnp.float32), flip) for flip, (send, _) in enumerate((up, down))]
        total = lax.psum(total, AXES)
        around = lat_edges(field)
        state = final_parts(field[0], (*around, *lon_edges(field, *around)), kernel)
        return (state, *parts, total[:9].reshape(3, 3, channels), total[9])
    ahead, behind = halving(False, *up, total), halving(True, *down, None)
    send, later = next(ahead), next(behind)
    arrived = ahead.send(send)
    send = ahead.send(after(arrived, later))
    field = after(field, send)
    arrived_later = behind.send(after(later, send))
    later = behind.send(arrived_later)
    around = lat_edges(field, lambda value: after(value, later))
    state = final_parts(field[0], (*around, *lon_edges(field, *around)), kernel)
    for at in range(1, 4):
        arrived = ahead.send(send)
        arrived_later = behind.send(later)
        send = ahead.send(after(arrived, later))
        later = behind.send(after(arrived_later, send))
    final_ahead = ahead.send(send)
    final_behind = behind.send(later)
    sds = jax.ShapeDtypeStruct
    part = sds(final_ahead[0].shape, jnp.float32)
    out = [part, part, sds((3, 3, channels), jnp.float32), sds((1, channels), jnp.float32)]
    up, down, taps, gain = call(
        finish_kernel,
        out,
        [*final_ahead, *final_behind],
        "vvvvv",
        "hhvv",
        scratch=[pltpu.VMEM(part.shape, part.dtype)] * 2 + [pltpu.SemaphoreType.DMA((2,))],
        moved=2**18,
    )
    return state, up, down, taps, gain.reshape(channels)


def local(cotangent, states, w_up, w_down, norm_gain, kernel, bilinear, lon_move, lat_move):
    steps, rows_out, cols_out, channels = states.shape
    tiles_lon, tiles_lat = lax.axis_size("lon"), lax.axis_size("lat")
    devices = tiles_lon * tiles_lat
    count = rows_out * cols_out
    tile = (rows_out, cols_out)
    share = channels // devices
    padded_share = -(-share // ROWS) * ROWS
    whole_share = share == padded_share
    group_size = channels // lon_move.shape[1]
    me = lax.axis_index("lon") * tiles_lat + lax.axis_index("lat")

    def as_blocks(value):
        value = value.reshape(devices, share, count)
        return value if whole_share else jnp.pad(value, ((0, 0), (0, padded_share - share), (0, 0)))

    def as_rows(blocks):
        return blocks[:, :share].reshape(channels, count)

    def as_grid(blocks):
        return blocks.reshape(tiles_lon, tiles_lat, *blocks.shape[1:])

    blocks = packed(cotangent, bilinear, devices)
    blocks, states_later = lax.optimization_barrier((blocks, states))
    arrived = as_grid(exchanged(blocks))
    group = me * share // group_size
    moves = jnp.stack([lon_move[:, group], lat_move[:, group]], axis=1)
    grid_now, weights = spatial("first", steps - 1, tile, padded_share, arrived, None, None, moves)

    taps = lax.dynamic_slice_in_dim(kernel.reshape(9, channels), me * share, share, 1).T
    taps = jnp.pad(taps, ((0, padded_share - share), (0, count - 9)))

    around = lat_edges(states_later)
    grid_now, *around = lax.optimization_barrier((grid_now, *around))
    around = (*around, *lon_edges_ring(states, *around))
    order = list(reversed(range(steps)))
    gain = norm_gain.reshape(1, channels)
    now, *others = order
    forward = {s: forward_parts(s, states, around, kernel, gain, w_up) for s in others}
    names = {k: {s: forward[s][at] for s in others} for at, k in enumerate(FORWARD)}

    def taken_back(grid):
        return as_rows(exchanged(grid.reshape(devices, padded_share, count)))

    def spread_on(s, field, grid_kernel=taps):
        arrived = as_grid(exchanged(as_blocks(field)))
        return spatial("mid", s, tile, padded_share, arrived, grid_kernel, weights, moves)[0]

    fields, grads, moved = {}, {}, {}
    (near,) = fetched([w_down], grid_now)
    here = after(taken_back(grid_now), near)
    parts = first_step(now, here, near, states, around, kernel, gain, w_up)
    for k, value in zip(("n", "turned", "hid", "pad"), parts):
        names[k][now] = value
    fields[now], grads[now], moved[now] = parts[4:]
    for s in others:
        grid_now = spread_on(s, fields[s + 1])
        here = taken_back(grid_now)
        wanted = ("slope", "n", "inv") + ("pad",) * (s == others[-1])
        near = fetched([names[k][s] for k in wanted], grid_now)
        if s == others[-1]:
            break
        here = after(here, (near, forward))
        fields[s], grads[s], moved[s] = network_back(here, w_down, w_up, gain, *near)

    earlier = lambda values: [values[s] for s in order[:-1]]
    all_of = lambda values: [values[s] for s in order]
    sums = channel_sums(tile, w_up, gain, *map(earlier, (names["pad"], fields, grads, names["n"])))
    here = after(here, (near, sums))
    field, total, send, keep = last_step(tile, here, w_down, w_up, gain, sums, near, all_of(names["turned"]), earlier(grads))
    down = down_gradients(here, earlier(moved), all_of(names["hid"]))
    field = field.reshape(cotangent.shape)
    return all_sums((send, keep), down, total, field, kernel)


def solution(mesh):
    placed = (
        P("lon", "lat", None),
        P(None, "lon", "lat", None),
        P(),
        P(),
        P(),
        P(),
        P(None, None, "lon", "lat"),
        P(),
        P(),
    )
    return jax.shard_map(
        local,
        mesh=mesh,
        in_specs=placed,
        out_specs=(P("lon", "lat", None), P("lon", "lat"), P("lon", "lat"), P(), P()),
        check_vma=False,
    )
```

```python
import functools

import jax
import jax.numpy as jnp
from jax import lax
from jax.experimental import pallas as pl
from jax.experimental.pallas import tpu as pltpu
from jax.sharding import PartitionSpec as P

EPSILON = 1e-06
AXES = ("lon", "lat")
ROWS = 16
LAT_REACH = 2
LON_REACH = 8
MIB = 1024 * 1024


def exchanged(blocks):
    return lax.all_to_all(blocks, AXES, split_axis=0, concat_axis=0, tiled=True)


SPACES = {"s": pltpu.SMEM, "v": pltpu.VMEM, "p": pltpu.VMEM, "h": pltpu.HBM}
PINNED = {"p": pltpu.VMEM, "h": pltpu.HBM}


def call(kernel, out_shape, operands, ins, outs, scratch=(), flops=0, moved=0, limit=8):
    operands = [
        pltpu.with_memory_space_constraint(value, PINNED[kind]) if kind in PINNED else value
        for kind, value in zip(ins, operands, strict=True)
    ]
    out_shape = [
        PINNED[kind](value.shape, value.dtype) if kind in PINNED else value
        for kind, value in zip(outs, out_shape, strict=True)
    ]
    return pl.pallas_call(
        kernel,
        out_shape=out_shape,
        in_specs=[pl.BlockSpec(memory_space=SPACES[kind]) for kind in ins],
        out_specs=[pl.BlockSpec(memory_space=SPACES[kind]) for kind in outs],
        scratch_shapes=scratch,
        compiler_params=pltpu.CompilerParams(vmem_limit_bytes=limit * MIB),
        cost_estimate=pl.CostEstimate(flops=flops, bytes_accessed=moved, transcendentals=0),
    )(*operands)


def copies(sems, first, pairs):
    started = [pltpu.make_async_copy(src, dst, sems.at[first + k]) for k, (src, dst) in enumerate(pairs)]
    for copy in started:
        copy.start()
    return started


def finish(started):
    for copy in started:
        copy.wait()


PIECES = 3
SUMS = 10
SUM_ROWS = 32


def pieces_of(value):
    value = value[:SUMS]
    parts = []
    for _ in range(PIECES):
        parts.append(value.astype(jnp.bfloat16).astype(jnp.float32))
        value = value - parts[-1]
    parts.append(jnp.zeros((SUM_ROWS - PIECES * SUMS, value.shape[1]), jnp.float32))
    return jnp.concatenate(parts, axis=0).astype(jnp.bfloat16)


def whole_of(parts):
    parts = parts.astype(jnp.float32)
    total = (parts[:SUMS] + parts[SUMS : 2 * SUMS]) + parts[2 * SUMS : 3 * SUMS]
    return jnp.concatenate([total, jnp.zeros((ROWS - SUMS, parts.shape[1]), jnp.float32)], axis=0)


def after(value, first):
    return lax.optimization_barrier((value, first))[0]


def pack_kernel(cotangent_hbm, weight_hbm, out_hbm, cotangent_ref, weight_ref, out_ref, sems):
    started = copies(sems, 0, [(cotangent_hbm, cotangent_ref), (weight_hbm, weight_ref)])
    channels = cotangent_ref.shape[1]
    devices, _, count = out_ref.shape
    share = channels // devices
    started[1].wait()
    rows = weight_ref.shape[0]
    weights = jnp.concatenate([weight_ref[:, i] for i in range(weight_ref.shape[1])], axis=1)
    weights = jnp.concatenate([weights, jnp.zeros((ROWS - rows, count), jnp.float32)], axis=0)
    weights = weights.astype(jnp.bfloat16)
    out_ref[:, share:] = jnp.broadcast_to(weights[None], (devices, ROWS, count))
    started[0].wait()
    turned = cotangent_ref[...].astype(jnp.float32).T.astype(jnp.bfloat16)
    out_ref[:, :share] = turned.reshape(devices, share, count)
    finish(copies(sems, 2, [(out_ref, out_hbm)]))


def packed(cotangent, bilinear, devices):
    rows_out, cols_out, channels = cotangent.shape
    steps, corners = bilinear.shape[:2]
    count = rows_out * cols_out
    share = channels // devices
    if share % ROWS:
        blocks = cotangent.reshape(count, channels).T.reshape(devices, share, count)
        blocks = jnp.pad(blocks, ((0, 0), (0, -share % ROWS), (0, 0)))
        weights = bilinear.reshape(steps * corners, count).astype(jnp.bfloat16)
        weights = jnp.pad(weights, ((0, ROWS - steps * corners), (0, 0)))
        return jnp.concatenate([blocks, jnp.broadcast_to(weights[None], (devices, ROWS, count))], axis=1)
    shape = (devices, share + ROWS, count)
    return call(
        pack_kernel,
        [jax.ShapeDtypeStruct(shape, jnp.bfloat16)],
        [cotangent.reshape(count, channels), bilinear.reshape(steps * corners, rows_out, cols_out)],
        "hh",
        "h",
        scratch=[
            pltpu.VMEM((count, channels), jnp.bfloat16),
            pltpu.VMEM((steps * corners, rows_out, cols_out), jnp.float32),
            pltpu.VMEM(shape, jnp.bfloat16),
            pltpu.SemaphoreType.DMA((3,)),
        ],
        moved=2**19,
    )[0]


def lat_edges(states, held=lambda value: value):
    lat, lat_at = lax.axis_size("lat"), lax.axis_index("lat")
    first, last = states[:, :, :1], states[:, :, -1:]
    if lat == 2:
        arrived = lax.ppermute(jnp.where(lat_at == 0, last, first), "lat", [(0, 1), (1, 0)])
        arrived = held(arrived)
        return jnp.where(lat_at == 0, 0, arrived), jnp.where(lat_at == 0, arrived, 0)
    return (
        lax.ppermute(last, "lat", [(i, i + 1) for i in range(lat - 1)]),
        lax.ppermute(first, "lat", [(i + 1, i) for i in range(lat - 1)]),
    )


def lon_edges(states, before, after):
    lon = lax.axis_size("lon")
    even = lax.axis_index("lon") % 2 == 0
    row = lambda place: jnp.concatenate([part[:, place] for part in (before, states, after)], axis=2)
    first, last = row(slice(0, 1)), row(slice(-1, None))
    with_next = lax.ppermute(jnp.where(even, last, first), "lon", [(i, i ^ 1) for i in range(lon)])
    pairs = [(i, (i - 1) % lon if i % 2 == 0 else (i + 1) % lon) for i in range(lon)]
    with_last = lax.ppermute(jnp.where(even, first, last), "lon", pairs)
    return jnp.where(even, with_last, with_next), jnp.where(even, with_next, with_last)


def lon_edges_ring(states, before, after):
    lon = lax.axis_size("lon")
    ahead = lambda value: lax.ppermute(value, "lon", [(i, (i + 1) % lon) for i in range(lon)])
    behind = lambda value: lax.ppermute(value, "lon", [(i, (i - 1) % lon) for i in range(lon)])
    row = lambda place: jnp.concatenate([part[:, place] for part in (before, states, after)], axis=2)
    return ahead(row(slice(-1, None))), behind(row(slice(0, 1)))


MARGIN = 8


def forward_math(step, places, sems, leaving, outs):
    states_ref, before_ref, after_ref, low_ref, high_ref, kernel_ref, gain_ref, up_ref = places
    n_ref, turned_ref, inv_ref, hid_ref, slope_ref, pad_ref, wide_ref = outs
    rows_out, cols_out, channels = states_ref.shape[1:]
    count = rows_out * cols_out
    mixed = states_ref[step].astype(jnp.float32)
    fill_margins(wide_ref, before_ref[step], after_ref[step], low_ref[step], high_ref[step], mixed)
    pad_ref[...] = wide_ref[...].astype(jnp.bfloat16)
    leaving("pad")
    for col_tap in range(3):
        place = MARGIN - 1 + col_tap
        shifted_cols = wide_ref[:, place : place + cols_out]
        for row_tap in range(3):
            tap = kernel_ref[row_tap, col_tap : col_tap + 1]
            mixed = mixed + tap[None] * shifted_cols[row_tap : row_tap + rows_out]
    mixed = mixed.reshape(count, channels)
    inv_root = lax.rsqrt(jnp.mean(mixed * mixed, axis=1, keepdims=True) + EPSILON)
    narrow = mixed * inv_root * gain_ref[...]
    n_ref[...] = narrow.astype(jnp.bfloat16)
    inv_ref[...] = jnp.broadcast_to(inv_root, inv_ref.shape)
    leaving("n", "inv")
    pre = jnp.dot(n_ref[...], up_ref[...], preferred_element_type=jnp.float32)
    sigmoid = jax.nn.sigmoid(pre)
    slope_ref[...] = (sigmoid * (1.0 + pre * (1.0 - sigmoid))).astype(jnp.bfloat16)
    leaving("slope")
    hid_ref[...] = (pre * sigmoid).astype(jnp.bfloat16)
    turned_ref[...] = narrow.T.astype(jnp.bfloat16)
    leaving("hid", "turned")


FORWARD = ("n", "turned", "inv", "hid", "slope", "pad")


def sender(sems, refs, goals, started):
    names = list(goals)

    def leave(*which):
        for name in which:
            if name in goals:
                started.extend(copies(sems, names.index(name), [(refs[name], goals[name])]))

    return leave


def forward_kernel(step, *refs):
    places, goals, outs, sems = refs[:8], refs[8:14], refs[14:21], refs[21]
    started = []
    leave = sender(sems, dict(zip(FORWARD, outs)), dict(zip(FORWARD, goals)), started)
    forward_math(step, places, sems, leave, outs)
    finish(started)


def forward_shapes(states, w_up):
    _, rows_out, cols_out, channels = states.shape
    hid = w_up.shape[1]
    count = rows_out * cols_out
    wide = (rows_out + 2, cols_out + 2 * MARGIN, channels)
    return [
        ((count, channels), jnp.bfloat16),
        ((channels, count), jnp.bfloat16),
        ((count, 128), jnp.float32),
        ((count, hid), jnp.bfloat16),
        ((count, hid), jnp.bfloat16),
        (wide, jnp.bfloat16),
    ]


def forward_scratch(shapes):
    scratch = [pltpu.VMEM(*shape) for shape in shapes]
    return scratch + [pltpu.VMEM(shapes[-1][0], jnp.float32)]


def forward_parts(step, states, around, kernel, norm_gain, w_up):
    shapes = forward_shapes(states, w_up)
    return call(
        functools.partial(forward_kernel, step),
        [jax.ShapeDtypeStruct(*shape) for shape in shapes],
        [states, *around, kernel, norm_gain, w_up],
        "vvvvvvvv",
        "hhhhhh",
        scratch=forward_scratch(shapes) + [pltpu.SemaphoreType.DMA((6,))],
        flops=2**27,
        moved=2**22,
        limit=12,
    )


LANES_BOTH = (((1,), (1,)), ((), ()))


def fetch_kernel(*refs):
    count = len(refs) // 2
    *pairs, sems = refs
    finish(copies(sems, 0, list(zip(pairs[:count], pairs[count:]))))


def fetched(values, first):
    values = after(values, first)
    return call(
        fetch_kernel,
        [jax.ShapeDtypeStruct(value.shape, value.dtype) for value in values],
        values,
        "h" * len(values),
        "v" * len(values),
        scratch=[pltpu.SemaphoreType.DMA((len(values),))],
        moved=2**19,
    )


def network_math(moved_ref, down_ref, up_ref, gain_ref, slope_ref, n_ref, inv_ref, out_ref, grad_ref, leave):
    leave("moved")
    moved = moved_ref[...].astype(jnp.float32).T
    grad_hidden = jnp.dot(moved.astype(jnp.bfloat16), down_ref[...], preferred_element_type=jnp.float32)
    grad_pre = (grad_hidden * slope_ref[...].astype(jnp.float32)).astype(jnp.bfloat16)
    grad_ref[...] = grad_pre
    leave("grad")
    grad_n = lax.dot_general(grad_pre, up_ref[...], LANES_BOTH, preferred_element_type=jnp.float32)
    narrow, gain = n_ref[...].astype(jnp.float32), gain_ref[...]
    mean = jnp.mean(grad_n * narrow, axis=1, keepdims=True)
    field = moved + inv_ref[:, :1] * (grad_n * gain - narrow * (mean / gain))
    out_ref[...] = field.T.astype(jnp.bfloat16)
    leave("field")


def network_kernel(moved_ref, down_ref, up_ref, gain_ref, slope_ref, n_ref, inv_ref, *refs):
    *goals, out_ref, grad_ref, sems = refs
    started = []
    names = ("field", "grad", "moved")
    leave = sender(sems, dict(zip(names, (out_ref, grad_ref, moved_ref))), dict(zip(names, goals)), started)
    network_math(moved_ref, down_ref, up_ref, gain_ref, slope_ref, n_ref, inv_ref, out_ref, grad_ref, leave)
    finish(started)


def first_kernel(step, *refs):
    (moved_ref, down_ref), places, refs = refs[:2], refs[2:10], refs[10:]
    goals, outs, (out_ref, grad_ref, sems) = refs[:7], refs[7:14], refs[14:]
    started = []
    names = ("n", "turned", "hid", "pad", "field", "grad", "moved")
    values = dict(zip(FORWARD, outs)) | {"field": out_ref, "grad": grad_ref, "moved": moved_ref}
    leave = sender(sems, values, dict(zip(names, goals)), started)
    forward_math(step, places, sems, leave, outs)
    n_ref, _, inv_ref, _, slope_ref = outs[:5]
    gain_ref, up_ref = places[6:]
    network_math(moved_ref, down_ref, up_ref, gain_ref, slope_ref, n_ref, inv_ref, out_ref, grad_ref, leave)
    finish(started)


def first_step(step, moved, w_down, states, around, kernel, norm_gain, w_up):
    shapes = forward_shapes(states, w_up)
    channels, count = moved.shape
    hid = w_down.shape[1]
    backs = [((channels, count), jnp.bfloat16), ((count, hid), jnp.bfloat16), ((channels, count), jnp.bfloat16)]
    results = [shapes[k] for k in (0, 1, 3, 5)] + backs
    return call(
        functools.partial(first_kernel, step),
        [jax.ShapeDtypeStruct(*shape) for shape in results],
        [moved, w_down, states, *around, kernel, norm_gain, w_up],
        "v" * 10,
        "h" * 7,
        scratch=forward_scratch(shapes) + [pltpu.VMEM(*shape) for shape in backs[:2]] + [pltpu.SemaphoreType.DMA((7,))],
        flops=2**28,
        moved=2**22,
        limit=16,
    )


def network_back(moved, w_down, w_up, norm_gain, slope, narrow, inv_root):
    channels, count = moved.shape
    hid = w_down.shape[1]
    shapes = [((channels, count), jnp.bfloat16), ((count, hid), jnp.bfloat16), ((channels, count), jnp.bfloat16)]
    return call(
        network_kernel,
        [jax.ShapeDtypeStruct(*shape) for shape in shapes],
        [moved, w_down, w_up, norm_gain, slope, narrow, inv_root],
        "vvvvvvv",
        "hhh",
        scratch=[pltpu.VMEM(*shape) for shape in shapes[:2]] + [pltpu.SemaphoreType.DMA((3,))],
        flops=4 * count * hid * channels,
        moved=4 * 2**20,
        limit=8,
    )


def stencil_sums(pad_ref, field, tile):
    rows_out, cols_out = tile
    field = field.reshape(rows_out, cols_out, -1)
    padded = pad_ref[...].astype(jnp.float32)
    result = [None] * 9
    for col_tap in range(3):
        place = MARGIN - 1 + col_tap
        shifted_cols = padded[:, place : place + cols_out]
        for row_tap in range(3):
            products = jnp.sum(shifted_cols[row_tap : row_tap + rows_out] * field, axis=0)
            result[3 * row_tap + col_tap] = jnp.sum(products, axis=0, keepdims=True)
    return result


def sums_rows(rows, term, gain):
    rows = rows + [jnp.sum(term, axis=0, keepdims=True) / gain, jnp.zeros((ROWS - 10, term.shape[1]), jnp.float32)]
    return jnp.concatenate(rows, axis=0)


def sums_kernel(steps, tile, up_ref, gain_ref, *refs):
    inputs, (out_ref, *refs) = refs[: 4 * steps], refs[4 * steps :]
    pads, fields, grads, narrows, sems = refs
    places = [(ref, place.at[k]) for k in range(steps) for ref, place in zip(inputs[4 * k : 4 * k + 4], refs[:4])]
    arriving = copies(sems, 0, places)
    rows, term = None, None
    for k in range(steps):
        finish(arriving[4 * k : 4 * k + 4])
        grad_n = lax.dot_general(grads[k], up_ref[...], LANES_BOTH, preferred_element_type=jnp.float32)
        product = grad_n * narrows[k].astype(jnp.float32)
        term = product if term is None else term + product
        more = stencil_sums(pads.at[k], fields[k].astype(jnp.float32).T, tile)
        rows = more if rows is None else [a + b for a, b in zip(rows, more)]
    out_ref[...] = sums_rows(rows, term, gain_ref[...])


def channel_sums(tile, w_up, norm_gain, pads, fields, grads, narrows):
    steps = len(fields)
    inputs = [value for group in zip(pads, fields, grads, narrows) for value in group]
    return call(
        functools.partial(sums_kernel, steps, tile),
        [jax.ShapeDtypeStruct((ROWS, fields[0].shape[0]), jnp.float32)],
        [w_up, norm_gain, *inputs],
        "vv" + "h" * 4 * steps,
        "v",
        scratch=[pltpu.VMEM((steps, *value.shape), value.dtype) for value in inputs[:4]]
        + [pltpu.SemaphoreType.DMA((4 * steps,))],
        moved=2**21,
        limit=12,
    )[0]


QUADRANTS = 4


def lon_bit(at):
    return lax.axis_index("lon") >> at & 1


def gradient_quadrants(left_ref, right_ref, send_ref, keep_ref):
    channels, width = left_ref.shape[0], right_ref.shape[1] // 2
    if keep_ref.ndim == 2:
        send_ref[:channels] = jnp.dot(left_ref[...], right_ref[...], preferred_element_type=jnp.float32).astype(jnp.bfloat16)
        keep_ref[...] = jnp.zeros_like(keep_ref)
        return
    size = channels // QUADRANTS
    groups = lax.axis_size("lon") // 4
    chunk = size // groups
    rows = []
    for core in (1 - lon_bit(0), lon_bit(0)):
        for x in range(2):
            for z in range(groups):
                start = pl.multiple_of((4 * z + 2 * x + core) * chunk, chunk)
                rows.append(left_ref[pl.ds(start, chunk)])
    rows = jnp.concatenate(rows, axis=0)
    value = jnp.dot(rows, right_ref[...], preferred_element_type=jnp.float32).astype(jnp.bfloat16)
    for q in range(QUADRANTS):
        x, lat = q // 2, q % 2
        columns = slice(lat * width, (lat + 1) * width)
        send_ref[q * size : (q + 1) * size] = value[x * size : (x + 1) * size, columns]
        keep_ref[q] = value[(2 + x) * size : (3 + x) * size, columns]


def quadrant_shapes(channels, hid, sums):
    if lax.axis_size("lat") != 2 or lax.axis_size("lon") != 16:
        return (channels, hid), (8, 128)
    return (channels + SUM_ROWS * sums, hid // 2), (QUADRANTS, channels // QUADRANTS, hid // 2)


def side_by_side(refs, goal_ref, axis):
    size = refs[0].shape[axis]
    places = [pl.ds(s * size, size) for s in range(len(refs))]
    return [(ref, goal_ref.at[:, place] if axis else goal_ref.at[place]) for ref, place in zip(refs, places)]


def last_kernel(steps, tile, moved_ref, down_ref, up_ref, gain_ref, sums_ref, *refs):
    slope_ref, n_ref, inv_ref, pad_ref, *refs = refs
    inputs, refs = refs[: 2 * steps - 1], refs[2 * steps - 1 :]
    field_ref, total_ref, send_ref, keep_ref, left_ref, right_ref, sems = refs
    count = slope_ref.shape[0]
    pairs = side_by_side(inputs[:steps], left_ref, 1) + side_by_side(inputs[steps:], right_ref, 0)
    later = copies(sems, 0, pairs)
    moved = moved_ref[...].astype(jnp.float32).T
    grad_hidden = jnp.dot(moved.astype(jnp.bfloat16), down_ref[...], preferred_element_type=jnp.float32)
    grad_pre = (grad_hidden * slope_ref[...].astype(jnp.float32)).astype(jnp.bfloat16)
    right_ref[(steps - 1) * count :] = grad_pre
    grad_n = lax.dot_general(grad_pre, up_ref[...], LANES_BOTH, preferred_element_type=jnp.float32)
    narrow, gain = n_ref[...].astype(jnp.float32), gain_ref[...]
    term = grad_n * narrow
    mean = jnp.mean(term, axis=1, keepdims=True)
    field = moved + inv_ref[:, :1] * (grad_n * gain - narrow * (mean / gain))
    field = field.astype(jnp.bfloat16)
    field_ref[...] = field
    total = sums_ref[...] + sums_rows(stencil_sums(pad_ref, field.astype(jnp.float32), tile), term, gain)
    total_ref[...] = total
    finish(later)
    gradient_quadrants(left_ref, right_ref, send_ref, keep_ref)
    if keep_ref.ndim > 2:
        send_ref[left_ref.shape[0] :] = pieces_of(total)


def last_step(tile, moved, w_down, w_up, norm_gain, sums, near, turned, grads):
    steps = len(turned)
    channels, count = moved.shape
    hid = w_down.shape[1]
    send, keep = quadrant_shapes(channels, hid, 1)
    sds = jax.ShapeDtypeStruct
    inputs = turned + grads
    return call(
        functools.partial(last_kernel, steps, tile),
        [
            sds((count, channels), jnp.bfloat16),
            sds((ROWS, channels), jnp.float32),
            sds(send, jnp.bfloat16),
            sds(keep, jnp.bfloat16),
        ],
        [moved, w_down, w_up, norm_gain, sums, *near, *inputs],
        "v" * 9 + "h" * len(inputs),
        "vppp",
        scratch=[pltpu.VMEM((channels, steps * count), jnp.bfloat16), pltpu.VMEM((steps * count, hid), jnp.bfloat16)]
        + [pltpu.SemaphoreType.DMA((len(inputs),))],
        flops=2**30,
        moved=6 * 2**20,
        limit=20,
    )


def down_kernel(steps, moved_ref, *refs):
    inputs, (send_ref, keep_ref, left_ref, right_ref, sems) = refs[: 2 * steps - 1], refs[2 * steps - 1 :]
    count = moved_ref.shape[1]
    pairs = side_by_side(inputs[: steps - 1], left_ref, 1) + side_by_side(inputs[steps - 1 :], right_ref, 0)
    arriving = copies(sems, 0, pairs)
    left_ref[:, (steps - 1) * count :] = moved_ref[...]
    finish(arriving)
    gradient_quadrants(left_ref, right_ref, send_ref, keep_ref)


def down_gradients(moved, moveds, hidden):
    steps = len(hidden)
    channels, count = moved.shape
    hid = hidden[0].shape[1]
    inputs = moveds + hidden
    return call(
        functools.partial(down_kernel, steps),
        [jax.ShapeDtypeStruct(shape, jnp.bfloat16) for shape in quadrant_shapes(channels, hid, 0)],
        [moved, *inputs],
        "v" + "h" * len(inputs),
        "pp",
        scratch=[pltpu.VMEM((channels, steps * count), jnp.bfloat16), pltpu.VMEM((steps * count, hid), jnp.bfloat16)]
        + [pltpu.SemaphoreType.DMA((len(inputs),))],
        flops=2**29,
        moved=2**21,
        limit=16,
    )


def fill_margins(wide_ref, before, after, low, high, middle):
    rows_out, cols_out, _ = middle.shape
    around = slice(MARGIN - 1, MARGIN + cols_out + 1)
    wide_ref[:1, around] = low.astype(jnp.float32)
    wide_ref[1 + rows_out :, around] = high.astype(jnp.float32)
    wide_ref[1 : 1 + rows_out, MARGIN - 1 : MARGIN] = before.astype(jnp.float32)
    wide_ref[1 : 1 + rows_out, MARGIN + cols_out : MARGIN + cols_out + 1] = after.astype(jnp.float32)
    wide_ref[1 : 1 + rows_out, MARGIN : MARGIN + cols_out] = middle


def final_kernel(field_ref, before_ref, after_ref, low_ref, high_ref, kernel_ref, out_ref, wide_ref):
    rows_out, cols_out, _ = field_ref.shape
    result = field_ref[...].astype(jnp.float32)
    fill_margins(wide_ref, before_ref[0], after_ref[0], low_ref[0], high_ref[0], result)
    for col_tap in range(3):
        place = MARGIN + 1 - col_tap
        shifted_cols = wide_ref[:, place : place + cols_out]
        for row_tap in range(3):
            tap = kernel_ref[row_tap, col_tap : col_tap + 1]
            result = result + tap[None] * shifted_cols[2 - row_tap : 2 - row_tap + rows_out]
    out_ref[...] = result.astype(jnp.bfloat16)


def final_parts(field, around, kernel):
    rows_out, cols_out, channels = field.shape
    return call(
        final_kernel,
        [jax.ShapeDtypeStruct(field.shape, jnp.bfloat16)],
        [field, *around, kernel],
        "v" * 6,
        "v",
        scratch=[pltpu.VMEM((rows_out + 2, cols_out + 2 * MARGIN, channels), jnp.float32)],
        moved=2**19,
    )[0]


def spatial_kernel(mode, step, near_lon, near_lat, *refs):
    refs = list(refs)
    take = lambda: refs.pop(0)
    with_stencil = mode != "first"
    move_ref = take()
    in_ref = take()
    kern_ref = take() if with_stencil else None
    weight_ref = take() if mode == "mid" else None
    out_hbm = take()
    saved_hbm = take() if mode == "first" else None
    out_ref, sems = take(), take()
    spread_ref = take()
    weight_ref = take() if mode == "first" else weight_ref
    tiles_lon, tiles_lat, _, lanes = in_ref.shape
    rows = out_ref.shape[2]
    started = []
    if mode == "first":
        weight_ref[...] = in_ref[:, :, rows:]
        started += copies(sems, 0, [(weight_ref, saved_hbm)])
    lane = lax.broadcasted_iota(jnp.int32, (rows, lanes), 1)
    col = lax.rem(lane, near_lat)
    lat_last, lat_first = col == near_lat - 1, col == 0
    lon_last, lon_first = lane >= lanes - near_lat, lane < near_lat
    tiles = [(a, b) for a in range(tiles_lon) for b in range(tiles_lat)]

    def turn(value, steps):
        return pltpu.roll(value, steps % lanes if isinstance(steps, int) else steps, 1)

    def lat_after(grid):
        turned = {key: turn(value, -1) for key, value in grid.items()}
        wrapped = {key: turn(grid[key], near_lat - 1) for key in tiles if key[1] > 0}
        return {(a, b): jnp.where(lat_last, wrapped.get((a, b + 1), 0.0), turned[a, b]) for a, b in tiles}

    def lat_before(grid):
        turned = {key: turn(value, 1) for key, value in grid.items()}
        wrapped = {key: turn(grid[key], 1 - near_lat) for key in tiles if key[1] < tiles_lat - 1}
        return {(a, b): jnp.where(lat_first, wrapped.get((a, b - 1), 0.0), turned[a, b]) for a, b in tiles}

    def lon_after(grid):
        return {
            (a, b): turn(jnp.where(lon_first, grid[(a + 1) % tiles_lon, b], grid[a, b]), -near_lat) for a, b in tiles
        }

    def lon_before(grid):
        return {(a, b): turn(jnp.where(lon_last, grid[(a - 1) % tiles_lon, b], grid[a, b]), near_lat) for a, b in tiles}

    grid = {(a, b): in_ref[a, b, :rows].astype(jnp.float32) for a, b in tiles}
    if with_stencil:
        taps = [
            [jnp.broadcast_to(kern_ref[:, 3 * a + b : 3 * a + b + 1], (rows, lanes)) for b in range(3)] for a in range(3)
        ]
        by_col = [lat_after(grid), grid, lat_before(grid)]
        mix = [
            {key: sum(taps[row][c] * by_col[c][key] for c in range(1, 3)) + taps[row][0] * by_col[0][key] for key in tiles}
            for row in range(3)
        ]
        high, low = lon_after(mix[0]), lon_before(mix[2])
        grid = {key: grid[key] + mix[1][key] + (high[key] + low[key]) for key in tiles}
    if mode == "mid":
        grid = {key: value.astype(jnp.bfloat16).astype(jnp.float32) for key, value in grid.items()}
    weights = {}
    for a, b in tiles:
        four = weight_ref[a, b].astype(jnp.float32)[4 * step : 4 * step + 4]
        weights[a, b] = [jnp.broadcast_to(four[k : k + 1], (rows, lanes)) for k in range(4)]
    weighted = [{key: weights[key][k] * grid[key] for key in tiles} for k in range(4)]
    own, lon = lat_after(weighted[2]), lat_after(weighted[3])
    lon = lon_after({key: weighted[1][key] + lon[key] for key in tiles})
    for a, b in tiles:
        value = (weighted[0][a, b] + own[a, b] + lon[a, b]).astype(jnp.bfloat16).astype(jnp.float32)
        for place in range(a, tiles_lon + LON_REACH, tiles_lon):
            spread_ref[place, b] = value
    spread_ref[:, tiles_lat:] = jnp.zeros((tiles_lon + LON_REACH, LAT_REACH, rows, lanes), jnp.float32)

    lon_move, lat_move = (jnp.max(move_ref[2 * step + k : 2 * step + k + 1]) for k in range(2))
    far_lon, off_lon = lon_move // near_lon, lax.rem(lon_move, near_lon)
    far_lat, off_lat = lat_move // near_lat, lax.rem(lat_move, near_lat)
    shift = off_lon * near_lat + off_lat
    turn_here = lax.rem(2 * lanes - shift, lanes)
    turn_next = lax.rem(2 * lanes - shift + near_lat, lanes)
    same_lon = lane >= off_lon * near_lat
    same_lat = col + off_lat < near_lat
    half = tiles_lon // 2
    for a in range(tiles_lon):
        met = [
            jnp.where(same_lon, spread_ref[far_lon + a, far_lat + b], spread_ref[far_lon + a + 1, far_lat + b])
            for b in range(tiles_lat + 1)
        ]
        for b in range(tiles_lat):
            value = jnp.where(same_lat, turn(met[b], turn_here), turn(met[b + 1], turn_next))
            out_ref[a, b] = value.astype(jnp.bfloat16)
        if (a + 1) % half == 0:
            part = pl.ds(a + 1 - half, half)
            started += copies(sems, 1 + a // half, [(out_ref.at[part], out_hbm.at[part])])
    finish(started)


def spatial(mode, step, tile, rows, field, kern, weights, moves):
    tiles_lon, tiles_lat, _, lanes = field.shape
    with_stencil = mode != "first"
    operands = [moves, field]
    operands += [kern] if with_stencil else []
    operands += [weights] if mode == "mid" else []
    out_shape = (tiles_lon, tiles_lat, rows, lanes)
    weight_shape = (tiles_lon, tiles_lat, ROWS, lanes)
    sds = jax.ShapeDtypeStruct
    out = [sds(out_shape, jnp.bfloat16)] + ([sds(weight_shape, jnp.bfloat16)] if mode == "first" else [])
    scratch = [pltpu.VMEM(out_shape, jnp.bfloat16), pltpu.SemaphoreType.DMA((4,))]
    spread_shape = (tiles_lon + LON_REACH, tiles_lat + LAT_REACH, rows, lanes)
    scratch += [pltpu.VMEM(spread_shape, jnp.float32)]
    scratch += [pltpu.VMEM(weight_shape, jnp.bfloat16)] * (mode == "first")
    return call(
        functools.partial(spatial_kernel, mode, step, *tile),
        out,
        operands,
        "vv" + "v" * with_stencil + "v" * (mode == "mid"),
        "h" * len(out),
        scratch=scratch,
        flops=2**22,
        moved=2**20,
        limit=max(8, 14 * tiles_lon * tiles_lat * rows * lanes * 4 // MIB),
    )


def halved(value, axis, bit, dim):
    count = lax.axis_size(axis)
    mine = lax.axis_index(axis) >> bit & 1
    kept = lax.dynamic_index_in_dim(value, mine, dim, keepdims=False)
    sent = lax.dynamic_index_in_dim(value, 1 - mine, dim, keepdims=False).astype(jnp.bfloat16)
    arrived = lax.ppermute(sent, axis, [(i, i ^ (1 << bit)) for i in range(count)])
    return kept + arrived.astype(jnp.float32)


def scattered(value, lat_first):
    channels, hid = value.shape
    lon_bits = lax.axis_size("lon").bit_length() - 1
    lat_bits = lax.axis_size("lat").bit_length() - 1
    rows = channels >> lon_bits
    value = value.reshape(*([2] * lon_bits), rows, *([2] * lat_bits), hid >> lat_bits)

    def over_lon(value, bit, left):
        return halved(value, "lon", bit, left.index(bit)), [k for k in left if k != bit]

    left_lon = list(range(lon_bits))[::-1]
    left_lat = list(range(lat_bits))[::-1]
    order = [("lon", 0), ("lon", 1)] + [("lat", k) for k in range(lat_bits)]
    if lat_first:
        order = [("lon", 0)] + [("lat", k) for k in range(lat_bits)] + [("lon", 1)]
    order += [("lon", k) for k in range(2, lon_bits)]
    for axis, bit in order:
        if axis == "lon":
            value, left_lon = over_lon(value, bit, left_lon)
        else:
            value = halved(value, "lat", bit, len(left_lon) + 1 + left_lat.index(bit))
            left_lat.remove(bit)
    return value


def add_parts(pairs, kept, arrived):
    for q, out_ref, place in pairs:
        value = kept(q).astype(jnp.float32) + arrived(q).astype(jnp.float32)
        out_ref[place] = value.astype(out_ref.dtype)


def first_axis(flip):
    core = lon_bit(0)
    return 1 - core if flip else core


def quadrant_kernel(flip, *refs):
    kept_ref, *total_refs, arrived_ref, send_ref, keep_ref = refs[: 4 + len(refs) // 6]
    axis, x, lat = first_axis(flip), lon_bit(1), lax.axis_index("lat")
    rows = kept_ref.shape[1]
    for j in range(2):
        kept = (1 - axis) * (2 * x + j) + axis * (2 * j + lat)
        sent = (1 - axis) * (2 * (1 - x) + j) + axis * (2 * j + 1 - lat)
        pairs = [(sent, send_ref, pl.ds(j * rows, rows)), (kept, keep_ref, j)]
        arrived = lambda q: arrived_ref[pl.ds(pl.multiple_of(q * rows, rows), rows)]
        add_parts(pairs, lambda q: kept_ref[q], arrived)
    if total_refs:
        chip = total_refs[0][...] + whole_of(arrived_ref[QUADRANTS * rows :])
        refs[-1][...] = chip
        send_ref[2 * rows :] = pieces_of(chip)


def half_kernel(flip, *refs):
    kept_ref, *total_refs, arrived_ref, send_ref, keep_ref = refs[: 4 + len(refs) // 6]
    axis, x, lat = first_axis(flip), lon_bit(1), lax.axis_index("lat")
    mine = (1 - axis) * lat + axis * x
    rows = kept_ref.shape[1]
    pairs = [(1 - mine, send_ref, pl.ds(0, rows)), (mine, keep_ref, slice(None))]
    arrived = lambda q: arrived_ref[pl.ds(pl.multiple_of(q * rows, rows), rows)]
    add_parts(pairs, lambda q: kept_ref[q], arrived)
    if total_refs:
        beside = arrived_ref[2 * rows :]
        refs[-1][...] = whole_of(beside)
        send_ref[rows : rows + SUM_ROWS] = pieces_of(total_refs[0][...])
        send_ref[rows + SUM_ROWS :] = beside


def rows_kernel(groups, bit_at, totals, *refs):
    kept_ref, *refs = refs
    total_refs, (arrived_ref, send_ref, keep_ref, *total_ref) = refs[:totals], refs[totals:]
    bit = lon_bit(bit_at)
    rows = kept_ref.shape[0]
    chunk = rows // (2 * groups)
    for p in range(groups):
        goal = pl.ds(p * chunk, chunk)
        places = [pl.multiple_of((2 * p + which) * chunk, chunk) for which in (1 - bit, bit)]
        pairs = [(places[0], send_ref, goal), (places[1], keep_ref, goal)]
        add_parts(pairs, lambda q: kept_ref[pl.ds(q, chunk)], lambda q: arrived_ref[pl.ds(q, chunk)])
    if totals:
        total = add_sums(total_refs, arrived_ref, rows)
        total_ref[0][...] = total
        send_ref[rows // 2 :] = pieces_of(total)


def add_sums(total_refs, arrived_ref, start):
    arrived = whole_of(arrived_ref[start : start + SUM_ROWS])
    if len(total_refs) == 1:
        return total_refs[0][...] + arrived
    chip, beside = (ref[...] for ref in total_refs)
    return (chip + whole_of(arrived_ref[start + SUM_ROWS :])) + (beside + arrived)


def finish_kernel(kept_ref, total_ref, arrived_ref, kept_down_ref, arrived_down_ref, up_hbm, down_hbm, taps_ref, gain_ref, *refs):
    up_ref, down_ref, sems = refs
    rows = kept_ref.shape[0]
    down_ref[...] = kept_down_ref[...] + arrived_down_ref[...].astype(jnp.float32)
    leaving = copies(sems, 0, [(down_ref, down_hbm)])
    up_ref[...] = kept_ref[...] + arrived_ref[:rows].astype(jnp.float32)
    leaving += copies(sems, 1, [(up_ref, up_hbm)])
    total = add_sums([total_ref], arrived_ref, rows)
    for k in range(9):
        taps_ref[k // 3, k % 3 : k % 3 + 1] = total[k : k + 1]
    gain_ref[...] = total[9:10]
    finish(leaving)


def halving(flip, send, keep, total):
    lon, lat = lax.axis_size("lon"), lax.axis_size("lat")
    places = [(i, j) for i in range(lon) for j in range(lat)]
    flat = lambda i, j: i * lat + j
    along_lat = lambda i: (i & 1) != flip
    sds = jax.ShapeDtypeStruct
    rows, width = keep.shape[1:]
    sums = [] if total is None else [total]
    with_sums = len(sums)
    plan = [
        (lambda i, j: (i ^ 1, j), functools.partial(quadrant_kernel, flip), (2, rows, width), 1),
        (
            lambda i, j: (i, j ^ 1) if along_lat(i) else (i ^ 2, j),
            functools.partial(half_kernel, flip),
            (rows, width),
            2,
        ),
        (
            lambda i, j: (i ^ 2, j) if along_lat(i) else (i, j ^ 1),
            functools.partial(rows_kernel, 2, 2, 2 * with_sums),
            (rows // 2, width),
            1,
        ),
        (lambda i, j: (i ^ 4, j), functools.partial(rows_kernel, 1, 3, with_sums), (rows // 4, width), 1),
    ]
    for at, (partner, kernel, shape, parts) in enumerate(plan):
        send = yield send
        arrived = lax.ppermute(send, AXES, [(flat(i, j), flat(*partner(i, j))) for i, j in places])
        arrived = yield arrived
        sent = shape[-2] * (shape[0] if len(shape) == 3 else 1) + SUM_ROWS * parts * with_sums
        out = [sds((sent, shape[-1]), jnp.bfloat16), sds(shape, jnp.float32)]
        out += [sds(value.shape, jnp.float32) for value in sums[:1]]
        operands = [keep, *sums, arrived]
        send, keep, *more = call(kernel, out, operands, "v" * len(operands), "p" * len(out), moved=2**19, limit=12)
        sums = sums + more if at == 1 else more
    send = yield send
    arrived = lax.ppermute(send, AXES, [(flat(i, j), flat(i ^ 8, j)) for i, j in places])
    yield (keep, *sums, arrived)


def all_sums(up, down, total, field, kernel):
    channels = total.shape[1]
    field = field[None]
    if up[1].ndim == 2:
        parts = [scattered(send.astype(jnp.float32), flip) for flip, (send, _) in enumerate((up, down))]
        total = lax.psum(total, AXES)
        around = lat_edges(field)
        state = final_parts(field[0], (*around, *lon_edges(field, *around)), kernel)
        return (state, *parts, total[:9].reshape(3, 3, channels), total[9])
    ahead, behind = halving(False, *up, total), halving(True, *down, None)
    send, later = next(ahead), next(behind)
    arrived = ahead.send(send)
    send = ahead.send(after(arrived, later))
    field = after(field, send)
    arrived_later = behind.send(after(later, send))
    later = behind.send(arrived_later)
    around = lat_edges(field, lambda value: after(value, later))
    state = final_parts(field[0], (*around, *lon_edges(field, *around)), kernel)
    for at in range(1, 4):
        arrived = ahead.send(send)
        arrived_later = behind.send(later)
        send = ahead.send(after(arrived, later))
        later = behind.send(after(arrived_later, send))
    final_ahead = ahead.send(send)
    final_behind = behind.send(later)
    sds = jax.ShapeDtypeStruct
    part = sds(final_ahead[0].shape, jnp.float32)
    out = [part, part, sds((3, 3, channels), jnp.float32), sds((1, channels), jnp.float32)]
    up, down, taps, gain = call(
        finish_kernel,
        out,
        [*final_ahead, *final_behind],
        "vvvvv",
        "hhvv",
        scratch=[pltpu.VMEM(part.shape, part.dtype)] * 2 + [pltpu.SemaphoreType.DMA((2,))],
        moved=2**18,
    )
    return state, up, down, taps, gain.reshape(channels)


def local(cotangent, states, w_up, w_down, norm_gain, kernel, bilinear, lon_move, lat_move):
    steps, rows_out, cols_out, channels = states.shape
    tiles_lon, tiles_lat = lax.axis_size("lon"), lax.axis_size("lat")
    devices = tiles_lon * tiles_lat
    count = rows_out * cols_out
    tile = (rows_out, cols_out)
    share = channels // devices
    padded_share = -(-share // ROWS) * ROWS
    whole_share = share == padded_share
    group_size = channels // lon_move.shape[1]
    me = lax.axis_index("lon") * tiles_lat + lax.axis_index("lat")

    def as_blocks(value):
        value = value.reshape(devices, share, count)
        return value if whole_share else jnp.pad(value, ((0, 0), (0, padded_share - share), (0, 0)))

    def as_rows(blocks):
        return blocks[:, :share].reshape(channels, count)

    def as_grid(blocks):
        return blocks.reshape(tiles_lon, tiles_lat, *blocks.shape[1:])

    blocks = packed(cotangent, bilinear, devices)
    blocks, states_later = lax.optimization_barrier((blocks, states))
    arrived = as_grid(exchanged(blocks))
    group = me * share // group_size
    moves = jnp.stack([lon_move[:, group], lat_move[:, group]], axis=1).reshape(2 * steps, 1)
    moves = jnp.broadcast_to(jnp.pad(moves, ((0, -2 * steps % 8), (0, 0))), (-(-2 * steps // 8) * 8, 128))
    grid_now, weights = spatial("first", steps - 1, tile, padded_share, arrived, None, None, moves)

    taps = lax.dynamic_slice_in_dim(kernel.reshape(9, channels), me * share, share, 1).T
    taps = jnp.pad(taps, ((0, padded_share - share), (0, count - 9)))

    around = lat_edges(states_later)
    around = (*around, *lon_edges(states, *around))
    order = list(reversed(range(steps)))
    gain = norm_gain.reshape(1, channels)
    forward = {s: forward_parts(s, states, around, kernel, gain, w_up) for s in order}
    names = {k: {s: forward[s][at] for s in order} for at, k in enumerate(FORWARD)}

    def taken_back(grid):
        return as_rows(exchanged(grid.reshape(devices, padded_share, count)))

    def spread_on(s, field, grid_kernel=taps):
        (near,) = fetched([weights], field)
        arrived = after(as_grid(exchanged(as_blocks(field))), near)
        return spatial("mid", s, tile, padded_share, arrived, grid_kernel, near, moves)[0]

    fields, grads, moved = {}, {}, {}
    for s in order:
        if s != order[0]:
            grid_now = spread_on(s, fields[s + 1])
        here = taken_back(grid_now)
        wanted = ("slope", "n", "inv") + ("pad",) * (s == order[-1])
        near = fetched([names[k][s] for k in wanted], grid_now)
        if s == order[-1]:
            break
        here = after(here, (near, forward) if s != order[0] else near)
        fields[s], grads[s], moved[s] = network_back(here, w_down, w_up, gain, *near)

    earlier = lambda values: [values[s] for s in order[:-1]]
    all_of = lambda values: [values[s] for s in order]
    sums = channel_sums(tile, w_up, gain, *map(earlier, (names["pad"], fields, grads, names["n"])))
    here = after(here, (near, sums))
    field, total, send, keep = last_step(tile, here, w_down, w_up, gain, sums, near, all_of(names["turned"]), earlier(grads))
    down = down_gradients(here, earlier(moved), all_of(names["hid"]))
    field = field.reshape(cotangent.shape)
    return all_sums((send, keep), down, total, field, kernel)


def solution(mesh):
    placed = (
        P("lon", "lat", None),
        P(None, "lon", "lat", None),
        P(),
        P(),
        P(),
        P(),
        P(None, None, "lon", "lat"),
        P(),
        P(),
    )
    return jax.shard_map(
        local,
        mesh=mesh,
        in_specs=placed,
        out_specs=(P("lon", "lat", None), P("lon", "lat"), P("lon", "lat"), P(), P()),
        check_vma=False,
    )
```

```python
import functools

import jax
import jax.numpy as jnp
from jax import lax
from jax.experimental import pallas as pl
from jax.experimental.pallas import tpu as pltpu
from jax.sharding import PartitionSpec as P

EPSILON = 1e-06
AXES = ("lon", "lat")
ROWS = 16
LAT_REACH = 2
LON_REACH = 8
MIB = 1024 * 1024


def exchanged(blocks):
    return lax.all_to_all(blocks, AXES, split_axis=0, concat_axis=0, tiled=True)


SPACES = {"s": pltpu.SMEM, "v": pltpu.VMEM, "p": pltpu.VMEM, "h": pltpu.HBM}
PINNED = {"p": pltpu.VMEM, "h": pltpu.HBM}


def call(kernel, out_shape, operands, ins, outs, scratch=(), flops=0, moved=0, limit=8):
    operands = [
        pltpu.with_memory_space_constraint(value, PINNED[kind]) if kind in PINNED else value
        for kind, value in zip(ins, operands, strict=True)
    ]
    out_shape = [
        PINNED[kind](value.shape, value.dtype) if kind in PINNED else value
        for kind, value in zip(outs, out_shape, strict=True)
    ]
    return pl.pallas_call(
        kernel,
        out_shape=out_shape,
        in_specs=[pl.BlockSpec(memory_space=SPACES[kind]) for kind in ins],
        out_specs=[pl.BlockSpec(memory_space=SPACES[kind]) for kind in outs],
        scratch_shapes=scratch,
        compiler_params=pltpu.CompilerParams(vmem_limit_bytes=limit * MIB),
        cost_estimate=pl.CostEstimate(flops=flops, bytes_accessed=moved, transcendentals=0),
    )(*operands)


def copies(sems, first, pairs):
    started = [pltpu.make_async_copy(src, dst, sems.at[first + k]) for k, (src, dst) in enumerate(pairs)]
    for copy in started:
        copy.start()
    return started


def finish(started):
    for copy in started:
        copy.wait()


PIECES = 3
SUMS = 10
SUM_ROWS = 32


def pieces_of(value):
    value = value[:SUMS]
    parts = []
    for _ in range(PIECES):
        parts.append(value.astype(jnp.bfloat16).astype(jnp.float32))
        value = value - parts[-1]
    parts.append(jnp.zeros((SUM_ROWS - PIECES * SUMS, value.shape[1]), jnp.float32))
    return jnp.concatenate(parts, axis=0).astype(jnp.bfloat16)


def whole_of(parts):
    parts = parts.astype(jnp.float32)
    total = (parts[:SUMS] + parts[SUMS : 2 * SUMS]) + parts[2 * SUMS : 3 * SUMS]
    return jnp.concatenate([total, jnp.zeros((ROWS - SUMS, parts.shape[1]), jnp.float32)], axis=0)


def after(value, first):
    return lax.optimization_barrier((value, first))[0]


def pack_kernel(cotangent_hbm, weight_hbm, out_hbm, cotangent_ref, weight_ref, out_ref, sems):
    started = copies(sems, 0, [(cotangent_hbm, cotangent_ref), (weight_hbm, weight_ref)])
    channels = cotangent_ref.shape[1]
    devices, _, count = out_ref.shape
    share = channels // devices
    started[1].wait()
    rows = weight_ref.shape[0]
    weights = jnp.concatenate([weight_ref[:, i] for i in range(weight_ref.shape[1])], axis=1)
    weights = jnp.concatenate([weights, jnp.zeros((ROWS - rows, count), jnp.float32)], axis=0)
    weights = weights.astype(jnp.bfloat16)
    out_ref[:, share:] = jnp.broadcast_to(weights[None], (devices, ROWS, count))
    started[0].wait()
    turned = cotangent_ref[...].astype(jnp.float32).T.astype(jnp.bfloat16)
    out_ref[:, :share] = turned.reshape(devices, share, count)
    finish(copies(sems, 2, [(out_ref, out_hbm)]))


def packed(cotangent, bilinear, devices):
    rows_out, cols_out, channels = cotangent.shape
    steps, corners = bilinear.shape[:2]
    count = rows_out * cols_out
    share = channels // devices
    if share % ROWS:
        blocks = cotangent.reshape(count, channels).T.reshape(devices, share, count)
        blocks = jnp.pad(blocks, ((0, 0), (0, -share % ROWS), (0, 0)))
        weights = bilinear.reshape(steps * corners, count).astype(jnp.bfloat16)
        weights = jnp.pad(weights, ((0, ROWS - steps * corners), (0, 0)))
        return jnp.concatenate([blocks, jnp.broadcast_to(weights[None], (devices, ROWS, count))], axis=1)
    shape = (devices, share + ROWS, count)
    return call(
        pack_kernel,
        [jax.ShapeDtypeStruct(shape, jnp.bfloat16)],
        [cotangent.reshape(count, channels), bilinear.reshape(steps * corners, rows_out, cols_out)],
        "hh",
        "h",
        scratch=[
            pltpu.VMEM((count, channels), jnp.bfloat16),
            pltpu.VMEM((steps * corners, rows_out, cols_out), jnp.float32),
            pltpu.VMEM(shape, jnp.bfloat16),
            pltpu.SemaphoreType.DMA((3,)),
        ],
        moved=2**19,
    )[0]


def lat_edges(states, held=lambda value: value):
    lat, lat_at = lax.axis_size("lat"), lax.axis_index("lat")
    first, last = states[:, :, :1], states[:, :, -1:]
    if lat == 2:
        arrived = lax.ppermute(jnp.where(lat_at == 0, last, first), "lat", [(0, 1), (1, 0)])
        arrived = held(arrived)
        return jnp.where(lat_at == 0, 0, arrived), jnp.where(lat_at == 0, arrived, 0)
    return (
        lax.ppermute(last, "lat", [(i, i + 1) for i in range(lat - 1)]),
        lax.ppermute(first, "lat", [(i + 1, i) for i in range(lat - 1)]),
    )


def lon_edges(states, before, after):
    lon = lax.axis_size("lon")
    even = lax.axis_index("lon") % 2 == 0
    row = lambda place: jnp.concatenate([part[:, place] for part in (before, states, after)], axis=2)
    first, last = row(slice(0, 1)), row(slice(-1, None))
    with_next = lax.ppermute(jnp.where(even, last, first), "lon", [(i, i ^ 1) for i in range(lon)])
    pairs = [(i, (i - 1) % lon if i % 2 == 0 else (i + 1) % lon) for i in range(lon)]
    with_last = lax.ppermute(jnp.where(even, first, last), "lon", pairs)
    return jnp.where(even, with_last, with_next), jnp.where(even, with_next, with_last)


MARGIN = 8


def forward_math(step, places, sems, leaving, outs):
    states_ref, before_ref, after_ref, low_ref, high_ref, kernel_ref, gain_ref, up_ref = places
    n_ref, turned_ref, inv_ref, hid_ref, slope_ref, pad_ref, wide_ref = outs
    rows_out, cols_out, channels = states_ref.shape[1:]
    count = rows_out * cols_out
    mixed = states_ref[step].astype(jnp.float32)
    fill_margins(wide_ref, before_ref[step], after_ref[step], low_ref[step], high_ref[step], mixed)
    pad_ref[...] = wide_ref[...].astype(jnp.bfloat16)
    leaving("pad")
    for col_tap in range(3):
        place = MARGIN - 1 + col_tap
        shifted_cols = wide_ref[:, place : place + cols_out]
        for row_tap in range(3):
            tap = kernel_ref[row_tap, col_tap : col_tap + 1]
            mixed = mixed + tap[None] * shifted_cols[row_tap : row_tap + rows_out]
    mixed = mixed.reshape(count, channels)
    inv_root = lax.rsqrt(jnp.mean(mixed * mixed, axis=1, keepdims=True) + EPSILON)
    narrow = mixed * inv_root * gain_ref[...]
    n_ref[...] = narrow.astype(jnp.bfloat16)
    inv_ref[...] = jnp.broadcast_to(inv_root, inv_ref.shape)
    leaving("n", "inv")
    pre = jnp.dot(n_ref[...], up_ref[...], preferred_element_type=jnp.float32)
    sigmoid = jax.nn.sigmoid(pre)
    slope_ref[...] = (sigmoid * (1.0 + pre * (1.0 - sigmoid))).astype(jnp.bfloat16)
    leaving("slope")
    hid_ref[...] = (pre * sigmoid).astype(jnp.bfloat16)
    turned_ref[...] = narrow.T.astype(jnp.bfloat16)
    leaving("hid", "turned")


FORWARD = ("n", "turned", "inv", "hid", "slope", "pad")


def sender(sems, refs, goals, started):
    names = list(goals)

    def leave(*which):
        for name in which:
            if name in goals:
                started.extend(copies(sems, names.index(name), [(refs[name], goals[name])]))

    return leave


def forward_kernel(step, *refs):
    places, goals, outs, sems = refs[:8], refs[8:14], refs[14:21], refs[21]
    started = []
    leave = sender(sems, dict(zip(FORWARD, outs)), dict(zip(FORWARD, goals)), started)
    forward_math(step, places, sems, leave, outs)
    finish(started)


def forward_shapes(states, w_up):
    _, rows_out, cols_out, channels = states.shape
    hid = w_up.shape[1]
    count = rows_out * cols_out
    wide = (rows_out + 2, cols_out + 2 * MARGIN, channels)
    return [
        ((count, channels), jnp.bfloat16),
        ((channels, count), jnp.bfloat16),
        ((count, 128), jnp.float32),
        ((count, hid), jnp.bfloat16),
        ((count, hid), jnp.bfloat16),
        (wide, jnp.bfloat16),
    ]


def forward_scratch(shapes):
    scratch = [pltpu.VMEM(*shape) for shape in shapes]
    return scratch + [pltpu.VMEM(shapes[-1][0], jnp.float32)]


def forward_parts(step, states, around, kernel, norm_gain, w_up):
    shapes = forward_shapes(states, w_up)
    return call(
        functools.partial(forward_kernel, step),
        [jax.ShapeDtypeStruct(*shape) for shape in shapes],
        [states, *around, kernel, norm_gain, w_up],
        "vvvvvvvv",
        "hhhhhh",
        scratch=forward_scratch(shapes) + [pltpu.SemaphoreType.DMA((6,))],
        flops=2**27,
        moved=2**22,
        limit=12,
    )


LANES_BOTH = (((1,), (1,)), ((), ()))


def fetch_kernel(*refs):
    count = len(refs) // 2
    *pairs, sems = refs
    finish(copies(sems, 0, list(zip(pairs[:count], pairs[count:]))))


def fetched(values, first):
    values = after(values, first)
    return call(
        fetch_kernel,
        [jax.ShapeDtypeStruct(value.shape, value.dtype) for value in values],
        values,
        "h" * len(values),
        "v" * len(values),
        scratch=[pltpu.SemaphoreType.DMA((len(values),))],
        moved=2**19,
    )


def network_math(moved_ref, down_ref, up_ref, gain_ref, slope_ref, n_ref, inv_ref, out_ref, grad_ref, leave):
    leave("moved")
    moved = moved_ref[...].astype(jnp.float32).T
    grad_hidden = jnp.dot(moved.astype(jnp.bfloat16), down_ref[...], preferred_element_type=jnp.float32)
    grad_pre = (grad_hidden * slope_ref[...].astype(jnp.float32)).astype(jnp.bfloat16)
    grad_ref[...] = grad_pre
    leave("grad")
    grad_n = lax.dot_general(grad_pre, up_ref[...], LANES_BOTH, preferred_element_type=jnp.float32)
    narrow, gain = n_ref[...].astype(jnp.float32), gain_ref[...]
    mean = jnp.mean(grad_n * narrow, axis=1, keepdims=True)
    field = moved + inv_ref[:, :1] * (grad_n * gain - narrow * (mean / gain))
    out_ref[...] = field.T.astype(jnp.bfloat16)
    leave("field")


def network_kernel(moved_ref, down_ref, up_ref, gain_ref, slope_ref, n_ref, inv_ref, *refs):
    *goals, out_ref, grad_ref, sems = refs
    started = []
    names = ("field", "grad", "moved")
    leave = sender(sems, dict(zip(names, (out_ref, grad_ref, moved_ref))), dict(zip(names, goals)), started)
    network_math(moved_ref, down_ref, up_ref, gain_ref, slope_ref, n_ref, inv_ref, out_ref, grad_ref, leave)
    finish(started)


def first_kernel(step, *refs):
    (moved_ref, down_ref), places, refs = refs[:2], refs[2:10], refs[10:]
    goals, outs, (out_ref, grad_ref, sems) = refs[:7], refs[7:14], refs[14:]
    started = []
    names = ("n", "turned", "hid", "pad", "field", "grad", "moved")
    values = dict(zip(FORWARD, outs)) | {"field": out_ref, "grad": grad_ref, "moved": moved_ref}
    leave = sender(sems, values, dict(zip(names, goals)), started)
    forward_math(step, places, sems, leave, outs)
    n_ref, _, inv_ref, _, slope_ref = outs[:5]
    gain_ref, up_ref = places[6:]
    network_math(moved_ref, down_ref, up_ref, gain_ref, slope_ref, n_ref, inv_ref, out_ref, grad_ref, leave)
    finish(started)


def first_step(step, moved, w_down, states, around, kernel, norm_gain, w_up):
    shapes = forward_shapes(states, w_up)
    channels, count = moved.shape
    hid = w_down.shape[1]
    backs = [((channels, count), jnp.bfloat16), ((count, hid), jnp.bfloat16), ((channels, count), jnp.bfloat16)]
    results = [shapes[k] for k in (0, 1, 3, 5)] + backs
    return call(
        functools.partial(first_kernel, step),
        [jax.ShapeDtypeStruct(*shape) for shape in results],
        [moved, w_down, states, *around, kernel, norm_gain, w_up],
        "v" * 10,
        "h" * 7,
        scratch=forward_scratch(shapes) + [pltpu.VMEM(*shape) for shape in backs[:2]] + [pltpu.SemaphoreType.DMA((7,))],
        flops=2**28,
        moved=2**22,
        limit=16,
    )


def network_back(moved, w_down, w_up, norm_gain, slope, narrow, inv_root):
    channels, count = moved.shape
    hid = w_down.shape[1]
    shapes = [((channels, count), jnp.bfloat16), ((count, hid), jnp.bfloat16), ((channels, count), jnp.bfloat16)]
    return call(
        network_kernel,
        [jax.ShapeDtypeStruct(*shape) for shape in shapes],
        [moved, w_down, w_up, norm_gain, slope, narrow, inv_root],
        "vvvvvvv",
        "hhh",
        scratch=[pltpu.VMEM(*shape) for shape in shapes[:2]] + [pltpu.SemaphoreType.DMA((3,))],
        flops=4 * count * hid * channels,
        moved=4 * 2**20,
        limit=8,
    )


def stencil_sums(pad_ref, field, tile):
    rows_out, cols_out = tile
    field = field.reshape(rows_out, cols_out, -1)
    padded = pad_ref[...].astype(jnp.float32)
    result = [None] * 9
    for col_tap in range(3):
        place = MARGIN - 1 + col_tap
        shifted_cols = padded[:, place : place + cols_out]
        for row_tap in range(3):
            products = jnp.sum(shifted_cols[row_tap : row_tap + rows_out] * field, axis=0)
            result[3 * row_tap + col_tap] = jnp.sum(products, axis=0, keepdims=True)
    return result


def sums_rows(rows, term, gain):
    rows = rows + [jnp.sum(term, axis=0, keepdims=True) / gain, jnp.zeros((ROWS - 10, term.shape[1]), jnp.float32)]
    return jnp.concatenate(rows, axis=0)


def sums_kernel(steps, tile, up_ref, gain_ref, *refs):
    inputs, (out_ref, *refs) = refs[: 4 * steps], refs[4 * steps :]
    pads, fields, grads, narrows, sems = refs
    places = [(ref, place.at[k]) for k in range(steps) for ref, place in zip(inputs[4 * k : 4 * k + 4], refs[:4])]
    arriving = copies(sems, 0, places)
    rows, term = None, None
    for k in range(steps):
        finish(arriving[4 * k : 4 * k + 4])
        grad_n = lax.dot_general(grads[k], up_ref[...], LANES_BOTH, preferred_element_type=jnp.float32)
        product = grad_n * narrows[k].astype(jnp.float32)
        term = product if term is None else term + product
        more = stencil_sums(pads.at[k], fields[k].astype(jnp.float32).T, tile)
        rows = more if rows is None else [a + b for a, b in zip(rows, more)]
    out_ref[...] = sums_rows(rows, term, gain_ref[...])


def channel_sums(tile, w_up, norm_gain, pads, fields, grads, narrows):
    steps = len(fields)
    inputs = [value for group in zip(pads, fields, grads, narrows) for value in group]
    return call(
        functools.partial(sums_kernel, steps, tile),
        [jax.ShapeDtypeStruct((ROWS, fields[0].shape[0]), jnp.float32)],
        [w_up, norm_gain, *inputs],
        "vv" + "h" * 4 * steps,
        "v",
        scratch=[pltpu.VMEM((steps, *value.shape), value.dtype) for value in inputs[:4]]
        + [pltpu.SemaphoreType.DMA((4 * steps,))],
        moved=2**21,
        limit=12,
    )[0]


QUADRANTS = 4


def lon_bit(at):
    return lax.axis_index("lon") >> at & 1


def gradient_quadrants(left_ref, right_ref, send_ref, keep_ref):
    channels, width = left_ref.shape[0], right_ref.shape[1] // 2
    if keep_ref.ndim == 2:
        send_ref[:channels] = jnp.dot(left_ref[...], right_ref[...], preferred_element_type=jnp.float32).astype(jnp.bfloat16)
        keep_ref[...] = jnp.zeros_like(keep_ref)
        return
    size = channels // QUADRANTS
    groups = lax.axis_size("lon") // 4
    chunk = size // groups
    rows = []
    for core in (1 - lon_bit(0), lon_bit(0)):
        for x in range(2):
            for z in range(groups):
                start = pl.multiple_of((4 * z + 2 * x + core) * chunk, chunk)
                rows.append(left_ref[pl.ds(start, chunk)])
    rows = jnp.concatenate(rows, axis=0)
    value = jnp.dot(rows, right_ref[...], preferred_element_type=jnp.float32).astype(jnp.bfloat16)
    for q in range(QUADRANTS):
        x, lat = q // 2, q % 2
        columns = slice(lat * width, (lat + 1) * width)
        send_ref[q * size : (q + 1) * size] = value[x * size : (x + 1) * size, columns]
        keep_ref[q] = value[(2 + x) * size : (3 + x) * size, columns]


def quadrant_shapes(channels, hid, sums):
    if lax.axis_size("lat") != 2 or lax.axis_size("lon") != 16:
        return (channels, hid), (8, 128)
    return (channels + SUM_ROWS * sums, hid // 2), (QUADRANTS, channels // QUADRANTS, hid // 2)


def side_by_side(refs, goal_ref, axis):
    size = refs[0].shape[axis]
    places = [pl.ds(s * size, size) for s in range(len(refs))]
    return [(ref, goal_ref.at[:, place] if axis else goal_ref.at[place]) for ref, place in zip(refs, places)]


def last_kernel(steps, tile, moved_ref, down_ref, up_ref, gain_ref, sums_ref, *refs):
    slope_ref, n_ref, inv_ref, pad_ref, *refs = refs
    inputs, refs = refs[: 2 * steps - 1], refs[2 * steps - 1 :]
    field_ref, total_ref, send_ref, keep_ref, left_ref, right_ref, sems = refs
    count = slope_ref.shape[0]
    pairs = side_by_side(inputs[:steps], left_ref, 1) + side_by_side(inputs[steps:], right_ref, 0)
    later = copies(sems, 0, pairs)
    moved = moved_ref[...].astype(jnp.float32).T
    grad_hidden = jnp.dot(moved.astype(jnp.bfloat16), down_ref[...], preferred_element_type=jnp.float32)
    grad_pre = (grad_hidden * slope_ref[...].astype(jnp.float32)).astype(jnp.bfloat16)
    right_ref[(steps - 1) * count :] = grad_pre
    grad_n = lax.dot_general(grad_pre, up_ref[...], LANES_BOTH, preferred_element_type=jnp.float32)
    narrow, gain = n_ref[...].astype(jnp.float32), gain_ref[...]
    term = grad_n * narrow
    mean = jnp.mean(term, axis=1, keepdims=True)
    field = moved + inv_ref[:, :1] * (grad_n * gain - narrow * (mean / gain))
    field = field.astype(jnp.bfloat16)
    field_ref[...] = field
    total = sums_ref[...] + sums_rows(stencil_sums(pad_ref, field.astype(jnp.float32), tile), term, gain)
    total_ref[...] = total
    finish(later)
    gradient_quadrants(left_ref, right_ref, send_ref, keep_ref)
    if keep_ref.ndim > 2:
        send_ref[left_ref.shape[0] :] = pieces_of(total)


def last_step(tile, moved, w_down, w_up, norm_gain, sums, near, turned, grads):
    steps = len(turned)
    channels, count = moved.shape
    hid = w_down.shape[1]
    send, keep = quadrant_shapes(channels, hid, 1)
    sds = jax.ShapeDtypeStruct
    inputs = turned + grads
    return call(
        functools.partial(last_kernel, steps, tile),
        [
            sds((count, channels), jnp.bfloat16),
            sds((ROWS, channels), jnp.float32),
            sds(send, jnp.bfloat16),
            sds(keep, jnp.bfloat16),
        ],
        [moved, w_down, w_up, norm_gain, sums, *near, *inputs],
        "v" * 9 + "h" * len(inputs),
        "vppp",
        scratch=[pltpu.VMEM((channels, steps * count), jnp.bfloat16), pltpu.VMEM((steps * count, hid), jnp.bfloat16)]
        + [pltpu.SemaphoreType.DMA((len(inputs),))],
        flops=2**30,
        moved=6 * 2**20,
        limit=20,
    )


def down_kernel(steps, moved_ref, *refs):
    inputs, (send_ref, keep_ref, left_ref, right_ref, sems) = refs[: 2 * steps - 1], refs[2 * steps - 1 :]
    count = moved_ref.shape[1]
    pairs = side_by_side(inputs[: steps - 1], left_ref, 1) + side_by_side(inputs[steps - 1 :], right_ref, 0)
    arriving = copies(sems, 0, pairs)
    left_ref[:, (steps - 1) * count :] = moved_ref[...]
    finish(arriving)
    gradient_quadrants(left_ref, right_ref, send_ref, keep_ref)


def down_gradients(moved, moveds, hidden):
    steps = len(hidden)
    channels, count = moved.shape
    hid = hidden[0].shape[1]
    inputs = moveds + hidden
    return call(
        functools.partial(down_kernel, steps),
        [jax.ShapeDtypeStruct(shape, jnp.bfloat16) for shape in quadrant_shapes(channels, hid, 0)],
        [moved, *inputs],
        "v" + "h" * len(inputs),
        "pp",
        scratch=[pltpu.VMEM((channels, steps * count), jnp.bfloat16), pltpu.VMEM((steps * count, hid), jnp.bfloat16)]
        + [pltpu.SemaphoreType.DMA((len(inputs),))],
        flops=2**29,
        moved=2**21,
        limit=16,
    )


def fill_margins(wide_ref, before, after, low, high, middle):
    rows_out, cols_out, _ = middle.shape
    around = slice(MARGIN - 1, MARGIN + cols_out + 1)
    wide_ref[:1, around] = low.astype(jnp.float32)
    wide_ref[1 + rows_out :, around] = high.astype(jnp.float32)
    wide_ref[1 : 1 + rows_out, MARGIN - 1 : MARGIN] = before.astype(jnp.float32)
    wide_ref[1 : 1 + rows_out, MARGIN + cols_out : MARGIN + cols_out + 1] = after.astype(jnp.float32)
    wide_ref[1 : 1 + rows_out, MARGIN : MARGIN + cols_out] = middle


def final_kernel(field_ref, before_ref, after_ref, low_ref, high_ref, kernel_ref, out_ref, wide_ref):
    rows_out, cols_out, _ = field_ref.shape
    result = field_ref[...].astype(jnp.float32)
    fill_margins(wide_ref, before_ref[0], after_ref[0], low_ref[0], high_ref[0], result)
    for col_tap in range(3):
        place = MARGIN + 1 - col_tap
        shifted_cols = wide_ref[:, place : place + cols_out]
        for row_tap in range(3):
            tap = kernel_ref[row_tap, col_tap : col_tap + 1]
            result = result + tap[None] * shifted_cols[2 - row_tap : 2 - row_tap + rows_out]
    out_ref[...] = result.astype(jnp.bfloat16)


def final_parts(field, around, kernel):
    rows_out, cols_out, channels = field.shape
    return call(
        final_kernel,
        [jax.ShapeDtypeStruct(field.shape, jnp.bfloat16)],
        [field, *around, kernel],
        "v" * 6,
        "v",
        scratch=[pltpu.VMEM((rows_out + 2, cols_out + 2 * MARGIN, channels), jnp.float32)],
        moved=2**19,
    )[0]


def spatial_kernel(mode, step, near_lon, near_lat, *refs):
    refs = list(refs)
    take = lambda: refs.pop(0)
    with_stencil = mode != "first"
    move_ref = take()
    in_ref = take()
    kern_ref = take() if with_stencil else None
    weight_ref = take() if mode == "mid" else None
    out_hbm = take()
    saved_hbm = take() if mode == "first" else None
    out_ref, sems = take(), take()
    spread_ref = take()
    weight_ref = take() if mode == "first" else weight_ref
    tiles_lon, tiles_lat, _, lanes = in_ref.shape
    rows = out_ref.shape[2]
    started = []
    if mode == "first":
        weight_ref[...] = in_ref[:, :, rows:]
        started += copies(sems, 0, [(weight_ref, saved_hbm)])
    lane = lax.broadcasted_iota(jnp.int32, (rows, lanes), 1)
    col = lax.rem(lane, near_lat)
    lat_last, lat_first = col == near_lat - 1, col == 0
    lon_last, lon_first = lane >= lanes - near_lat, lane < near_lat
    tiles = [(a, b) for a in range(tiles_lon) for b in range(tiles_lat)]

    def turn(value, steps):
        return pltpu.roll(value, steps % lanes if isinstance(steps, int) else steps, 1)

    def lat_after(grid):
        turned = {key: turn(value, -1) for key, value in grid.items()}
        wrapped = {key: turn(grid[key], near_lat - 1) for key in tiles if key[1] > 0}
        return {(a, b): jnp.where(lat_last, wrapped.get((a, b + 1), 0.0), turned[a, b]) for a, b in tiles}

    def lat_before(grid):
        turned = {key: turn(value, 1) for key, value in grid.items()}
        wrapped = {key: turn(grid[key], 1 - near_lat) for key in tiles if key[1] < tiles_lat - 1}
        return {(a, b): jnp.where(lat_first, wrapped.get((a, b - 1), 0.0), turned[a, b]) for a, b in tiles}

    def lon_after(grid):
        return {
            (a, b): turn(jnp.where(lon_first, grid[(a + 1) % tiles_lon, b], grid[a, b]), -near_lat) for a, b in tiles
        }

    def lon_before(grid):
        return {(a, b): turn(jnp.where(lon_last, grid[(a - 1) % tiles_lon, b], grid[a, b]), near_lat) for a, b in tiles}

    grid = {(a, b): in_ref[a, b, :rows].astype(jnp.float32) for a, b in tiles}
    if with_stencil:
        taps = [
            [jnp.broadcast_to(kern_ref[:, 3 * a + b : 3 * a + b + 1], (rows, lanes)) for b in range(3)] for a in range(3)
        ]
        by_col = [lat_after(grid), grid, lat_before(grid)]
        mix = [
            {key: sum(taps[row][c] * by_col[c][key] for c in range(1, 3)) + taps[row][0] * by_col[0][key] for key in tiles}
            for row in range(3)
        ]
        high, low = lon_after(mix[0]), lon_before(mix[2])
        grid = {key: grid[key] + mix[1][key] + (high[key] + low[key]) for key in tiles}
    if mode == "mid":
        grid = {key: value.astype(jnp.bfloat16).astype(jnp.float32) for key, value in grid.items()}
    weights = {}
    for a, b in tiles:
        four = weight_ref[a, b].astype(jnp.float32)[4 * step : 4 * step + 4]
        weights[a, b] = [jnp.broadcast_to(four[k : k + 1], (rows, lanes)) for k in range(4)]
    weighted = [{key: weights[key][k] * grid[key] for key in tiles} for k in range(4)]
    own, lon = lat_after(weighted[2]), lat_after(weighted[3])
    lon = lon_after({key: weighted[1][key] + lon[key] for key in tiles})
    for a, b in tiles:
        value = (weighted[0][a, b] + own[a, b] + lon[a, b]).astype(jnp.bfloat16).astype(jnp.float32)
        for place in range(a, tiles_lon + LON_REACH, tiles_lon):
            spread_ref[place, b] = value
    spread_ref[:, tiles_lat:] = jnp.zeros((tiles_lon + LON_REACH, LAT_REACH, rows, lanes), jnp.float32)

    lon_move, lat_move = (jnp.max(move_ref[2 * step + k : 2 * step + k + 1]) for k in range(2))
    far_lon, off_lon = lon_move // near_lon, lax.rem(lon_move, near_lon)
    far_lat, off_lat = lat_move // near_lat, lax.rem(lat_move, near_lat)
    shift = off_lon * near_lat + off_lat
    turn_here = lax.rem(2 * lanes - shift, lanes)
    turn_next = lax.rem(2 * lanes - shift + near_lat, lanes)
    same_lon = lane >= off_lon * near_lat
    same_lat = col + off_lat < near_lat
    half = tiles_lon // 2
    for a in range(tiles_lon):
        met = [
            jnp.where(same_lon, spread_ref[far_lon + a, far_lat + b], spread_ref[far_lon + a + 1, far_lat + b])
            for b in range(tiles_lat + 1)
        ]
        for b in range(tiles_lat):
            value = jnp.where(same_lat, turn(met[b], turn_here), turn(met[b + 1], turn_next))
            out_ref[a, b] = value.astype(jnp.bfloat16)
        if (a + 1) % half == 0:
            part = pl.ds(a + 1 - half, half)
            started += copies(sems, 1 + a // half, [(out_ref.at[part], out_hbm.at[part])])
    finish(started)


def spatial(mode, step, tile, rows, field, kern, weights, moves):
    tiles_lon, tiles_lat, _, lanes = field.shape
    with_stencil = mode != "first"
    operands = [moves, field]
    operands += [kern] if with_stencil else []
    operands += [weights] if mode == "mid" else []
    out_shape = (tiles_lon, tiles_lat, rows, lanes)
    weight_shape = (tiles_lon, tiles_lat, ROWS, lanes)
    sds = jax.ShapeDtypeStruct
    out = [sds(out_shape, jnp.bfloat16)] + ([sds(weight_shape, jnp.bfloat16)] if mode == "first" else [])
    scratch = [pltpu.VMEM(out_shape, jnp.bfloat16), pltpu.SemaphoreType.DMA((4,))]
    spread_shape = (tiles_lon + LON_REACH, tiles_lat + LAT_REACH, rows, lanes)
    scratch += [pltpu.VMEM(spread_shape, jnp.float32)]
    scratch += [pltpu.VMEM(weight_shape, jnp.bfloat16)] * (mode == "first")
    return call(
        functools.partial(spatial_kernel, mode, step, *tile),
        out,
        operands,
        "vv" + "v" * with_stencil + "v" * (mode == "mid"),
        "h" * len(out),
        scratch=scratch,
        flops=2**22,
        moved=2**20,
        limit=max(8, 14 * tiles_lon * tiles_lat * rows * lanes * 4 // MIB),
    )


def halved(value, axis, bit, dim):
    count = lax.axis_size(axis)
    mine = lax.axis_index(axis) >> bit & 1
    kept = lax.dynamic_index_in_dim(value, mine, dim, keepdims=False)
    sent = lax.dynamic_index_in_dim(value, 1 - mine, dim, keepdims=False).astype(jnp.bfloat16)
    arrived = lax.ppermute(sent, axis, [(i, i ^ (1 << bit)) for i in range(count)])
    return kept + arrived.astype(jnp.float32)


def scattered(value, lat_first):
    channels, hid = value.shape
    lon_bits = lax.axis_size("lon").bit_length() - 1
    lat_bits = lax.axis_size("lat").bit_length() - 1
    rows = channels >> lon_bits
    value = value.reshape(*([2] * lon_bits), rows, *([2] * lat_bits), hid >> lat_bits)

    def over_lon(value, bit, left):
        return halved(value, "lon", bit, left.index(bit)), [k for k in left if k != bit]

    left_lon = list(range(lon_bits))[::-1]
    left_lat = list(range(lat_bits))[::-1]
    order = [("lon", 0), ("lon", 1)] + [("lat", k) for k in range(lat_bits)]
    if lat_first:
        order = [("lon", 0)] + [("lat", k) for k in range(lat_bits)] + [("lon", 1)]
    order += [("lon", k) for k in range(2, lon_bits)]
    for axis, bit in order:
        if axis == "lon":
            value, left_lon = over_lon(value, bit, left_lon)
        else:
            value = halved(value, "lat", bit, len(left_lon) + 1 + left_lat.index(bit))
            left_lat.remove(bit)
    return value


def add_parts(pairs, kept, arrived):
    for q, out_ref, place in pairs:
        value = kept(q).astype(jnp.float32) + arrived(q).astype(jnp.float32)
        out_ref[place] = value.astype(out_ref.dtype)


def first_axis(flip):
    core = lon_bit(0)
    return 1 - core if flip else core


def quadrant_kernel(flip, *refs):
    kept_ref, *total_refs, arrived_ref, send_ref, keep_ref = refs[: 4 + len(refs) // 6]
    axis, x, lat = first_axis(flip), lon_bit(1), lax.axis_index("lat")
    rows = kept_ref.shape[1]
    for j in range(2):
        kept = (1 - axis) * (2 * x + j) + axis * (2 * j + lat)
        sent = (1 - axis) * (2 * (1 - x) + j) + axis * (2 * j + 1 - lat)
        pairs = [(sent, send_ref, pl.ds(j * rows, rows)), (kept, keep_ref, j)]
        arrived = lambda q: arrived_ref[pl.ds(pl.multiple_of(q * rows, rows), rows)]
        add_parts(pairs, lambda q: kept_ref[q], arrived)
    if total_refs:
        chip = total_refs[0][...] + whole_of(arrived_ref[QUADRANTS * rows :])
        refs[-1][...] = chip
        send_ref[2 * rows :] = pieces_of(chip)


def half_kernel(flip, *refs):
    kept_ref, *total_refs, arrived_ref, send_ref, keep_ref = refs[: 4 + len(refs) // 6]
    axis, x, lat = first_axis(flip), lon_bit(1), lax.axis_index("lat")
    mine = (1 - axis) * lat + axis * x
    rows = kept_ref.shape[1]
    pairs = [(1 - mine, send_ref, pl.ds(0, rows)), (mine, keep_ref, slice(None))]
    arrived = lambda q: arrived_ref[pl.ds(pl.multiple_of(q * rows, rows), rows)]
    add_parts(pairs, lambda q: kept_ref[q], arrived)
    if total_refs:
        beside = arrived_ref[2 * rows :]
        refs[-1][...] = whole_of(beside)
        send_ref[rows : rows + SUM_ROWS] = pieces_of(total_refs[0][...])
        send_ref[rows + SUM_ROWS :] = beside


def rows_kernel(groups, bit_at, totals, *refs):
    kept_ref, *refs = refs
    total_refs, (arrived_ref, send_ref, keep_ref, *total_ref) = refs[:totals], refs[totals:]
    bit = lon_bit(bit_at)
    rows = kept_ref.shape[0]
    chunk = rows // (2 * groups)
    for p in range(groups):
        goal = pl.ds(p * chunk, chunk)
        places = [pl.multiple_of((2 * p + which) * chunk, chunk) for which in (1 - bit, bit)]
        pairs = [(places[0], send_ref, goal), (places[1], keep_ref, goal)]
        add_parts(pairs, lambda q: kept_ref[pl.ds(q, chunk)], lambda q: arrived_ref[pl.ds(q, chunk)])
    if totals:
        total = add_sums(total_refs, arrived_ref, rows)
        total_ref[0][...] = total
        send_ref[rows // 2 :] = pieces_of(total)


def add_sums(total_refs, arrived_ref, start):
    arrived = whole_of(arrived_ref[start : start + SUM_ROWS])
    if len(total_refs) == 1:
        return total_refs[0][...] + arrived
    chip, beside = (ref[...] for ref in total_refs)
    return (chip + whole_of(arrived_ref[start + SUM_ROWS :])) + (beside + arrived)


def finish_kernel(kept_ref, total_ref, arrived_ref, kept_down_ref, arrived_down_ref, *refs):
    *goals, up_ref, down_ref, taps_ref, gain_ref, sems = refs
    rows = kept_ref.shape[0]
    total = add_sums([total_ref], arrived_ref, rows)
    for k in range(9):
        taps_ref[k // 3, k % 3 : k % 3 + 1] = total[k : k + 1]
    gain_ref[...] = total[9:10]
    up_ref[...] = kept_ref[...] + arrived_ref[:rows].astype(jnp.float32)
    down_ref[...] = kept_down_ref[...] + arrived_down_ref[...].astype(jnp.float32)
    finish(copies(sems, 0, list(zip((up_ref, down_ref, taps_ref, gain_ref), goals))))


def halving(flip, send, keep, total):
    lon, lat = lax.axis_size("lon"), lax.axis_size("lat")
    places = [(i, j) for i in range(lon) for j in range(lat)]
    flat = lambda i, j: i * lat + j
    along_lat = lambda i: (i & 1) != flip
    sds = jax.ShapeDtypeStruct
    rows, width = keep.shape[1:]
    sums = [] if total is None else [total]
    with_sums = len(sums)
    plan = [
        (lambda i, j: (i ^ 1, j), functools.partial(quadrant_kernel, flip), (2, rows, width), 1),
        (
            lambda i, j: (i, j ^ 1) if along_lat(i) else (i ^ 2, j),
            functools.partial(half_kernel, flip),
            (rows, width),
            2,
        ),
        (
            lambda i, j: (i ^ 2, j) if along_lat(i) else (i, j ^ 1),
            functools.partial(rows_kernel, 2, 2, 2 * with_sums),
            (rows // 2, width),
            1,
        ),
        (lambda i, j: (i ^ 4, j), functools.partial(rows_kernel, 1, 3, with_sums), (rows // 4, width), 1),
    ]
    for at, (partner, kernel, shape, parts) in enumerate(plan):
        send = yield send
        arrived = lax.ppermute(send, AXES, [(flat(i, j), flat(*partner(i, j))) for i, j in places])
        arrived = yield arrived
        sent = shape[-2] * (shape[0] if len(shape) == 3 else 1) + SUM_ROWS * parts * with_sums
        out = [sds((sent, shape[-1]), jnp.bfloat16), sds(shape, jnp.float32)]
        out += [sds(value.shape, jnp.float32) for value in sums[:1]]
        operands = [keep, *sums, arrived]
        send, keep, *more = call(kernel, out, operands, "v" * len(operands), "p" * len(out), moved=2**19, limit=12)
        sums = sums + more if at == 1 else more
    send = yield send
    arrived = lax.ppermute(send, AXES, [(flat(i, j), flat(i ^ 8, j)) for i, j in places])
    yield (keep, *sums, arrived)


def all_sums(up, down, total, field, kernel):
    channels = total.shape[1]
    field = field[None]
    if up[1].ndim == 2:
        parts = [scattered(send.astype(jnp.float32), flip) for flip, (send, _) in enumerate((up, down))]
        total = lax.psum(total, AXES)
        around = lat_edges(field)
        state = final_parts(field[0], (*around, *lon_edges(field, *around)), kernel)
        return (state, *parts, total[:9].reshape(3, 3, channels), total[9])
    ahead, behind = halving(False, *up, total), halving(True, *down, None)
    send, later = next(ahead), next(behind)
    arrived = ahead.send(send)
    send = ahead.send(after(arrived, later))
    field = after(field, send)
    arrived_later = behind.send(after(later, send))
    later = behind.send(arrived_later)
    around = lat_edges(field, lambda value: after(value, later))
    state = final_parts(field[0], (*around, *lon_edges(field, *around)), kernel)
    for at in range(1, 4):
        arrived = ahead.send(send)
        arrived_later = behind.send(later)
        send = ahead.send(after(arrived, later))
        later = behind.send(arrived_later)
    final_ahead = ahead.send(send)
    final_behind = behind.send(later)
    sds = jax.ShapeDtypeStruct
    part = sds(final_ahead[0].shape, jnp.float32)
    out = [part, part, sds((3, 3, channels), jnp.float32), sds((1, channels), jnp.float32)]
    up, down, taps, gain = call(
        finish_kernel,
        out,
        [*final_ahead, *final_behind],
        "vvvvv",
        "hhhh",
        scratch=[pltpu.VMEM(value.shape, value.dtype) for value in out] + [pltpu.SemaphoreType.DMA((4,))],
        moved=2**18,
    )
    return state, up, down, taps, gain.reshape(channels)


def local(cotangent, states, w_up, w_down, norm_gain, kernel, bilinear, lon_move, lat_move):
    steps, rows_out, cols_out, channels = states.shape
    tiles_lon, tiles_lat = lax.axis_size("lon"), lax.axis_size("lat")
    devices = tiles_lon * tiles_lat
    count = rows_out * cols_out
    tile = (rows_out, cols_out)
    share = channels // devices
    padded_share = -(-share // ROWS) * ROWS
    whole_share = share == padded_share
    group_size = channels // lon_move.shape[1]
    me = lax.axis_index("lon") * tiles_lat + lax.axis_index("lat")

    def as_blocks(value):
        value = value.reshape(devices, share, count)
        return value if whole_share else jnp.pad(value, ((0, 0), (0, padded_share - share), (0, 0)))

    def as_rows(blocks):
        return blocks[:, :share].reshape(channels, count)

    def as_grid(blocks):
        return blocks.reshape(tiles_lon, tiles_lat, *blocks.shape[1:])

    blocks = packed(cotangent, bilinear, devices)
    blocks, states_later = lax.optimization_barrier((blocks, states))
    arrived = as_grid(exchanged(blocks))
    group = me * share // group_size
    moves = jnp.stack([lon_move[:, group], lat_move[:, group]], axis=1).reshape(2 * steps, 1)
    moves = jnp.broadcast_to(jnp.pad(moves, ((0, -2 * steps % 8), (0, 0))), (-(-2 * steps // 8) * 8, 128))
    grid_now, weights = spatial("first", steps - 1, tile, padded_share, arrived, None, None, moves)

    taps = lax.dynamic_slice_in_dim(kernel.reshape(9, channels), me * share, share, 1).T
    taps = jnp.pad(taps, ((0, padded_share - share), (0, count - 9)))

    around = lat_edges(states_later)
    around = (*around, *lon_edges(states, *around))
    order = list(reversed(range(steps)))
    gain = norm_gain.reshape(1, channels)
    forward = {s: forward_parts(s, states, around, kernel, gain, w_up) for s in order}
    names = {k: {s: forward[s][at] for s in order} for at, k in enumerate(FORWARD)}

    def taken_back(grid):
        return as_rows(exchanged(grid.reshape(devices, padded_share, count)))

    def spread_on(s, field, grid_kernel=taps):
        (near,) = fetched([weights], field)
        arrived = after(as_grid(exchanged(as_blocks(field))), near)
        return spatial("mid", s, tile, padded_share, arrived, grid_kernel, near, moves)[0]

    fields, grads, moved = {}, {}, {}
    for s in order:
        if s != order[0]:
            grid_now = spread_on(s, fields[s + 1])
        here = taken_back(grid_now)
        wanted = ("slope", "n", "inv") + ("pad",) * (s == order[-1])
        near = fetched([names[k][s] for k in wanted], grid_now)
        if s == order[-1]:
            break
        here = after(here, (near, forward) if s != order[0] else near)
        fields[s], grads[s], moved[s] = network_back(here, w_down, w_up, gain, *near)

    earlier = lambda values: [values[s] for s in order[:-1]]
    all_of = lambda values: [values[s] for s in order]
    sums = channel_sums(tile, w_up, gain, *map(earlier, (names["pad"], fields, grads, names["n"])))
    here = after(here, (near, sums))
    field, total, send, keep = last_step(tile, here, w_down, w_up, gain, sums, near, all_of(names["turned"]), earlier(grads))
    down = down_gradients(here, earlier(moved), all_of(names["hid"]))
    field = field.reshape(cotangent.shape)
    return all_sums((send, keep), down, total, field, kernel)


def solution(mesh):
    placed = (
        P("lon", "lat", None),
        P(None, "lon", "lat", None),
        P(),
        P(),
        P(),
        P(),
        P(None, None, "lon", "lat"),
        P(),
        P(),
    )
    return jax.shard_map(
        local,
        mesh=mesh,
        in_specs=placed,
        out_specs=(P("lon", "lat", None), P("lon", "lat"), P("lon", "lat"), P(), P()),
        check_vma=False,
    )
```

```python
import functools

import jax
import jax.numpy as jnp
from jax import lax
from jax.experimental import pallas as pl
from jax.experimental.pallas import tpu as pltpu
from jax.sharding import PartitionSpec as P

EPSILON = 1e-06
AXES = ("lon", "lat")
ROWS = 16
LAT_REACH = 2
LON_REACH = 8
MIB = 1024 * 1024


def exchanged(blocks):
    return lax.all_to_all(blocks, AXES, split_axis=0, concat_axis=0, tiled=True)


SPACES = {"s": pltpu.SMEM, "v": pltpu.VMEM, "p": pltpu.VMEM, "h": pltpu.HBM}
PINNED = {"p": pltpu.VMEM, "h": pltpu.HBM}


def call(kernel, out_shape, operands, ins, outs, scratch=(), flops=0, moved=0, limit=8):
    operands = [
        pltpu.with_memory_space_constraint(value, PINNED[kind]) if kind in PINNED else value
        for kind, value in zip(ins, operands, strict=True)
    ]
    out_shape = [
        PINNED[kind](value.shape, value.dtype) if kind in PINNED else value
        for kind, value in zip(outs, out_shape, strict=True)
    ]
    return pl.pallas_call(
        kernel,
        out_shape=out_shape,
        in_specs=[pl.BlockSpec(memory_space=SPACES[kind]) for kind in ins],
        out_specs=[pl.BlockSpec(memory_space=SPACES[kind]) for kind in outs],
        scratch_shapes=scratch,
        compiler_params=pltpu.CompilerParams(vmem_limit_bytes=limit * MIB),
        cost_estimate=pl.CostEstimate(flops=flops, bytes_accessed=moved, transcendentals=0),
    )(*operands)


def copies(sems, first, pairs):
    started = [pltpu.make_async_copy(src, dst, sems.at[first + k]) for k, (src, dst) in enumerate(pairs)]
    for copy in started:
        copy.start()
    return started


def finish(started):
    for copy in started:
        copy.wait()


PIECES = 3
SUMS = 10
SUM_ROWS = 32


def pieces_of(value):
    value = value[:SUMS]
    parts = []
    for _ in range(PIECES):
        parts.append(value.astype(jnp.bfloat16).astype(jnp.float32))
        value = value - parts[-1]
    parts.append(jnp.zeros((SUM_ROWS - PIECES * SUMS, value.shape[1]), jnp.float32))
    return jnp.concatenate(parts, axis=0).astype(jnp.bfloat16)


def whole_of(parts):
    parts = parts.astype(jnp.float32)
    total = (parts[:SUMS] + parts[SUMS : 2 * SUMS]) + parts[2 * SUMS : 3 * SUMS]
    return jnp.concatenate([total, jnp.zeros((ROWS - SUMS, parts.shape[1]), jnp.float32)], axis=0)


def after(value, first):
    return lax.optimization_barrier((value, first))[0]


def pack_kernel(cotangent_hbm, weight_hbm, out_hbm, cotangent_ref, weight_ref, out_ref, sems):
    started = copies(sems, 0, [(cotangent_hbm, cotangent_ref), (weight_hbm, weight_ref)])
    channels = cotangent_ref.shape[1]
    devices, _, count = out_ref.shape
    share = channels // devices
    started[1].wait()
    rows = weight_ref.shape[0]
    weights = jnp.concatenate([weight_ref[:, i] for i in range(weight_ref.shape[1])], axis=1)
    weights = jnp.concatenate([weights, jnp.zeros((ROWS - rows, count), jnp.float32)], axis=0)
    weights = weights.astype(jnp.bfloat16)
    out_ref[:, share:] = jnp.broadcast_to(weights[None], (devices, ROWS, count))
    started[0].wait()
    turned = cotangent_ref[...].astype(jnp.float32).T.astype(jnp.bfloat16)
    out_ref[:, :share] = turned.reshape(devices, share, count)
    finish(copies(sems, 2, [(out_ref, out_hbm)]))


def packed(cotangent, bilinear, devices):
    rows_out, cols_out, channels = cotangent.shape
    steps, corners = bilinear.shape[:2]
    count = rows_out * cols_out
    share = channels // devices
    if share % ROWS:
        blocks = cotangent.reshape(count, channels).T.reshape(devices, share, count)
        blocks = jnp.pad(blocks, ((0, 0), (0, -share % ROWS), (0, 0)))
        weights = bilinear.reshape(steps * corners, count).astype(jnp.bfloat16)
        weights = jnp.pad(weights, ((0, ROWS - steps * corners), (0, 0)))
        return jnp.concatenate([blocks, jnp.broadcast_to(weights[None], (devices, ROWS, count))], axis=1)
    shape = (devices, share + ROWS, count)
    return call(
        pack_kernel,
        [jax.ShapeDtypeStruct(shape, jnp.bfloat16)],
        [cotangent.reshape(count, channels), bilinear.reshape(steps * corners, rows_out, cols_out)],
        "hh",
        "h",
        scratch=[
            pltpu.VMEM((count, channels), jnp.bfloat16),
            pltpu.VMEM((steps * corners, rows_out, cols_out), jnp.float32),
            pltpu.VMEM(shape, jnp.bfloat16),
            pltpu.SemaphoreType.DMA((3,)),
        ],
        moved=2**19,
    )[0]


def lat_edges(states, held=lambda value: value):
    lat, lat_at = lax.axis_size("lat"), lax.axis_index("lat")
    first, last = states[:, :, :1], states[:, :, -1:]
    if lat == 2:
        arrived = lax.ppermute(jnp.where(lat_at == 0, last, first), "lat", [(0, 1), (1, 0)])
        arrived = held(arrived)
        return jnp.where(lat_at == 0, 0, arrived), jnp.where(lat_at == 0, arrived, 0)
    return (
        lax.ppermute(last, "lat", [(i, i + 1) for i in range(lat - 1)]),
        lax.ppermute(first, "lat", [(i + 1, i) for i in range(lat - 1)]),
    )


def lon_edges(states, before, after):
    lon = lax.axis_size("lon")
    even = lax.axis_index("lon") % 2 == 0
    row = lambda place: jnp.concatenate([part[:, place] for part in (before, states, after)], axis=2)
    first, last = row(slice(0, 1)), row(slice(-1, None))
    with_next = lax.ppermute(jnp.where(even, last, first), "lon", [(i, i ^ 1) for i in range(lon)])
    pairs = [(i, (i - 1) % lon if i % 2 == 0 else (i + 1) % lon) for i in range(lon)]
    with_last = lax.ppermute(jnp.where(even, first, last), "lon", pairs)
    return jnp.where(even, with_last, with_next), jnp.where(even, with_next, with_last)


MARGIN = 8


def forward_math(step, places, sems, leaving, outs):
    states_ref, before_ref, after_ref, low_ref, high_ref, kernel_ref, gain_ref, up_ref = places
    n_ref, turned_ref, inv_ref, hid_ref, slope_ref, pad_ref, wide_ref = outs
    rows_out, cols_out, channels = states_ref.shape[1:]
    count = rows_out * cols_out
    mixed = states_ref[step].astype(jnp.float32)
    fill_margins(wide_ref, before_ref[step], after_ref[step], low_ref[step], high_ref[step], mixed)
    pad_ref[...] = wide_ref[...].astype(jnp.bfloat16)
    leaving("pad")
    for col_tap in range(3):
        place = MARGIN - 1 + col_tap
        shifted_cols = wide_ref[:, place : place + cols_out]
        for row_tap in range(3):
            tap = kernel_ref[row_tap, col_tap : col_tap + 1]
            mixed = mixed + tap[None] * shifted_cols[row_tap : row_tap + rows_out]
    mixed = mixed.reshape(count, channels)
    inv_root = lax.rsqrt(jnp.mean(mixed * mixed, axis=1, keepdims=True) + EPSILON)
    narrow = mixed * inv_root * gain_ref[...]
    n_ref[...] = narrow.astype(jnp.bfloat16)
    inv_ref[...] = jnp.broadcast_to(inv_root, inv_ref.shape)
    leaving("n", "inv")
    pre = jnp.dot(n_ref[...], up_ref[...], preferred_element_type=jnp.float32)
    sigmoid = jax.nn.sigmoid(pre)
    slope_ref[...] = (sigmoid * (1.0 + pre * (1.0 - sigmoid))).astype(jnp.bfloat16)
    leaving("slope")
    hid_ref[...] = (pre * sigmoid).astype(jnp.bfloat16)
    turned_ref[...] = narrow.T.astype(jnp.bfloat16)
    leaving("hid", "turned")


FORWARD = ("n", "turned", "inv", "hid", "slope", "pad")


def sender(sems, refs, goals, started):
    names = list(goals)

    def leave(*which):
        for name in which:
            if name in goals:
                started.extend(copies(sems, names.index(name), [(refs[name], goals[name])]))

    return leave


def forward_kernel(step, *refs):
    places, goals, outs, sems = refs[:8], refs[8:14], refs[14:21], refs[21]
    started = []
    leave = sender(sems, dict(zip(FORWARD, outs)), dict(zip(FORWARD, goals)), started)
    forward_math(step, places, sems, leave, outs)
    finish(started)


def forward_shapes(states, w_up):
    _, rows_out, cols_out, channels = states.shape
    hid = w_up.shape[1]
    count = rows_out * cols_out
    wide = (rows_out + 2, cols_out + 2 * MARGIN, channels)
    return [
        ((count, channels), jnp.bfloat16),
        ((channels, count), jnp.bfloat16),
        ((count, 128), jnp.float32),
        ((count, hid), jnp.bfloat16),
        ((count, hid), jnp.bfloat16),
        (wide, jnp.bfloat16),
    ]


def forward_scratch(shapes):
    scratch = [pltpu.VMEM(*shape) for shape in shapes]
    return scratch + [pltpu.VMEM(shapes[-1][0], jnp.float32)]


def forward_parts(step, states, around, kernel, norm_gain, w_up):
    shapes = forward_shapes(states, w_up)
    return call(
        functools.partial(forward_kernel, step),
        [jax.ShapeDtypeStruct(*shape) for shape in shapes],
        [states, *around, kernel, norm_gain, w_up],
        "vvvvvvvv",
        "hhhhhh",
        scratch=forward_scratch(shapes) + [pltpu.SemaphoreType.DMA((6,))],
        flops=2**27,
        moved=2**22,
        limit=12,
    )


LANES_BOTH = (((1,), (1,)), ((), ()))


def fetch_kernel(*refs):
    count = len(refs) // 2
    *pairs, sems = refs
    finish(copies(sems, 0, list(zip(pairs[:count], pairs[count:]))))


def fetched(values, first):
    values = after(values, first)
    return call(
        fetch_kernel,
        [jax.ShapeDtypeStruct(value.shape, value.dtype) for value in values],
        values,
        "h" * len(values),
        "v" * len(values),
        scratch=[pltpu.SemaphoreType.DMA((len(values),))],
        moved=2**19,
    )


def network_math(moved_ref, down_ref, up_ref, gain_ref, slope_ref, n_ref, inv_ref, out_ref, grad_ref, leave):
    leave("moved")
    moved = moved_ref[...].astype(jnp.float32).T
    grad_hidden = jnp.dot(moved.astype(jnp.bfloat16), down_ref[...], preferred_element_type=jnp.float32)
    grad_pre = (grad_hidden * slope_ref[...].astype(jnp.float32)).astype(jnp.bfloat16)
    grad_ref[...] = grad_pre
    leave("grad")
    grad_n = lax.dot_general(grad_pre, up_ref[...], LANES_BOTH, preferred_element_type=jnp.float32)
    narrow, gain = n_ref[...].astype(jnp.float32), gain_ref[...]
    mean = jnp.mean(grad_n * narrow, axis=1, keepdims=True)
    field = moved + inv_ref[:, :1] * (grad_n * gain - narrow * (mean / gain))
    out_ref[...] = field.T.astype(jnp.bfloat16)
    leave("field")


def network_kernel(moved_ref, down_ref, up_ref, gain_ref, slope_ref, n_ref, inv_ref, *refs):
    *goals, out_ref, grad_ref, sems = refs
    started = []
    names = ("field", "grad", "moved")
    leave = sender(sems, dict(zip(names, (out_ref, grad_ref, moved_ref))), dict(zip(names, goals)), started)
    network_math(moved_ref, down_ref, up_ref, gain_ref, slope_ref, n_ref, inv_ref, out_ref, grad_ref, leave)
    finish(started)


def first_kernel(step, *refs):
    (moved_ref, down_ref), places, refs = refs[:2], refs[2:10], refs[10:]
    goals, outs, (out_ref, grad_ref, sems) = refs[:7], refs[7:14], refs[14:]
    started = []
    names = ("n", "turned", "hid", "pad", "field", "grad", "moved")
    values = dict(zip(FORWARD, outs)) | {"field": out_ref, "grad": grad_ref, "moved": moved_ref}
    leave = sender(sems, values, dict(zip(names, goals)), started)
    forward_math(step, places, sems, leave, outs)
    n_ref, _, inv_ref, _, slope_ref = outs[:5]
    gain_ref, up_ref = places[6:]
    network_math(moved_ref, down_ref, up_ref, gain_ref, slope_ref, n_ref, inv_ref, out_ref, grad_ref, leave)
    finish(started)


def first_step(step, moved, w_down, states, around, kernel, norm_gain, w_up):
    shapes = forward_shapes(states, w_up)
    channels, count = moved.shape
    hid = w_down.shape[1]
    backs = [((channels, count), jnp.bfloat16), ((count, hid), jnp.bfloat16), ((channels, count), jnp.bfloat16)]
    results = [shapes[k] for k in (0, 1, 3, 5)] + backs
    return call(
        functools.partial(first_kernel, step),
        [jax.ShapeDtypeStruct(*shape) for shape in results],
        [moved, w_down, states, *around, kernel, norm_gain, w_up],
        "v" * 10,
        "h" * 7,
        scratch=forward_scratch(shapes) + [pltpu.VMEM(*shape) for shape in backs[:2]] + [pltpu.SemaphoreType.DMA((7,))],
        flops=2**28,
        moved=2**22,
        limit=16,
    )


def network_back(moved, w_down, w_up, norm_gain, slope, narrow, inv_root):
    channels, count = moved.shape
    hid = w_down.shape[1]
    shapes = [((channels, count), jnp.bfloat16), ((count, hid), jnp.bfloat16), ((channels, count), jnp.bfloat16)]
    return call(
        network_kernel,
        [jax.ShapeDtypeStruct(*shape) for shape in shapes],
        [moved, w_down, w_up, norm_gain, slope, narrow, inv_root],
        "vvvvvvv",
        "hhh",
        scratch=[pltpu.VMEM(*shape) for shape in shapes[:2]] + [pltpu.SemaphoreType.DMA((3,))],
        flops=4 * count * hid * channels,
        moved=4 * 2**20,
        limit=8,
    )


def stencil_sums(pad_ref, field, tile):
    rows_out, cols_out = tile
    field = field.reshape(rows_out, cols_out, -1)
    padded = pad_ref[...].astype(jnp.float32)
    result = [None] * 9
    for col_tap in range(3):
        place = MARGIN - 1 + col_tap
        shifted_cols = padded[:, place : place + cols_out]
        for row_tap in range(3):
            products = jnp.sum(shifted_cols[row_tap : row_tap + rows_out] * field, axis=0)
            result[3 * row_tap + col_tap] = jnp.sum(products, axis=0, keepdims=True)
    return result


def sums_rows(rows, term, gain):
    rows = rows + [jnp.sum(term, axis=0, keepdims=True) / gain, jnp.zeros((ROWS - 10, term.shape[1]), jnp.float32)]
    return jnp.concatenate(rows, axis=0)


def sums_kernel(steps, tile, up_ref, gain_ref, *refs):
    inputs, (out_ref, *refs) = refs[: 4 * steps], refs[4 * steps :]
    pads, fields, grads, narrows, sems = refs
    places = [(ref, place.at[k]) for k in range(steps) for ref, place in zip(inputs[4 * k : 4 * k + 4], refs[:4])]
    arriving = copies(sems, 0, places)
    rows, term = None, None
    for k in range(steps):
        finish(arriving[4 * k : 4 * k + 4])
        grad_n = lax.dot_general(grads[k], up_ref[...], LANES_BOTH, preferred_element_type=jnp.float32)
        product = grad_n * narrows[k].astype(jnp.float32)
        term = product if term is None else term + product
        more = stencil_sums(pads.at[k], fields[k].astype(jnp.float32).T, tile)
        rows = more if rows is None else [a + b for a, b in zip(rows, more)]
    out_ref[...] = sums_rows(rows, term, gain_ref[...])


def channel_sums(tile, w_up, norm_gain, pads, fields, grads, narrows):
    steps = len(fields)
    inputs = [value for group in zip(pads, fields, grads, narrows) for value in group]
    return call(
        functools.partial(sums_kernel, steps, tile),
        [jax.ShapeDtypeStruct((ROWS, fields[0].shape[0]), jnp.float32)],
        [w_up, norm_gain, *inputs],
        "vv" + "h" * 4 * steps,
        "v",
        scratch=[pltpu.VMEM((steps, *value.shape), value.dtype) for value in inputs[:4]]
        + [pltpu.SemaphoreType.DMA((4 * steps,))],
        moved=2**21,
        limit=12,
    )[0]


QUADRANTS = 4


def lon_bit(at):
    return lax.axis_index("lon") >> at & 1


def gradient_quadrants(left_ref, right_ref, send_ref, keep_ref):
    channels, width = left_ref.shape[0], right_ref.shape[1] // 2
    if keep_ref.ndim == 2:
        send_ref[:channels] = jnp.dot(left_ref[...], right_ref[...], preferred_element_type=jnp.float32).astype(jnp.bfloat16)
        keep_ref[...] = jnp.zeros_like(keep_ref)
        return
    size = channels // QUADRANTS
    groups = lax.axis_size("lon") // 4
    chunk = size // groups
    rows = []
    for core in (1 - lon_bit(0), lon_bit(0)):
        for x in range(2):
            for z in range(groups):
                start = pl.multiple_of((4 * z + 2 * x + core) * chunk, chunk)
                rows.append(left_ref[pl.ds(start, chunk)])
    rows = jnp.concatenate(rows, axis=0)
    value = jnp.dot(rows, right_ref[...], preferred_element_type=jnp.float32).astype(jnp.bfloat16)
    for q in range(QUADRANTS):
        x, lat = q // 2, q % 2
        columns = slice(lat * width, (lat + 1) * width)
        send_ref[q * size : (q + 1) * size] = value[x * size : (x + 1) * size, columns]
        keep_ref[q] = value[(2 + x) * size : (3 + x) * size, columns]


def quadrant_shapes(channels, hid, sums):
    if lax.axis_size("lat") != 2 or lax.axis_size("lon") != 16:
        return (channels, hid), (8, 128)
    return (channels + SUM_ROWS * sums, hid // 2), (QUADRANTS, channels // QUADRANTS, hid // 2)


def side_by_side(refs, goal_ref, axis):
    size = refs[0].shape[axis]
    places = [pl.ds(s * size, size) for s in range(len(refs))]
    return [(ref, goal_ref.at[:, place] if axis else goal_ref.at[place]) for ref, place in zip(refs, places)]


def last_kernel(steps, tile, moved_ref, down_ref, up_ref, gain_ref, sums_ref, *refs):
    slope_ref, n_ref, inv_ref, pad_ref, *refs = refs
    inputs, hidden, refs = refs[: 2 * steps - 1], refs[2 * steps - 1 : 3 * steps - 1], refs[3 * steps - 1 :]
    field_ref, total_ref, send_ref, keep_ref, hidden_ref, left_ref, right_ref, sems = refs
    count = slope_ref.shape[0]
    pairs = side_by_side(inputs[:steps], left_ref, 1) + side_by_side(inputs[steps:], right_ref, 0)
    later = copies(sems, 0, pairs)
    last = copies(sems, len(pairs), side_by_side(hidden, hidden_ref, 0))
    moved = moved_ref[...].astype(jnp.float32).T
    grad_hidden = jnp.dot(moved.astype(jnp.bfloat16), down_ref[...], preferred_element_type=jnp.float32)
    grad_pre = (grad_hidden * slope_ref[...].astype(jnp.float32)).astype(jnp.bfloat16)
    right_ref[(steps - 1) * count :] = grad_pre
    grad_n = lax.dot_general(grad_pre, up_ref[...], LANES_BOTH, preferred_element_type=jnp.float32)
    narrow, gain = n_ref[...].astype(jnp.float32), gain_ref[...]
    term = grad_n * narrow
    mean = jnp.mean(term, axis=1, keepdims=True)
    field = moved + inv_ref[:, :1] * (grad_n * gain - narrow * (mean / gain))
    field = field.astype(jnp.bfloat16)
    field_ref[...] = field
    total = sums_ref[...] + sums_rows(stencil_sums(pad_ref, field.astype(jnp.float32), tile), term, gain)
    total_ref[...] = total
    finish(later)
    gradient_quadrants(left_ref, right_ref, send_ref, keep_ref)
    if keep_ref.ndim > 2:
        send_ref[left_ref.shape[0] :] = pieces_of(total)
    finish(last)


def last_step(tile, moved, w_down, w_up, norm_gain, sums, near, turned, grads, hidden):
    steps = len(turned)
    channels, count = moved.shape
    hid = w_down.shape[1]
    send, keep = quadrant_shapes(channels, hid, 1)
    sds = jax.ShapeDtypeStruct
    inputs = turned + grads + hidden
    return call(
        functools.partial(last_kernel, steps, tile),
        [
            sds((count, channels), jnp.bfloat16),
            sds((ROWS, channels), jnp.float32),
            sds(send, jnp.bfloat16),
            sds(keep, jnp.bfloat16),
            sds((steps * count, hid), jnp.bfloat16),
        ],
        [moved, w_down, w_up, norm_gain, sums, *near, *inputs],
        "v" * 9 + "h" * len(inputs),
        "vpppv",
        scratch=[pltpu.VMEM((channels, steps * count), jnp.bfloat16), pltpu.VMEM((steps * count, hid), jnp.bfloat16)]
        + [pltpu.SemaphoreType.DMA((len(inputs),))],
        flops=2**30,
        moved=6 * 2**20,
        limit=20,
    )


def down_kernel(steps, moved_ref, right_ref, *refs):
    inputs, (send_ref, keep_ref, left_ref, sems) = refs[: steps - 1], refs[steps - 1 :]
    count = moved_ref.shape[1]
    arriving = copies(sems, 0, side_by_side(inputs, left_ref, 1))
    left_ref[:, (steps - 1) * count :] = moved_ref[...]
    finish(arriving)
    gradient_quadrants(left_ref, right_ref, send_ref, keep_ref)


def down_gradients(moved, moveds, hidden):
    steps = 1 + len(moveds)
    channels, count = moved.shape
    hid = hidden.shape[1]
    return call(
        functools.partial(down_kernel, steps),
        [jax.ShapeDtypeStruct(shape, jnp.bfloat16) for shape in quadrant_shapes(channels, hid, 0)],
        [moved, hidden, *moveds],
        "vv" + "h" * len(moveds),
        "pp",
        scratch=[pltpu.VMEM((channels, steps * count), jnp.bfloat16), pltpu.SemaphoreType.DMA((len(moveds),))],
        flops=2**29,
        moved=2**21,
        limit=16,
    )


def fill_margins(wide_ref, before, after, low, high, middle):
    rows_out, cols_out, _ = middle.shape
    around = slice(MARGIN - 1, MARGIN + cols_out + 1)
    wide_ref[:1, around] = low.astype(jnp.float32)
    wide_ref[1 + rows_out :, around] = high.astype(jnp.float32)
    wide_ref[1 : 1 + rows_out, MARGIN - 1 : MARGIN] = before.astype(jnp.float32)
    wide_ref[1 : 1 + rows_out, MARGIN + cols_out : MARGIN + cols_out + 1] = after.astype(jnp.float32)
    wide_ref[1 : 1 + rows_out, MARGIN : MARGIN + cols_out] = middle


def final_kernel(field_ref, before_ref, after_ref, low_ref, high_ref, kernel_ref, out_ref, wide_ref):
    rows_out, cols_out, _ = field_ref.shape
    result = field_ref[...].astype(jnp.float32)
    fill_margins(wide_ref, before_ref[0], after_ref[0], low_ref[0], high_ref[0], result)
    for col_tap in range(3):
        place = MARGIN + 1 - col_tap
        shifted_cols = wide_ref[:, place : place + cols_out]
        for row_tap in range(3):
            tap = kernel_ref[row_tap, col_tap : col_tap + 1]
            result = result + tap[None] * shifted_cols[2 - row_tap : 2 - row_tap + rows_out]
    out_ref[...] = result.astype(jnp.bfloat16)


def final_parts(field, around, kernel):
    rows_out, cols_out, channels = field.shape
    return call(
        final_kernel,
        [jax.ShapeDtypeStruct(field.shape, jnp.bfloat16)],
        [field, *around, kernel],
        "v" * 6,
        "v",
        scratch=[pltpu.VMEM((rows_out + 2, cols_out + 2 * MARGIN, channels), jnp.float32)],
        moved=2**19,
    )[0]


def spatial_kernel(mode, step, near_lon, near_lat, *refs):
    refs = list(refs)
    take = lambda: refs.pop(0)
    with_stencil = mode != "first"
    move_ref = take()
    in_ref = take()
    kern_ref = take() if with_stencil else None
    weight_ref = take() if mode == "mid" else None
    out_hbm = take()
    saved_hbm = take() if mode == "first" else None
    out_ref, sems = take(), take()
    spread_ref = take()
    weight_ref = take() if mode == "first" else weight_ref
    tiles_lon, tiles_lat, _, lanes = in_ref.shape
    rows = out_ref.shape[2]
    started = []
    if mode == "first":
        weight_ref[...] = in_ref[:, :, rows:]
        started += copies(sems, 0, [(weight_ref, saved_hbm)])
    lane = lax.broadcasted_iota(jnp.int32, (rows, lanes), 1)
    col = lax.rem(lane, near_lat)
    lat_last, lat_first = col == near_lat - 1, col == 0
    lon_last, lon_first = lane >= lanes - near_lat, lane < near_lat
    tiles = [(a, b) for a in range(tiles_lon) for b in range(tiles_lat)]

    def turn(value, steps):
        return pltpu.roll(value, steps % lanes if isinstance(steps, int) else steps, 1)

    def lat_after(grid):
        turned = {key: turn(value, -1) for key, value in grid.items()}
        wrapped = {key: turn(grid[key], near_lat - 1) for key in tiles if key[1] > 0}
        return {(a, b): jnp.where(lat_last, wrapped.get((a, b + 1), 0.0), turned[a, b]) for a, b in tiles}

    def lat_before(grid):
        turned = {key: turn(value, 1) for key, value in grid.items()}
        wrapped = {key: turn(grid[key], 1 - near_lat) for key in tiles if key[1] < tiles_lat - 1}
        return {(a, b): jnp.where(lat_first, wrapped.get((a, b - 1), 0.0), turned[a, b]) for a, b in tiles}

    def lon_after(grid):
        return {
            (a, b): turn(jnp.where(lon_first, grid[(a + 1) % tiles_lon, b], grid[a, b]), -near_lat) for a, b in tiles
        }

    def lon_before(grid):
        return {(a, b): turn(jnp.where(lon_last, grid[(a - 1) % tiles_lon, b], grid[a, b]), near_lat) for a, b in tiles}

    grid = {(a, b): in_ref[a, b, :rows].astype(jnp.float32) for a, b in tiles}
    if with_stencil:
        taps = [
            [jnp.broadcast_to(kern_ref[:, 3 * a + b : 3 * a + b + 1], (rows, lanes)) for b in range(3)] for a in range(3)
        ]
        by_col = [lat_after(grid), grid, lat_before(grid)]
        mix = [
            {key: sum(taps[row][c] * by_col[c][key] for c in range(1, 3)) + taps[row][0] * by_col[0][key] for key in tiles}
            for row in range(3)
        ]
        high, low = lon_after(mix[0]), lon_before(mix[2])
        grid = {key: grid[key] + mix[1][key] + (high[key] + low[key]) for key in tiles}
    if mode == "mid":
        grid = {key: value.astype(jnp.bfloat16).astype(jnp.float32) for key, value in grid.items()}
    weights = {}
    for a, b in tiles:
        four = weight_ref[a, b].astype(jnp.float32)[4 * step : 4 * step + 4]
        weights[a, b] = [jnp.broadcast_to(four[k : k + 1], (rows, lanes)) for k in range(4)]
    weighted = [{key: weights[key][k] * grid[key] for key in tiles} for k in range(4)]
    own, lon = lat_after(weighted[2]), lat_after(weighted[3])
    lon = lon_after({key: weighted[1][key] + lon[key] for key in tiles})
    for a, b in tiles:
        value = (weighted[0][a, b] + own[a, b] + lon[a, b]).astype(jnp.bfloat16).astype(jnp.float32)
        for place in range(a, tiles_lon + LON_REACH, tiles_lon):
            spread_ref[place, b] = value
    spread_ref[:, tiles_lat:] = jnp.zeros((tiles_lon + LON_REACH, LAT_REACH, rows, lanes), jnp.float32)

    lon_move, lat_move = (jnp.max(move_ref[2 * step + k : 2 * step + k + 1]) for k in range(2))
    far_lon, off_lon = lon_move // near_lon, lax.rem(lon_move, near_lon)
    far_lat, off_lat = lat_move // near_lat, lax.rem(lat_move, near_lat)
    shift = off_lon * near_lat + off_lat
    turn_here = lax.rem(2 * lanes - shift, lanes)
    turn_next = lax.rem(2 * lanes - shift + near_lat, lanes)
    same_lon = lane >= off_lon * near_lat
    same_lat = col + off_lat < near_lat
    half = tiles_lon // 2
    for a in range(tiles_lon):
        met = [
            jnp.where(same_lon, spread_ref[far_lon + a, far_lat + b], spread_ref[far_lon + a + 1, far_lat + b])
            for b in range(tiles_lat + 1)
        ]
        for b in range(tiles_lat):
            value = jnp.where(same_lat, turn(met[b], turn_here), turn(met[b + 1], turn_next))
            out_ref[a, b] = value.astype(jnp.bfloat16)
        if (a + 1) % half == 0:
            part = pl.ds(a + 1 - half, half)
            started += copies(sems, 1 + a // half, [(out_ref.at[part], out_hbm.at[part])])
    finish(started)


def spatial(mode, step, tile, rows, field, kern, weights, moves):
    tiles_lon, tiles_lat, _, lanes = field.shape
    with_stencil = mode != "first"
    operands = [moves, field]
    operands += [kern] if with_stencil else []
    operands += [weights] if mode == "mid" else []
    out_shape = (tiles_lon, tiles_lat, rows, lanes)
    weight_shape = (tiles_lon, tiles_lat, ROWS, lanes)
    sds = jax.ShapeDtypeStruct
    out = [sds(out_shape, jnp.bfloat16)] + ([sds(weight_shape, jnp.bfloat16)] if mode == "first" else [])
    scratch = [pltpu.VMEM(out_shape, jnp.bfloat16), pltpu.SemaphoreType.DMA((4,))]
    spread_shape = (tiles_lon + LON_REACH, tiles_lat + LAT_REACH, rows, lanes)
    scratch += [pltpu.VMEM(spread_shape, jnp.float32)]
    scratch += [pltpu.VMEM(weight_shape, jnp.bfloat16)] * (mode == "first")
    return call(
        functools.partial(spatial_kernel, mode, step, *tile),
        out,
        operands,
        "vv" + "v" * with_stencil + "v" * (mode == "mid"),
        "h" * len(out),
        scratch=scratch,
        flops=2**22,
        moved=2**20,
        limit=max(8, 14 * tiles_lon * tiles_lat * rows * lanes * 4 // MIB),
    )


def halved(value, axis, bit, dim):
    count = lax.axis_size(axis)
    mine = lax.axis_index(axis) >> bit & 1
    kept = lax.dynamic_index_in_dim(value, mine, dim, keepdims=False)
    sent = lax.dynamic_index_in_dim(value, 1 - mine, dim, keepdims=False).astype(jnp.bfloat16)
    arrived = lax.ppermute(sent, axis, [(i, i ^ (1 << bit)) for i in range(count)])
    return kept + arrived.astype(jnp.float32)


def scattered(value, lat_first):
    channels, hid = value.shape
    lon_bits = lax.axis_size("lon").bit_length() - 1
    lat_bits = lax.axis_size("lat").bit_length() - 1
    rows = channels >> lon_bits
    value = value.reshape(*([2] * lon_bits), rows, *([2] * lat_bits), hid >> lat_bits)

    def over_lon(value, bit, left):
        return halved(value, "lon", bit, left.index(bit)), [k for k in left if k != bit]

    left_lon = list(range(lon_bits))[::-1]
    left_lat = list(range(lat_bits))[::-1]
    order = [("lon", 0), ("lon", 1)] + [("lat", k) for k in range(lat_bits)]
    if lat_first:
        order = [("lon", 0)] + [("lat", k) for k in range(lat_bits)] + [("lon", 1)]
    order += [("lon", k) for k in range(2, lon_bits)]
    for axis, bit in order:
        if axis == "lon":
            value, left_lon = over_lon(value, bit, left_lon)
        else:
            value = halved(value, "lat", bit, len(left_lon) + 1 + left_lat.index(bit))
            left_lat.remove(bit)
    return value


def add_parts(pairs, kept, arrived):
    for q, out_ref, place in pairs:
        value = kept(q).astype(jnp.float32) + arrived(q).astype(jnp.float32)
        out_ref[place] = value.astype(out_ref.dtype)


def first_axis(flip):
    core = lon_bit(0)
    return 1 - core if flip else core


def quadrant_kernel(flip, *refs):
    kept_ref, *total_refs, arrived_ref, send_ref, keep_ref = refs[: 4 + len(refs) // 6]
    axis, x, lat = first_axis(flip), lon_bit(1), lax.axis_index("lat")
    rows = kept_ref.shape[1]
    for j in range(2):
        kept = (1 - axis) * (2 * x + j) + axis * (2 * j + lat)
        sent = (1 - axis) * (2 * (1 - x) + j) + axis * (2 * j + 1 - lat)
        pairs = [(sent, send_ref, pl.ds(j * rows, rows)), (kept, keep_ref, j)]
        arrived = lambda q: arrived_ref[pl.ds(pl.multiple_of(q * rows, rows), rows)]
        add_parts(pairs, lambda q: kept_ref[q], arrived)
    if total_refs:
        chip = total_refs[0][...] + whole_of(arrived_ref[QUADRANTS * rows :])
        refs[-1][...] = chip
        send_ref[2 * rows :] = pieces_of(chip)


def half_kernel(flip, *refs):
    kept_ref, *total_refs, arrived_ref, send_ref, keep_ref = refs[: 4 + len(refs) // 6]
    axis, x, lat = first_axis(flip), lon_bit(1), lax.axis_index("lat")
    mine = (1 - axis) * lat + axis * x
    rows = kept_ref.shape[1]
    pairs = [(1 - mine, send_ref, pl.ds(0, rows)), (mine, keep_ref, slice(None))]
    arrived = lambda q: arrived_ref[pl.ds(pl.multiple_of(q * rows, rows), rows)]
    add_parts(pairs, lambda q: kept_ref[q], arrived)
    if total_refs:
        beside = arrived_ref[2 * rows :]
        refs[-1][...] = whole_of(beside)
        send_ref[rows : rows + SUM_ROWS] = pieces_of(total_refs[0][...])
        send_ref[rows + SUM_ROWS :] = beside


def rows_kernel(groups, bit_at, totals, *refs):
    kept_ref, *refs = refs
    total_refs, (arrived_ref, send_ref, keep_ref, *total_ref) = refs[:totals], refs[totals:]
    bit = lon_bit(bit_at)
    rows = kept_ref.shape[0]
    chunk = rows // (2 * groups)
    for p in range(groups):
        goal = pl.ds(p * chunk, chunk)
        places = [pl.multiple_of((2 * p + which) * chunk, chunk) for which in (1 - bit, bit)]
        pairs = [(places[0], send_ref, goal), (places[1], keep_ref, goal)]
        add_parts(pairs, lambda q: kept_ref[pl.ds(q, chunk)], lambda q: arrived_ref[pl.ds(q, chunk)])
    if totals:
        total = add_sums(total_refs, arrived_ref, rows)
        total_ref[0][...] = total
        send_ref[rows // 2 :] = pieces_of(total)


def add_sums(total_refs, arrived_ref, start):
    arrived = whole_of(arrived_ref[start : start + SUM_ROWS])
    if len(total_refs) == 1:
        return total_refs[0][...] + arrived
    chip, beside = (ref[...] for ref in total_refs)
    return (chip + whole_of(arrived_ref[start + SUM_ROWS :])) + (beside + arrived)


def finish_kernel(kept_ref, total_ref, arrived_ref, kept_down_ref, arrived_down_ref, *refs):
    *goals, up_ref, down_ref, taps_ref, gain_ref, sems = refs
    rows = kept_ref.shape[0]
    total = add_sums([total_ref], arrived_ref, rows)
    for k in range(9):
        taps_ref[k // 3, k % 3 : k % 3 + 1] = total[k : k + 1]
    gain_ref[...] = total[9:10]
    up_ref[...] = kept_ref[...] + arrived_ref[:rows].astype(jnp.float32)
    down_ref[...] = kept_down_ref[...] + arrived_down_ref[...].astype(jnp.float32)
    finish(copies(sems, 0, list(zip((up_ref, down_ref, taps_ref, gain_ref), goals))))


def halving(flip, send, keep, total):
    lon, lat = lax.axis_size("lon"), lax.axis_size("lat")
    places = [(i, j) for i in range(lon) for j in range(lat)]
    flat = lambda i, j: i * lat + j
    along_lat = lambda i: (i & 1) != flip
    sds = jax.ShapeDtypeStruct
    rows, width = keep.shape[1:]
    sums = [] if total is None else [total]
    with_sums = len(sums)
    plan = [
        (lambda i, j: (i ^ 1, j), functools.partial(quadrant_kernel, flip), (2, rows, width), 1),
        (
            lambda i, j: (i, j ^ 1) if along_lat(i) else (i ^ 2, j),
            functools.partial(half_kernel, flip),
            (rows, width),
            2,
        ),
        (
            lambda i, j: (i ^ 2, j) if along_lat(i) else (i, j ^ 1),
            functools.partial(rows_kernel, 2, 2, 2 * with_sums),
            (rows // 2, width),
            1,
        ),
        (lambda i, j: (i ^ 4, j), functools.partial(rows_kernel, 1, 3, with_sums), (rows // 4, width), 1),
    ]
    for at, (partner, kernel, shape, parts) in enumerate(plan):
        send = yield send
        arrived = lax.ppermute(send, AXES, [(flat(i, j), flat(*partner(i, j))) for i, j in places])
        arrived = yield arrived
        sent = shape[-2] * (shape[0] if len(shape) == 3 else 1) + SUM_ROWS * parts * with_sums
        out = [sds((sent, shape[-1]), jnp.bfloat16), sds(shape, jnp.float32)]
        out += [sds(value.shape, jnp.float32) for value in sums[:1]]
        operands = [keep, *sums, arrived]
        send, keep, *more = call(kernel, out, operands, "v" * len(operands), "p" * len(out), moved=2**19, limit=12)
        sums = sums + more if at == 1 else more
    send = yield send
    arrived = lax.ppermute(send, AXES, [(flat(i, j), flat(i ^ 8, j)) for i, j in places])
    yield (keep, *sums, arrived)


def all_sums(up, down, total, field, kernel):
    channels = total.shape[1]
    field = field[None]
    if up[1].ndim == 2:
        parts = [scattered(send.astype(jnp.float32), flip) for flip, (send, _) in enumerate((up, down))]
        total = lax.psum(total, AXES)
        around = lat_edges(field)
        state = final_parts(field[0], (*around, *lon_edges(field, *around)), kernel)
        return (state, *parts, total[:9].reshape(3, 3, channels), total[9])
    ahead, behind = halving(False, *up, total), halving(True, *down, None)
    send, later = next(ahead), next(behind)
    arrived = ahead.send(send)
    send = ahead.send(after(arrived, later))
    field = after(field, send)
    arrived_later = behind.send(after(later, send))
    later = behind.send(arrived_later)
    around = lat_edges(field, lambda value: after(value, later))
    state = final_parts(field[0], (*around, *lon_edges(field, *around)), kernel)
    for at in range(1, 4):
        arrived = ahead.send(send)
        arrived_later = behind.send(later)
        send = ahead.send(after(arrived, later))
        later = behind.send(arrived_later)
    final_ahead = ahead.send(send)
    final_behind = behind.send(later)
    sds = jax.ShapeDtypeStruct
    part = sds(final_ahead[0].shape, jnp.float32)
    out = [part, part, sds((3, 3, channels), jnp.float32), sds((1, channels), jnp.float32)]
    up, down, taps, gain = call(
        finish_kernel,
        out,
        [*final_ahead, *final_behind],
        "vvvvv",
        "hhhh",
        scratch=[pltpu.VMEM(value.shape, value.dtype) for value in out] + [pltpu.SemaphoreType.DMA((4,))],
        moved=2**18,
    )
    return state, up, down, taps, gain.reshape(channels)


def local(cotangent, states, w_up, w_down, norm_gain, kernel, bilinear, lon_move, lat_move):
    steps, rows_out, cols_out, channels = states.shape
    tiles_lon, tiles_lat = lax.axis_size("lon"), lax.axis_size("lat")
    devices = tiles_lon * tiles_lat
    count = rows_out * cols_out
    tile = (rows_out, cols_out)
    share = channels // devices
    padded_share = -(-share // ROWS) * ROWS
    whole_share = share == padded_share
    group_size = channels // lon_move.shape[1]
    me = lax.axis_index("lon") * tiles_lat + lax.axis_index("lat")

    def as_blocks(value):
        value = value.reshape(devices, share, count)
        return value if whole_share else jnp.pad(value, ((0, 0), (0, padded_share - share), (0, 0)))

    def as_rows(blocks):
        return blocks[:, :share].reshape(channels, count)

    def as_grid(blocks):
        return blocks.reshape(tiles_lon, tiles_lat, *blocks.shape[1:])

    blocks = packed(cotangent, bilinear, devices)
    blocks, states_later = lax.optimization_barrier((blocks, states))
    arrived = as_grid(exchanged(blocks))
    group = me * share // group_size
    moves = jnp.stack([lon_move[:, group], lat_move[:, group]], axis=1).reshape(2 * steps, 1)
    moves = jnp.broadcast_to(jnp.pad(moves, ((0, -2 * steps % 8), (0, 0))), (-(-2 * steps // 8) * 8, 128))
    grid_now, weights = spatial("first", steps - 1, tile, padded_share, arrived, None, None, moves)

    taps = lax.dynamic_slice_in_dim(kernel.reshape(9, channels), me * share, share, 1).T
    taps = jnp.pad(taps, ((0, padded_share - share), (0, count - 9)))

    around = lat_edges(states_later)
    around = (*around, *lon_edges(states, *around))
    order = list(reversed(range(steps)))
    gain = norm_gain.reshape(1, channels)
    forward = {s: forward_parts(s, states, around, kernel, gain, w_up) for s in order}
    names = {k: {s: forward[s][at] for s in order} for at, k in enumerate(FORWARD)}

    def taken_back(grid):
        return as_rows(exchanged(grid.reshape(devices, padded_share, count)))

    def spread_on(s, field, grid_kernel=taps):
        (near,) = fetched([weights], field)
        arrived = after(as_grid(exchanged(as_blocks(field))), near)
        return spatial("mid", s, tile, padded_share, arrived, grid_kernel, near, moves)[0]

    fields, grads, moved = {}, {}, {}
    for s in order:
        if s != order[0]:
            grid_now = spread_on(s, fields[s + 1])
        here = taken_back(grid_now)
        wanted = ("slope", "n", "inv") + ("pad",) * (s == order[-1])
        near = fetched([names[k][s] for k in wanted], grid_now)
        if s == order[-1]:
            break
        here = after(here, (near, forward) if s != order[0] else near)
        fields[s], grads[s], moved[s] = network_back(here, w_down, w_up, gain, *near)

    earlier = lambda values: [values[s] for s in order[:-1]]
    all_of = lambda values: [values[s] for s in order]
    sums = channel_sums(tile, w_up, gain, *map(earlier, (names["pad"], fields, grads, names["n"])))
    here = after(here, (near, sums))
    parts = (all_of(names["turned"]), earlier(grads), all_of(names["hid"]))
    field, total, send, keep, hidden = last_step(tile, here, w_down, w_up, gain, sums, near, *parts)
    down = down_gradients(here, earlier(moved), hidden)
    field = field.reshape(cotangent.shape)
    return all_sums((send, keep), down, total, field, kernel)


def solution(mesh):
    placed = (
        P("lon", "lat", None),
        P(None, "lon", "lat", None),
        P(),
        P(),
        P(),
        P(),
        P(None, None, "lon", "lat"),
        P(),
        P(),
    )
    return jax.shard_map(
        local,
        mesh=mesh,
        in_specs=placed,
        out_specs=(P("lon", "lat", None), P("lon", "lat"), P("lon", "lat"), P(), P()),
        check_vma=False,
    )
```

```python
import functools

import jax
import jax.numpy as jnp
from jax import lax
from jax.experimental import pallas as pl
from jax.experimental.pallas import tpu as pltpu
from jax.sharding import PartitionSpec as P

EPSILON = 1e-06
AXES = ("lon", "lat")
ROWS = 16
LAT_REACH = 2
LON_REACH = 8
MIB = 1024 * 1024


def exchanged(blocks):
    return lax.all_to_all(blocks, AXES, split_axis=0, concat_axis=0, tiled=True)


SPACES = {"s": pltpu.SMEM, "v": pltpu.VMEM, "p": pltpu.VMEM, "h": pltpu.HBM}
PINNED = {"p": pltpu.VMEM, "h": pltpu.HBM}


def call(kernel, out_shape, operands, ins, outs, scratch=(), flops=0, moved=0, limit=8):
    operands = [
        pltpu.with_memory_space_constraint(value, PINNED[kind]) if kind in PINNED else value
        for kind, value in zip(ins, operands, strict=True)
    ]
    out_shape = [
        PINNED[kind](value.shape, value.dtype) if kind in PINNED else value
        for kind, value in zip(outs, out_shape, strict=True)
    ]
    return pl.pallas_call(
        kernel,
        out_shape=out_shape,
        in_specs=[pl.BlockSpec(memory_space=SPACES[kind]) for kind in ins],
        out_specs=[pl.BlockSpec(memory_space=SPACES[kind]) for kind in outs],
        scratch_shapes=scratch,
        compiler_params=pltpu.CompilerParams(vmem_limit_bytes=limit * MIB),
        cost_estimate=pl.CostEstimate(flops=flops, bytes_accessed=moved, transcendentals=0),
    )(*operands)


def copies(sems, first, pairs):
    started = [pltpu.make_async_copy(src, dst, sems.at[first + k]) for k, (src, dst) in enumerate(pairs)]
    for copy in started:
        copy.start()
    return started


def finish(started):
    for copy in started:
        copy.wait()


PIECES = 3
SUMS = 10
SUM_ROWS = 32


def pieces_of(value):
    value = value[:SUMS]
    parts = []
    for _ in range(PIECES):
        parts.append(value.astype(jnp.bfloat16).astype(jnp.float32))
        value = value - parts[-1]
    parts.append(jnp.zeros((SUM_ROWS - PIECES * SUMS, value.shape[1]), jnp.float32))
    return jnp.concatenate(parts, axis=0).astype(jnp.bfloat16)


def whole_of(parts):
    parts = parts.astype(jnp.float32)
    total = (parts[:SUMS] + parts[SUMS : 2 * SUMS]) + parts[2 * SUMS : 3 * SUMS]
    return jnp.concatenate([total, jnp.zeros((ROWS - SUMS, parts.shape[1]), jnp.float32)], axis=0)


def after(value, first):
    return lax.optimization_barrier((value, first))[0]


def pack_kernel(cotangent_hbm, weight_hbm, out_hbm, cotangent_ref, weight_ref, out_ref, sems):
    started = copies(sems, 0, [(cotangent_hbm, cotangent_ref), (weight_hbm, weight_ref)])
    channels = cotangent_ref.shape[1]
    devices, _, count = out_ref.shape
    share = channels // devices
    started[1].wait()
    rows = weight_ref.shape[0]
    weights = jnp.concatenate([weight_ref[:, i] for i in range(weight_ref.shape[1])], axis=1)
    weights = jnp.concatenate([weights, jnp.zeros((ROWS - rows, count), jnp.float32)], axis=0)
    weights = weights.astype(jnp.bfloat16)
    out_ref[:, share:] = jnp.broadcast_to(weights[None], (devices, ROWS, count))
    started[0].wait()
    turned = cotangent_ref[...].astype(jnp.float32).T.astype(jnp.bfloat16)
    out_ref[:, :share] = turned.reshape(devices, share, count)
    finish(copies(sems, 2, [(out_ref, out_hbm)]))


def packed(cotangent, bilinear, devices):
    rows_out, cols_out, channels = cotangent.shape
    steps, corners = bilinear.shape[:2]
    count = rows_out * cols_out
    share = channels // devices
    if share % ROWS:
        blocks = cotangent.reshape(count, channels).T.reshape(devices, share, count)
        blocks = jnp.pad(blocks, ((0, 0), (0, -share % ROWS), (0, 0)))
        weights = bilinear.reshape(steps * corners, count).astype(jnp.bfloat16)
        weights = jnp.pad(weights, ((0, ROWS - steps * corners), (0, 0)))
        return jnp.concatenate([blocks, jnp.broadcast_to(weights[None], (devices, ROWS, count))], axis=1)
    shape = (devices, share + ROWS, count)
    return call(
        pack_kernel,
        [jax.ShapeDtypeStruct(shape, jnp.bfloat16)],
        [cotangent.reshape(count, channels), bilinear.reshape(steps * corners, rows_out, cols_out)],
        "hh",
        "h",
        scratch=[
            pltpu.VMEM((count, channels), jnp.bfloat16),
            pltpu.VMEM((steps * corners, rows_out, cols_out), jnp.float32),
            pltpu.VMEM(shape, jnp.bfloat16),
            pltpu.SemaphoreType.DMA((3,)),
        ],
        moved=2**19,
    )[0]


def lat_edges(states, held=lambda value: value):
    lat, lat_at = lax.axis_size("lat"), lax.axis_index("lat")
    first, last = states[:, :, :1], states[:, :, -1:]
    if lat == 2:
        arrived = lax.ppermute(jnp.where(lat_at == 0, last, first), "lat", [(0, 1), (1, 0)])
        arrived = held(arrived)
        return jnp.where(lat_at == 0, 0, arrived), jnp.where(lat_at == 0, arrived, 0)
    return (
        lax.ppermute(last, "lat", [(i, i + 1) for i in range(lat - 1)]),
        lax.ppermute(first, "lat", [(i + 1, i) for i in range(lat - 1)]),
    )


def lon_edges(states, before, after):
    lon = lax.axis_size("lon")
    even = lax.axis_index("lon") % 2 == 0
    row = lambda place: jnp.concatenate([part[:, place] for part in (before, states, after)], axis=2)
    first, last = row(slice(0, 1)), row(slice(-1, None))
    with_next = lax.ppermute(jnp.where(even, last, first), "lon", [(i, i ^ 1) for i in range(lon)])
    pairs = [(i, (i - 1) % lon if i % 2 == 0 else (i + 1) % lon) for i in range(lon)]
    with_last = lax.ppermute(jnp.where(even, first, last), "lon", pairs)
    return jnp.where(even, with_last, with_next), jnp.where(even, with_next, with_last)


MARGIN = 8


def forward_math(step, places, sems, leaving, outs):
    states_ref, before_ref, after_ref, low_ref, high_ref, kernel_ref, gain_ref, up_ref = places
    n_ref, turned_ref, inv_ref, hid_ref, slope_ref, pad_ref, wide_ref = outs
    rows_out, cols_out, channels = states_ref.shape[1:]
    count = rows_out * cols_out
    mixed = states_ref[step].astype(jnp.float32)
    fill_margins(wide_ref, before_ref[step], after_ref[step], low_ref[step], high_ref[step], mixed)
    pad_ref[...] = wide_ref[...].astype(jnp.bfloat16)
    leaving("pad")
    for col_tap in range(3):
        place = MARGIN - 1 + col_tap
        shifted_cols = wide_ref[:, place : place + cols_out]
        for row_tap in range(3):
            tap = kernel_ref[row_tap, col_tap : col_tap + 1]
            mixed = mixed + tap[None] * shifted_cols[row_tap : row_tap + rows_out]
    mixed = mixed.reshape(count, channels)
    inv_root = lax.rsqrt(jnp.mean(mixed * mixed, axis=1, keepdims=True) + EPSILON)
    narrow = mixed * inv_root * gain_ref[...]
    n_ref[...] = narrow.astype(jnp.bfloat16)
    inv_ref[...] = jnp.broadcast_to(inv_root, inv_ref.shape)
    leaving("n", "inv")
    pre = jnp.dot(n_ref[...], up_ref[...], preferred_element_type=jnp.float32)
    sigmoid = jax.nn.sigmoid(pre)
    slope_ref[...] = (sigmoid * (1.0 + pre * (1.0 - sigmoid))).astype(jnp.bfloat16)
    leaving("slope")
    hid_ref[...] = (pre * sigmoid).astype(jnp.bfloat16)
    turned_ref[...] = narrow.T.astype(jnp.bfloat16)
    leaving("hid", "turned")


FORWARD = ("n", "turned", "inv", "hid", "slope", "pad")


def sender(sems, refs, goals, started):
    names = list(goals)

    def leave(*which):
        for name in which:
            if name in goals:
                started.extend(copies(sems, names.index(name), [(refs[name], goals[name])]))

    return leave


def forward_kernel(step, *refs):
    places, goals, outs, sems = refs[:8], refs[8:14], refs[14:21], refs[21]
    started = []
    leave = sender(sems, dict(zip(FORWARD, outs)), dict(zip(FORWARD, goals)), started)
    forward_math(step, places, sems, leave, outs)
    finish(started)


def forward_shapes(states, w_up):
    _, rows_out, cols_out, channels = states.shape
    hid = w_up.shape[1]
    count = rows_out * cols_out
    wide = (rows_out + 2, cols_out + 2 * MARGIN, channels)
    return [
        ((count, channels), jnp.bfloat16),
        ((channels, count), jnp.bfloat16),
        ((count, 128), jnp.float32),
        ((count, hid), jnp.bfloat16),
        ((count, hid), jnp.bfloat16),
        (wide, jnp.bfloat16),
    ]


def forward_scratch(shapes):
    scratch = [pltpu.VMEM(*shape) for shape in shapes]
    return scratch + [pltpu.VMEM(shapes[-1][0], jnp.float32)]


def forward_parts(step, states, around, kernel, norm_gain, w_up):
    shapes = forward_shapes(states, w_up)
    return call(
        functools.partial(forward_kernel, step),
        [jax.ShapeDtypeStruct(*shape) for shape in shapes],
        [states, *around, kernel, norm_gain, w_up],
        "vvvvvvvv",
        "hhhhhh",
        scratch=forward_scratch(shapes) + [pltpu.SemaphoreType.DMA((6,))],
        flops=2**27,
        moved=2**22,
        limit=12,
    )


LANES_BOTH = (((1,), (1,)), ((), ()))


def fetch_kernel(*refs):
    count = len(refs) // 2
    *pairs, sems = refs
    finish(copies(sems, 0, list(zip(pairs[:count], pairs[count:]))))


def fetched(values, first):
    values = after(values, first)
    return call(
        fetch_kernel,
        [jax.ShapeDtypeStruct(value.shape, value.dtype) for value in values],
        values,
        "h" * len(values),
        "v" * len(values),
        scratch=[pltpu.SemaphoreType.DMA((len(values),))],
        moved=2**19,
    )


def network_math(moved_ref, down_ref, up_ref, gain_ref, slope_ref, n_ref, inv_ref, out_ref, grad_ref, leave):
    leave("moved")
    moved = moved_ref[...].astype(jnp.float32).T
    grad_hidden = jnp.dot(moved.astype(jnp.bfloat16), down_ref[...], preferred_element_type=jnp.float32)
    grad_pre = (grad_hidden * slope_ref[...].astype(jnp.float32)).astype(jnp.bfloat16)
    grad_ref[...] = grad_pre
    leave("grad")
    grad_n = lax.dot_general(grad_pre, up_ref[...], LANES_BOTH, preferred_element_type=jnp.float32)
    narrow, gain = n_ref[...].astype(jnp.float32), gain_ref[...]
    mean = jnp.mean(grad_n * narrow, axis=1, keepdims=True)
    field = moved + inv_ref[:, :1] * (grad_n * gain - narrow * (mean / gain))
    out_ref[...] = field.T.astype(jnp.bfloat16)
    leave("field")


def network_kernel(moved_ref, down_ref, up_ref, gain_ref, slope_ref, n_ref, inv_ref, *refs):
    *goals, out_ref, grad_ref, sems = refs
    started = []
    names = ("field", "grad", "moved")
    leave = sender(sems, dict(zip(names, (out_ref, grad_ref, moved_ref))), dict(zip(names, goals)), started)
    network_math(moved_ref, down_ref, up_ref, gain_ref, slope_ref, n_ref, inv_ref, out_ref, grad_ref, leave)
    finish(started)


def first_kernel(step, *refs):
    (moved_ref, down_ref), places, refs = refs[:2], refs[2:10], refs[10:]
    goals, outs, (out_ref, grad_ref, sems) = refs[:7], refs[7:14], refs[14:]
    started = []
    names = ("n", "turned", "hid", "pad", "field", "grad", "moved")
    values = dict(zip(FORWARD, outs)) | {"field": out_ref, "grad": grad_ref, "moved": moved_ref}
    leave = sender(sems, values, dict(zip(names, goals)), started)
    forward_math(step, places, sems, leave, outs)
    n_ref, _, inv_ref, _, slope_ref = outs[:5]
    gain_ref, up_ref = places[6:]
    network_math(moved_ref, down_ref, up_ref, gain_ref, slope_ref, n_ref, inv_ref, out_ref, grad_ref, leave)
    finish(started)


def first_step(step, moved, w_down, states, around, kernel, norm_gain, w_up):
    shapes = forward_shapes(states, w_up)
    channels, count = moved.shape
    hid = w_down.shape[1]
    backs = [((channels, count), jnp.bfloat16), ((count, hid), jnp.bfloat16), ((channels, count), jnp.bfloat16)]
    results = [shapes[k] for k in (0, 1, 3, 5)] + backs
    return call(
        functools.partial(first_kernel, step),
        [jax.ShapeDtypeStruct(*shape) for shape in results],
        [moved, w_down, states, *around, kernel, norm_gain, w_up],
        "v" * 10,
        "h" * 7,
        scratch=forward_scratch(shapes) + [pltpu.VMEM(*shape) for shape in backs[:2]] + [pltpu.SemaphoreType.DMA((7,))],
        flops=2**28,
        moved=2**22,
        limit=16,
    )


def network_back(moved, w_down, w_up, norm_gain, slope, narrow, inv_root):
    channels, count = moved.shape
    hid = w_down.shape[1]
    shapes = [((channels, count), jnp.bfloat16), ((count, hid), jnp.bfloat16), ((channels, count), jnp.bfloat16)]
    return call(
        network_kernel,
        [jax.ShapeDtypeStruct(*shape) for shape in shapes],
        [moved, w_down, w_up, norm_gain, slope, narrow, inv_root],
        "vvvvvvv",
        "hhh",
        scratch=[pltpu.VMEM(*shape) for shape in shapes[:2]] + [pltpu.SemaphoreType.DMA((3,))],
        flops=4 * count * hid * channels,
        moved=4 * 2**20,
        limit=8,
    )


def stencil_sums(pad_ref, field, tile):
    rows_out, cols_out = tile
    field = field.reshape(rows_out, cols_out, -1)
    padded = pad_ref[...].astype(jnp.float32)
    result = [None] * 9
    for col_tap in range(3):
        place = MARGIN - 1 + col_tap
        shifted_cols = padded[:, place : place + cols_out]
        for row_tap in range(3):
            products = jnp.sum(shifted_cols[row_tap : row_tap + rows_out] * field, axis=0)
            result[3 * row_tap + col_tap] = jnp.sum(products, axis=0, keepdims=True)
    return result


def sums_rows(rows, term, gain):
    rows = rows + [jnp.sum(term, axis=0, keepdims=True) / gain, jnp.zeros((ROWS - 10, term.shape[1]), jnp.float32)]
    return jnp.concatenate(rows, axis=0)


def sums_kernel(steps, tile, up_ref, gain_ref, *refs):
    inputs, (out_ref, *refs) = refs[: 4 * steps], refs[4 * steps :]
    pads, fields, grads, narrows, sems = refs
    places = [(ref, place.at[k]) for k in range(steps) for ref, place in zip(inputs[4 * k : 4 * k + 4], refs[:4])]
    arriving = copies(sems, 0, places)
    rows, term = None, None
    for k in range(steps):
        finish(arriving[4 * k : 4 * k + 4])
        grad_n = lax.dot_general(grads[k], up_ref[...], LANES_BOTH, preferred_element_type=jnp.float32)
        product = grad_n * narrows[k].astype(jnp.float32)
        term = product if term is None else term + product
        more = stencil_sums(pads.at[k], fields[k].astype(jnp.float32).T, tile)
        rows = more if rows is None else [a + b for a, b in zip(rows, more)]
    out_ref[...] = sums_rows(rows, term, gain_ref[...])


def channel_sums(tile, w_up, norm_gain, pads, fields, grads, narrows):
    steps = len(fields)
    inputs = [value for group in zip(pads, fields, grads, narrows) for value in group]
    return call(
        functools.partial(sums_kernel, steps, tile),
        [jax.ShapeDtypeStruct((ROWS, fields[0].shape[0]), jnp.float32)],
        [w_up, norm_gain, *inputs],
        "vv" + "h" * 4 * steps,
        "v",
        scratch=[pltpu.VMEM((steps, *value.shape), value.dtype) for value in inputs[:4]]
        + [pltpu.SemaphoreType.DMA((4 * steps,))],
        moved=2**21,
        limit=12,
    )[0]


QUADRANTS = 4


def lon_bit(at):
    return lax.axis_index("lon") >> at & 1


def gradient_quadrants(left_ref, right_ref, send_ref, keep_ref):
    channels, width = left_ref.shape[0], right_ref.shape[1] // 2
    if keep_ref.ndim == 2:
        send_ref[:channels] = jnp.dot(left_ref[...], right_ref[...], preferred_element_type=jnp.float32).astype(jnp.bfloat16)
        keep_ref[...] = jnp.zeros_like(keep_ref)
        return
    size = channels // QUADRANTS
    groups = lax.axis_size("lon") // 4
    chunk = size // groups
    rows = []
    for core in (1 - lon_bit(0), lon_bit(0)):
        for x in range(2):
            for z in range(groups):
                start = pl.multiple_of((4 * z + 2 * x + core) * chunk, chunk)
                rows.append(left_ref[pl.ds(start, chunk)])
    rows = jnp.concatenate(rows, axis=0)
    value = jnp.dot(rows, right_ref[...], preferred_element_type=jnp.float32).astype(jnp.bfloat16)
    for q in range(QUADRANTS):
        x, lat = q // 2, q % 2
        columns = slice(lat * width, (lat + 1) * width)
        send_ref[q * size : (q + 1) * size] = value[x * size : (x + 1) * size, columns]
        keep_ref[q] = value[(2 + x) * size : (3 + x) * size, columns]


def quadrant_shapes(channels, hid, sums):
    if lax.axis_size("lat") != 2 or lax.axis_size("lon") != 16:
        return (channels, hid), (8, 128)
    return (channels + SUM_ROWS * sums, hid // 2), (QUADRANTS, channels // QUADRANTS, hid // 2)


def side_by_side(refs, goal_ref, axis):
    size = refs[0].shape[axis]
    places = [pl.ds(s * size, size) for s in range(len(refs))]
    return [(ref, goal_ref.at[:, place] if axis else goal_ref.at[place]) for ref, place in zip(refs, places)]


def last_kernel(steps, tile, moved_ref, down_ref, up_ref, gain_ref, sums_ref, *refs):
    slope_ref, n_ref, inv_ref, pad_ref, *refs = refs
    inputs, hidden, refs = refs[: 2 * steps - 1], refs[2 * steps - 1 : 3 * steps - 1], refs[3 * steps - 1 :]
    field_ref, total_ref, send_ref, keep_ref, hidden_ref, left_ref, right_ref, sems = refs
    count = slope_ref.shape[0]
    pairs = side_by_side(inputs[:steps], left_ref, 1) + side_by_side(inputs[steps:], right_ref, 0)
    later = copies(sems, 0, pairs)
    last = copies(sems, len(pairs), side_by_side(hidden, hidden_ref, 0))
    moved = moved_ref[...].astype(jnp.float32).T
    grad_hidden = jnp.dot(moved.astype(jnp.bfloat16), down_ref[...], preferred_element_type=jnp.float32)
    grad_pre = (grad_hidden * slope_ref[...].astype(jnp.float32)).astype(jnp.bfloat16)
    right_ref[(steps - 1) * count :] = grad_pre
    grad_n = lax.dot_general(grad_pre, up_ref[...], LANES_BOTH, preferred_element_type=jnp.float32)
    narrow, gain = n_ref[...].astype(jnp.float32), gain_ref[...]
    term = grad_n * narrow
    mean = jnp.mean(term, axis=1, keepdims=True)
    field = moved + inv_ref[:, :1] * (grad_n * gain - narrow * (mean / gain))
    field = field.astype(jnp.bfloat16)
    field_ref[...] = field
    total = sums_ref[...] + sums_rows(stencil_sums(pad_ref, field.astype(jnp.float32), tile), term, gain)
    total_ref[...] = total
    finish(later)
    gradient_quadrants(left_ref, right_ref, send_ref, keep_ref)
    if keep_ref.ndim > 2:
        send_ref[left_ref.shape[0] :] = pieces_of(total)
    finish(last)


def last_step(tile, moved, w_down, w_up, norm_gain, sums, near, turned, grads, hidden):
    steps = len(turned)
    channels, count = moved.shape
    hid = w_down.shape[1]
    send, keep = quadrant_shapes(channels, hid, 1)
    sds = jax.ShapeDtypeStruct
    inputs = turned + grads + hidden
    return call(
        functools.partial(last_kernel, steps, tile),
        [
            sds((count, channels), jnp.bfloat16),
            sds((ROWS, channels), jnp.float32),
            sds(send, jnp.bfloat16),
            sds(keep, jnp.bfloat16),
            sds((steps * count, hid), jnp.bfloat16),
        ],
        [moved, w_down, w_up, norm_gain, sums, *near, *inputs],
        "v" * 9 + "h" * len(inputs),
        "vpppv",
        scratch=[pltpu.VMEM((channels, steps * count), jnp.bfloat16), pltpu.VMEM((steps * count, hid), jnp.bfloat16)]
        + [pltpu.SemaphoreType.DMA((len(inputs),))],
        flops=2**30,
        moved=6 * 2**20,
        limit=20,
    )


def down_kernel(steps, moved_ref, right_ref, *refs):
    inputs, (send_ref, keep_ref, left_ref, sems) = refs[: steps - 1], refs[steps - 1 :]
    count = moved_ref.shape[1]
    arriving = copies(sems, 0, side_by_side(inputs, left_ref, 1))
    left_ref[:, (steps - 1) * count :] = moved_ref[...]
    finish(arriving)
    gradient_quadrants(left_ref, right_ref, send_ref, keep_ref)


def down_gradients(moved, moveds, hidden):
    steps = 1 + len(moveds)
    channels, count = moved.shape
    hid = hidden.shape[1]
    return call(
        functools.partial(down_kernel, steps),
        [jax.ShapeDtypeStruct(shape, jnp.bfloat16) for shape in quadrant_shapes(channels, hid, 0)],
        [moved, hidden, *moveds],
        "vv" + "h" * len(moveds),
        "pp",
        scratch=[pltpu.VMEM((channels, steps * count), jnp.bfloat16), pltpu.SemaphoreType.DMA((len(moveds),))],
        flops=2**29,
        moved=2**21,
        limit=16,
    )


def fill_margins(wide_ref, before, after, low, high, middle):
    rows_out, cols_out, _ = middle.shape
    around = slice(MARGIN - 1, MARGIN + cols_out + 1)
    wide_ref[:1, around] = low.astype(jnp.float32)
    wide_ref[1 + rows_out :, around] = high.astype(jnp.float32)
    wide_ref[1 : 1 + rows_out, MARGIN - 1 : MARGIN] = before.astype(jnp.float32)
    wide_ref[1 : 1 + rows_out, MARGIN + cols_out : MARGIN + cols_out + 1] = after.astype(jnp.float32)
    wide_ref[1 : 1 + rows_out, MARGIN : MARGIN + cols_out] = middle


def final_kernel(field_ref, before_ref, after_ref, low_ref, high_ref, kernel_ref, out_ref, wide_ref):
    rows_out, cols_out, _ = field_ref.shape
    result = field_ref[...].astype(jnp.float32)
    fill_margins(wide_ref, before_ref[0], after_ref[0], low_ref[0], high_ref[0], result)
    for col_tap in range(3):
        place = MARGIN + 1 - col_tap
        shifted_cols = wide_ref[:, place : place + cols_out]
        for row_tap in range(3):
            tap = kernel_ref[row_tap, col_tap : col_tap + 1]
            result = result + tap[None] * shifted_cols[2 - row_tap : 2 - row_tap + rows_out]
    out_ref[...] = result.astype(jnp.bfloat16)


def final_parts(field, around, kernel):
    rows_out, cols_out, channels = field.shape
    return call(
        final_kernel,
        [jax.ShapeDtypeStruct(field.shape, jnp.bfloat16)],
        [field, *around, kernel],
        "v" * 6,
        "v",
        scratch=[pltpu.VMEM((rows_out + 2, cols_out + 2 * MARGIN, channels), jnp.float32)],
        moved=2**19,
    )[0]


def spatial_kernel(mode, step, near_lon, near_lat, *refs):
    refs = list(refs)
    take = lambda: refs.pop(0)
    with_stencil = mode != "first"
    move_ref = take()
    in_ref = take()
    kern_ref = take() if with_stencil else None
    weight_ref = take() if mode == "mid" else None
    out_hbm = take()
    saved_hbm = take() if mode == "first" else None
    out_ref, sems = take(), take()
    spread_ref = take()
    weight_ref = take() if mode == "first" else weight_ref
    tiles_lon, tiles_lat, _, lanes = in_ref.shape
    rows = out_ref.shape[2]
    started = []
    if mode == "first":
        weight_ref[...] = in_ref[:, :, rows:]
        started += copies(sems, 0, [(weight_ref, saved_hbm)])
    lane = lax.broadcasted_iota(jnp.int32, (rows, lanes), 1)
    col = lax.rem(lane, near_lat)
    lat_last, lat_first = col == near_lat - 1, col == 0
    lon_last, lon_first = lane >= lanes - near_lat, lane < near_lat
    tiles = [(a, b) for a in range(tiles_lon) for b in range(tiles_lat)]

    def turn(value, steps):
        return pltpu.roll(value, steps % lanes if isinstance(steps, int) else steps, 1)

    def lat_after(grid):
        turned = {key: turn(value, -1) for key, value in grid.items()}
        wrapped = {key: turn(grid[key], near_lat - 1) for key in tiles if key[1] > 0}
        return {(a, b): jnp.where(lat_last, wrapped.get((a, b + 1), 0.0), turned[a, b]) for a, b in tiles}

    def lat_before(grid):
        turned = {key: turn(value, 1) for key, value in grid.items()}
        wrapped = {key: turn(grid[key], 1 - near_lat) for key in tiles if key[1] < tiles_lat - 1}
        return {(a, b): jnp.where(lat_first, wrapped.get((a, b - 1), 0.0), turned[a, b]) for a, b in tiles}

    def lon_after(grid):
        return {
            (a, b): turn(jnp.where(lon_first, grid[(a + 1) % tiles_lon, b], grid[a, b]), -near_lat) for a, b in tiles
        }

    def lon_before(grid):
        return {(a, b): turn(jnp.where(lon_last, grid[(a - 1) % tiles_lon, b], grid[a, b]), near_lat) for a, b in tiles}

    grid = {(a, b): in_ref[a, b, :rows].astype(jnp.float32) for a, b in tiles}
    if with_stencil:
        taps = [
            [jnp.broadcast_to(kern_ref[:, 3 * a + b : 3 * a + b + 1], (rows, lanes)) for b in range(3)] for a in range(3)
        ]
        by_col = [lat_after(grid), grid, lat_before(grid)]
        mix = [
            {key: sum(taps[row][c] * by_col[c][key] for c in range(1, 3)) + taps[row][0] * by_col[0][key] for key in tiles}
            for row in range(3)
        ]
        high, low = lon_after(mix[0]), lon_before(mix[2])
        grid = {key: grid[key] + mix[1][key] + (high[key] + low[key]) for key in tiles}
    if mode == "mid":
        grid = {key: value.astype(jnp.bfloat16).astype(jnp.float32) for key, value in grid.items()}
    weights = {}
    for a, b in tiles:
        four = weight_ref[a, b].astype(jnp.float32)[4 * step : 4 * step + 4]
        weights[a, b] = [jnp.broadcast_to(four[k : k + 1], (rows, lanes)) for k in range(4)]
    weighted = [{key: weights[key][k] * grid[key] for key in tiles} for k in range(4)]
    own, lon = lat_after(weighted[2]), lat_after(weighted[3])
    lon = lon_after({key: weighted[1][key] + lon[key] for key in tiles})
    for a, b in tiles:
        value = (weighted[0][a, b] + own[a, b] + lon[a, b]).astype(jnp.bfloat16).astype(jnp.float32)
        for place in range(a, tiles_lon + LON_REACH, tiles_lon):
            spread_ref[place, b] = value
    spread_ref[:, tiles_lat:] = jnp.zeros((tiles_lon + LON_REACH, LAT_REACH, rows, lanes), jnp.float32)

    lon_move, lat_move = (jnp.max(move_ref[2 * step + k : 2 * step + k + 1]) for k in range(2))
    far_lon, off_lon = lon_move // near_lon, lax.rem(lon_move, near_lon)
    far_lat, off_lat = lat_move // near_lat, lax.rem(lat_move, near_lat)
    shift = off_lon * near_lat + off_lat
    turn_here = lax.rem(2 * lanes - shift, lanes)
    turn_next = lax.rem(2 * lanes - shift + near_lat, lanes)
    same_lon = lane >= off_lon * near_lat
    same_lat = col + off_lat < near_lat
    half = tiles_lon // 2
    for a in range(tiles_lon):
        met = [
            jnp.where(same_lon, spread_ref[far_lon + a, far_lat + b], spread_ref[far_lon + a + 1, far_lat + b])
            for b in range(tiles_lat + 1)
        ]
        for b in range(tiles_lat):
            value = jnp.where(same_lat, turn(met[b], turn_here), turn(met[b + 1], turn_next))
            out_ref[a, b] = value.astype(jnp.bfloat16)
        if (a + 1) % half == 0:
            part = pl.ds(a + 1 - half, half)
            started += copies(sems, 1 + a // half, [(out_ref.at[part], out_hbm.at[part])])
    finish(started)


def spatial(mode, step, tile, rows, field, kern, weights, moves):
    tiles_lon, tiles_lat, _, lanes = field.shape
    with_stencil = mode != "first"
    operands = [moves, field]
    operands += [kern] if with_stencil else []
    operands += [weights] if mode == "mid" else []
    out_shape = (tiles_lon, tiles_lat, rows, lanes)
    weight_shape = (tiles_lon, tiles_lat, ROWS, lanes)
    sds = jax.ShapeDtypeStruct
    out = [sds(out_shape, jnp.bfloat16)] + ([sds(weight_shape, jnp.bfloat16)] if mode == "first" else [])
    scratch = [pltpu.VMEM(out_shape, jnp.bfloat16), pltpu.SemaphoreType.DMA((4,))]
    spread_shape = (tiles_lon + LON_REACH, tiles_lat + LAT_REACH, rows, lanes)
    scratch += [pltpu.VMEM(spread_shape, jnp.float32)]
    scratch += [pltpu.VMEM(weight_shape, jnp.bfloat16)] * (mode == "first")
    return call(
        functools.partial(spatial_kernel, mode, step, *tile),
        out,
        operands,
        "vv" + "v" * with_stencil + "v" * (mode == "mid"),
        "h" * len(out),
        scratch=scratch,
        flops=2**22,
        moved=2**20,
        limit=max(8, 14 * tiles_lon * tiles_lat * rows * lanes * 4 // MIB),
    )


def halved(value, axis, bit, dim):
    count = lax.axis_size(axis)
    mine = lax.axis_index(axis) >> bit & 1
    kept = lax.dynamic_index_in_dim(value, mine, dim, keepdims=False)
    sent = lax.dynamic_index_in_dim(value, 1 - mine, dim, keepdims=False).astype(jnp.bfloat16)
    arrived = lax.ppermute(sent, axis, [(i, i ^ (1 << bit)) for i in range(count)])
    return kept + arrived.astype(jnp.float32)


def scattered(value, lat_first):
    channels, hid = value.shape
    lon_bits = lax.axis_size("lon").bit_length() - 1
    lat_bits = lax.axis_size("lat").bit_length() - 1
    rows = channels >> lon_bits
    value = value.reshape(*([2] * lon_bits), rows, *([2] * lat_bits), hid >> lat_bits)

    def over_lon(value, bit, left):
        return halved(value, "lon", bit, left.index(bit)), [k for k in left if k != bit]

    left_lon = list(range(lon_bits))[::-1]
    left_lat = list(range(lat_bits))[::-1]
    order = [("lon", 0), ("lon", 1)] + [("lat", k) for k in range(lat_bits)]
    if lat_first:
        order = [("lon", 0)] + [("lat", k) for k in range(lat_bits)] + [("lon", 1)]
    order += [("lon", k) for k in range(2, lon_bits)]
    for axis, bit in order:
        if axis == "lon":
            value, left_lon = over_lon(value, bit, left_lon)
        else:
            value = halved(value, "lat", bit, len(left_lon) + 1 + left_lat.index(bit))
            left_lat.remove(bit)
    return value


def add_parts(pairs, kept, arrived):
    for q, out_ref, place in pairs:
        value = kept(q).astype(jnp.float32) + arrived(q).astype(jnp.float32)
        out_ref[place] = value.astype(out_ref.dtype)


def first_axis(flip):
    core = lon_bit(0)
    return 1 - core if flip else core


def quadrant_kernel(flip, *refs):
    kept_ref, *total_refs, arrived_ref, send_ref, keep_ref = refs[: 4 + len(refs) // 6]
    axis, x, lat = first_axis(flip), lon_bit(1), lax.axis_index("lat")
    rows = kept_ref.shape[1]
    for j in range(2):
        kept = (1 - axis) * (2 * x + j) + axis * (2 * j + lat)
        sent = (1 - axis) * (2 * (1 - x) + j) + axis * (2 * j + 1 - lat)
        pairs = [(sent, send_ref, pl.ds(j * rows, rows)), (kept, keep_ref, j)]
        arrived = lambda q: arrived_ref[pl.ds(pl.multiple_of(q * rows, rows), rows)]
        add_parts(pairs, lambda q: kept_ref[q], arrived)
    if total_refs:
        chip = total_refs[0][...] + whole_of(arrived_ref[QUADRANTS * rows :])
        refs[-1][...] = chip
        send_ref[2 * rows :] = pieces_of(chip)


def half_kernel(flip, *refs):
    kept_ref, *total_refs, arrived_ref, send_ref, keep_ref = refs[: 4 + len(refs) // 6]
    axis, x, lat = first_axis(flip), lon_bit(1), lax.axis_index("lat")
    mine = (1 - axis) * lat + axis * x
    rows = kept_ref.shape[1]
    pairs = [(1 - mine, send_ref, pl.ds(0, rows)), (mine, keep_ref, slice(None))]
    arrived = lambda q: arrived_ref[pl.ds(pl.multiple_of(q * rows, rows), rows)]
    add_parts(pairs, lambda q: kept_ref[q], arrived)
    if total_refs:
        beside = arrived_ref[2 * rows :]
        refs[-1][...] = whole_of(beside)
        send_ref[rows : rows + SUM_ROWS] = pieces_of(total_refs[0][...])
        send_ref[rows + SUM_ROWS :] = beside


def rows_kernel(groups, bit_at, totals, *refs):
    kept_ref, *refs = refs
    total_refs, (arrived_ref, send_ref, keep_ref, *total_ref) = refs[:totals], refs[totals:]
    bit = lon_bit(bit_at)
    rows = kept_ref.shape[0]
    chunk = rows // (2 * groups)
    for p in range(groups):
        goal = pl.ds(p * chunk, chunk)
        places = [pl.multiple_of((2 * p + which) * chunk, chunk) for which in (1 - bit, bit)]
        pairs = [(places[0], send_ref, goal), (places[1], keep_ref, goal)]
        add_parts(pairs, lambda q: kept_ref[pl.ds(q, chunk)], lambda q: arrived_ref[pl.ds(q, chunk)])
    if totals:
        total = add_sums(total_refs, arrived_ref, rows)
        total_ref[0][...] = total
        send_ref[rows // 2 :] = pieces_of(total)


def add_sums(total_refs, arrived_ref, start):
    arrived = whole_of(arrived_ref[start : start + SUM_ROWS])
    if len(total_refs) == 1:
        return total_refs[0][...] + arrived
    chip, beside = (ref[...] for ref in total_refs)
    return (chip + whole_of(arrived_ref[start + SUM_ROWS :])) + (beside + arrived)


def finish_kernel(kept_ref, total_ref, arrived_ref, kept_down_ref, arrived_down_ref, *refs):
    *goals, up_ref, down_ref, taps_ref, gain_ref, sems = refs
    rows = kept_ref.shape[0]
    total = add_sums([total_ref], arrived_ref, rows)
    for k in range(9):
        taps_ref[k // 3, k % 3 : k % 3 + 1] = total[k : k + 1]
    gain_ref[...] = total[9:10]
    up_ref[...] = kept_ref[...] + arrived_ref[:rows].astype(jnp.float32)
    down_ref[...] = kept_down_ref[...] + arrived_down_ref[...].astype(jnp.float32)
    finish(copies(sems, 0, list(zip((up_ref, down_ref, taps_ref, gain_ref), goals))))


def halving(flip, send, keep, total):
    lon, lat = lax.axis_size("lon"), lax.axis_size("lat")
    places = [(i, j) for i in range(lon) for j in range(lat)]
    flat = lambda i, j: i * lat + j
    along_lat = lambda i: (i & 1) != flip
    sds = jax.ShapeDtypeStruct
    rows, width = keep.shape[1:]
    sums = [] if total is None else [total]
    with_sums = len(sums)
    plan = [
        (lambda i, j: (i ^ 1, j), functools.partial(quadrant_kernel, flip), (2, rows, width), 1),
        (
            lambda i, j: (i, j ^ 1) if along_lat(i) else (i ^ 2, j),
            functools.partial(half_kernel, flip),
            (rows, width),
            2,
        ),
        (
            lambda i, j: (i ^ 2, j) if along_lat(i) else (i, j ^ 1),
            functools.partial(rows_kernel, 2, 2, 2 * with_sums),
            (rows // 2, width),
            1,
        ),
        (lambda i, j: (i ^ 4, j), functools.partial(rows_kernel, 1, 3, with_sums), (rows // 4, width), 1),
    ]
    for at, (partner, kernel, shape, parts) in enumerate(plan):
        send = yield send
        arrived = lax.ppermute(send, AXES, [(flat(i, j), flat(*partner(i, j))) for i, j in places])
        arrived = yield arrived
        sent = shape[-2] * (shape[0] if len(shape) == 3 else 1) + SUM_ROWS * parts * with_sums
        out = [sds((sent, shape[-1]), jnp.bfloat16), sds(shape, jnp.float32)]
        out += [sds(value.shape, jnp.float32) for value in sums[:1]]
        operands = [keep, *sums, arrived]
        send, keep, *more = call(kernel, out, operands, "v" * len(operands), "p" * len(out), moved=2**19, limit=12)
        sums = sums + more if at == 1 else more
    send = yield send
    arrived = lax.ppermute(send, AXES, [(flat(i, j), flat(i ^ 8, j)) for i, j in places])
    yield (keep, *sums, arrived)


def all_sums(up, down, total, field, kernel):
    channels = total.shape[1]
    field = field[None]
    if up[1].ndim == 2:
        parts = [scattered(send.astype(jnp.float32), flip) for flip, (send, _) in enumerate((up, down))]
        total = lax.psum(total, AXES)
        around = lat_edges(field)
        state = final_parts(field[0], (*around, *lon_edges(field, *around)), kernel)
        return (state, *parts, total[:9].reshape(3, 3, channels), total[9])
    ahead, behind = halving(False, *up, total), halving(True, *down, None)
    send, later = next(ahead), next(behind)
    arrived = ahead.send(send)
    send = ahead.send(after(arrived, later))
    field = after(field, send)
    arrived_later = behind.send(after(later, send))
    later = behind.send(arrived_later)
    for at in range(1, 4):
        arrived = ahead.send(send)
        arrived_later = behind.send(later)
        send = ahead.send(after(arrived, later))
        later = behind.send(arrived_later)
        if at == 1:
            around = lat_edges(field, lambda value: after(value, send))
            state = final_parts(field[0], (*around, *lon_edges(field, *around)), kernel)
    final_ahead = ahead.send(send)
    final_behind = behind.send(later)
    sds = jax.ShapeDtypeStruct
    part = sds(final_ahead[0].shape, jnp.float32)
    out = [part, part, sds((3, 3, channels), jnp.float32), sds((1, channels), jnp.float32)]
    up, down, taps, gain = call(
        finish_kernel,
        out,
        [*final_ahead, *final_behind],
        "vvvvv",
        "hhhh",
        scratch=[pltpu.VMEM(value.shape, value.dtype) for value in out] + [pltpu.SemaphoreType.DMA((4,))],
        moved=2**18,
    )
    return state, up, down, taps, gain.reshape(channels)


def local(cotangent, states, w_up, w_down, norm_gain, kernel, bilinear, lon_move, lat_move):
    steps, rows_out, cols_out, channels = states.shape
    tiles_lon, tiles_lat = lax.axis_size("lon"), lax.axis_size("lat")
    devices = tiles_lon * tiles_lat
    count = rows_out * cols_out
    tile = (rows_out, cols_out)
    share = channels // devices
    padded_share = -(-share // ROWS) * ROWS
    whole_share = share == padded_share
    group_size = channels // lon_move.shape[1]
    me = lax.axis_index("lon") * tiles_lat + lax.axis_index("lat")

    def as_blocks(value):
        value = value.reshape(devices, share, count)
        return value if whole_share else jnp.pad(value, ((0, 0), (0, padded_share - share), (0, 0)))

    def as_rows(blocks):
        return blocks[:, :share].reshape(channels, count)

    def as_grid(blocks):
        return blocks.reshape(tiles_lon, tiles_lat, *blocks.shape[1:])

    blocks = packed(cotangent, bilinear, devices)
    blocks, states_later = lax.optimization_barrier((blocks, states))
    arrived = as_grid(exchanged(blocks))
    group = me * share // group_size
    moves = jnp.stack([lon_move[:, group], lat_move[:, group]], axis=1).reshape(2 * steps, 1)
    moves = jnp.broadcast_to(jnp.pad(moves, ((0, -2 * steps % 8), (0, 0))), (-(-2 * steps // 8) * 8, 128))
    grid_now, weights = spatial("first", steps - 1, tile, padded_share, arrived, None, None, moves)

    taps = lax.dynamic_slice_in_dim(kernel.reshape(9, channels), me * share, share, 1).T
    taps = jnp.pad(taps, ((0, padded_share - share), (0, count - 9)))

    around = lat_edges(states_later)
    around = (*around, *lon_edges(states, *around))
    order = list(reversed(range(steps)))
    gain = norm_gain.reshape(1, channels)
    forward = {s: forward_parts(s, states, around, kernel, gain, w_up) for s in order}
    names = {k: {s: forward[s][at] for s in order} for at, k in enumerate(FORWARD)}

    def taken_back(grid):
        return as_rows(exchanged(grid.reshape(devices, padded_share, count)))

    def spread_on(s, field, grid_kernel=taps):
        (near,) = fetched([weights], field)
        arrived = after(as_grid(exchanged(as_blocks(field))), near)
        return spatial("mid", s, tile, padded_share, arrived, grid_kernel, near, moves)[0]

    fields, grads, moved = {}, {}, {}
    for s in order:
        if s != order[0]:
            grid_now = spread_on(s, fields[s + 1])
        here = taken_back(grid_now)
        wanted = ("slope", "n", "inv") + ("pad",) * (s == order[-1])
        near = fetched([names[k][s] for k in wanted], grid_now)
        if s == order[-1]:
            break
        here = after(here, (near, forward) if s != order[0] else near)
        fields[s], grads[s], moved[s] = network_back(here, w_down, w_up, gain, *near)

    earlier = lambda values: [values[s] for s in order[:-1]]
    all_of = lambda values: [values[s] for s in order]
    sums = channel_sums(tile, w_up, gain, *map(earlier, (names["pad"], fields, grads, names["n"])))
    here = after(here, (near, sums))
    parts = (all_of(names["turned"]), earlier(grads), all_of(names["hid"]))
    field, total, send, keep, hidden = last_step(tile, here, w_down, w_up, gain, sums, near, *parts)
    down = down_gradients(here, earlier(moved), hidden)
    field = field.reshape(cotangent.shape)
    return all_sums((send, keep), down, total, field, kernel)


def solution(mesh):
    placed = (
        P("lon", "lat", None),
        P(None, "lon", "lat", None),
        P(),
        P(),
        P(),
        P(),
        P(None, None, "lon", "lat"),
        P(),
        P(),
    )
    return jax.shard_map(
        local,
        mesh=mesh,
        in_specs=placed,
        out_specs=(P("lon", "lat", None), P("lon", "lat"), P("lon", "lat"), P(), P()),
        check_vma=False,
    )
```
